32 devices in a mesh: frame: 4 (over y, x), pos: 8 (over z, core).
Axes of the slice: x: 2, y: 2, z: 4, core: 2. Of those that a mesh axis runs over, the one named last changes fastest.
Arguments:
- tokens: bfloat16 [4, 48, 56, 768], P(None, 'frame', 'pos'), may hold values from -6 to 6
- class_tokens: bfloat16 [4, 3, 768], replicated, may hold values from -6 to 6
- clip_frames: int32 [4, 3], replicated, may hold values from 5 to 38, as said below
- cotangent: bfloat16 [4, 48, 56, 768], P(None, 'frame', 'pos'), may hold values from -6 to 6
- temporal_qkv: bfloat16 [768, 2304], P(('frame', 'pos')), may hold values from -0.21875 to 0.21875
- temporal_proj: bfloat16 [768, 768], P(('frame', 'pos')), may hold values from -1.25 to 1.25
- temporal_fc: bfloat16 [768, 768], P(('frame', 'pos')), may hold values from -0.21875 to 0.21875
- spatial_qkv: bfloat16 [768, 2304], P(('frame', 'pos')), may hold values from -0.21875 to 0.21875
- spatial_proj: bfloat16 [768, 768], P(('frame', 'pos')), may hold values from -1.75 to 1.75
- mlp_in: bfloat16 [768, 3072], P(('frame', 'pos')), may hold values from -0.21875 to 0.21875
- mlp_out: bfloat16 [3072, 768], P(('frame', 'pos')), may hold values from -0.109375 to 0.109375
- mlp_in_bias: bfloat16 [3072], P(('frame', 'pos')), may hold values from -2 to 2
- norm_gains: bfloat16 [768, 3], P(('frame', 'pos')), may hold values from 0.5 to 1.5
- norm_shifts: bfloat16 [768, 3], P(('frame', 'pos')), may hold values from -1.1953125 to 1.1953125
- biases: bfloat16 [768, 8], P(('frame', 'pos')), may hold values from -1.1953125 to 1.1953125
Outputs:
- block_out: bfloat16 [4, 48, 56, 768], P(None, 'frame', 'pos')
- tokens_grad: float32 [4, 48, 56, 768], P(None, 'frame', 'pos')
- class_grad: float32 [4, 3, 768], replicated
- grad_temporal_qkv: float32 [768, 2304], P(('frame', 'pos'))
- grad_temporal_proj: float32 [768, 768], P(('frame', 'pos'))
- grad_temporal_fc: float32 [768, 768], P(('frame', 'pos'))
- grad_spatial_qkv: float32 [768, 2304], P(('frame', 'pos'))
- grad_spatial_proj: float32 [768, 768], P(('frame', 'pos'))
- grad_mlp_in: float32 [768, 3072], P(('frame', 'pos'))
- grad_mlp_out: float32 [3072, 768], P(('frame', 'pos'))
- grad_mlp_in_bias: float32 [3072], P(('frame', 'pos'))
- grad_norm_gains: float32 [768, 3], P(('frame', 'pos'))
- grad_norm_shifts: float32 [768, 3], P(('frame', 'pos'))
- grad_biases: float32 [768, 8], P(('frame', 'pos'))
The draws below stay inside these ranges and needn't reach their ends.
Inputs may be any that keep to these rules, and one draw needn't show every extreme that they name: `clip_frames`: in each micro-batch the 3 counts add up to 48; clips lie end to end from frame 0, and one clip of each micro-batch holds frames among the first 12 and among the last 12.
All inputs are finite; a program needn't handle non-finite values.
Results may differ from the reference program's by a relative error of at most 0.02.
Values may be sent and summed in bfloat16 or wider, within the bound.
No kernel may reach another device: no remote copies, remote signals or barrier semaphores. Data moves between devices by JAX's collectives and lax.ppermute only.
A program may use at most 448 MiB of HBM per device.

```python
import jax
import jax.numpy as jnp
from jax import lax

D = 768
HEADS = 12
HEAD = 64
FF = 3072
FR_DEV = 12
MB = 4
CLIPS = 3
FRAMES = 48
POS = 56
SHORT_MIN = 5


def draw_clip_frames(key, part):
    key = jax.random.fold_in(key, 7)
    key_short, key_long = jax.random.split(key)
    short_most = max(SHORT_MIN, (FR_DEV - 1) // (CLIPS - 1))
    shorts = jax.random.randint(key_short, (MB, CLIPS - 1), SHORT_MIN, short_most + 1).astype(jnp.int32)
    first_batch = jnp.arange(MB, dtype=jnp.int32)[:, None] == 0
    shorts = jnp.where(first_batch, jnp.full_like(shorts, SHORT_MIN), shorts).astype(jnp.int32)
    long_slot = jax.random.randint(key_long, (MB, 1), 0, CLIPS).astype(jnp.int32)
    slot_index = jnp.arange(CLIPS, dtype=jnp.int32)[None, :]
    filler = jnp.zeros((MB, 1), jnp.int32)
    before = jnp.concatenate([shorts, filler], axis=1)
    after = jnp.concatenate([filler, shorts], axis=1)
    long_count = FRAMES - jnp.sum(shorts, axis=1, keepdims=True)
    return jnp.where(slot_index < long_slot, before, jnp.where(slot_index == long_slot, long_count, after)).astype(jnp.int32)


def block_levels(stream_key, dims, shards, low, high):
    def one(dim, shards_of):
        draws = jax.random.uniform(jax.random.fold_in(jax.random.fold_in(stream_key, 6), dim), (shards_of,), jnp.float32, low / len(shards), high / len(shards))
        return jnp.repeat(jnp.exp(draws), dims[dim] // shards_of).reshape((-1,) + (1,) * (len(dims) - dim - 1))

    gain = one(*shards[0])
    for cut in shards[1:]:
        gain = gain * one(*cut)
    return gain


def gaussian(rng, shape, scale, most, cuts=(), kind=jnp.bfloat16):
    values = jax.random.normal(rng, shape, jnp.float32) * scale
    if len(cuts) > 0:
        values = block_levels(rng, shape, cuts, -0.22, 0.18) * values
    return jnp.clip(values, min=-most, max=most).astype(kind)


def setup_inputs(seed: int = 0) -> dict:
    key_list = jax.random.split(jax.random.key(seed), 16)
    tokens = gaussian(key_list[0], (MB, FRAMES, POS, D), 1.0, 6.0, ((1, 4), (2, 8)))
    class_tokens = gaussian(key_list[1], (MB, CLIPS, D), 1.0, 6.0)
    clip_frames = draw_clip_frames(jax.random.fold_in(key_list[15], 71), 0)
    cotangent = gaussian(key_list[3], (MB, FRAMES, POS, D), 1.0, 6.0, ((1, 4), (2, 8)))
    temporal_qkv = gaussian(key_list[4], (D, 3 * D), D ** -0.5, 0.21875, ((0, 32),))
    temporal_proj = gaussian(key_list[5], (D, D), (D // 32) ** -0.5, 1.25, ((0, 32),))
    temporal_fc = gaussian(key_list[6], (D, D), D ** -0.5, 0.21875, ((0, 32),))
    spatial_qkv = gaussian(key_list[7], (D, 3 * D), D ** -0.5, 0.21875, ((0, 32),))
    spatial_proj = gaussian(key_list[8], (D, D), (D // 64) ** -0.5, 1.75, ((0, 32),))
    mlp_in = gaussian(key_list[9], (D, FF), D ** -0.5, 0.21875, ((0, 32),))
    mlp_out = gaussian(key_list[10], (FF, D), FF ** -0.5, 0.109375, ((0, 32),))
    mlp_in_bias = gaussian(key_list[11], (FF,), 0.3, 2.0, ((0, 32),))
    norm_gains = jnp.clip(1.0 + 0.1 * jax.random.normal(key_list[12], (D, 3), jnp.float32), 0.5, 1.5).astype(jnp.bfloat16)
    norm_shifts = gaussian(key_list[13], (D, 3), 0.2, 1.1953125, ((0, 32),))
    biases = gaussian(key_list[14], (D, 8), 0.2, 1.1953125, ((0, 32),))
    return dict(tokens=tokens, class_tokens=class_tokens, clip_frames=clip_frames, cotangent=cotangent, temporal_qkv=temporal_qkv, temporal_proj=temporal_proj, temporal_fc=temporal_fc, spatial_qkv=spatial_qkv, spatial_proj=spatial_proj, mlp_in=mlp_in, mlp_out=mlp_out, mlp_in_bias=mlp_in_bias, norm_gains=norm_gains, norm_shifts=norm_shifts, biases=biases)


HIGHEST = lax.Precision.HIGHEST

@jax.custom_vjp
def low(v):
    return lax.optimization_barrier(v.astype(jnp.bfloat16)).astype(jnp.float32)

@jax.custom_vjp
def low_back(v):
    return v

def low_keep(v):
    return (low(v), None)

def low_pass(kept, grad):
    return (grad,)

def back_keep(v):
    return (v, None)

def back_low(kept, grad):
    return (low(grad),)
low.defvjp(low_keep, low_pass)
low_back.defvjp(back_keep, back_low)

def layer_norm(values, gain_vec, shift_vec):
    centred = values - lax.optimization_barrier(jnp.mean(values, axis=-1, keepdims=True))
    spread = lax.optimization_barrier(jnp.mean(centred * centred, axis=-1, keepdims=True))
    return centred * lax.rsqrt(spread + 1e-06) * gain_vec + shift_vec

def project(values, matrix):
    return jnp.einsum('...d,de->...e', values, matrix, precision=HIGHEST)

def frame_clips(counts):
    clip_ends = jnp.cumsum(counts).astype(jnp.int32)
    frame_ids = jnp.arange(FRAMES, dtype=jnp.int32)
    return lax.optimization_barrier(jnp.sum((frame_ids[:, None] >= clip_ends[None, :]).astype(jnp.int32), axis=1)).astype(jnp.int32)

def temporal_attention(queries, keys, values, clip_of):
    scores = jnp.einsum('fphe,gphe->phfg', queries, keys, precision=HIGHEST) * 0.125
    scores = low_back(scores)
    same_clip = clip_of[:, None] == clip_of[None, :]
    scores = jnp.where(same_clip[None, None], scores, -1000000000.0)
    top_score = lax.optimization_barrier(jnp.max(scores, axis=-1, keepdims=True))
    exp_score = jnp.exp(scores - top_score)
    prob_time = low(exp_score / lax.optimization_barrier(jnp.sum(exp_score, axis=-1, keepdims=True)))
    return jnp.einsum('phfg,gphe->fphe', prob_time, values, precision=HIGHEST)

def spatial_attention(queries, keys, values, class_keys, class_values):
    patch_score = low_back(jnp.einsum('fphe,fqhe->fhpq', queries, keys, precision=HIGHEST) * 0.125)
    class_score = low_back(jnp.einsum('fphe,fhe->fhp', queries, class_keys, precision=HIGHEST) * 0.125)
    top_score = jnp.maximum(lax.optimization_barrier(jnp.max(patch_score, axis=-1)), class_score)
    exp_patch = jnp.exp(patch_score - top_score[..., None])
    exp_class = jnp.exp(class_score - top_score)
    total_exp = lax.optimization_barrier(jnp.sum(exp_patch, axis=-1)) + exp_class
    prob_patch = low(exp_patch / total_exp[..., None])
    prob_class = low(exp_class / total_exp)
    mixed = jnp.einsum('fhpq,fqhe->fphe', prob_patch, values, precision=HIGHEST)
    return mixed + jnp.einsum('fhp,fhe->fphe', prob_class, class_values, precision=HIGHEST)

def layer_batch(params, tokens, class_tokens, counts):
    w_tqkv, w_tproj, w_tfc, w_sqkv, w_sproj, w_in, w_out, in_bias, gains, shifts, bias_cols = params
    clip_of = frame_clips(counts)
    zero_row = jnp.zeros((D,), jnp.float32)
    normed = low(layer_norm(tokens, gains[:, 0], shifts[:, 0]))
    packed = project(normed, w_tqkv) + jnp.concatenate([bias_cols[:, 0], zero_row, bias_cols[:, 1]])
    packed = low_back(low(packed))
    split_t = packed.reshape(FRAMES, POS, 3, HEADS, HEAD)
    attended = temporal_attention(split_t[:, :, 0], split_t[:, :, 1], split_t[:, :, 2], clip_of)
    attended = low_back(low(attended.reshape(FRAMES, POS, D)))
    projected = low_back(low(project(attended, w_tproj) + bias_cols[:, 2]))
    temporal = tokens + low_back(project(projected, w_tfc) + bias_cols[:, 3])
    normed = low(layer_norm(temporal, gains[:, 1], shifts[:, 1]))
    class_normed = low(layer_norm(class_tokens, gains[:, 1], shifts[:, 1]))
    packed = project(normed, w_sqkv) + jnp.concatenate([bias_cols[:, 4], zero_row, bias_cols[:, 5]])
    packed = low_back(low(packed))
    class_packed = project(class_normed, w_sqkv[:, D:]) + jnp.concatenate([zero_row, bias_cols[:, 5]])
    class_packed = low_back(low(class_packed))
    split_s = packed.reshape(FRAMES, POS, 3, HEADS, HEAD)
    class_split = class_packed[clip_of].reshape(FRAMES, 2, HEADS, HEAD)
    attended = spatial_attention(split_s[:, :, 0], split_s[:, :, 1], split_s[:, :, 2], class_split[:, 0], class_split[:, 1])
    attended = low_back(low(attended.reshape(FRAMES, POS, D)))
    spatial = temporal + low_back(project(attended, w_sproj) + bias_cols[:, 6])
    normed = low(layer_norm(spatial, gains[:, 2], shifts[:, 2]))
    hidden = low_back(project(normed, w_in) + in_bias)
    activated = low(jax.nn.gelu(hidden, approximate=False))
    return spatial + low_back(project(activated, w_out) + bias_cols[:, 7])

def reference(tokens, class_tokens, clip_frames, cotangent, temporal_qkv, temporal_proj, temporal_fc, spatial_qkv, spatial_proj, mlp_in, mlp_out, mlp_in_bias, norm_gains, norm_shifts, biases):
    params = tuple((weight_arg.astype(jnp.float32) for weight_arg in (temporal_qkv, temporal_proj, temporal_fc, spatial_qkv, spatial_proj, mlp_in, mlp_out, mlp_in_bias, norm_gains, norm_shifts, biases)))

    def forward(inputs, class_in, weights):

        def micro_batch(pieces):
            return layer_batch(weights, pieces[0], pieces[1], pieces[2])
        return lax.map(jax.checkpoint(micro_batch), (inputs, class_in, clip_frames))
    result, pullback = jax.vjp(forward, tokens.astype(jnp.float32), class_tokens.astype(jnp.float32), params)
    grad_tokens, grad_class, grad_params = pullback(cotangent.astype(jnp.float32))
    return (result.astype(jnp.bfloat16), grad_tokens, grad_class, grad_params[0], grad_params[1], grad_params[2], grad_params[3], grad_params[4], grad_params[5], grad_params[6], grad_params[7], grad_params[8], grad_params[9], grad_params[10])
```

```python
from functools import partial

import jax
import jax.numpy as jnp
from jax import lax
from jax.sharding import PartitionSpec as P

D = 768
HEADS = 12
HEAD = 64
MB = 4
CLIPS = 3
AXES = ("frame", "pos")


def norm_forward(values, gain_vec, shift_vec):
    centred = values - jnp.mean(values, axis=-1, keepdims=True)
    inv_std = lax.rsqrt(jnp.mean(centred * centred, axis=-1, keepdims=True) + 1e-06)
    normal = centred * inv_std
    return (normal * gain_vec + shift_vec, normal, inv_std)


def norm_backward(upstream, normal, inv_std, gain_vec):
    grad_gain = jnp.sum(upstream * normal, axis=0)
    grad_shift = jnp.sum(upstream, axis=0)
    scaled_grad = upstream * gain_vec
    centred = scaled_grad - jnp.mean(scaled_grad, axis=-1, keepdims=True)
    grad_in = inv_std * (centred - normal * jnp.mean(scaled_grad * normal, axis=-1, keepdims=True))
    return (grad_in, grad_gain, grad_shift)


def matmul(left_mat, right_mat):
    return jnp.dot(left_mat, right_mat, preferred_element_type=jnp.float32)


def outer_sum(left_mat, right_mat):
    return lax.dot_general(
        left_mat, right_mat, (((0,), (0,)), ((), ())), preferred_element_type=jnp.float32
    ).astype(jnp.bfloat16)


def back_mul(upstream, weight):
    return lax.dot_general(
        upstream, weight, (((1,), (1,)), ((), ())), preferred_element_type=jnp.float32
    )


def column_sum(values):
    return jnp.sum(values.astype(jnp.float32), axis=0)


def split_heads(values):
    return values.reshape(values.shape[0], HEADS, HEAD)


def attention_forward(query, keys, values, allowed):
    scores = (
        jnp.einsum(
            "qhe,khe->hqk", split_heads(query), split_heads(keys), preferred_element_type=jnp.float32
        )
        * 0.125
    )
    scores = jnp.where(allowed[None], scores, -1000000000.0)
    top_score = jnp.max(scores, axis=-1, keepdims=True)
    log_total = top_score + jnp.log(jnp.sum(jnp.exp(scores - top_score), axis=-1, keepdims=True))
    probs = jnp.exp(scores - log_total).astype(jnp.bfloat16)
    mixed = jnp.einsum(
        "hqk,khe->qhe", probs, split_heads(values), preferred_element_type=jnp.float32
    )
    return (mixed.reshape(query.shape).astype(jnp.bfloat16), log_total)


def attention_backward(query, keys, values, allowed, log_total, grad_mixed):
    query, keys, values, grad_mixed = (
        split_heads(query),
        split_heads(keys),
        split_heads(values),
        split_heads(grad_mixed),
    )
    scores = jnp.einsum("qhe,khe->hqk", query, keys, preferred_element_type=jnp.float32) * 0.125
    scores = jnp.where(allowed[None], scores, -1000000000.0)
    probs = jnp.exp(scores - log_total)
    dprob = jnp.einsum("qhe,khe->hqk", grad_mixed, values, preferred_element_type=jnp.float32)
    delta = jnp.sum(dprob * probs, axis=-1, keepdims=True)
    dscore = (probs * (dprob - delta)).astype(jnp.bfloat16)
    probs_b = probs.astype(jnp.bfloat16)
    grad_query = jnp.einsum("hqk,khe->qhe", dscore, keys, preferred_element_type=jnp.float32) * 0.125
    grad_keys = jnp.einsum("hqk,qhe->khe", dscore, query, preferred_element_type=jnp.float32) * 0.125
    grad_values = jnp.einsum("hqk,qhe->khe", probs_b, grad_mixed, preferred_element_type=jnp.float32)
    flat = lambda g: g.reshape(g.shape[0], D).astype(jnp.bfloat16)
    return (flat(grad_query), flat(grad_keys), flat(grad_values))


def on_device(
    tokens,
    class_tokens,
    clip_frames,
    cotangent,
    temporal_qkv,
    temporal_proj,
    temporal_fc,
    spatial_qkv,
    spatial_proj,
    mlp_in,
    mlp_out,
    mlp_in_bias,
    norm_gains,
    norm_shifts,
    biases,
):
    bf16, f32 = jnp.bfloat16, jnp.float32
    frame_size, pos_size = lax.axis_size("frame"), lax.axis_size("pos")
    frame_index, pos_index = lax.axis_index("frame"), lax.axis_index("pos")
    frame_count, pos_count = tokens.shape[1], tokens.shape[2]
    shard = norm_gains.shape[0]
    slots = pos_count + 1
    share = frame_size // MB
    my_slots = slots // share
    all_frames = frame_count * frame_size
    my_frames = all_frames // pos_size
    rows_count = all_frames * my_slots
    micro = frame_index // share

    gather = partial(lax.all_gather, axis_name=AXES, axis=0, tiled=True)
    small = jnp.concatenate(
        [mlp_in_bias.reshape(shard, 4), norm_gains, norm_shifts, biases], axis=1
    )
    chunk_t = gather(jnp.concatenate([temporal_qkv, temporal_proj, temporal_fc], axis=1))
    small = gather(small).astype(f32)
    chunk_s = gather(jnp.concatenate([spatial_qkv, spatial_proj], axis=1))
    w_in = gather(mlp_in)
    w_out = gather(mlp_out)
    w_tqkv, w_tproj, w_tfc = chunk_t[:, : 3 * D], chunk_t[:, 3 * D : 4 * D], chunk_t[:, 4 * D :]
    w_sqkv, w_sproj = chunk_s[:, : 3 * D], chunk_s[:, 3 * D :]
    in_bias = small[:, :4].reshape(-1)
    rows_small = small[:, 4:].T
    gains, shifts, bias_rows = rows_small[:3], rows_small[3:6], rows_small[6:]
    zero_row = jnp.zeros((D,), f32)
    temporal_bias = jnp.concatenate([bias_rows[0], zero_row, bias_rows[1]])
    spatial_bias = jnp.concatenate([bias_rows[4], zero_row, bias_rows[5]])

    def frame_hop(values):
        return lax.all_to_all(values, "frame", 0, 0, tiled=True)

    def pos_hop(values):
        parts = values.reshape(pos_size, rows_count // pos_size, D)
        return lax.all_to_all(parts, "pos", 0, 0, tiled=True).reshape(rows_count, D)

    def to_temporal(values):
        padded = jnp.pad(values, ((0, 0), (0, 0), (0, 1), (0, 0)))
        padded = padded.reshape(MB, frame_count, share, my_slots, D).transpose(0, 2, 1, 3, 4)
        return frame_hop(padded.reshape(frame_size, frame_count * my_slots, D)).reshape(
            rows_count, D
        )

    def from_temporal(values):
        parts = frame_hop(values.reshape(frame_size, frame_count * my_slots, D))
        parts = parts.reshape(MB, share, frame_count, my_slots, D).transpose(0, 2, 1, 3, 4)
        return parts.reshape(MB, frame_count, slots, D)[:, :, :pos_count]

    def partners(values, step):
        perm = [
            (f, f // share * share + (f % share + step) % share) for f in range(frame_size)
        ]
        return lax.ppermute(values, "frame", perm)

    row_ids = jnp.arange(rows_count, dtype=jnp.int32)
    row_slot = row_ids % my_slots
    clip_ends = jnp.cumsum(lax.dynamic_index_in_dim(clip_frames, micro, 0, keepdims=False))
    clip_of = lambda frame: jnp.sum(
        (frame[:, None] >= clip_ends[None, :]).astype(jnp.int32), axis=1
    )
    group_t = row_slot * CLIPS + clip_of(row_ids // my_slots)
    allowed_t = group_t[:, None] == group_t[None, :]
    frame_s = row_ids // my_slots % my_frames
    clip_s = clip_of(pos_index * my_frames + frame_s)
    first_source = row_ids < my_frames * my_slots

    def key_masks(share_index):
        padding = row_slot + share_index * my_slots == slots - 1
        is_class = padding & first_source
        return is_class, is_class | ~padding

    allowed_s = []
    for step in range(share):
        _, valid = key_masks((frame_index + share - step) % share)
        allowed_s.append((frame_s[:, None] == frame_s[None, :]) & valid[None, :])
    allowed_s = jnp.concatenate(allowed_s, axis=1)
    is_class, _ = key_masks(frame_index % share)

    rows_in = to_temporal(tokens).astype(f32)
    normed_f, normal_t, inv_std_t = norm_forward(rows_in, gains[0], shifts[0])
    normed_t = normed_f.astype(bf16)
    packed_t = (matmul(normed_t, w_tqkv) + temporal_bias).astype(bf16)
    query_t, keys_t, values_t = packed_t[:, :D], packed_t[:, D : 2 * D], packed_t[:, 2 * D :]
    mixed_t, log_total_t = attention_forward(query_t, keys_t, values_t, allowed_t)
    projected = (matmul(mixed_t, w_tproj) + bias_rows[2]).astype(bf16)
    temporal = (rows_in + matmul(projected, w_tfc) + bias_rows[3]).astype(bf16)
    temporal = pos_hop(temporal).astype(f32)
    class_rows = lax.dynamic_index_in_dim(class_tokens, micro, 0, keepdims=False).astype(f32)
    choose = (clip_s[:, None] == jnp.arange(CLIPS)[None, :]) & is_class[:, None]
    class_rows = jnp.einsum("rc,cd->rd", choose.astype(f32), class_rows, precision="highest")
    temporal = jnp.where(is_class[:, None], class_rows, temporal)
    normed_f, normal_s, inv_std_s = norm_forward(temporal, gains[1], shifts[1])
    normed_s = normed_f.astype(bf16)
    packed_s = (matmul(normed_s, w_sqkv) + spatial_bias).astype(bf16)
    query_s = packed_s[:, :D]
    pairs_s = [packed_s[:, D:]]
    for step in range(1, share):
        pairs_s.append(partners(packed_s[:, D:], step))
    pairs_s = jnp.concatenate(pairs_s, axis=0)
    keys_s, values_s = pairs_s[:, :D], pairs_s[:, D:]
    mixed_s, log_total_s = attention_forward(query_s, keys_s, values_s, allowed_s)
    spatial = temporal + matmul(mixed_s, w_sproj) + bias_rows[6]
    normed_f, normal_m, inv_std_m = norm_forward(spatial, gains[2], shifts[2])
    normed_m = normed_f.astype(bf16)
    hidden = matmul(normed_m, w_in) + in_bias
    activated, gelu_back = jax.vjp(partial(jax.nn.gelu, approximate=False), hidden)
    activated = activated.astype(bf16)
    result = (spatial + matmul(activated, w_out) + bias_rows[7]).astype(bf16)
    block_out = from_temporal(pos_hop(result))
    grad_out = pos_hop(to_temporal(cotangent))
    acc_out = outer_sum(activated, grad_out)
    grad_hidden = gelu_back(back_mul(grad_out, w_out))[0].astype(bf16)
    acc_in = outer_sum(normed_m, grad_hidden)
    grad_ln, gain_m, shift_m = norm_backward(
        back_mul(grad_hidden, w_in), normal_m, inv_std_m, gains[2]
    )
    grad_spatial = grad_out.astype(f32) + grad_ln
    grad_spatial_b = grad_spatial.astype(bf16)
    acc_sproj = outer_sum(mixed_s, grad_spatial_b)
    grad_mixed = back_mul(grad_spatial_b, w_sproj).astype(bf16)
    grad_query, grad_keys, grad_values = attention_backward(
        query_s, keys_s, values_s, allowed_s, log_total_s, grad_mixed
    )
    grad_pairs = jnp.concatenate([grad_keys, grad_values], axis=1)
    own_pairs = grad_pairs[:rows_count]
    for step in range(1, share):
        theirs = grad_pairs[step * rows_count : (step + 1) * rows_count]
        own_pairs = (own_pairs.astype(f32) + partners(theirs, share - step).astype(f32)).astype(bf16)
    grad_packed_s = jnp.concatenate([grad_query, own_pairs], axis=1)
    acc_sqkv = outer_sum(normed_s, grad_packed_s)
    grad_ln, gain_s, shift_s = norm_backward(
        back_mul(grad_packed_s, w_sqkv), normal_s, inv_std_s, gains[1]
    )
    class_part = jnp.einsum("rc,rd->cd", choose.astype(f32), grad_ln, precision="highest")
    grad_temporal = jnp.where(is_class[:, None], 0.0, grad_spatial + grad_ln).astype(bf16)
    grad_temporal = pos_hop(grad_temporal)
    acc_tfc = outer_sum(projected, grad_temporal)
    grad_proj = back_mul(grad_temporal, w_tfc).astype(bf16)
    acc_tproj = outer_sum(mixed_t, grad_proj)
    grad_mixed_t = back_mul(grad_proj, w_tproj).astype(bf16)
    grad_packed_t = jnp.concatenate(
        attention_backward(query_t, keys_t, values_t, allowed_t, log_total_t, grad_mixed_t), axis=1
    )
    acc_tqkv = outer_sum(normed_t, grad_packed_t)
    grad_ln, gain_t, shift_t = norm_backward(
        back_mul(grad_packed_t, w_tqkv), normal_t, inv_std_t, gains[0]
    )
    tokens_grad = from_temporal((grad_temporal.astype(f32) + grad_ln).astype(bf16)).astype(f32)

    class_all = jnp.zeros((MB, CLIPS, D), f32)
    class_all = lax.dynamic_update_index_in_dim(class_all, class_part, micro, 0)
    class_grad = lax.psum(class_all, AXES)
    scatter = partial(lax.psum_scatter, axis_name=AXES, scatter_dimension=0, tiled=True)
    sum_s = column_sum(grad_packed_s)
    sum_t = column_sum(grad_packed_t)
    small_grads = jnp.stack(
        [gain_t, gain_s, gain_m, shift_t, shift_s, shift_m]
        + [sum_t[:D], sum_t[2 * D :], column_sum(grad_proj), column_sum(grad_temporal)]
        + [sum_s[:D], sum_s[2 * D :], column_sum(grad_spatial_b), column_sum(grad_out)],
        axis=1,
    )
    small_grads = jnp.concatenate([column_sum(grad_hidden).reshape(D, 4), small_grads], axis=1)
    small_grads = scatter(small_grads)
    acc_out = scatter(acc_out).astype(f32)
    acc_in = scatter(acc_in).astype(f32)
    acc_s = scatter(jnp.concatenate([acc_sqkv, acc_sproj], axis=1)).astype(f32)
    acc_t = scatter(jnp.concatenate([acc_tqkv, acc_tproj, acc_tfc], axis=1)).astype(f32)
    return (
        block_out,
        tokens_grad,
        class_grad,
        acc_t[:, : 3 * D],
        acc_t[:, 3 * D : 4 * D],
        acc_t[:, 4 * D :],
        acc_s[:, : 3 * D],
        acc_s[:, 3 * D :],
        acc_in,
        acc_out,
        small_grads[:, :4].reshape(-1),
        small_grads[:, 4:7],
        small_grads[:, 7:10],
        small_grads[:, 10:],
    )


def solution(mesh):
    rows = P(AXES, None)
    wide = P(None, "frame", "pos", None)
    placed = (wide, P(), P(), wide) + (rows,) * 7 + (P(AXES),) + (rows,) * 3
    return jax.shard_map(
        on_device,
        mesh=mesh,
        in_specs=placed,
        out_specs=(wide, wide, P()) + (rows,) * 7 + (P(AXES),) + (rows,) * 3,
        check_vma=False,
    )
```

```python
from functools import partial

import jax
import jax.numpy as jnp
from jax import lax
from jax.experimental import pallas as pl
from jax.experimental.pallas import tpu as pltpu
from jax.sharding import PartitionSpec as P

D = 768
HEADS = 12
HEAD = 64
MB = 4
CLIPS = 3
AXES = ("frame", "pos")


def send(values, perm):
    return lax.ppermute(values, AXES, perm)


def tie(value, *before):
    return lax.optimization_barrier((value,) + before)[0]


class Layout:
    def __init__(self):
        self.frames, self.chips = lax.axis_size("frame"), lax.axis_size("pos") // 2
        self.bits = self.frames.bit_length() - 1
        self.frame, self.chip = lax.axis_index("frame"), lax.axis_index("pos") // 2
        self.core = lax.axis_index("pos") % 2
        self.swap = self.perm(lambda f, z, c: (f, z, 1 - c))
        self.along = [self.perm(lambda f, z, c, i=i: (f, z ^ i, c)) for i in range(1, self.chips)]
        self.across = [
            self.perm(lambda f, z, c, k=k: (f ^ (1 << self.bit(k, c)), z, c))
            for k in range(self.bits)
        ]

    def bit(self, step, core):
        return (step + core) % self.bits

    def perm(self, to):
        pairs = []
        for f in range(self.frames):
            for z in range(self.chips):
                for c in range(2):
                    g, y, d = to(f, z, c)
                    pairs.append(
                        ((f * self.chips + z) * 2 + c, (g * self.chips + y) * 2 + d)
                    )
        return pairs

    def table(self):
        rows = []
        for core in (self.core, 1 - self.core):
            blocks = []
            for b in range(self.frames * self.chips):
                flags, i = b // self.chips, b % self.chips
                f = self.frame
                for k in range(self.bits):
                    if flags >> k & 1:
                        f = f ^ (1 << ((k + core) % self.bits))
                blocks.append(f * self.chips + (self.chip ^ i))
            rows.append(jnp.stack(blocks))
        return jnp.concatenate([jnp.stack(rows).reshape(-1), self.core[None]]).astype(jnp.int32)

    def pick(self, low, high):
        return jnp.where(self.core == 0, low, high), jnp.where(self.core == 0, high, low)

    def chip_rows(self, mats):
        low = jnp.concatenate([m[:, : m.shape[1] // 2] for m in mats], axis=1)
        high = jnp.concatenate([m[:, m.shape[1] // 2 :] for m in mats], axis=1)
        keep, give = self.pick(low, high)
        got = send(give, self.swap)
        first, second = self.pick(keep, got)
        return jnp.concatenate([first, second], axis=0)

    def gather(self, owned):
        block = jnp.stack([owned] + [send(owned, p) for p in self.along])
        for p in self.across:
            block = jnp.concatenate([block, send(block, p)])
        return block, send(block, self.swap)

    def scatter(self, mine, other):
        f32, bf16 = jnp.float32, jnp.bfloat16
        got = send(other, self.swap)
        for p in reversed(self.across):
            half = mine.shape[0] // 2
            far = (mine[half:].astype(f32) + got[half:].astype(f32)).astype(bf16)
            mine = (mine[:half].astype(f32) + got[:half].astype(f32)).astype(bf16)
            got = send(far, p)
        mine = mine.astype(f32) + got.astype(f32)
        total = mine[0]
        parts = mine.astype(bf16)
        for i, p in enumerate(self.along):
            total = total + send(parts[i + 1], p).astype(f32)
        rows = total.shape[0] // 2
        first, second = total[:rows], total[rows:]
        keep, give = self.pick(first, second)
        got = send(give, self.swap)
        return self.pick(keep, got)

    def split(self, low, high, widths):
        mats, at = [], 0
        for width in widths:
            half = width // 2
            mats.append(jnp.concatenate([low[:, at : at + half], high[:, at : at + half]], axis=1))
            at += half
        return mats


def join_kernel(blocks, rows, widths, table, mine, other, *refs):
    outs, sem = refs[: len(widths)], refs[-1]
    core = table[2 * blocks]

    def body(b, carry):
        for side, source in ((0, mine), (1, other)):
            row = pl.multiple_of(table[side * blocks + b] * rows, rows)
            half = core if side == 0 else 1 - core
            at = 0
            for i, width in enumerate(widths):
                w = width // 2
                pltpu.make_async_copy(
                    source.at[b, :, at : at + w],
                    outs[i].at[pl.ds(row, rows), pl.ds(pl.multiple_of(half * w, 128), w)],
                    sem.at[i],
                ).start()
                at += w
        return carry

    lax.fori_loop(0, blocks, body, 0)
    for i in range(len(widths)):
        pltpu.make_async_copy(outs[i], outs[i], sem.at[i]).wait()


def join(layout, table, mine, other, widths):
    blocks, rows, _ = mine.shape
    if rows % 16:
        order = jnp.argsort(table[: 2 * blocks].reshape(2, blocks), axis=1)
        halves = [a[o].reshape(blocks * rows, -1) for a, o in zip((mine, other), order)]
        return layout.split(*layout.pick(*halves), widths)
    anywhere = pl.BlockSpec(memory_space=pl.ANY)
    return pl.pallas_call(
        partial(join_kernel, blocks, rows, widths),
        out_shape=[jax.ShapeDtypeStruct((blocks * rows, w), mine.dtype) for w in widths],
        in_specs=[pl.BlockSpec(memory_space=pltpu.SMEM), anywhere, anywhere],
        out_specs=[pl.BlockSpec(memory_space=pltpu.VMEM)] * len(widths),
        scratch_shapes=[pltpu.SemaphoreType.DMA((len(widths),))],
        compiler_params=pltpu.CompilerParams(vmem_limit_bytes=48 << 20),
        name="join",
    )(table, mine, other)


def part_kernel(blocks, rows, widths, table, *refs):
    mats, mine, other, sem = refs[: len(widths)], refs[-3], refs[-2], refs[-1]
    core = table[2 * blocks]

    def body(b, carry):
        for side, target in ((0, mine), (1, other)):
            row = pl.multiple_of(table[side * blocks + b] * rows, rows)
            half = core if side == 0 else 1 - core
            at = 0
            for i, width in enumerate(widths):
                w = width // 2
                pltpu.make_async_copy(
                    mats[i].at[pl.ds(row, rows), pl.ds(pl.multiple_of(half * w, 128), w)],
                    target.at[b, :, at : at + w],
                    sem.at[side],
                ).start()
                at += w
        return carry

    lax.fori_loop(0, blocks, body, 0)
    pltpu.make_async_copy(mine, mine, sem.at[0]).wait()
    pltpu.make_async_copy(other, other, sem.at[1]).wait()


def part(layout, table, mats, blocks):
    widths = [m.shape[1] for m in mats]
    rows = mats[0].shape[0] // blocks
    if rows % 16:
        low = jnp.concatenate([m[:, : m.shape[1] // 2] for m in mats], axis=1)
        high = jnp.concatenate([m[:, m.shape[1] // 2 :] for m in mats], axis=1)
        order = table[: 2 * blocks].reshape(2, blocks)
        return [a.reshape(blocks, rows, -1)[o] for a, o in zip(layout.pick(low, high), order)]
    anywhere = pl.BlockSpec(memory_space=pl.ANY)
    shape = jax.ShapeDtypeStruct((blocks, rows, sum(widths) // 2), mats[0].dtype)
    return pl.pallas_call(
        partial(part_kernel, blocks, rows, widths),
        out_shape=[shape, shape],
        in_specs=[pl.BlockSpec(memory_space=pltpu.SMEM)]
        + [pl.BlockSpec(memory_space=pltpu.VMEM)] * len(mats),
        out_specs=[anywhere, anywhere],
        scratch_shapes=[pltpu.SemaphoreType.DMA((2,))],
        compiler_params=pltpu.CompilerParams(vmem_limit_bytes=48 << 20),
        name="part",
    )(table, *mats)


def norm_forward(values, gain_vec, shift_vec):
    centred = values - jnp.mean(values, axis=-1, keepdims=True)
    inv_std = lax.rsqrt(jnp.mean(centred * centred, axis=-1, keepdims=True) + 1e-06)
    normal = centred * inv_std
    return (normal * gain_vec + shift_vec, normal, inv_std)


def norm_backward(upstream, normal, inv_std, gain_vec):
    grad_gain = jnp.sum(upstream * normal, axis=0)
    grad_shift = jnp.sum(upstream, axis=0)
    scaled_grad = upstream * gain_vec
    centred = scaled_grad - jnp.mean(scaled_grad, axis=-1, keepdims=True)
    grad_in = inv_std * (centred - normal * jnp.mean(scaled_grad * normal, axis=-1, keepdims=True))
    return (grad_in, grad_gain, grad_shift)


def matmul(left_mat, right_mat):
    return jnp.dot(left_mat, right_mat, preferred_element_type=jnp.float32)


def outer_sum(left_mat, right_mat):
    return lax.dot_general(
        left_mat, right_mat, (((0,), (0,)), ((), ())), preferred_element_type=jnp.float32
    ).astype(jnp.bfloat16)


def back_mul(upstream, weight):
    return lax.dot_general(
        upstream, weight, (((1,), (1,)), ((), ())), preferred_element_type=jnp.float32
    )


def column_sum(values):
    return jnp.sum(values.astype(jnp.float32), axis=0)


def split_heads(values):
    return values.reshape(values.shape[0], HEADS, HEAD)


def attention_forward(query, keys, values, allowed):
    scores = (
        jnp.einsum(
            "qhe,khe->hqk", split_heads(query), split_heads(keys), preferred_element_type=jnp.float32
        )
        * 0.125
    )
    scores = jnp.where(allowed[None], scores, -1000000000.0)
    top_score = jnp.max(scores, axis=-1, keepdims=True)
    log_total = top_score + jnp.log(jnp.sum(jnp.exp(scores - top_score), axis=-1, keepdims=True))
    probs = jnp.exp(scores - log_total).astype(jnp.bfloat16)
    mixed = jnp.einsum(
        "hqk,khe->qhe", probs, split_heads(values), preferred_element_type=jnp.float32
    )
    return (mixed.reshape(query.shape).astype(jnp.bfloat16), log_total)


def attention_backward(query, keys, values, allowed, log_total, grad_mixed):
    query, keys, values, grad_mixed = (
        split_heads(query),
        split_heads(keys),
        split_heads(values),
        split_heads(grad_mixed),
    )
    scores = jnp.einsum("qhe,khe->hqk", query, keys, preferred_element_type=jnp.float32) * 0.125
    scores = jnp.where(allowed[None], scores, -1000000000.0)
    probs = jnp.exp(scores - log_total)
    dprob = jnp.einsum("qhe,khe->hqk", grad_mixed, values, preferred_element_type=jnp.float32)
    delta = jnp.sum(dprob * probs, axis=-1, keepdims=True)
    dscore = (probs * (dprob - delta)).astype(jnp.bfloat16)
    probs_b = probs.astype(jnp.bfloat16)
    grad_query = jnp.einsum("hqk,khe->qhe", dscore, keys, preferred_element_type=jnp.float32) * 0.125
    grad_keys = jnp.einsum("hqk,qhe->khe", dscore, query, preferred_element_type=jnp.float32) * 0.125
    grad_values = jnp.einsum("hqk,qhe->khe", probs_b, grad_mixed, preferred_element_type=jnp.float32)
    flat = lambda g: g.reshape(g.shape[0], D).astype(jnp.bfloat16)
    return (flat(grad_query), flat(grad_keys), flat(grad_values))


def on_device(
    tokens,
    class_tokens,
    clip_frames,
    cotangent,
    temporal_qkv,
    temporal_proj,
    temporal_fc,
    spatial_qkv,
    spatial_proj,
    mlp_in,
    mlp_out,
    mlp_in_bias,
    norm_gains,
    norm_shifts,
    biases,
):
    bf16, f32 = jnp.bfloat16, jnp.float32
    frame_size, pos_size = lax.axis_size("frame"), lax.axis_size("pos")
    frame_index, pos_index = lax.axis_index("frame"), lax.axis_index("pos")
    frame_count, pos_count = tokens.shape[1], tokens.shape[2]
    shard = norm_gains.shape[0]
    slots = pos_count + 1
    share = frame_size // MB
    my_slots = slots // share
    all_frames = frame_count * frame_size
    my_frames = all_frames // pos_size
    rows_count = all_frames * my_slots
    micro = frame_index // share

    layout = Layout()
    table = layout.table()
    blocks = frame_size * pos_size // 2
    small = jnp.concatenate(
        [mlp_in_bias.reshape(shard, 4), norm_gains, norm_shifts, biases], axis=1
    )
    small = jnp.pad(small, ((0, 0), (0, 256 - small.shape[1])))
    widths_t, widths_s, widths_in, widths_out = (3 * D, D, D, 256), (3 * D, D), (4 * D,), (D,)
    gathered, last = [], None
    for mats in (
        (temporal_qkv, temporal_proj, temporal_fc, small),
        (spatial_qkv, spatial_proj),
        (mlp_in,),
        (mlp_out,),
    ):
        gathered.append(layout.gather(layout.chip_rows(mats)))
    w_tqkv, w_tproj, w_tfc, small = join(layout, table, *gathered[0], widths_t)
    w_sqkv, w_sproj = join(layout, table, *gathered[1], widths_s)
    (w_in,) = join(layout, table, *gathered[2], widths_in)
    (w_out,) = join(layout, table, *gathered[3], widths_out)
    small = small[:, :18].astype(f32)
    in_bias = small[:, :4].reshape(-1)
    rows_small = small[:, 4:].T
    gains, shifts, bias_rows = rows_small[:3], rows_small[3:6], rows_small[6:]
    zero_row = jnp.zeros((D,), f32)
    temporal_bias = jnp.concatenate([bias_rows[0], zero_row, bias_rows[1]])
    spatial_bias = jnp.concatenate([bias_rows[4], zero_row, bias_rows[5]])

    def frame_hop(values):
        return lax.all_to_all(values, "frame", 0, 0, tiled=True)

    def pos_hop(values):
        parts = values.reshape(pos_size, rows_count // pos_size, D)
        return lax.all_to_all(parts, "pos", 0, 0, tiled=True).reshape(rows_count, D)

    def to_temporal(values):
        padded = jnp.pad(values, ((0, 0), (0, 0), (0, 1), (0, 0)))
        padded = padded.reshape(MB, frame_count, share, my_slots, D).transpose(0, 2, 1, 3, 4)
        return frame_hop(padded.reshape(frame_size, frame_count * my_slots, D)).reshape(
            rows_count, D
        )

    def from_temporal(values):
        parts = frame_hop(values.reshape(frame_size, frame_count * my_slots, D))
        parts = parts.reshape(MB, share, frame_count, my_slots, D).transpose(0, 2, 1, 3, 4)
        return parts.reshape(MB, frame_count, slots, D)[:, :, :pos_count]

    def partners(values, step):
        perm = [
            (f, f // share * share + (f % share + step) % share) for f in range(frame_size)
        ]
        return lax.ppermute(values, "frame", perm)

    row_ids = jnp.arange(rows_count, dtype=jnp.int32)
    row_slot = row_ids % my_slots
    clip_ends = jnp.cumsum(lax.dynamic_index_in_dim(clip_frames, micro, 0, keepdims=False))
    clip_of = lambda frame: jnp.sum(
        (frame[:, None] >= clip_ends[None, :]).astype(jnp.int32), axis=1
    )
    group_t = row_slot * CLIPS + clip_of(row_ids // my_slots)
    allowed_t = group_t[:, None] == group_t[None, :]
    frame_s = row_ids // my_slots % my_frames
    clip_s = clip_of(pos_index * my_frames + frame_s)
    first_source = row_ids < my_frames * my_slots

    def key_masks(share_index):
        padding = row_slot + share_index * my_slots == slots - 1
        is_class = padding & first_source
        return is_class, is_class | ~padding

    allowed_s = []
    for step in range(share):
        _, valid = key_masks((frame_index + share - step) % share)
        allowed_s.append((frame_s[:, None] == frame_s[None, :]) & valid[None, :])
    allowed_s = jnp.concatenate(allowed_s, axis=1)
    is_class, _ = key_masks(frame_index % share)

    rows_in = to_temporal(tokens).astype(f32)
    normed_f, normal_t, inv_std_t = norm_forward(rows_in, gains[0], shifts[0])
    normed_t = normed_f.astype(bf16)
    packed_t = (matmul(normed_t, w_tqkv) + temporal_bias).astype(bf16)
    query_t, keys_t, values_t = packed_t[:, :D], packed_t[:, D : 2 * D], packed_t[:, 2 * D :]
    mixed_t, log_total_t = attention_forward(query_t, keys_t, values_t, allowed_t)
    projected = (matmul(mixed_t, w_tproj) + bias_rows[2]).astype(bf16)
    temporal = (rows_in + matmul(projected, w_tfc) + bias_rows[3]).astype(bf16)
    temporal = pos_hop(temporal).astype(f32)
    class_rows = lax.dynamic_index_in_dim(class_tokens, micro, 0, keepdims=False).astype(f32)
    choose = (clip_s[:, None] == jnp.arange(CLIPS)[None, :]) & is_class[:, None]
    class_rows = jnp.einsum("rc,cd->rd", choose.astype(f32), class_rows, precision="highest")
    temporal = jnp.where(is_class[:, None], class_rows, temporal)
    normed_f, normal_s, inv_std_s = norm_forward(temporal, gains[1], shifts[1])
    normed_s = normed_f.astype(bf16)
    packed_s = (matmul(normed_s, w_sqkv) + spatial_bias).astype(bf16)
    query_s = packed_s[:, :D]
    pairs_s = [packed_s[:, D:]]
    for step in range(1, share):
        pairs_s.append(partners(packed_s[:, D:], step))
    pairs_s = jnp.concatenate(pairs_s, axis=0)
    keys_s, values_s = pairs_s[:, :D], pairs_s[:, D:]
    mixed_s, log_total_s = attention_forward(query_s, keys_s, values_s, allowed_s)
    spatial = temporal + matmul(mixed_s, w_sproj) + bias_rows[6]
    normed_f, normal_m, inv_std_m = norm_forward(spatial, gains[2], shifts[2])
    normed_m = normed_f.astype(bf16)
    hidden = matmul(normed_m, w_in) + in_bias
    activated, gelu_back = jax.vjp(partial(jax.nn.gelu, approximate=False), hidden)
    activated = activated.astype(bf16)
    result = (spatial + matmul(activated, w_out) + bias_rows[7]).astype(bf16)
    block_out = from_temporal(pos_hop(result))
    grad_out = pos_hop(to_temporal(cotangent))
    acc_out = outer_sum(activated, grad_out)
    grad_hidden = gelu_back(back_mul(grad_out, w_out))[0].astype(bf16)
    acc_in = outer_sum(normed_m, grad_hidden)
    grad_ln, gain_m, shift_m = norm_backward(
        back_mul(grad_hidden, w_in), normal_m, inv_std_m, gains[2]
    )
    grad_spatial = grad_out.astype(f32) + grad_ln
    grad_spatial_b = grad_spatial.astype(bf16)
    acc_sproj = outer_sum(mixed_s, grad_spatial_b)
    grad_mixed = back_mul(grad_spatial_b, w_sproj).astype(bf16)
    grad_query, grad_keys, grad_values = attention_backward(
        query_s, keys_s, values_s, allowed_s, log_total_s, grad_mixed
    )
    grad_pairs = jnp.concatenate([grad_keys, grad_values], axis=1)
    own_pairs = grad_pairs[:rows_count]
    for step in range(1, share):
        theirs = grad_pairs[step * rows_count : (step + 1) * rows_count]
        own_pairs = (own_pairs.astype(f32) + partners(theirs, share - step).astype(f32)).astype(bf16)
    grad_packed_s = jnp.concatenate([grad_query, own_pairs], axis=1)
    acc_sqkv = outer_sum(normed_s, grad_packed_s)
    grad_ln, gain_s, shift_s = norm_backward(
        back_mul(grad_packed_s, w_sqkv), normal_s, inv_std_s, gains[1]
    )
    class_part = jnp.einsum("rc,rd->cd", choose.astype(f32), grad_ln, precision="highest")
    grad_temporal = jnp.where(is_class[:, None], 0.0, grad_spatial + grad_ln).astype(bf16)
    grad_temporal = pos_hop(grad_temporal)
    acc_tfc = outer_sum(projected, grad_temporal)
    grad_proj = back_mul(grad_temporal, w_tfc).astype(bf16)
    acc_tproj = outer_sum(mixed_t, grad_proj)
    grad_mixed_t = back_mul(grad_proj, w_tproj).astype(bf16)
    grad_packed_t = jnp.concatenate(
        attention_backward(query_t, keys_t, values_t, allowed_t, log_total_t, grad_mixed_t), axis=1
    )
    acc_tqkv = outer_sum(normed_t, grad_packed_t)
    grad_ln, gain_t, shift_t = norm_backward(
        back_mul(grad_packed_t, w_tqkv), normal_t, inv_std_t, gains[0]
    )
    tokens_grad = from_temporal((grad_temporal.astype(f32) + grad_ln).astype(bf16)).astype(f32)

    class_all = jnp.zeros((MB, CLIPS, D), f32)
    class_all = lax.dynamic_update_index_in_dim(class_all, class_part, micro, 0)
    class_grad = lax.psum(class_all, AXES)
    sum_s = column_sum(grad_packed_s)
    sum_t = column_sum(grad_packed_t)
    small_grads = jnp.stack(
        [gain_t, gain_s, gain_m, shift_t, shift_s, shift_m]
        + [sum_t[:D], sum_t[2 * D :], column_sum(grad_proj), column_sum(grad_temporal)]
        + [sum_s[:D], sum_s[2 * D :], column_sum(grad_spatial_b), column_sum(grad_out)],
        axis=1,
    )
    small_grads = jnp.concatenate([column_sum(grad_hidden).reshape(D, 4), small_grads], axis=1)
    small_grads = jnp.pad(small_grads, ((0, 0), (0, 256 - small_grads.shape[1]))).astype(bf16)
    scatter = lambda mats, widths: layout.split(
        *layout.scatter(*part(layout, table, mats, blocks)), widths
    )
    (acc_out,) = scatter([acc_out], widths_out)
    (acc_in,) = scatter([acc_in], widths_in)
    acc_sqkv, acc_sproj = scatter([acc_sqkv, acc_sproj], widths_s)
    acc_tqkv, acc_tproj, acc_tfc, small_grads = scatter(
        [acc_tqkv, acc_tproj, acc_tfc, small_grads], widths_t
    )
    return (
        block_out,
        tokens_grad,
        class_grad,
        acc_tqkv,
        acc_tproj,
        acc_tfc,
        acc_sqkv,
        acc_sproj,
        acc_in,
        acc_out,
        small_grads[:, :4].reshape(-1),
        small_grads[:, 4:7],
        small_grads[:, 7:10],
        small_grads[:, 10:18],
    )


def solution(mesh):
    rows = P(AXES, None)
    wide = P(None, "frame", "pos", None)
    placed = (wide, P(), P(), wide) + (rows,) * 7 + (P(AXES),) + (rows,) * 3
    return jax.shard_map(
        on_device,
        mesh=mesh,
        in_specs=placed,
        out_specs=(wide, wide, P()) + (rows,) * 7 + (P(AXES),) + (rows,) * 3,
        check_vma=False,
    )
```

```python
from functools import partial

import jax
import jax.numpy as jnp
from jax import lax
from jax.experimental import pallas as pl
from jax.experimental.pallas import tpu as pltpu
from jax.sharding import PartitionSpec as P

D = 768
HEADS = 12
HEAD = 64
FF = 4 * D
MB = 4
CLIPS = 3
AXES = ("frame", "pos")
TILE = 256
SMALL = 256
f32, bf16 = jnp.float32, jnp.bfloat16
GAIN, SHIFT, BIAS = 4, 7, 10


def send(values, perm):
    return lax.ppermute(values, AXES, perm)


def tie(value, *before):
    return lax.optimization_barrier((value,) + before)[0] if before else value


class Layout:
    def __init__(self):
        self.frames, self.chips = lax.axis_size("frame"), lax.axis_size("pos") // 2
        self.bits = self.frames.bit_length() - 1
        self.frame, self.chip = lax.axis_index("frame"), lax.axis_index("pos") // 2
        self.core = lax.axis_index("pos") % 2
        self.swap = self.perm(lambda f, z, c: (f, z, 1 - c))
        self.along = [self.perm(lambda f, z, c, i=i: (f, z ^ i, c)) for i in range(1, self.chips)]
        self.across = [
            self.perm(lambda f, z, c, k=k: (f ^ (1 << self.bit(k, c)), z, c))
            for k in range(self.bits)
        ]

        share = self.frames // MB
        steps = lambda n: [1 << k for k in range(n.bit_length() - 1)]
        self.within = [self.swap]
        self.within += [self.perm(lambda f, z, c, k=k: (f, z ^ k, c)) for k in steps(self.chips)]
        self.within += [self.perm(lambda f, z, c, k=k: (f ^ k, z, c)) for k in steps(share)]
        self.between = [
            self.perm(lambda f, z, c, k=k * share: (f ^ k, z, c)) for k in steps(MB)
        ]

    def bit(self, step, core):
        return (step + core) % self.bits

    def perm(self, to):
        pairs = []
        for f in range(self.frames):
            for z in range(self.chips):
                for c in range(2):
                    g, y, d = to(f, z, c)
                    pairs.append(
                        ((f * self.chips + z) * 2 + c, (g * self.chips + y) * 2 + d)
                    )
        return pairs

    def table(self):
        rows = []
        for core in (self.core, 1 - self.core):
            blocks = []
            for b in range(self.frames * self.chips):
                flags, i = b // self.chips, b % self.chips
                f = self.frame
                for k in range(self.bits):
                    if flags >> k & 1:
                        f = f ^ (1 << ((k + core) % self.bits))
                blocks.append(f * self.chips + (self.chip ^ i))
            rows.append(jnp.stack(blocks))
        return jnp.concatenate([jnp.stack(rows).reshape(-1), self.core[None]]).astype(jnp.int32)

    def pick(self, low, high):
        return jnp.where(self.core == 0, low, high), jnp.where(self.core == 0, high, low)

    def halves(self, mats):
        low = jnp.concatenate([m[:, : m.shape[1] // 2] for m in mats], axis=1)
        high = jnp.concatenate([m[:, m.shape[1] // 2 :] for m in mats], axis=1)
        return self.pick(low, high)

    def chip_rows(self, keep, got):
        return jnp.concatenate(self.pick(keep, got), axis=0)

    def split(self, low, high, widths):
        mats, at = [], 0
        for width in widths:
            half = width // 2
            mats.append(jnp.concatenate([low[:, at : at + half], high[:, at : at + half]], axis=1))
            at += half
        return mats


class Way:
    def __init__(self, layout, *state):
        self.layout, self.state = layout, state


def meet(*things):
    values = tuple(t.state if isinstance(t, Way) else t for t in things)
    values = lax.optimization_barrier(values)
    out = []
    for thing, value in zip(things, values):
        if isinstance(thing, Way):
            thing.state = value
        else:
            out.append(value)
    return out[0] if len(out) == 1 else out


class Gather(Way):
    def along(self):
        (block,) = self.state
        self.state = (block,) + tuple(send(block, p) for p in self.layout.along)

    def across(self, step):
        if step == 0:
            self.state = (jnp.stack(self.state),)
        self.state += tuple(send(piece, self.layout.across[step]) for piece in self.state)

    def swap(self):
        self.state = (self.state, tuple(send(piece, self.layout.swap) for piece in self.state))


class Scatter(Way):
    def __init__(self, layout, mine, other):
        near = [mine[0]], [send(other[0], layout.swap)]
        far = [mine[1]], [send(other[1], layout.swap)]
        super().__init__(layout, tuple(near[0] + near[1]), tuple(far[0] + far[1]))

    def across(self, step):
        near, far = self.state
        if far is None:
            half = near[0].shape[0] // 2
            near, far = tuple(a[:half] for a in near), tuple(a[half:] for a in near)
        far = total(far).astype(bf16)
        self.state = (near + (send(far, self.layout.across[step]),), None)
        return far

    def along(self):
        near, _ = self.state
        parts = total(near)
        away = parts.astype(bf16)
        self.state = (parts[0],) + tuple(
            send(away[i + 1], p) for i, p in enumerate(self.layout.along)
        )

    def swap(self):
        sums = total(self.state)
        rows = sums.shape[0] // 2
        keep, give = self.layout.pick(sums[:rows], sums[rows:])
        self.state = (keep, send(give, self.layout.swap))

    def finish(self, widths):
        return self.layout.split(*self.layout.pick(*self.state), widths)


def total(values):
    out = values[0].astype(f32)
    for value in values[1:]:
        out = out + value.astype(f32)
    return out


class Chunk:
    def __init__(self, layout, widths, rows):
        self.layout, self.widths, self.rows = layout, widths, rows
        self.count = layout.frames * layout.chips
        self.table = layout.table()
        self.half = sum(widths) // 2
        self.whole = bool(rows % 16)
        if self.whole:
            core = layout.core.astype(jnp.int32)
            self.index = jnp.stack([jnp.zeros_like(core)] * 2 + [core])
            self.blocks, self.block_rows = 1, self.count * rows
        else:
            self.index = self.table
            self.blocks, self.block_rows = self.count, rows

    def load(self, way):
        mine, other = way.state
        if self.whole:
            order = jnp.argsort(self.table[: 2 * self.count].reshape(2, -1), axis=1)
            mine, other = [
                (jnp.concatenate(a)[o].reshape(1, self.block_rows, -1),)
                for a, o in zip((mine, other), order)
            ]
        self.mine, self.other = mine, other
        return self

    def operands(self):
        pieces = [[(a, "h") for a in side] for side in (self.mine, self.other)]
        return [[(self.index, "s")] + pieces]

    def grads(self):
        if self.whole:
            piece = [((1, self.block_rows, self.half), bf16, "h")]
        else:
            piece = [((self.count // 2, self.block_rows, self.half), bf16, "h")] * 2
        return [[piece, piece]]

    def at(self, which):
        return sum(self.widths[:which]) // 2

    def fetch(self, which, weights, dst, sem):
        self._copies(which, *weights, dst, sem, True)

    def store(self, which, table, src, grads, sem):
        self._copies(which, table, *grads, src, sem, False)

    def _copies(self, which, table, mine, other, mat, sem, into):
        at, w = self.at(which), self.widths[which] // 2
        core = table[2 * self.blocks]
        for side, pieces in ((0, mine), (1, other)):
            half = core if side == 0 else 1 - core
            first = side * self.blocks
            for piece in pieces:

                def body(b, carry, piece=piece, first=first, half=half):
                    row = pl.multiple_of(table[first + b] * self.block_rows, 16)
                    block = piece.at[b, :, at : at + w]
                    place = mat.at[
                        pl.ds(row, self.block_rows), pl.ds(pl.multiple_of(half * w, 128), w)
                    ]
                    pair = (block, place) if into else (place, block)
                    pltpu.make_async_copy(*pair, sem).start()
                    return carry

                lax.fori_loop(0, piece.shape[0], body, 0)
                first += piece.shape[0]

    def scatter(self, mine, other):
        if self.whole:
            order = self.table[: 2 * self.count].reshape(2, -1)
            mine, other = [
                a[0].reshape(self.count, self.rows, -1)[o] for a, o in zip((mine, other), order)
            ]
            half = self.count // 2
            mine, other = [(a[:half], a[half:]) for a in (mine, other)]
        return Scatter(self.layout, mine, other)


def arrived(mat, sem):
    pltpu.make_async_copy(mat, mat, sem).wait()


SPACE = {"s": pltpu.SMEM, "v": pltpu.VMEM, "h": pltpu.HBM}


def flat(items):
    return [leaf for item in items for leaf in (flat(item) if isinstance(item, list) else [item])]


def nest(items, leaves):
    return [nest(item, leaves) if isinstance(item, list) else next(leaves) for item in items]


def call(name, body, ins, outs, scratch, sems, flops, alias=None):
    operands, results = flat(ins), flat(outs)
    bytes_of = lambda shape, kind: jnp.dtype(kind).itemsize * _size(shape)
    size = sum(bytes_of(a.shape, a.dtype) for a, space in operands if space == "v")
    size += sum(bytes_of(shape, kind) for shape, kind, space in results if space == "v")
    size += sum(bytes_of(shape, kind) for shape, kind in scratch)
    moved = sum(bytes_of(a.shape, a.dtype) for a, _ in operands)
    moved += sum(bytes_of(shape, kind) for shape, kind, _ in results)
    aliases = {}
    for i, o in (alias or {}).items():
        start, end = len(flat(ins[:i])), len(flat(outs[:o]))
        for k in range(len(flat([ins[i]]))):
            aliases[start + k] = end + k

    def kernel(*refs):
        leaves = iter(refs)
        body(*nest(ins, leaves), *nest(outs, leaves), *leaves)

    values = pl.pallas_call(
        kernel,
        out_shape=[jax.ShapeDtypeStruct(shape, kind) for shape, kind, _ in results],
        in_specs=[pl.BlockSpec(memory_space=SPACE[space]) for _, space in operands],
        out_specs=[pl.BlockSpec(memory_space=SPACE[space]) for _, _, space in results],
        scratch_shapes=[pltpu.VMEM(shape, kind) for shape, kind in scratch]
        + [pltpu.SemaphoreType.DMA((sems,))],
        input_output_aliases=aliases,
        compiler_params=pltpu.CompilerParams(
            vmem_limit_bytes=min(int(size * 1.1) + (12 << 20), 60 << 20)
        ),
        cost_estimate=pl.CostEstimate(flops=flops, bytes_accessed=moved, transcendentals=0),
        name=name,
    )(*[a for a, _ in operands])
    return nest(outs, iter(values))


def _size(shape):
    total = 1
    for n in shape:
        total *= n
    return total


def tiles(width, body, size=TILE):
    def step(j, carry):
        body(pl.ds(pl.multiple_of(j * size, size), size))
        return carry

    lax.fori_loop(0, width // size, step, 0)


def dot(a, b):
    return jnp.dot(a, b, preferred_element_type=f32)


def dot_t(a, b):
    return lax.dot_general(a, b, (((1,), (1,)), ((), ())), preferred_element_type=f32)


def normalise(values):
    centred = values - jnp.mean(values, axis=-1, keepdims=True)
    inv_std = lax.rsqrt(jnp.mean(centred * centred, axis=-1, keepdims=True) + 1e-06)
    return centred * inv_std, inv_std


def norm_rows(values, small, which):
    normal, _ = normalise(values)
    return normal * small[GAIN + which : GAIN + which + 1] + small[SHIFT + which : SHIFT + which + 1]


def norm_back(values, upstream, small, which):
    normal, inv_std = normalise(values)
    product = upstream * normal
    grad_gain = jnp.sum(product, axis=0, keepdims=True)
    grad_shift = jnp.sum(upstream, axis=0, keepdims=True)
    gain = small[GAIN + which : GAIN + which + 1]
    scaled = upstream * gain
    mean = jnp.mean(scaled, axis=-1, keepdims=True)
    mean_normal = jnp.mean(product * gain, axis=-1, keepdims=True)
    return inv_std * (scaled - mean - normal * mean_normal), grad_gain, grad_shift


def column_sum(values):
    return jnp.sum(values.astype(f32), axis=0, keepdims=True)


def set_mask(mask, key_ids, query_ids):
    mask[...] = jnp.where(key_ids[...] == query_ids[...], 0.0, -1000000000.0)


def head_lanes(h, value):
    lane = lax.broadcasted_iota(jnp.int32, (1, 2 * HEAD), 1)
    return jnp.where(lane // HEAD == h, value, 0.0)


def only(values, lanes):
    return (values.astype(f32) * lanes).astype(bf16)


def attend(query, q_at, pairs, k_at, v_at, mask, mixed, lse):
    def pair(i, carry):
        cols = lambda at: pl.ds(pl.multiple_of(at + i * 2 * HEAD, 2 * HEAD), 2 * HEAD)
        queries, keys = query[:, cols(q_at)], pairs[:, cols(k_at)]
        values = pairs[:, cols(v_at)].astype(f32).T.astype(bf16)
        outs = []
        for h in range(2):
            score = dot_t(keys, only(queries, head_lanes(h, 0.125))) + mask[...]
            top = jnp.max(score, axis=0, keepdims=True)
            weight = jnp.exp(score - top)
            total = jnp.sum(weight, axis=0, keepdims=True)
            lse[pl.ds(2 * i + h, 1), :] = top + jnp.log(total)
            probs = (weight * (1.0 / total)).astype(bf16)
            outs.append(dot(values[h * HEAD : (h + 1) * HEAD], probs))
        mixed[:, cols(0)] = jnp.concatenate(outs, axis=0).T.astype(bf16)
        return carry

    lax.fori_loop(0, HEADS // 2, pair, 0)


def attend_back(query, q_at, pairs, k_at, v_at, mask, lse, grad, out_q, out_pairs, gk_at, gv_at):
    def pair(i, carry):
        cols = lambda at: pl.ds(pl.multiple_of(at + i * 2 * HEAD, 2 * HEAD), 2 * HEAD)
        queries, keys, values = query[:, cols(q_at)], pairs[:, cols(k_at)], pairs[:, cols(v_at)]
        upstream = grad[:, cols(0)]
        keys_across = keys.astype(f32).T.astype(bf16)
        grad_keys = grad_values = 0.0
        outs = []
        for h in range(2):
            queries_h = only(queries, head_lanes(h, 0.125))
            upstream_h = only(upstream, head_lanes(h, 1.0))
            score = dot_t(keys, queries_h) + mask[...]
            probs = jnp.exp(score - lse[pl.ds(2 * i + h, 1), :])
            dprob = dot_t(values, upstream_h)
            delta = jnp.sum(probs * dprob, axis=0, keepdims=True)
            dscore = (probs * (dprob - delta)).astype(bf16)
            grad_keys += dot(dscore, queries_h)
            grad_values += dot(probs.astype(bf16), upstream_h)
            outs.append(dot(keys_across[h * HEAD : (h + 1) * HEAD], dscore))
        out_q[:, cols(0)] = (jnp.concatenate(outs, axis=0).T * 0.125).astype(bf16)
        out_pairs[:, cols(gk_at)] = grad_keys.astype(bf16)
        out_pairs[:, cols(gv_at)] = grad_values.astype(bf16)
        return carry

    lax.fori_loop(0, HEADS // 2, pair, 0)


def qkv_tiles(x, w, bias, small, which, packed):
    bias[:, :D] = small[BIAS + which : BIAS + which + 1]
    bias[:, D : 2 * D] = jnp.zeros((1, D), f32)
    bias[:, 2 * D :] = small[BIAS + which + 1 : BIAS + which + 2]

    def tile(cols):
        packed[:, cols] = (dot(x[...], w[:, cols]) + bias[:, cols]).astype(bf16)

    tiles(3 * D, tile)


def across(mat, out):
    for at in range(0, mat.shape[1], 128):
        out[at : at + 128, :] = mat[:, at : at + 128].astype(f32).T.astype(bf16)


def temporal_qkv_kernel(chunk, weights, rows, packed, small, w, raw, x, bias, sem):
    chunk.fetch(3, weights, raw, sem.at[0])
    chunk.fetch(0, weights, w, sem.at[1])
    arrived(raw, sem.at[0])
    small[...] = raw[:, :128].astype(f32).T[: small.shape[0]]
    x[...] = norm_rows(rows[...].astype(f32), small, 0).astype(bf16)
    arrived(w, sem.at[1])
    qkv_tiles(x, w, bias, small, 0, packed)


def temporal_mix_kernel(
    chunk, weights, packed, rows, key_ids, query_ids, small,
    mixed, projected, lse, temporal, w_proj, w_fc, mask, sem,
):
    chunk.fetch(1, weights, w_proj, sem.at[0])
    chunk.fetch(2, weights, w_fc, sem.at[1])
    set_mask(mask, key_ids, query_ids)
    attend(packed, 0, packed, D, 2 * D, mask, mixed, lse)
    arrived(w_proj, sem.at[0])

    def project(cols):
        bias = small[BIAS + 2 : BIAS + 3, cols]
        projected[:, cols] = (dot(mixed[...], w_proj[:, cols]) + bias).astype(bf16)

    tiles(D, project)
    arrived(w_fc, sem.at[1])

    def residual(cols):
        added = dot(projected[...], w_fc[:, cols]) + small[BIAS + 3 : BIAS + 4, cols]
        temporal[:, cols] = (rows[:, cols].astype(f32) + added).astype(bf16)

    tiles(D, residual)


def spatial_qkv_kernel(
    chunk, weights, rows, choose, class_rows, is_class, small,
    temporal, packed, w, x, bias, sem,
):
    chunk.fetch(0, weights, w, sem.at[0])
    values = jnp.where(
        is_class[...] > 0, dot(choose[...], class_rows[...]), rows[...].astype(f32)
    )
    temporal[...] = values.astype(bf16)
    x[...] = norm_rows(values, small, 1).astype(bf16)
    arrived(w, sem.at[0])
    qkv_tiles(x, w, bias, small, 4, packed)


def spatial_mix_kernel(
    chunk, k_at, weights, packed, pairs, key_ids, query_ids, temporal, small,
    mixed, lse, spatial, w, mask, sem,
):
    chunk.fetch(1, weights, w, sem.at[0])
    set_mask(mask, key_ids, query_ids)
    attend(packed, 0, pairs, k_at, k_at + D, mask, mixed, lse)
    arrived(w, sem.at[0])

    def residual(cols):
        added = dot(mixed[...], w[:, cols]) + small[BIAS + 6 : BIAS + 7, cols]
        spatial[:, cols] = temporal[:, cols].astype(f32) + added

    tiles(D, residual)


def hidden_kernel(
    chunk, weights, spatial, in_bias, small, normed, activated, slope, w, sem
):
    chunk.fetch(0, weights, w, sem.at[0])
    normed[...] = norm_rows(spatial[...], small, 2).astype(bf16)
    arrived(w, sem.at[0])

    def tile(cols):
        hidden = dot(normed[...], w[:, cols]) + in_bias[:, cols]
        below = 0.5 + 0.5 * lax.erf(hidden * 0.7071067811865476)
        density = jnp.exp(hidden * hidden * -0.5) * 0.3989422804014327
        activated[:, cols] = (hidden * below).astype(bf16)
        slope[:, cols] = (below + hidden * density).astype(bf16)

    tiles(FF, tile)


def out_grad_kernel(chunk, table, activated, grad_out, grads, grad, sem):
    def tile(cols):
        grad[cols, :] = dot(activated[:, cols].astype(f32).T.astype(bf16), grad_out[...]).astype(bf16)

    tiles(FF, tile)
    chunk.store(0, table, grad, grads, sem.at[0])
    arrived(grad, sem.at[0])


def mlp_back_kernel(
    chunk_in, chunk_out, weights_in, weights_out,
    grad_out, slope, spatial, small, grad_hidden, in_bias, grad_spatial, sums,
    w_in, w_out, total, sem,
):
    chunk_out.fetch(0, weights_out, w_out, sem.at[0])
    chunk_in.fetch(0, weights_in, w_in, sem.at[1])
    total[...] = jnp.zeros_like(total)
    arrived(w_out, sem.at[0])
    arrived(w_in, sem.at[1])

    def tile(cols):
        grad = (dot_t(grad_out[...], w_out[cols, :]) * slope[:, cols].astype(f32)).astype(bf16)
        grad_hidden[:, cols] = grad
        in_bias[:, cols] = column_sum(grad)
        total[...] += dot_t(grad, w_in[:, cols])

    tiles(FF, tile)
    back, gain, shift = norm_back(spatial[...], total[...], small, 2)
    upstream = grad_out[...].astype(f32)
    result = upstream + back
    grad_spatial[...] = result
    sums[0:1] = gain
    sums[1:2] = shift
    sums[2:3] = column_sum(upstream)
    sums[3:4] = column_sum(result.astype(bf16))
    sums[4:8] = jnp.zeros((4, D), f32)


def in_grad_kernel(chunk, table, normed, grad_hidden, grads, normed_t, grad, sem):
    across(normed, normed_t)

    def tile(cols):
        grad[:, cols] = dot(normed_t[...], grad_hidden[:, cols]).astype(bf16)

    tiles(FF, tile)
    chunk.store(0, table, grad, grads, sem.at[0])
    arrived(grad, sem.at[0])


def block_out_kernel(
    chunk, weights, activated, spatial, small, result, w, total, sem
):
    chunk.fetch(0, weights, w, sem.at[0])
    total[...] = spatial[...] + small[BIAS + 7 : BIAS + 8]
    arrived(w, sem.at[0])

    def tile(cols):
        total[...] += dot(activated[:, cols], w[cols, :])

    tiles(FF, tile)
    result[...] = total[...].astype(bf16)


def spatial_attention_back_kernel(
    chunk, k_at, weights, grad_spatial, mixed, packed, pairs, key_ids, query_ids, lse,
    grads, grad_query, grad_pairs,
    w, upstream, mixed_t, grad, grad_mixed, mask, sem,
):
    chunk.fetch(1, weights, w, sem.at[0])
    upstream[...] = grad_spatial[...].astype(bf16)
    set_mask(mask, key_ids, query_ids)
    arrived(w, sem.at[0])

    def back(cols):
        grad_mixed[:, cols] = dot_t(upstream[...], w[cols, :]).astype(bf16)

    tiles(D, back)
    across(mixed, mixed_t)

    def tile(cols):
        grad[:, cols] = dot(mixed_t[...], upstream[:, cols]).astype(bf16)

    tiles(D, tile)
    chunk.store(1, weights[0], grad, grads, sem.at[1])
    attend_back(
        packed, 0, pairs, k_at, k_at + D, mask, lse, grad_mixed, grad_query, grad_pairs, 0, D
    )
    arrived(grad, sem.at[1])


def qkv_back(normed_t, grad_packed, w, grad, total):
    total[...] = jnp.zeros_like(total)

    def tile(cols):
        grad[:, cols] = dot(normed_t[...], grad_packed[:, cols]).astype(bf16)
        total[...] += dot_t(grad_packed[:, cols], w[:, cols])

    tiles(3 * D, tile)


def spatial_qkv_back_kernel(
    chunk, weights, grad_query, grad_pairs, temporal, grad_spatial, choose, is_class,
    small, old, grads, grad_temporal, class_part, sums,
    w, packed, normed, normed_t, grad, total, sem,
):
    chunk.fetch(0, weights, w, sem.at[0])
    packed[:, :D] = grad_query[...]
    packed[:, D:] = grad_pairs[...]
    values = temporal[...].astype(f32)
    normed[...] = norm_rows(values, small, 1).astype(bf16)
    across(normed, normed_t)
    arrived(w, sem.at[0])
    qkv_back(normed_t, packed, w, grad, total)
    chunk.store(0, weights[0], grad, grads, sem.at[1])
    back, gain, shift = norm_back(values, total[...], small, 1)
    result = grad_spatial[...] + back
    grad_temporal[...] = jnp.where(is_class[...] > 0, 0.0, result).astype(bf16)
    class_part[...] = jnp.zeros_like(class_part)
    for c in range(CLIPS):
        class_part[c : c + 1] = column_sum(back * choose[:, c : c + 1].astype(f32))
    sums[0:1] = gain
    sums[1:2] = shift
    sums[2:3] = column_sum(packed[:, :D])
    sums[3:4] = column_sum(packed[:, 2 * D :])
    sums[4:8] = jnp.zeros((4, D), f32)
    arrived(grad, sem.at[1])


def temporal_proj_back_kernel(
    chunk, chunk_back, weights, grad_temporal, projected, mixed,
    grads, grad_mixed, sums,
    w_proj, w_fc, grad_proj, proj_t, mixed_t, acc_proj, acc_fc, sem,
):
    chunk.fetch(2, weights, w_fc, sem.at[0])
    chunk.fetch(1, weights, w_proj, sem.at[1])
    across(projected, proj_t)

    def fc_tile(cols):
        acc_fc[:, cols] = dot(proj_t[...], grad_temporal[:, cols]).astype(bf16)

    tiles(D, fc_tile)
    chunk_back.store(1, weights[0], acc_fc, grads, sem.at[2])
    arrived(w_fc, sem.at[0])

    def fc_back(cols):
        grad_proj[:, cols] = dot_t(grad_temporal[...], w_fc[cols, :]).astype(bf16)

    tiles(D, fc_back)
    across(mixed, mixed_t)

    def proj_tile(cols):
        acc_proj[:, cols] = dot(mixed_t[...], grad_proj[:, cols]).astype(bf16)

    tiles(D, proj_tile)
    chunk_back.store(0, weights[0], acc_proj, grads, sem.at[3])
    arrived(w_proj, sem.at[1])

    def proj_back(cols):
        grad_mixed[:, cols] = dot_t(grad_proj[...], w_proj[cols, :]).astype(bf16)

    tiles(D, proj_back)
    sums[0:1] = column_sum(grad_temporal[...])
    sums[1:2] = column_sum(grad_proj[...])
    sums[2:8] = jnp.zeros((6, D), f32)
    arrived(acc_fc, sem.at[2])
    arrived(acc_proj, sem.at[3])


def temporal_attention_back_kernel(
    chunk, chunk_back, weights, packed, key_ids, query_ids, lse, grad_mixed, rows, grad_temporal,
    small, in_bias, sums_m, sums_s, sums_t,
    grads, tokens_grad,
    w, mask, grad_packed, normed, normed_t, grad, total, rows_small, raw, sem,
):
    chunk.fetch(0, weights, w, sem.at[0])
    set_mask(mask, key_ids, query_ids)
    attend_back(
        packed, 0, packed, D, 2 * D, mask, lse, grad_mixed, grad_packed, grad_packed, D, 2 * D
    )
    values = rows[...].astype(f32)
    normed[...] = norm_rows(values, small, 0).astype(bf16)
    across(normed, normed_t)
    arrived(w, sem.at[0])
    qkv_back(normed_t, grad_packed, w, grad, total)
    chunk_back.store(0, weights[0], grad, grads, sem.at[1])
    back, gain, shift = norm_back(values, total[...], small, 0)
    tokens_grad[...] = (grad_temporal[...].astype(f32) + back).astype(bf16)
    rows_small[...] = jnp.zeros_like(rows_small)
    rows_small[0:4] = in_bias[...]
    for i, (gain_row, shift_row) in enumerate(
        ((gain, shift), (sums_s[0:1], sums_s[1:2]), (sums_m[0:1], sums_m[1:2]))
    ):
        rows_small[GAIN + i : GAIN + i + 1] = gain_row
        rows_small[SHIFT + i : SHIFT + i + 1] = shift_row
    for i, row in enumerate(
        (
            column_sum(grad_packed[:, :D]),
            column_sum(grad_packed[:, 2 * D :]),
            sums_t[1:2],
            sums_t[0:1],
            sums_s[2:3],
            sums_s[3:4],
            sums_m[3:4],
            sums_m[2:3],
        )
    ):
        rows_small[BIAS + i : BIAS + i + 1] = row
    raw[:, :128] = rows_small[...].T.astype(bf16)
    raw[:, 128:] = jnp.zeros((D, 128), bf16)
    chunk_back.store(1, weights[0], raw, grads, sem.at[2])
    arrived(grad, sem.at[1])
    arrived(raw, sem.at[2])


def on_device(
    tokens,
    class_tokens,
    clip_frames,
    cotangent,
    temporal_qkv,
    temporal_proj,
    temporal_fc,
    spatial_qkv,
    spatial_proj,
    mlp_in,
    mlp_out,
    mlp_in_bias,
    norm_gains,
    norm_shifts,
    biases,
):
    frame_size, pos_size = lax.axis_size("frame"), lax.axis_size("pos")
    frame_index, pos_index = lax.axis_index("frame"), lax.axis_index("pos")
    frame_count, pos_count = tokens.shape[1], tokens.shape[2]
    shard = norm_gains.shape[0]
    slots = pos_count + 1
    share = frame_size // MB
    my_slots = slots // share
    all_frames = frame_count * frame_size
    my_frames = all_frames // pos_size
    rows_count = all_frames * my_slots
    micro = frame_index // share

    layout = Layout()
    small = jnp.concatenate(
        [mlp_in_bias.reshape(shard, 4), norm_gains, norm_shifts, biases], axis=1
    )
    small = jnp.pad(small, ((0, 0), (0, SMALL - small.shape[1])))
    keep_t, give_t = layout.halves((temporal_qkv, temporal_proj, temporal_fc, small))
    keep_s, give_s = layout.halves((spatial_qkv, spatial_proj))
    keep_in, give_in = layout.halves((mlp_in,))
    keep_out, give_out = layout.halves((mlp_out,))
    got_t = send(give_t, layout.swap)
    got = send(tie(jnp.concatenate([give_s, give_in], axis=1), give_t), layout.swap)
    got_out = send(tie(give_out, give_t), layout.swap)
    cut = keep_s.shape[1]
    way_t = Gather(layout, layout.chip_rows(keep_t, got_t))
    way_s = Gather(layout, layout.chip_rows(keep_s, got[:, :cut]))
    way_in = Gather(layout, layout.chip_rows(keep_in, got[:, cut:]))
    way_out = Gather(layout, layout.chip_rows(keep_out, got_out))
    chunk_t = Chunk(layout, (3 * D, D, D, SMALL), 2 * shard)
    chunk_s = Chunk(layout, (3 * D, D), 2 * shard)
    chunk_in = Chunk(layout, (FF,), 2 * shard)
    chunk_out = Chunk(layout, (D,), 8 * shard)
    chunk_proj = Chunk(layout, (D, D), 2 * shard)
    chunk_qkv = Chunk(layout, (3 * D, SMALL), 2 * shard)
    later = range(1, layout.bits)

    def frame_hop(values):
        return lax.all_to_all(values, "frame", 0, 0, tiled=True)

    def pos_hop(values):
        parts = values.reshape(pos_size, rows_count // pos_size, D)
        return lax.all_to_all(parts, "pos", 0, 0, tiled=True).reshape(rows_count, D)

    def to_temporal(values):
        padded = jnp.pad(values, ((0, 0), (0, 0), (0, 1), (0, 0)))
        padded = padded.reshape(MB, frame_count, share, my_slots, D).transpose(0, 2, 1, 3, 4)
        return frame_hop(padded.reshape(frame_size, frame_count * my_slots, D)).reshape(
            rows_count, D
        )

    def from_temporal(values):
        parts = frame_hop(values.reshape(frame_size, frame_count * my_slots, D))
        parts = parts.reshape(MB, share, frame_count, my_slots, D).transpose(0, 2, 1, 3, 4)
        return parts.reshape(MB, frame_count, slots, D)[:, :, :pos_count]

    def partners(values, step):
        perm = [(f, f // share * share + (f % share + step) % share) for f in range(frame_size)]
        return lax.ppermute(values, "frame", perm)

    row_ids = jnp.arange(rows_count, dtype=jnp.int32)
    row_slot = row_ids % my_slots
    clip_ends = jnp.cumsum(lax.dynamic_index_in_dim(clip_frames, micro, 0, keepdims=False))
    clip_of = lambda frame: jnp.sum(
        (frame[:, None] >= clip_ends[None, :]).astype(jnp.int32), axis=1
    )
    group_t = row_slot * CLIPS + clip_of(row_ids // my_slots)
    ids_t = [(group_t[:, None], "v"), (group_t[None, :], "v")]
    frame_s = row_ids // my_slots % my_frames
    clip_s = clip_of(pos_index * my_frames + frame_s)
    first_source = row_ids < my_frames * my_slots

    def key_masks(share_index):
        padding = row_slot + share_index * my_slots == slots - 1
        is_class = padding & first_source
        return is_class, is_class | ~padding

    keys_s = []
    for step in range(share):
        _, valid = key_masks((frame_index + share - step) % share)
        keys_s.append(jnp.where(valid, frame_s, -1))
    ids_s = [(jnp.concatenate(keys_s)[:, None], "v"), (frame_s[None, :], "v")]
    is_class, _ = key_masks(frame_index % share)
    choose = (clip_s[:, None] == jnp.arange(8)[None, :]) & is_class[:, None]
    choose = (choose.astype(bf16), "v")
    class_rows = lax.dynamic_index_in_dim(class_tokens, micro, 0, keepdims=False)
    class_rows = (jnp.pad(class_rows, ((0, 8 - CLIPS), (0, 0))), "v")
    is_class = (is_class.astype(jnp.int32)[:, None], "v")

    n = rows_count
    narrow, wide, full = (n, D), (n, 3 * D), (n, FF)
    heads = (16, n)
    flops = lambda columns: 2 * n * D * columns

    way_t.along()
    rows = to_temporal(tokens)
    rows = meet(way_t, way_s, way_in, way_out, rows)
    way_t.across(0)
    way_s.along()
    meet(way_t, way_s)
    for step in later:
        way_t.across(step)
    way_in.state = (tie(way_in.state[0], way_s.state[1]),)
    way_in.along()
    meet(way_t, way_in)
    way_t.swap()
    way_s.across(0)
    cotangent = meet(way_t, way_s, cotangent)
    for step in later:
        way_s.across(step)
    way_out.state = (tie(way_out.state[0], way_in.state[1]),)
    way_out.along()
    packed_t, small_t = call(
        "temporal_qkv",
        partial(temporal_qkv_kernel, chunk_t),
        chunk_t.load(way_t).operands() + [(rows, "v")],
        [(wide, bf16, "v"), ((32, D), f32, "v")],
        [((D, 3 * D), bf16), ((D, SMALL), bf16), (narrow, bf16), ((1, 3 * D), f32)],
        2,
        flops(3 * D),
    )
    small = (small_t, "v")
    grad_out = to_temporal(cotangent)
    mixed_t, projected, lse_t, temporal = call(
        "temporal_mix",
        partial(temporal_mix_kernel, chunk_t),
        chunk_t.operands() + [(packed_t, "v"), (rows, "v")] + ids_t + [small],
        [(narrow, bf16, "v"), (narrow, bf16, "v"), (heads, f32, "v"), (narrow, bf16, "v")],
        [((D, D), bf16), ((D, D), bf16), ((n, n), f32)],
        2,
        flops(2 * D + 4 * n),
    )
    temporal = meet(way_s, way_out, temporal)
    temporal = pos_hop(temporal)
    way_s.swap()
    way_in.across(0)
    temporal, grad_out = meet(way_s, way_in, temporal, grad_out)
    for step in later:
        way_in.across(step)
    grad_out = pos_hop(grad_out)
    temporal, packed_s = call(
        "spatial_qkv",
        partial(spatial_qkv_kernel, chunk_s),
        chunk_s.load(way_s).operands() + [(temporal, "v"), choose, class_rows, is_class, small],
        [(narrow, bf16, "v"), (wide, bf16, "v")],
        [((D, 3 * D), bf16), (narrow, bf16), ((1, 3 * D), f32)],
        1,
        flops(3 * D),
    )
    temporal = (temporal, "v")
    pairs, k_at = packed_s, D
    if share > 1:
        pairs = [packed_s[:, D:]]
        for step in range(1, share):
            pairs.append(partners(packed_s[:, D:], step))
        pairs, k_at = jnp.concatenate(pairs, axis=0), 0
    all_keys = share * n
    mixed_s, lse_s, spatial = call(
        "spatial_mix",
        partial(spatial_mix_kernel, chunk_s, k_at),
        chunk_s.operands() + [(packed_s, "v"), (pairs, "v")] + ids_s + [temporal, small],
        [(narrow, bf16, "v"), (heads, f32, "v"), (narrow, f32, "v")],
        [((D, D), bf16), ((all_keys, n), f32)],
        1,
        flops(D + 4 * all_keys),
    )
    spatial, grad_out = meet(way_in, spatial, grad_out)
    spatial, grad_out = (spatial, "v"), (grad_out, "v")
    way_in.swap()
    way_out.across(0)
    meet(way_in, way_out)
    for step in later:
        way_out.across(step)
    in_bias = (small_t[:4].T.reshape(1, FF), "v")
    normed_m, activated, slope = call(
        "hidden",
        partial(hidden_kernel, chunk_in),
        chunk_in.load(way_in).operands() + [spatial, in_bias, small],
        [(narrow, bf16, "v"), (full, bf16, "v"), (full, bf16, "v")],
        [((D, FF), bf16)],
        1,
        flops(FF),
    )
    activated = (activated, "v")
    (acc_out,) = call(
        "mlp_out_grad",
        partial(out_grad_kernel, chunk_out),
        [(chunk_out.index, "s"), activated, grad_out],
        chunk_out.grads(),
        [((FF, D), bf16)],
        1,
        flops(FF),
    )
    acc_out, slope = meet(way_out, acc_out, slope)
    way_out.swap()
    back_out = chunk_out.scatter(*acc_out)
    slope = meet(way_out, back_out, slope)
    for step in reversed(later):
        back_out.across(step)
    grad_hidden, grad_in_bias, grad_spatial, sums_m = call(
        "mlp_back",
        partial(mlp_back_kernel, chunk_in, chunk_out),
        chunk_in.operands()
        + chunk_out.load(way_out).operands()
        + [grad_out, (slope, "v"), spatial, small],
        [(full, bf16, "v"), ((1, FF), f32, "v"), (narrow, f32, "v"), ((8, D), f32, "v")],
        [((D, FF), bf16), ((FF, D), bf16), (narrow, f32)],
        2,
        flops(2 * FF),
    )
    grad_hidden = meet(back_out, grad_hidden)
    back_out.across(0)
    (acc_in,) = call(
        "mlp_in_grad",
        partial(in_grad_kernel, chunk_in),
        [(chunk_in.index, "s"), (normed_m, "v"), (grad_hidden, "v")],
        chunk_in.grads(),
        [((D, n), bf16), ((D, FF), bf16)],
        1,
        flops(FF),
    )
    acc_in, grad_spatial = meet(back_out, acc_in, grad_spatial)
    back_in = chunk_in.scatter(*acc_in)
    grad_spatial = meet(back_in, grad_spatial)
    for step in reversed(later):
        back_in.across(step)
    back_out.along()
    grad_spatial = (grad_spatial, "v")
    acc_s, grad_query, grad_pairs = call(
        "spatial_attention_back",
        partial(spatial_attention_back_kernel, chunk_s, k_at),
        chunk_s.operands()
        + [grad_spatial, (mixed_s, "v"), (packed_s, "v"), (pairs, "v")]
        + ids_s
        + [(lse_s, "v")],
        chunk_s.grads() + [(narrow, bf16, "v"), ((all_keys, 2 * D), bf16, "v")],
        [((D, D), bf16), (narrow, bf16), ((D, n), bf16), ((D, D), bf16), (narrow, bf16)]
        + [((all_keys, n), f32)],
        2,
        flops(2 * D + 10 * all_keys),
    )
    grad_query, grad_pairs = meet(back_in, back_out, grad_query, grad_pairs)
    back_in.across(0)
    back_out.swap()
    own_pairs = grad_pairs[:n]
    for step in range(1, share):
        theirs = partners(grad_pairs[step * n : (step + 1) * n], share - step)
        own_pairs = (own_pairs.astype(f32) + theirs.astype(f32)).astype(bf16)
    acc_s, grad_temporal, class_part, sums_s = call(
        "spatial_qkv_back",
        partial(spatial_qkv_back_kernel, chunk_s),
        chunk_s.operands()
        + [(grad_query, "v"), (own_pairs, "v"), temporal, grad_spatial, choose, is_class, small]
        + [[[(a, "h") for a in side] for side in acc_s]],
        chunk_s.grads() + [(narrow, bf16, "v"), ((8, D), f32, "v"), ((8, D), f32, "v")],
        [((D, 3 * D), bf16), (wide, bf16), (narrow, bf16), ((D, n), bf16)]
        + [((D, 3 * D), bf16), (narrow, f32)],
        2,
        flops(6 * D),
        {8: 0},
    )
    acc_s, grad_temporal, class_part = meet(back_in, back_out, acc_s, grad_temporal, class_part)
    grad_temporal = pos_hop(grad_temporal)
    back_s = chunk_s.scatter(*acc_s)
    activated = meet(back_s, activated[0])
    for step in reversed(later):
        far = back_s.across(step)
    (result,) = call(
        "block_out",
        partial(block_out_kernel, chunk_out),
        chunk_out.operands() + [(tie(activated, far), "v"), spatial, small],
        [(narrow, bf16, "v")],
        [((FF, D), bf16), (narrow, f32)],
        1,
        flops(FF),
    )
    grad_temporal, class_part, result = meet(back_s, back_in, grad_temporal, class_part, result)
    back_s.across(0)
    back_in.along()
    class_sum = class_part[:CLIPS]
    class_sum = class_sum + send(class_sum, layout.within[0])
    grad_temporal = (grad_temporal, "v")
    acc_proj, grad_mixed_t, sums_t = call(
        "temporal_proj_back",
        partial(temporal_proj_back_kernel, chunk_t, chunk_proj),
        chunk_t.operands() + [grad_temporal, (projected, "v"), (mixed_t, "v")],
        chunk_proj.grads() + [(narrow, bf16, "v"), ((8, D), f32, "v")],
        [((D, D), bf16), ((D, D), bf16), (narrow, bf16), ((D, n), bf16), ((D, n), bf16)]
        + [((D, D), bf16), ((D, D), bf16)],
        4,
        flops(4 * D),
    )
    acc_proj, grad_mixed_t, class_sum, result = meet(
        back_s, back_in, acc_proj, grad_mixed_t, class_sum, result
    )
    back_proj = chunk_proj.scatter(*acc_proj)
    grad_mixed_t, result = meet(back_proj, back_in, grad_mixed_t, result)
    for step in reversed(later):
        back_proj.across(step)
    back_s.along()
    back_in.swap()
    result = pos_hop(result)
    class_sum = class_sum + send(class_sum, layout.within[1])
    acc_qkv, tokens_grad = call(
        "temporal_attention_back",
        partial(temporal_attention_back_kernel, chunk_t, chunk_qkv),
        chunk_t.operands()
        + [(packed_t, "v")]
        + ids_t
        + [(lse_t, "v"), (grad_mixed_t, "v"), (rows, "v"), grad_temporal, small]
        + [(grad_in_bias.reshape(D, 4).T, "v"), (sums_m, "v"), (sums_s, "v"), (sums_t, "v")],
        chunk_qkv.grads() + [(narrow, bf16, "v")],
        [((D, 3 * D), bf16), ((n, n), f32), (wide, bf16), (narrow, bf16), ((D, n), bf16)]
        + [((D, 3 * D), bf16), (narrow, f32), ((128, D), f32), ((D, SMALL), bf16)],
        3,
        flops(6 * D + 10 * n),
    )
    acc_qkv, tokens_grad, class_sum, result = meet(
        back_s, back_in, back_proj, acc_qkv, tokens_grad, class_sum, result
    )
    back_qkv = chunk_qkv.scatter(*acc_qkv)
    back_proj.across(0)
    for perm in layout.within[2:]:
        class_sum = class_sum + send(class_sum, perm)
    result, class_sum = meet(back_qkv, back_proj, result, class_sum)
    for step in reversed(later):
        back_qkv.across(step)
    back_s.swap()
    back_proj.along()
    block_out = from_temporal(result)
    class_grad = jnp.zeros((MB, CLIPS, D), f32)
    class_grad = lax.dynamic_update_index_in_dim(class_grad, class_sum, micro, 0)
    class_grad = class_grad + send(class_grad, layout.between[0])
    tokens_grad, class_grad, block_out = meet(
        back_qkv, back_s, back_proj, tokens_grad, class_grad, block_out
    )
    back_qkv.across(0)
    back_proj.swap()
    for perm in layout.between[1:]:
        class_grad = class_grad + send(class_grad, perm)
    tokens_grad, class_grad = meet(back_qkv, back_proj, tokens_grad, class_grad)
    back_qkv.along()
    tokens_grad = from_temporal(tokens_grad).astype(f32)
    tokens_grad = meet(back_qkv, tokens_grad)
    back_qkv.swap()

    (acc_out,) = back_out.finish(chunk_out.widths)
    (acc_in,) = back_in.finish(chunk_in.widths)
    acc_sqkv, acc_sproj = back_s.finish(chunk_s.widths)
    acc_tproj, acc_tfc = back_proj.finish(chunk_proj.widths)
    acc_tqkv, small_grads = back_qkv.finish(chunk_qkv.widths)
    return (
        block_out,
        tokens_grad,
        class_grad,
        acc_tqkv,
        acc_tproj,
        acc_tfc,
        acc_sqkv,
        acc_sproj,
        acc_in,
        acc_out,
        small_grads[:, :4].reshape(-1),
        small_grads[:, 4:7],
        small_grads[:, 7:10],
        small_grads[:, 10:18],
    )


def solution(mesh):
    rows = P(AXES, None)
    wide = P(None, "frame", "pos", None)
    placed = (wide, P(), P(), wide) + (rows,) * 7 + (P(AXES),) + (rows,) * 3
    return jax.shard_map(
        on_device,
        mesh=mesh,
        in_specs=placed,
        out_specs=(wide, wide, P()) + (rows,) * 7 + (P(AXES),) + (rows,) * 3,
        check_vma=False,
    )
```

```python
from functools import partial

import jax
import jax.numpy as jnp
from jax import lax
from jax.experimental import pallas as pl
from jax.experimental.pallas import tpu as pltpu
from jax.sharding import PartitionSpec as P

D = 768
HEADS = 12
HEAD = 64
FF = 4 * D
MB = 4
CLIPS = 3
AXES = ("frame", "pos")
TILE = 768
SMALL = 256
f32, bf16 = jnp.float32, jnp.bfloat16
GAIN, SHIFT, BIAS = 4, 7, 10


def send(values, perm):
    return lax.ppermute(values, AXES, perm)


def tie(value, *before):
    return lax.optimization_barrier((value,) + before)[0] if before else value


class Layout:
    def __init__(self):
        self.frames, self.chips = lax.axis_size("frame"), lax.axis_size("pos") // 2
        self.bits = self.frames.bit_length() - 1
        self.frame, self.chip = lax.axis_index("frame"), lax.axis_index("pos") // 2
        self.core = lax.axis_index("pos") % 2
        self.core_index = self.core.astype(jnp.int32).reshape(1)
        self.swap = self.perm(lambda f, z, c: (f, z, 1 - c))
        self.along = [self.perm(lambda f, z, c, i=i: (f, z ^ i, c)) for i in range(1, self.chips)]
        self.across = [
            self.perm(lambda f, z, c, k=k: (f ^ (1 << self.bit(k, c)), z, c))
            for k in range(self.bits)
        ]

        share = self.frames // MB
        steps = lambda n: [1 << k for k in range(n.bit_length() - 1)]
        self.within = [self.swap]
        self.within += [self.perm(lambda f, z, c, k=k: (f, z ^ k, c)) for k in steps(self.chips)]
        self.within += [self.perm(lambda f, z, c, k=k: (f ^ k, z, c)) for k in steps(share)]

    def bit(self, step, core):
        return (step + core) % self.bits

    def perm(self, to):
        pairs = []
        for f in range(self.frames):
            for z in range(self.chips):
                for c in range(2):
                    g, y, d = to(f, z, c)
                    pairs.append(
                        ((f * self.chips + z) * 2 + c, (g * self.chips + y) * 2 + d)
                    )
        return pairs

    def table(self):
        rows = []
        for core in (self.core, 1 - self.core):
            blocks = []
            for b in range(self.frames * self.chips):
                flags, i = b // self.chips, b % self.chips
                f = self.frame
                for k in range(self.bits):
                    if flags >> k & 1:
                        f = f ^ (1 << ((k + core) % self.bits))
                blocks.append(f * self.chips + (self.chip ^ i))
            rows.append(jnp.stack(blocks))
        return jnp.concatenate([jnp.stack(rows).reshape(-1), self.core[None]]).astype(jnp.int32)

    def pick(self, low, high):
        return jnp.where(self.core == 0, low, high), jnp.where(self.core == 0, high, low)

    def chip_rows(self, keep, got):
        return jnp.concatenate(self.pick(keep, got), axis=0)


class Way:
    def __init__(self, layout, *state):
        self.layout, self.state = layout, state


def meet(*things):
    values = tuple(t.state if isinstance(t, Way) else t for t in things)
    values = lax.optimization_barrier(values)
    out = []
    for thing, value in zip(things, values):
        if isinstance(thing, Way):
            thing.state = value
        else:
            out.append(value)
    return out[0] if len(out) == 1 else out


class Gather(Way):
    def along(self):
        ((block,), _) = self.state
        self.state = ((block,) + tuple(send(block, p) for p in self.layout.along), ())

    def across(self, step):
        mine, _ = self.state
        block = jnp.stack(mine) if step == 0 else jnp.concatenate(mine)
        self.state = ((block, send(block, self.layout.across[step])), ())

    def swap(self, count=None):
        mine, other = self.state
        other += tuple(send(a, self.layout.swap) for a in mine[len(other) : count])
        self.state = (mine, other)


class Scatter(Way):
    def __init__(self, layout, mine, other):
        near, far = [(a, send(b, layout.swap)) for a, b in zip(mine, other)]
        super().__init__(layout, near, far)
        self.count = near[0].shape[0]

    def across(self, step):
        near, far = self.state
        if not far:
            self.count //= 2
            far = tuple(a[self.count : 2 * self.count] for a in near)
        far = total(far).astype(bf16)
        self.state = (near + (send(far, self.layout.across[step]),), ())
        return far

    def along(self):
        near, _ = self.state
        parts = total(tuple(a[: self.count] for a in near))
        away = parts.astype(bf16)
        self.state = (parts[0],) + tuple(
            send(away[i + 1], p) for i, p in enumerate(self.layout.along)
        )

    def swap(self):
        rows, width = self.state[0].shape
        kept = ((rows // 2, width), f32, "v")
        keep, give = call(
            "sum_parts",
            sum_parts_kernel,
            [(self.layout.core_index, "s"), [(a, "v") for a in self.state]],
            [kept, kept],
            [],
            1,
            0,
        )
        self.state = (keep, send(give, self.layout.swap))

    def finish(self, widths):
        keep, got = self.state
        rows = keep.shape[0]
        outs = [((rows, width), f32, "v") for width in widths if width != SMALL]
        if SMALL in widths:
            outs += [((count, rows), f32, "v") for count in (4, 3, 3, 8)]
        return call(
            "finish",
            partial(finish_kernel, widths),
            [(self.layout.core_index, "s"), (keep, "v"), (got, "v")],
            outs,
            [((128, 128), f32)],
            1,
            0,
        )


def total(values):
    out = values[0].astype(f32)
    for value in values[1:]:
        out = out + value.astype(f32)
    return out


class Chunk:
    def __init__(self, layout, widths, rows):
        self.layout, self.widths, self.rows = layout, widths, rows
        self.count = layout.frames * layout.chips
        self.table = layout.table()
        self.half = sum(widths) // 2
        self.whole = bool(rows % 16)
        if self.whole:
            core = layout.core.astype(jnp.int32)
            self.index = jnp.stack([jnp.zeros_like(core)] * 2 + [core])
            self.blocks, self.block_rows = 1, self.count * rows
        else:
            self.index = self.table
            self.blocks, self.block_rows = self.count, rows

    def load(self, way):
        mine, other = way.state
        if self.whole:
            order = jnp.argsort(self.table[: 2 * self.count].reshape(2, -1), axis=1)
            mine, other = [
                (jnp.concatenate(a)[o].reshape(1, self.block_rows, -1),)
                for a, o in zip((mine, other), order)
            ]
        self.mine, self.other = mine, other
        return self

    def operands(self):
        pieces = [[(a, "h") for a in side] for side in (self.mine, self.other)]
        return [[(self.index, "s")] + pieces]

    def grads(self):
        if self.whole:
            piece = [((1, self.block_rows, self.half), bf16, "h")]
        else:
            piece = [((self.count // 2, self.block_rows, self.half), bf16, "h")] * 2
        return [[piece, piece]]

    def at(self, which):
        return sum(self.widths[:which]) // 2

    def fetch(self, which, weights, dst, sem):
        self._copies(which, *weights, dst, sem, True)

    def store(self, which, table, src, grads, sem):
        self._copies(which, table, *grads, src, sem, False)

    def _copies(self, which, table, mine, other, mat, sem, into):
        at, w = self.at(which), self.widths[which] // 2
        core = table[2 * self.blocks]
        for side, pieces in ((0, mine), (1, other)):
            half = core if side == 0 else 1 - core
            first = side * self.blocks
            for piece in pieces:

                def body(b, carry, piece=piece, first=first, half=half):
                    row = pl.multiple_of(table[first + b] * self.block_rows, 16)
                    block = piece.at[b, :, at : at + w]
                    place = mat.at[
                        pl.ds(row, self.block_rows), pl.ds(pl.multiple_of(half * w, 128), w)
                    ]
                    pair = (block, place) if into else (place, block)
                    pltpu.make_async_copy(*pair, sem).start()
                    return carry

                lax.fori_loop(0, piece.shape[0], body, 0)
                first += piece.shape[0]

    def scatter(self, mine, other):
        if self.whole:
            order = self.table[: 2 * self.count].reshape(2, -1)
            mine, other = [
                a[0].reshape(self.count, self.rows, -1)[o] for a, o in zip((mine, other), order)
            ]
            half = self.count // 2
            mine, other = [(a[:half], a[half:]) for a in (mine, other)]
        return Scatter(self.layout, mine, other)


def pack_kernel(widths, small, core, *refs):
    mats, (keep, give) = refs[: len(widths)], refs[-4:-2]
    turned = refs[-2]
    at = 0
    first = core[0] == 0
    for mat, width in zip(mats, widths):
        w = width // 2
        low, high = mat[:, :w], mat[:, w:]
        keep[:, at : at + w] = jnp.where(first, low, high)
        give[:, at : at + w] = jnp.where(first, high, low)
        at += w
    if small:
        rows = keep.shape[0]
        turned[...] = jnp.zeros_like(turned)
        place = 0
        for ref in refs[len(widths) : -4]:
            count = ref.shape[0]
            turned[place : place + count, :rows] = ref[...].astype(f32)
            place += count
        values = turned[...].T[:rows].astype(bf16)
        zeros = jnp.zeros_like(values)
        keep[:, at:] = jnp.where(first, values, zeros)
        give[:, at:] = jnp.where(first, zeros, values)


def pack(layout, mats, small=()):
    rows = mats[0].shape[0]
    width = sum(m.shape[1] for m in mats) // 2 + (SMALL // 2 if small else 0)
    half = ((rows, width), bf16, "v")
    return call(
        "pack",
        partial(pack_kernel, [m.shape[1] for m in mats], len(small)),
        [(layout.core_index, "s")] + [(m, "v") for m in mats] + [(m, "v") for m in small],
        [half, half],
        [((128, 128), f32)],
        1,
        0,
    )


def sum_parts_kernel(core, parts, keep, give, sem):
    values = total([p[...] for p in parts])
    rows = keep.shape[0]
    first = core[0] == 0
    keep[...] = jnp.where(first, values[:rows], values[rows:])
    give[...] = jnp.where(first, values[rows:], values[:rows])


def finish_kernel(widths, core, keep, got, *refs):
    outs, turned = refs[:-2], refs[-2]
    first = core[0] == 0
    at = 0
    for i, width in enumerate(widths):
        w = width // 2
        mine, other = keep[:, at : at + w], got[:, at : at + w]
        low = jnp.where(first, mine, other)
        if width != SMALL:
            outs[i][:, :w] = low
            outs[i][:, w:] = jnp.where(first, other, mine)
        else:
            rows = keep.shape[0]
            turned[...] = jnp.zeros_like(turned)
            turned[:rows, :] = low
            values = turned[...].T
            place = 0
            for out in outs[i:]:
                out[...] = values[place : place + out.shape[0], :rows]
                place += out.shape[0]
        at += w


def arrived(mat, sem):
    pltpu.make_async_copy(mat, mat, sem).wait()


SPACE = {"s": pltpu.SMEM, "v": pltpu.VMEM, "h": pltpu.HBM}


def flat(items):
    return [leaf for item in items for leaf in (flat(item) if isinstance(item, list) else [item])]


def nest(items, leaves):
    return [nest(item, leaves) if isinstance(item, list) else next(leaves) for item in items]


def call(name, body, ins, outs, scratch, sems, flops, alias=None):
    operands, results = flat(ins), flat(outs)
    bytes_of = lambda shape, kind: jnp.dtype(kind).itemsize * _size(shape)
    size = sum(bytes_of(a.shape, a.dtype) for a, space in operands if space == "v")
    size += sum(bytes_of(shape, kind) for shape, kind, space in results if space == "v")
    size += sum(bytes_of(shape, kind) for shape, kind in scratch)
    moved = sum(bytes_of(a.shape, a.dtype) for a, _ in operands)
    moved += sum(bytes_of(shape, kind) for shape, kind, _ in results)
    aliases = {}
    for i, o in (alias or {}).items():
        start, end = len(flat(ins[:i])), len(flat(outs[:o]))
        for k in range(len(flat([ins[i]]))):
            aliases[start + k] = end + k

    def kernel(*refs):
        leaves = iter(refs)
        body(*nest(ins, leaves), *nest(outs, leaves), *leaves)

    values = pl.pallas_call(
        kernel,
        out_shape=[jax.ShapeDtypeStruct(shape, kind) for shape, kind, _ in results],
        in_specs=[pl.BlockSpec(memory_space=SPACE[space]) for _, space in operands],
        out_specs=[pl.BlockSpec(memory_space=SPACE[space]) for _, _, space in results],
        scratch_shapes=[pltpu.VMEM(shape, kind) for shape, kind in scratch]
        + [pltpu.SemaphoreType.DMA((sems,))],
        input_output_aliases=aliases,
        compiler_params=pltpu.CompilerParams(
            vmem_limit_bytes=min(int(size * 1.1) + (12 << 20), 60 << 20)
        ),
        cost_estimate=pl.CostEstimate(flops=flops, bytes_accessed=moved, transcendentals=0),
        name=name,
    )(*[a for a, _ in operands])
    return nest(outs, iter(values))


def _size(shape):
    total = 1
    for n in shape:
        total *= n
    return total


def tiles(width, body, size=TILE):
    def step(j, carry):
        body(pl.ds(pl.multiple_of(j * size, size), size))
        return carry

    lax.fori_loop(0, width // size, step, 0)


def dot(a, b):
    return jnp.dot(a, b, preferred_element_type=f32)


def dot_t(a, b):
    return lax.dot_general(a, b, (((1,), (1,)), ((), ())), preferred_element_type=f32)


def normalise(values):
    centred = values - jnp.mean(values, axis=-1, keepdims=True)
    inv_std = lax.rsqrt(jnp.mean(centred * centred, axis=-1, keepdims=True) + 1e-06)
    return centred * inv_std, inv_std


def norm_rows(values, small, which):
    normal, _ = normalise(values)
    return normal * small[GAIN + which : GAIN + which + 1] + small[SHIFT + which : SHIFT + which + 1]


def norm_back(values, upstream, small, which):
    normal, inv_std = normalise(values)
    product = upstream * normal
    grad_gain = jnp.sum(product, axis=0, keepdims=True)
    grad_shift = jnp.sum(upstream, axis=0, keepdims=True)
    gain = small[GAIN + which : GAIN + which + 1]
    scaled = upstream * gain
    mean = jnp.mean(scaled, axis=-1, keepdims=True)
    mean_normal = jnp.mean(product * gain, axis=-1, keepdims=True)
    return inv_std * (scaled - mean - normal * mean_normal), grad_gain, grad_shift


def column_sum(values):
    return jnp.sum(values.astype(f32), axis=0, keepdims=True)


def set_mask(mask, key_ids, query_ids):
    mask[...] = jnp.where(key_ids[...] == query_ids[...], 0.0, -1000000000.0)


def regroup(values, flat, out, groups):
    count = out.shape[0] // groups
    for c in range(flat.shape[0]):
        cols = slice(c * 128, (c + 1) * 128)
        flat[c] = values[:, cols]
        for g in range(groups):
            out[g * count : (g + 1) * count, cols] = flat[c, pl.ds(g, count, stride=groups), :]


def ungroup(grouped, flat, groups):
    count = grouped.shape[0] // groups
    for c in range(flat.shape[0]):
        cols = slice(c * 128, (c + 1) * 128)
        for g in range(groups):
            flat[c, pl.ds(g, count, stride=groups), :] = grouped[g * count : (g + 1) * count, cols]
    return jnp.concatenate([flat[c] for c in range(flat.shape[0])], axis=1)


def swap_groups(source, out, outer, inner):
    size = source.shape[0] // (outer * inner)
    for i in range(outer):
        for j in range(inner):
            to, at = (j * outer + i) * size, (i * inner + j) * size
            out[to : to + size, :] = source[at : at + size, :]


def both_heads(values, scale):
    lane = lax.broadcasted_iota(jnp.int32, (1, 2 * HEAD), 1)
    wide = values.astype(f32)
    parts = [jnp.where(lane // HEAD == h, wide * scale, 0.0) for h in range(2)]
    return jnp.concatenate(parts, axis=0).astype(bf16)


def own_heads(across):
    size = across.shape[1] // 2
    return jnp.concatenate([across[:HEAD, :size], across[HEAD:, size:]], axis=0).T


def key_rows(pairs, cols, start, size, rows):
    parts = [pairs[at + start : at + start + size, cols] for at in range(0, pairs.shape[0], rows)]
    return parts[0] if len(parts) == 1 else jnp.concatenate(parts, axis=0)


def attend(query, q_at, pairs, k_at, v_at, mask, mixed, lse):
    rows, size = query.shape[0], mask.shape[1] // 2
    blocks = range(rows // size)

    def pair(i, carry):
        cols = lambda at: pl.ds(pl.multiple_of(at + i * 2 * HEAD, 2 * HEAD), 2 * HEAD)
        here = [slice(b * size, (b + 1) * size) for b in blocks]
        queries = [both_heads(query[h, cols(q_at)], 0.125) for h in here]
        keys = [key_rows(pairs, cols(k_at), b * size, size, rows) for b in blocks]
        values = [key_rows(pairs, cols(v_at), b * size, size, rows).T for b in blocks]
        score = [dot_t(keys[b], queries[b]) + mask[...] for b in blocks]
        top = [jnp.max(score[b], axis=0, keepdims=True) for b in blocks]
        weight = [jnp.exp(score[b] - top[b]) for b in blocks]
        norm = [jnp.sum(weight[b], axis=0, keepdims=True) for b in blocks]
        probs = [(weight[b] * (1.0 / norm[b])).astype(bf16) for b in blocks]
        out = [own_heads(dot(values[b], probs[b])).astype(bf16) for b in blocks]
        for b in blocks:
            lse[pl.ds(i * len(blocks) + b, 1), :] = top[b] + jnp.log(norm[b])
            mixed[here[b], cols(0)] = out[b]
        return carry

    lax.fori_loop(0, HEADS // 2, pair, 0, unroll=HEADS // 2)


def attend_back(query, q_at, pairs, k_at, v_at, mask, lse, grad, out_q, out_pairs, gk_at, gv_at):
    rows, size = query.shape[0], mask.shape[1] // 2
    blocks = range(rows // size)

    def pair(i, carry):
        cols = lambda at: pl.ds(pl.multiple_of(at + i * 2 * HEAD, 2 * HEAD), 2 * HEAD)
        here = [slice(b * size, (b + 1) * size) for b in blocks]
        keys = [key_rows(pairs, cols(k_at), b * size, size, rows) for b in blocks]
        values = [key_rows(pairs, cols(v_at), b * size, size, rows) for b in blocks]
        queries = [both_heads(query[h, cols(q_at)], 0.125) for h in here]
        upstream = [both_heads(grad[h, cols(0)], 1.0) for h in here]
        logs = [lse[pl.ds(i * len(blocks) + b, 1), :] for b in blocks]
        across_keys = [keys[b].T for b in blocks]
        score = [dot_t(keys[b], queries[b]) + mask[...] for b in blocks]
        dprob = [dot_t(values[b], upstream[b]) for b in blocks]
        probs = [jnp.exp(score[b] - logs[b]) for b in blocks]
        delta = [jnp.sum(probs[b] * dprob[b], axis=0, keepdims=True) for b in blocks]
        dscore = [(probs[b] * (dprob[b] - delta[b])).astype(bf16) for b in blocks]
        grad_keys = [dot(dscore[b], queries[b]).astype(bf16) for b in blocks]
        grad_values = [dot(probs[b].astype(bf16), upstream[b]).astype(bf16) for b in blocks]
        grad_queries = [
            (own_heads(dot(across_keys[b], dscore[b])) * 0.125).astype(bf16) for b in blocks
        ]
        for b in blocks:
            out_q[here[b], cols(0)] = grad_queries[b]
            for part in range(0, pairs.shape[0], rows):
                there = slice(part + b * size, part + (b + 1) * size)
                seen = slice(part // rows * size, (part // rows + 1) * size)
                out_pairs[there, cols(gk_at)] = grad_keys[b][seen]
                out_pairs[there, cols(gv_at)] = grad_values[b][seen]
        return carry

    lax.fori_loop(0, HEADS // 2, pair, 0, unroll=HEADS // 2)


def qkv_tiles(x, w, bias, small, which, packed):
    bias[:, :D] = small[BIAS + which : BIAS + which + 1]
    bias[:, D : 2 * D] = jnp.zeros((1, D), f32)
    bias[:, 2 * D :] = small[BIAS + which + 1 : BIAS + which + 2]

    def tile(cols):
        packed[:, cols] = (dot(x[...], w[:, cols]) + bias[:, cols]).astype(bf16)

    tiles(3 * D, tile)


def across(mat, out):
    for at in range(0, mat.shape[1], 128):
        out[at : at + 128, :] = mat[:, at : at + 128].astype(f32).T.astype(bf16)


def temporal_qkv_kernel(
    chunk, slots, weights, rows, packed, small, w, raw, x, bias, flat, grouped, sem
):
    chunk.fetch(3, weights, raw, sem.at[0])
    chunk.fetch(0, weights, w, sem.at[1])
    arrived(raw, sem.at[0])
    small[...] = raw[:, :128].astype(f32).T[: small.shape[0]]
    regroup(norm_rows(rows[...].astype(f32), small, 0), flat, grouped, slots)
    x[...] = grouped[...].astype(bf16)
    arrived(w, sem.at[1])
    qkv_tiles(x, w, bias, small, 0, packed)


def temporal_mix_kernel(
    chunk, slots, weights, packed, rows, key_ids, query_ids, small,
    mixed, projected, lse, temporal, w_proj, w_fc, mask, grouped, flat, sem,
):
    chunk.fetch(1, weights, w_proj, sem.at[0])
    chunk.fetch(2, weights, w_fc, sem.at[1])
    set_mask(mask, key_ids, query_ids)
    attend(packed, 0, packed, D, 2 * D, mask, mixed, lse)
    arrived(w_proj, sem.at[0])

    def project(cols):
        bias = small[BIAS + 2 : BIAS + 3, cols]
        projected[:, cols] = (dot(mixed[...], w_proj[:, cols]) + bias).astype(bf16)

    tiles(D, project)
    arrived(w_fc, sem.at[1])

    def residual(cols):
        grouped[:, cols] = dot(projected[...], w_fc[:, cols]) + small[BIAS + 3 : BIAS + 4, cols]

    tiles(D, residual)
    temporal[...] = (rows[...].astype(f32) + ungroup(grouped, flat, slots)).astype(bf16)


def spatial_qkv_kernel(
    chunk, sources, frames, weights, rows, choose, class_rows, is_class, small,
    temporal, packed, w, x, bias, flat, grouped, sem,
):
    chunk.fetch(0, weights, w, sem.at[0])
    flat[...] = rows[...].astype(f32)
    swap_groups(flat, grouped, sources, frames)
    values = jnp.where(is_class[...] > 0, dot(choose[...], class_rows[...]), grouped[...])
    temporal[...] = values.astype(bf16)
    x[...] = norm_rows(values, small, 1).astype(bf16)
    arrived(w, sem.at[0])
    qkv_tiles(x, w, bias, small, 4, packed)


def spatial_mix_kernel(
    chunk, k_at, weights, packed, pairs, key_ids, query_ids, temporal, small,
    mixed, lse, spatial, w, mask, sem,
):
    chunk.fetch(1, weights, w, sem.at[0])
    set_mask(mask, key_ids, query_ids)
    attend(packed, 0, pairs, k_at, k_at + D, mask, mixed, lse)
    arrived(w, sem.at[0])

    def residual(cols):
        added = dot(mixed[...], w[:, cols]) + small[BIAS + 6 : BIAS + 7, cols]
        spatial[:, cols] = temporal[:, cols].astype(f32) + added

    tiles(D, residual)


def hidden_kernel(
    chunk, weights, spatial, in_bias, small, normed, activated, slope, w, sem
):
    chunk.fetch(0, weights, w, sem.at[0])
    normed[...] = norm_rows(spatial[...], small, 2).astype(bf16)
    arrived(w, sem.at[0])

    def tile(cols):
        hidden = dot(normed[...], w[:, cols]) + in_bias[:, cols]
        below = 0.5 + 0.5 * lax.erf(hidden * 0.7071067811865476)
        density = jnp.exp(hidden * hidden * -0.5) * 0.3989422804014327
        activated[:, cols] = (hidden * below).astype(bf16)
        slope[:, cols] = (below + hidden * density).astype(bf16)

    tiles(FF, tile)


def out_grad_kernel(chunk, table, activated, grad_out, grads, grad, sem):
    def tile(cols):
        turned = activated[:, cols].astype(f32).T.astype(bf16)
        grad[cols, :] = dot(turned, grad_out[...]).astype(bf16)

    tiles(FF, tile)
    chunk.store(0, table, grad, grads, sem.at[0])
    arrived(grad, sem.at[0])


def mlp_back_kernel(
    chunk_in, chunk_out, weights_in, weights_out,
    grad_out, slope, spatial, small, grad_hidden, in_bias, grad_spatial, sums,
    w_in, w_out, total, sem,
):
    chunk_out.fetch(0, weights_out, w_out, sem.at[0])
    chunk_in.fetch(0, weights_in, w_in, sem.at[1])
    arrived(w_out, sem.at[0])

    def tile(cols):
        grad = (dot_t(grad_out[...], w_out[cols, :]) * slope[:, cols].astype(f32)).astype(bf16)
        grad_hidden[:, cols] = grad
        in_bias[:, cols] = column_sum(grad)

    tiles(FF, tile)
    arrived(w_in, sem.at[1])

    def back(cols):
        total[:, cols] = dot_t(grad_hidden[...], w_in[cols, :])

    tiles(D, back, D // 2)
    back, gain, shift = norm_back(spatial[...], total[...], small, 2)
    upstream = grad_out[...].astype(f32)
    result = upstream + back
    grad_spatial[...] = result
    sums[0:1] = gain
    sums[1:2] = shift
    sums[2:3] = column_sum(upstream)
    sums[3:4] = column_sum(result.astype(bf16))
    sums[4:8] = jnp.zeros((4, D), f32)


def in_grad_kernel(chunk, table, normed, grad_hidden, grads, normed_t, grad, sem):
    across(normed, normed_t)

    def tile(cols):
        grad[:, cols] = dot(normed_t[...], grad_hidden[:, cols]).astype(bf16)

    tiles(FF, tile)
    chunk.store(0, table, grad, grads, sem.at[0])
    arrived(grad, sem.at[0])


def block_out_kernel(
    chunk, sources, frames, weights, activated, spatial, small, result, w, total, flat, sem
):
    chunk.fetch(0, weights, w, sem.at[0])
    arrived(w, sem.at[0])

    def tile(cols):
        added = dot(activated[...], w[:, cols]) + small[BIAS + 7 : BIAS + 8, cols]
        total[:, cols] = spatial[:, cols] + added

    tiles(D, tile, D // 2)
    swap_groups(total, flat, frames, sources)
    result[...] = flat[...].astype(bf16)


def spatial_attention_back_kernel(
    chunk, k_at, weights, grad_spatial, mixed, packed, pairs, key_ids, query_ids, lse,
    grad, grad_query, grad_pairs,
    w, upstream, mixed_t, grad_mixed, mask, sem,
):
    chunk.fetch(1, weights, w, sem.at[0])
    upstream[...] = grad_spatial[...].astype(bf16)
    set_mask(mask, key_ids, query_ids)
    arrived(w, sem.at[0])

    def back(cols):
        grad_mixed[:, cols] = dot_t(upstream[...], w[cols, :]).astype(bf16)

    tiles(D, back)
    across(mixed, mixed_t)

    def tile(cols):
        grad[:, cols] = dot(mixed_t[...], upstream[:, cols]).astype(bf16)

    tiles(D, tile)
    attend_back(
        packed, 0, pairs, k_at, k_at + D, mask, lse, grad_mixed, grad_query, grad_pairs, 0, D
    )


def qkv_back(normed_t, grad_packed, w, grad, total):
    def back(cols):
        total[:, cols] = dot_t(grad_packed[...], w[cols, :])

    tiles(D, back, D // 2)

    def tile(cols):
        grad[:, cols] = dot(normed_t[...], grad_packed[:, cols]).astype(bf16)

    tiles(3 * D, tile)


def spatial_qkv_back_kernel(
    chunk, chunk_back, sources, frames, weights, grad_query, grad_pairs, temporal, grad_spatial, choose, is_class,
    small, grads, grad_temporal, class_part, sums,
    w, packed, normed, normed_t, grad, total, flat, sem,
):
    chunk.fetch(0, weights, w, sem.at[0])
    packed[:, :D] = grad_query[...]
    packed[:, D:] = grad_pairs[...]
    values = temporal[...].astype(f32)
    normed[...] = norm_rows(values, small, 1).astype(bf16)
    across(normed, normed_t)
    arrived(w, sem.at[0])
    qkv_back(normed_t, packed, w, grad, total)
    chunk_back.store(0, weights[0], grad, grads, sem.at[1])
    back, gain, shift = norm_back(values, total[...], small, 1)
    total[...] = jnp.where(is_class[...] > 0, 0.0, grad_spatial[...] + back)
    swap_groups(total, flat, frames, sources)
    grad_temporal[...] = flat[...].astype(bf16)
    class_part[...] = jnp.zeros_like(class_part)
    for c in range(CLIPS):
        class_part[c : c + 1] = column_sum(back * choose[:, c : c + 1].astype(f32))
    sums[0:1] = gain
    sums[1:2] = shift
    sums[2:3] = column_sum(packed[:, :D])
    sums[3:4] = column_sum(packed[:, 2 * D :])
    sums[4:8] = jnp.zeros((4, D), f32)
    arrived(grad, sem.at[1])


def temporal_proj_back_kernel(
    chunk, chunk_back, slots, weights, acc_spatial, grad_rows, projected, mixed,
    grads, grad_mixed, sums,
    w_proj, w_fc, grad_proj, proj_t, mixed_t, acc_proj, acc_fc, grad_temporal, flat, grouped, sem,
):
    chunk.fetch(2, weights, w_fc, sem.at[0])
    chunk.fetch(1, weights, w_proj, sem.at[1])
    chunk_back.store(0, weights[0], acc_spatial, grads, sem.at[4])
    regroup(grad_rows[...].astype(f32), flat, grouped, slots)
    grad_temporal[...] = grouped[...].astype(bf16)
    across(projected, proj_t)

    def fc_tile(cols):
        acc_fc[:, cols] = dot(proj_t[...], grad_temporal[:, cols]).astype(bf16)

    tiles(D, fc_tile)
    chunk_back.store(2, weights[0], acc_fc, grads, sem.at[2])
    arrived(w_fc, sem.at[0])

    def fc_back(cols):
        grad_proj[:, cols] = dot_t(grad_temporal[...], w_fc[cols, :]).astype(bf16)

    tiles(D, fc_back)
    across(mixed, mixed_t)

    def proj_tile(cols):
        acc_proj[:, cols] = dot(mixed_t[...], grad_proj[:, cols]).astype(bf16)

    tiles(D, proj_tile)
    chunk_back.store(1, weights[0], acc_proj, grads, sem.at[3])
    arrived(w_proj, sem.at[1])

    def proj_back(cols):
        grad_mixed[:, cols] = dot_t(grad_proj[...], w_proj[cols, :]).astype(bf16)

    tiles(D, proj_back)
    sums[0:1] = column_sum(grad_temporal[...])
    sums[1:2] = column_sum(grad_proj[...])
    sums[2:8] = jnp.zeros((6, D), f32)
    arrived(acc_fc, sem.at[2])
    arrived(acc_proj, sem.at[3])
    arrived(acc_spatial, sem.at[4])


def temporal_attention_back_kernel(
    chunk, chunk_back, slots, weights, packed, key_ids, query_ids, lse, grad_mixed, rows, grad_temporal,
    small, in_bias, sums_m, sums_s, sums_t,
    grads, tokens_grad,
    w, mask, grad_packed, normed, normed_t, grad, total, flat, rows_small, raw, sem,
):
    chunk.fetch(0, weights, w, sem.at[0])
    set_mask(mask, key_ids, query_ids)
    attend_back(
        packed, 0, packed, D, 2 * D, mask, lse, grad_mixed, grad_packed, grad_packed, D, 2 * D
    )
    values = rows[...].astype(f32)
    regroup(norm_rows(values, small, 0), flat, total, slots)
    normed[...] = total[...].astype(bf16)
    across(normed, normed_t)
    arrived(w, sem.at[0])
    qkv_back(normed_t, grad_packed, w, grad, total)
    chunk_back.store(0, weights[0], grad, grads, sem.at[1])
    back, gain, shift = norm_back(values, ungroup(total, flat, slots), small, 0)
    tokens_grad[...] = (grad_temporal[...].astype(f32) + back).astype(bf16)
    rows_small[...] = jnp.zeros_like(rows_small)
    rows_small[0:4] = in_bias[...]
    for i, (gain_row, shift_row) in enumerate(
        ((gain, shift), (sums_s[0:1], sums_s[1:2]), (sums_m[0:1], sums_m[1:2]))
    ):
        rows_small[GAIN + i : GAIN + i + 1] = gain_row
        rows_small[SHIFT + i : SHIFT + i + 1] = shift_row
    for i, row in enumerate(
        (
            column_sum(grad_packed[:, :D]),
            column_sum(grad_packed[:, 2 * D :]),
            sums_t[1:2],
            sums_t[0:1],
            sums_s[2:3],
            sums_s[3:4],
            sums_m[3:4],
            sums_m[2:3],
        )
    ):
        rows_small[BIAS + i : BIAS + i + 1] = row
    raw[:, :128] = rows_small[...].T.astype(bf16)
    raw[:, 128:] = jnp.zeros((D, 128), bf16)
    chunk_back.store(1, weights[0], raw, grads, sem.at[2])
    arrived(grad, sem.at[1])
    arrived(raw, sem.at[2])


def on_device(
    tokens,
    class_tokens,
    clip_frames,
    cotangent,
    temporal_qkv,
    temporal_proj,
    temporal_fc,
    spatial_qkv,
    spatial_proj,
    mlp_in,
    mlp_out,
    mlp_in_bias,
    norm_gains,
    norm_shifts,
    biases,
):
    frame_size, pos_size = lax.axis_size("frame"), lax.axis_size("pos")
    frame_index, pos_index = lax.axis_index("frame"), lax.axis_index("pos")
    frame_count, pos_count = tokens.shape[1], tokens.shape[2]
    shard = norm_gains.shape[0]
    slots = pos_count + 1
    share = frame_size // MB
    my_slots = slots // share
    all_frames = frame_count * frame_size
    my_frames = all_frames // pos_size
    rows_count = all_frames * my_slots
    micro = frame_index // share

    layout = Layout()
    small = (mlp_in_bias.reshape(4, shard), norm_gains.T, norm_shifts.T, biases.T)
    keep_t, give_t = pack(layout, (temporal_qkv, temporal_proj, temporal_fc), small)
    keep, give = pack(layout, (spatial_qkv, spatial_proj, mlp_in))
    keep_out, give_out = pack(layout, (mlp_out,))
    got_t = send(give_t, layout.swap)
    got = send(tie(give, give_t), layout.swap)
    got_out = send(tie(give_out, give_t), layout.swap)
    way_t = Gather(layout, (layout.chip_rows(keep_t, got_t),), ())
    rest = layout.chip_rows(keep, got)
    way_s = Gather(layout, (rest[:, : 2 * D],), ())
    way_in = Gather(layout, (rest[:, 2 * D :],), ())
    way_out = Gather(layout, (layout.chip_rows(keep_out, got_out),), ())
    chunk_t = Chunk(layout, (3 * D, D, D, SMALL), 2 * shard)
    chunk_s = Chunk(layout, (3 * D, D), 2 * shard)
    chunk_in = Chunk(layout, (FF,), 2 * shard)
    chunk_out = Chunk(layout, (D,), 8 * shard)
    chunk_proj = Chunk(layout, (D, D, D), 2 * shard)
    chunk_sqkv = Chunk(layout, (3 * D,), 2 * shard)
    chunk_qkv = Chunk(layout, (3 * D, SMALL), 2 * shard)
    later = range(1, layout.bits)

    def frame_hop(values):
        return lax.all_to_all(values, "frame", 0, 0, tiled=True)

    def pos_hop(values):
        parts = values.reshape(pos_size, rows_count // pos_size, D)
        return lax.all_to_all(parts, "pos", 0, 0, tiled=True).reshape(rows_count, D)

    def to_temporal(*arrays):
        parts = []
        for values in arrays:
            padded = jnp.pad(values, ((0, 0), (0, 0), (0, 1), (0, 0)))
            padded = padded.reshape(MB, frame_count, share, my_slots, D).transpose(0, 2, 1, 3, 4)
            parts.append(padded.reshape(frame_size, frame_count * my_slots, D))
        hopped = frame_hop(jnp.concatenate(parts, axis=1)).reshape(frame_size, len(arrays), -1, D)
        return [hopped[:, i].reshape(rows_count, D) for i in range(len(arrays))]

    def from_temporal(values, extra=None):
        parts = values.reshape(frame_size, frame_count * my_slots, D)
        if extra is not None:
            extra = jnp.broadcast_to(extra, (frame_size,) + extra.shape)
            parts = jnp.concatenate([parts, extra], axis=1)
        hopped = frame_hop(parts)
        parts = hopped[:, : frame_count * my_slots]
        parts = parts.reshape(MB, share, frame_count, my_slots, D).transpose(0, 2, 1, 3, 4)
        parts = parts.reshape(MB, frame_count, slots, D)[:, :, :pos_count]
        return parts if extra is None else (parts, hopped[:, frame_count * my_slots :])

    def partners(values, step):
        perm = [(f, f // share * share + (f % share + step) % share) for f in range(frame_size)]
        return lax.ppermute(values, "frame", perm)

    n = rows_count
    clip_ends = jnp.cumsum(lax.dynamic_index_in_dim(clip_frames, micro, 0, keepdims=False))
    clip_of = lambda frame: jnp.sum(
        (frame[:, None] >= clip_ends[None, :]).astype(jnp.int32), axis=1
    )
    size_t = all_frames * max(1, 128 // all_frames)
    ids = jnp.arange(size_t, dtype=jnp.int32)
    ids = ids // all_frames * CLIPS + clip_of(ids % all_frames)
    ids_t = [(ids[:, None], "v"), (jnp.tile(ids, 2)[None, :], "v")]
    frame_rows = n // my_frames
    size_s = frame_rows * max(1, 128 // frame_rows)
    row_ids = jnp.arange(n, dtype=jnp.int32)
    frame_s, row_slot = row_ids // frame_rows, row_ids % my_slots
    first_source = row_ids % frame_rows < my_slots

    def key_masks(share_index):
        padding = row_slot + share_index * my_slots == slots - 1
        is_class = padding & first_source
        return is_class, is_class | ~padding

    keys_s = []
    for step in range(share):
        _, valid = key_masks((frame_index + share - step) % share)
        keys_s.append(jnp.where(valid, frame_s, -1)[:size_s])
    ids_s = [
        (jnp.concatenate(keys_s)[:, None], "v"),
        (jnp.tile(frame_s[:size_s], 2)[None, :], "v"),
    ]
    is_class, _ = key_masks(frame_index % share)
    clip_s = clip_of(pos_index * my_frames + frame_s)
    choose = (clip_s[:, None] == jnp.arange(8)[None, :]) & is_class[:, None]
    choose = (choose.astype(bf16), "v")
    class_rows = lax.dynamic_index_in_dim(class_tokens, micro, 0, keepdims=False)
    class_rows = (jnp.pad(class_rows, ((0, 8 - CLIPS), (0, 0))), "v")
    is_class = (is_class.astype(jnp.int32)[:, None], "v")

    narrow, wide, full = (n, D), (n, 3 * D), (n, FF)
    heads = lambda size: (-(-HEADS // 2 * (n // size) // 8) * 8, 2 * size)
    columns = (D // 128, n, 128)
    lse_shape_t, lse_shape_s = heads(size_t), heads(size_s)
    mask_t, mask_s = (size_t, 2 * size_t), (share * size_s, 2 * size_s)
    flops = lambda columns: 2 * n * D * columns

    way_t.along()
    rows, grad_out = to_temporal(tokens, cotangent)
    rows, grad_out = meet(way_t, way_s, way_in, way_out, rows, grad_out)
    way_t.across(0)
    way_s.along()
    meet(way_t, way_s)
    for step in later:
        way_t.across(step)
    way_t.swap(1)
    way_in.state = tie(way_in.state, way_s.state)
    way_in.along()
    meet(way_t, way_in)
    way_t.swap()
    way_s.across(0)
    meet(way_t, way_s, way_out)
    for step in later:
        way_s.across(step)
    way_out.along()
    packed_t, small_t = call(
        "temporal_qkv",
        partial(temporal_qkv_kernel, chunk_t, my_slots),
        chunk_t.load(way_t).operands() + [(rows, "v")],
        [(wide, bf16, "v"), ((32, D), f32, "v")],
        [((D, 3 * D), bf16), ((D, SMALL), bf16), (narrow, bf16), ((1, 3 * D), f32)]
        + [(columns, f32), (narrow, f32)],
        2,
        flops(3 * D),
    )
    small = (small_t, "v")
    mixed_t, projected, lse_t, temporal = call(
        "temporal_mix",
        partial(temporal_mix_kernel, chunk_t, my_slots),
        chunk_t.operands() + [(packed_t, "v"), (rows, "v")] + ids_t + [small],
        [(narrow, bf16, "v"), (narrow, bf16, "v"), (lse_shape_t, f32, "v"), (narrow, bf16, "v")],
        [((D, D), bf16), ((D, D), bf16), (mask_t, f32), (narrow, f32), (columns, f32)],
        2,
        flops(2 * D + 4 * n),
    )
    temporal, grad_out, small_t = meet(way_s, way_out, temporal, grad_out, small_t)
    temporal = pos_hop(temporal)
    way_s.swap()
    way_in.across(0)
    way_out.across(0)
    in_bias = small_t[:4].reshape(4, -1, shard).transpose(1, 0, 2).reshape(1, FF)
    temporal, in_bias = meet(way_s, way_in, way_out, temporal, in_bias)
    small = (small_t, "v")
    for step in later:
        way_in.across(step)
    way_in.swap(1)
    grad_out = pos_hop(grad_out).reshape(pos_size, my_frames, my_slots, D)
    grad_out = grad_out.transpose(1, 0, 2, 3).reshape(n, D)
    temporal, packed_s = call(
        "spatial_qkv",
        partial(spatial_qkv_kernel, chunk_s, pos_size, my_frames),
        chunk_s.load(way_s).operands() + [(temporal, "v"), choose, class_rows, is_class, small],
        [(narrow, bf16, "v"), (wide, bf16, "v")],
        [((D, 3 * D), bf16), (narrow, bf16), ((1, 3 * D), f32)] + [(narrow, f32)] * 2,
        1,
        flops(3 * D),
    )
    temporal = (temporal, "v")
    pairs, k_at = packed_s, D
    if share > 1:
        pairs = [packed_s[:, D:]]
        for step in range(1, share):
            pairs.append(partners(packed_s[:, D:], step))
        pairs, k_at = jnp.concatenate(pairs, axis=0), 0
    all_keys = share * n
    mixed_s, lse_s, spatial = call(
        "spatial_mix",
        partial(spatial_mix_kernel, chunk_s, k_at),
        chunk_s.operands() + [(packed_s, "v"), (pairs, "v")] + ids_s + [temporal, small],
        [(narrow, bf16, "v"), (lse_shape_s, f32, "v"), (narrow, f32, "v")],
        [((D, D), bf16), (mask_s, f32)],
        1,
        flops(D + 4 * all_keys),
    )
    spatial, grad_out = meet(way_in, spatial, grad_out)
    spatial, grad_out = (spatial, "v"), (grad_out, "v")
    way_in.swap()
    meet(way_in, way_out)
    for step in later:
        way_out.across(step)
    way_out.swap(1)
    in_bias = (in_bias, "v")
    normed_m, activated, slope = call(
        "hidden",
        partial(hidden_kernel, chunk_in),
        chunk_in.load(way_in).operands() + [spatial, in_bias, small],
        [(narrow, bf16, "v"), (full, bf16, "v"), (full, bf16, "v")],
        [((D, FF), bf16)],
        1,
        flops(FF),
    )
    activated = (activated, "v")
    (acc_out,) = call(
        "mlp_out_grad",
        partial(out_grad_kernel, chunk_out),
        [(chunk_out.index, "s"), activated, grad_out],
        chunk_out.grads(),
        [((FF, D), bf16)],
        1,
        flops(FF),
    )
    acc_out, slope = meet(way_out, acc_out, slope)
    way_out.swap()
    back_out = chunk_out.scatter(*acc_out)
    slope = meet(way_out, back_out, slope)
    for step in reversed(later):
        back_out.across(step)
    grad_hidden, grad_in_bias, grad_spatial, sums_m = call(
        "mlp_back",
        partial(mlp_back_kernel, chunk_in, chunk_out),
        chunk_in.operands()
        + chunk_out.load(way_out).operands()
        + [grad_out, (slope, "v"), spatial, small],
        [(full, bf16, "v"), ((1, FF), f32, "v"), (narrow, f32, "v"), ((8, D), f32, "v")],
        [((D, FF), bf16), ((FF, D), bf16), (narrow, f32)],
        2,
        flops(2 * FF),
    )
    grad_hidden, grad_in_bias = meet(back_out, grad_hidden, grad_in_bias)
    back_out.across(0)
    (acc_in,) = call(
        "mlp_in_grad",
        partial(in_grad_kernel, chunk_in),
        [(chunk_in.index, "s"), (normed_m, "v"), (grad_hidden, "v")],
        chunk_in.grads(),
        [((D, n), bf16), ((D, FF), bf16)],
        1,
        flops(FF),
    )
    acc_in, grad_spatial = meet(back_out, acc_in, grad_spatial)
    back_in = chunk_in.scatter(*acc_in)
    back_out.along()
    (result,) = call(
        "block_out",
        partial(block_out_kernel, chunk_out, pos_size, my_frames),
        chunk_out.operands() + [activated, spatial, small],
        [(narrow, bf16, "v")],
        [((FF, D), bf16), (narrow, f32), (narrow, f32)],
        1,
        flops(FF),
    )
    grad_spatial, result = meet(back_in, grad_spatial, result)
    for step in reversed(later):
        back_in.across(step)
    grad_spatial = (grad_spatial, "v")
    acc_sproj, grad_query, grad_pairs = call(
        "spatial_attention_back",
        partial(spatial_attention_back_kernel, chunk_s, k_at),
        chunk_s.operands()
        + [grad_spatial, (mixed_s, "v"), (packed_s, "v"), (pairs, "v")]
        + ids_s
        + [(lse_s, "v")],
        [((D, D), bf16, "v"), (narrow, bf16, "v"), ((all_keys, 2 * D), bf16, "v")],
        [((D, D), bf16), (narrow, bf16), ((D, n), bf16), (narrow, bf16)]
        + [(mask_s, f32)],
        2,
        flops(2 * D + 10 * all_keys),
    )
    grad_query, grad_pairs, result = meet(back_in, back_out, grad_query, grad_pairs, result)
    back_in.across(0)
    result = pos_hop(result)
    own_pairs = grad_pairs[:n]
    for step in range(1, share):
        theirs = partners(grad_pairs[step * n : (step + 1) * n], share - step)
        own_pairs = (own_pairs.astype(f32) + theirs.astype(f32)).astype(bf16)
    acc_s, grad_temporal, class_part, sums_s = call(
        "spatial_qkv_back",
        partial(spatial_qkv_back_kernel, chunk_s, chunk_sqkv, pos_size, my_frames),
        chunk_s.operands()
        + [(grad_query, "v"), (own_pairs, "v"), temporal, grad_spatial, choose, is_class, small],
        chunk_sqkv.grads() + [(narrow, bf16, "v"), ((8, D), f32, "v"), ((8, D), f32, "v")],
        [((D, 3 * D), bf16), (wide, bf16), (narrow, bf16), ((D, n), bf16)]
        + [((D, 3 * D), bf16), (narrow, f32), (narrow, f32)],
        2,
        flops(6 * D),
    )
    acc_s, grad_temporal, class_part, result = meet(
        back_in, acc_s, grad_temporal, class_part, result
    )
    grad_temporal = pos_hop(grad_temporal)
    back_s = chunk_sqkv.scatter(*acc_s)
    meet(back_s)
    for step in reversed(later):
        back_s.across(step)
    back_out.swap()
    block_in_bias = grad_in_bias.reshape(-1, 4, shard).transpose(1, 0, 2).reshape(4, D)
    grad_temporal, block_in_bias = meet(back_s, back_out, grad_temporal, block_in_bias)
    back_s.across(0)
    block_out = from_temporal(result)
    (acc_out,) = back_out.finish(chunk_out.widths)
    class_sum = class_part
    class_sum = class_sum + send(class_sum, layout.within[0])
    grad_temporal = (grad_temporal, "v")
    acc_proj, grad_mixed_t, sums_t = call(
        "temporal_proj_back",
        partial(temporal_proj_back_kernel, chunk_t, chunk_proj, my_slots),
        chunk_t.operands()
        + [(acc_sproj, "v"), grad_temporal, (projected, "v"), (mixed_t, "v")],
        chunk_proj.grads() + [(narrow, bf16, "v"), ((8, D), f32, "v")],
        [((D, D), bf16), ((D, D), bf16), (narrow, bf16), ((D, n), bf16), ((D, n), bf16)]
        + [((D, D), bf16), ((D, D), bf16), (narrow, bf16), (columns, f32), (narrow, f32)],
        5,
        flops(4 * D),
    )
    acc_proj, grad_mixed_t, class_sum, acc_out = meet(
        back_s, acc_proj, grad_mixed_t, class_sum, acc_out
    )
    back_proj = chunk_proj.scatter(*acc_proj)
    class_sum = class_sum + send(class_sum, layout.within[1])
    grad_mixed_t, class_sum, block_out = meet(back_proj, grad_mixed_t, class_sum, block_out)
    for step in reversed(later):
        back_proj.across(step)
    back_in.along()
    for perm in layout.within[2:]:
        class_sum = class_sum + send(class_sum, perm)
    acc_qkv, tokens_grad = call(
        "temporal_attention_back",
        partial(temporal_attention_back_kernel, chunk_t, chunk_qkv, my_slots),
        chunk_t.operands()
        + [(packed_t, "v")]
        + ids_t
        + [(lse_t, "v"), (grad_mixed_t, "v"), (rows, "v"), grad_temporal, small]
        + [(block_in_bias, "v"), (sums_m, "v"), (sums_s, "v"), (sums_t, "v")],
        chunk_qkv.grads() + [(narrow, bf16, "v")],
        [((D, 3 * D), bf16), (mask_t, f32), (wide, bf16), (narrow, bf16), ((D, n), bf16)]
        + [((D, 3 * D), bf16), (narrow, f32), (columns, f32), ((128, D), f32), ((D, SMALL), bf16)],
        3,
        flops(6 * D + 10 * n),
    )
    acc_qkv, tokens_grad, class_sum = meet(back_in, back_proj, acc_qkv, tokens_grad, class_sum)
    back_qkv = chunk_qkv.scatter(*acc_qkv)
    back_proj.across(0)
    meet(back_qkv, back_proj)
    for step in reversed(later):
        back_qkv.across(step)
    back_s.along()
    back_in.swap()
    meet(back_qkv, back_s, back_proj, back_in)
    back_qkv.across(0)
    back_proj.along()
    back_s.swap()
    (acc_in,) = back_in.finish(chunk_in.widths)
    tokens_grad, class_sum, acc_in = meet(
        back_qkv, back_proj, back_s, tokens_grad, class_sum, acc_in
    )
    back_qkv.along()
    back_proj.swap()
    (acc_sqkv,) = back_s.finish(chunk_sqkv.widths)
    class_sum = jnp.concatenate([class_sum, jnp.zeros_like(class_sum)]).astype(bf16)
    tokens_grad, class_all = from_temporal(tokens_grad, class_sum)
    tokens_grad = tokens_grad.astype(f32)
    class_grad = class_all[::share, :CLIPS].astype(f32)
    tokens_grad, class_grad, acc_sqkv = meet(
        back_qkv, back_proj, tokens_grad, class_grad, acc_sqkv
    )
    back_qkv.swap()
    acc_sproj, acc_tproj, acc_tfc = back_proj.finish(chunk_proj.widths)
    acc_tqkv, in_bias_grad, gains_grad, shifts_grad, biases_grad = back_qkv.finish(
        chunk_qkv.widths
    )
    return (
        block_out,
        tokens_grad,
        class_grad,
        acc_tqkv,
        acc_tproj,
        acc_tfc,
        acc_sqkv,
        acc_sproj,
        acc_in,
        acc_out,
        in_bias_grad.reshape(-1),
        gains_grad.T,
        shifts_grad.T,
        biases_grad.T,
    )


def solution(mesh):
    rows = P(AXES, None)
    wide = P(None, "frame", "pos", None)
    placed = (wide, P(), P(), wide) + (rows,) * 7 + (P(AXES),) + (rows,) * 3
    return jax.shard_map(
        on_device,
        mesh=mesh,
        in_specs=placed,
        out_specs=(wide, wide, P()) + (rows,) * 7 + (P(AXES),) + (rows,) * 3,
        check_vma=False,
    )
```

```python
from functools import partial

import jax
import jax.numpy as jnp
from jax import lax
from jax.experimental import pallas as pl
from jax.experimental.pallas import tpu as pltpu
from jax.sharding import PartitionSpec as P

D = 768
HEADS = 12
HEAD = 64
FF = 4 * D
MB = 4
CLIPS = 3
AXES = ("frame", "pos")
TILE = 768
SMALL = 256
f32, bf16 = jnp.float32, jnp.bfloat16
GAIN, SHIFT, BIAS = 4, 7, 10


def send(values, perm):
    return lax.ppermute(values, AXES, perm)


def tie(value, *before):
    return lax.optimization_barrier((value,) + before)[0] if before else value


class Layout:
    def __init__(self):
        self.frames, self.chips = lax.axis_size("frame"), lax.axis_size("pos") // 2
        self.bits = self.frames.bit_length() - 1
        self.frame, self.chip = lax.axis_index("frame"), lax.axis_index("pos") // 2
        self.core = lax.axis_index("pos") % 2
        self.core_index = self.core.astype(jnp.int32).reshape(1)
        self.swap = self.perm(lambda f, z, c: (f, z, 1 - c))
        self.steps = range(1, self.chips)
        self.some = range(self.chips * 3 // 4, self.chips)
        self.others = range(1, self.chips * 3 // 4)
        self.along = [self.perm(lambda f, z, c, i=i: (f, z ^ i, c)) for i in range(1, self.chips)]
        self.across = [
            self.perm(lambda f, z, c, k=k: (f ^ (1 << self.bit(k, c)), z, c))
            for k in range(self.bits)
        ]

        share = self.frames // MB
        steps = lambda n: [1 << k for k in range(n.bit_length() - 1)]
        self.within = [self.swap]
        self.within += [self.perm(lambda f, z, c, k=k: (f, z ^ k, c)) for k in steps(self.chips)]
        self.within += [self.perm(lambda f, z, c, k=k: (f ^ k, z, c)) for k in steps(share)]

    def bit(self, step, core):
        return (step + core) % self.bits

    def perm(self, to):
        pairs = []
        for f in range(self.frames):
            for z in range(self.chips):
                for c in range(2):
                    g, y, d = to(f, z, c)
                    pairs.append(
                        ((f * self.chips + z) * 2 + c, (g * self.chips + y) * 2 + d)
                    )
        return pairs

    def table(self):
        rows = []
        for core in (self.core, 1 - self.core):
            blocks = []
            for b in range(self.frames * self.chips):
                flags, i = b // self.chips, b % self.chips
                f = self.frame
                for k in range(self.bits):
                    if flags >> k & 1:
                        f = f ^ (1 << ((k + core) % self.bits))
                blocks.append(f * self.chips + (self.chip ^ i))
            rows.append(jnp.stack(blocks))
        return jnp.concatenate([jnp.stack(rows).reshape(-1), self.core[None]]).astype(jnp.int32)

    def pick(self, low, high):
        return jnp.where(self.core == 0, low, high), jnp.where(self.core == 0, high, low)

    def chip_rows(self, keep, got):
        return jnp.concatenate(self.pick(keep, got), axis=0)


class Way:
    def __init__(self, layout, *state):
        self.layout, self.state = layout, state


def meet(*things):
    values = tuple(t.state if isinstance(t, Way) else t for t in things)
    values = lax.optimization_barrier(values)
    out = []
    for thing, value in zip(things, values):
        if isinstance(thing, Way):
            thing.state = value
        else:
            out.append(value)
    return out[0] if len(out) == 1 else out


class Gather(Way):
    def along(self, steps):
        block, got = self.state
        new = {i: send(block, self.layout.along[i - 1]) for i in steps}
        self.state = (block, {**got, **new})

    def across(self, step):
        mine, other = self.state
        if step == 0:
            mine = tuple(a[None] for a in [mine] + [other[i] for i in self.layout.steps])
        block = merge(mine)
        self.state = ((block, send(block, self.layout.across[step])), ())

    def swap(self, count=None):
        mine, other = self.state
        other += tuple(send(a, self.layout.swap) for a in mine[len(other) : count])
        self.state = (mine, other)


class Scatter(Way):
    def __init__(self, layout, mine, other):
        near, far = [(a, send(b, layout.swap)) for a, b in zip(mine, other)]
        super().__init__(layout, near, far)
        self.count = near[0].shape[0]

    def across(self, step):
        near, far = self.state
        start = 0
        if not far:
            self.count //= 2
            far, start = near, self.count
        far = fold(far, start, self.count)
        self.state = (near + (send(far, self.layout.across[step]),), ())
        return far

    def sums(self):
        near, _ = self.state
        _, rows, width = near[0].shape
        own, *away = call(
            "fold_blocks",
            partial(fold_blocks_kernel, len(near)),
            [(a, "x") for a in near],
            [((rows, width), f32, "x")] + [((rows, width), bf16, "x")] * (self.count - 1),
            [],
            1,
            0,
        )
        self.state = (own, dict(zip(self.layout.steps, away)))

    def along(self, steps):
        own, away = self.state
        new = {i: send(away[i], self.layout.along[i - 1]) for i in steps}
        self.state = (own, {**away, **new})

    def swap(self):
        own, got = self.state
        rows, width = own.shape
        kept = ((rows // 2, width), f32, "x")
        keep, give = call(
            "sum_parts",
            sum_parts_kernel,
            [(self.layout.core_index, "s"), [(a, "x") for a in [own, *got.values()]]],
            [kept, kept],
            [],
            1,
            0,
        )
        self.state = (keep, send(give, self.layout.swap))

    def finish(self, widths):
        keep, got = self.state
        rows = keep.shape[0]
        outs = [((rows, width), f32, "v") for width in widths if width != SMALL]
        if SMALL in widths:
            outs += [((count, rows), f32, "v") for count in (4, 3, 3, 8)]
        return call(
            "finish",
            partial(finish_kernel, widths),
            [(self.layout.core_index, "s"), (keep, "x"), (got, "x")],
            outs,
            [((128, 128), f32)],
            1,
            0,
        )


def total(values):
    out = values[0].astype(f32)
    for value in values[1:]:
        out = out + value.astype(f32)
    return out


class Chunk:
    def __init__(self, layout, widths, rows):
        self.layout, self.widths, self.rows = layout, widths, rows
        self.count = layout.frames * layout.chips
        self.table = layout.table()
        self.half = sum(widths) // 2
        self.whole = bool(rows % 16)
        if self.whole:
            core = layout.core.astype(jnp.int32)
            self.index = jnp.stack([jnp.zeros_like(core)] * 2 + [core])
            self.blocks, self.block_rows = 1, self.count * rows
        else:
            self.index = self.table
            self.blocks, self.block_rows = self.count, rows

    def load(self, way):
        mine, other = way.state
        if self.whole:
            order = jnp.argsort(self.table[: 2 * self.count].reshape(2, -1), axis=1)
            mine, other = [
                (jnp.concatenate(a)[o].reshape(1, self.block_rows, -1),)
                for a, o in zip((mine, other), order)
            ]
        self.mine, self.other = mine, other
        return self

    def operands(self):
        pieces = [[(a, "h") for a in side] for side in (self.mine, self.other)]
        return [[(self.index, "s")] + pieces]

    def grads(self):
        if self.whole:
            piece = [((1, self.block_rows, self.half), bf16, "x")]
        else:
            piece = [((self.count // 2, self.block_rows, self.half), bf16, "x")] * 2
        return [[piece, piece]]

    def at(self, which):
        return sum(self.widths[:which]) // 2

    def fetch(self, which, weights, dst, sem):
        self._copies(which, *weights, dst, sem, True)

    def store(self, which, table, src, grads, sem):
        self._copies(which, table, *grads, src, sem, False)

    def _copies(self, which, table, mine, other, mat, sem, into):
        at, w = self.at(which), self.widths[which] // 2
        core = table[2 * self.blocks]
        for side, pieces in ((0, mine), (1, other)):
            half = core if side == 0 else 1 - core
            first = side * self.blocks
            for piece in pieces:

                def body(b, carry, piece=piece, first=first, half=half):
                    row = pl.multiple_of(table[first + b] * self.block_rows, 16)
                    block = piece.at[b, :, at : at + w]
                    place = mat.at[
                        pl.ds(row, self.block_rows), pl.ds(pl.multiple_of(half * w, 128), w)
                    ]
                    pair = (block, place) if into else (place, block)
                    pltpu.make_async_copy(*pair, sem).start()
                    return carry

                lax.fori_loop(0, piece.shape[0], body, 0)
                first += piece.shape[0]

    def scatter(self, mine, other):
        if self.whole:
            order = self.table[: 2 * self.count].reshape(2, -1)
            mine, other = [
                a[0].reshape(self.count, self.rows, -1)[o] for a, o in zip((mine, other), order)
            ]
            half = self.count // 2
            mine, other = [(a[:half], a[half:]) for a in (mine, other)]
        return Scatter(self.layout, mine, other)


def merge_kernel(count, *refs):
    out, at = refs[count], 0
    for ref in refs[:count]:
        out[at : at + ref.shape[0]] = ref[...]
        at += ref.shape[0]


def merge(blocks):
    if blocks[0].shape[1] % 16:
        return jnp.concatenate(blocks)
    shape = (sum(a.shape[0] for a in blocks),) + blocks[0].shape[1:]
    return call(
        "merge",
        partial(merge_kernel, len(blocks)),
        [(a, "x") for a in blocks],
        [(shape, blocks[0].dtype, "x")],
        [],
        1,
        0,
    )[0]


def fold_kernel(count, start, *refs):
    out = refs[count]

    def block(b, carry):
        out[b] = total([ref[start + b] for ref in refs[:count]]).astype(bf16)
        return carry

    lax.fori_loop(0, out.shape[0], block, 0)


def fold(values, start, count):
    shape = (count,) + values[0].shape[1:]
    return call(
        "fold",
        partial(fold_kernel, len(values), start),
        [(a, "x") for a in values],
        [(shape, bf16, "x")],
        [],
        1,
        0,
    )[0]


def fold_blocks_kernel(count, *refs):
    refs, outs = refs[:count], refs[count:-1]
    for b, out in enumerate(outs):
        out[...] = total([ref[b] for ref in refs]).astype(out.dtype)


def pack_kernel(widths, small, core, *refs):
    mats, (keep, give) = refs[: len(widths)], refs[-4:-2]
    turned = refs[-2]
    at = 0
    first = core[0] == 0
    for mat, width in zip(mats, widths):
        w = width // 2
        low, high = mat[:, :w], mat[:, w:]
        keep[:, at : at + w] = jnp.where(first, low, high)
        give[:, at : at + w] = jnp.where(first, high, low)
        at += w
    if small:
        rows = keep.shape[0]
        turned[...] = jnp.zeros_like(turned)
        place = 0
        for ref in refs[len(widths) : -4]:
            count = ref.shape[0]
            turned[place : place + count, :rows] = ref[...].astype(f32)
            place += count
        values = turned[...].T[:rows].astype(bf16)
        zeros = jnp.zeros_like(values)
        keep[:, at:] = jnp.where(first, values, zeros)
        give[:, at:] = jnp.where(first, zeros, values)


def pack(layout, mats, small=()):
    rows = mats[0].shape[0]
    width = sum(m.shape[1] for m in mats) // 2 + (SMALL // 2 if small else 0)
    half = ((rows, width), bf16, "x")
    return call(
        "pack",
        partial(pack_kernel, [m.shape[1] for m in mats], len(small)),
        [(layout.core_index, "s")] + [(m, "w") for m in mats] + [(m, "w") for m in small],
        [half, half],
        [((128, 128), f32)],
        1,
        0,
    )


def sum_parts_kernel(core, parts, keep, give, sem):
    values = total([p[...] for p in parts])
    rows = keep.shape[0]
    first = core[0] == 0
    keep[...] = jnp.where(first, values[:rows], values[rows:])
    give[...] = jnp.where(first, values[rows:], values[:rows])


def finish_kernel(widths, core, keep, got, *refs):
    outs, turned = refs[:-2], refs[-2]
    first = core[0] == 0
    at = 0
    for i, width in enumerate(widths):
        w = width // 2
        mine, other = keep[:, at : at + w], got[:, at : at + w]
        low = jnp.where(first, mine, other)
        if width != SMALL:
            outs[i][:, :w] = low
            outs[i][:, w:] = jnp.where(first, other, mine)
        else:
            rows = keep.shape[0]
            turned[...] = jnp.zeros_like(turned)
            turned[:rows, :] = low
            values = turned[...].T
            place = 0
            for out in outs[i:]:
                out[...] = values[place : place + out.shape[0], :rows]
                place += out.shape[0]
        at += w


def arrived(mat, sem):
    pltpu.make_async_copy(mat, mat, sem).wait()


SPACE = {"s": pltpu.SMEM, "h": pltpu.HBM, "v": pltpu.VMEM, "w": pltpu.VMEM, "x": pltpu.VMEM}
HELD = {"h": pltpu.HBM, "w": pltpu.HBM, "x": pltpu.VMEM}


def held(value, space):
    return pltpu.with_memory_space_constraint(value, HELD[space]) if space in HELD else value


def result(shape, kind, space):
    return HELD[space](shape, kind) if space in HELD else jax.ShapeDtypeStruct(shape, kind)


def flat(items):
    return [leaf for item in items for leaf in (flat(item) if isinstance(item, list) else [item])]


def nest(items, leaves):
    return [nest(item, leaves) if isinstance(item, list) else next(leaves) for item in items]


def call(name, body, ins, outs, scratch, sems, flops, alias=None):
    operands, results = flat(ins), flat(outs)
    bytes_of = lambda shape, kind: jnp.dtype(kind).itemsize * _size(shape)
    size = sum(bytes_of(a.shape, a.dtype) for a, space in operands if space in "vwx")
    size += sum(bytes_of(shape, kind) for shape, kind, space in results if space in "vwx")
    size += sum(bytes_of(shape, kind) for shape, kind in scratch)
    moved = sum(bytes_of(a.shape, a.dtype) for a, _ in operands)
    moved += sum(bytes_of(shape, kind) for shape, kind, _ in results)
    aliases = {}
    for i, o in (alias or {}).items():
        start, end = len(flat(ins[:i])), len(flat(outs[:o]))
        for k in range(len(flat([ins[i]]))):
            aliases[start + k] = end + k

    def kernel(*refs):
        leaves = iter(refs)
        body(*nest(ins, leaves), *nest(outs, leaves), *leaves)

    values = pl.pallas_call(
        kernel,
        out_shape=[result(*r) for r in results],
        in_specs=[pl.BlockSpec(memory_space=SPACE[space]) for _, space in operands],
        out_specs=[pl.BlockSpec(memory_space=SPACE[space]) for _, _, space in results],
        scratch_shapes=[pltpu.VMEM(shape, kind) for shape, kind in scratch]
        + [pltpu.SemaphoreType.DMA((sems,))],
        input_output_aliases=aliases,
        compiler_params=pltpu.CompilerParams(
            vmem_limit_bytes=min(int(size * 1.1) + (6 << 20), 60 << 20)
        ),
        cost_estimate=pl.CostEstimate(flops=flops, bytes_accessed=moved, transcendentals=0),
        name=name,
    )(*[held(a, space) for a, space in operands])
    return nest(outs, iter(values))


def _size(shape):
    total = 1
    for n in shape:
        total *= n
    return total


def tiles(width, body, size=TILE):
    def step(j, carry):
        body(pl.ds(pl.multiple_of(j * size, size), size))
        return carry

    lax.fori_loop(0, width // size, step, 0)


def dot(a, b):
    return jnp.dot(a, b, preferred_element_type=f32)


def dot_t(a, b):
    return lax.dot_general(a, b, (((1,), (1,)), ((), ())), preferred_element_type=f32)


def normalise(values):
    centred = values - jnp.mean(values, axis=-1, keepdims=True)
    inv_std = lax.rsqrt(jnp.mean(centred * centred, axis=-1, keepdims=True) + 1e-06)
    return centred * inv_std, inv_std


def norm_rows(values, small, which):
    normal, _ = normalise(values)
    return normal * small[GAIN + which : GAIN + which + 1] + small[SHIFT + which : SHIFT + which + 1]


def norm_back(values, upstream, small, which):
    normal, inv_std = normalise(values)
    product = upstream * normal
    grad_gain = jnp.sum(product, axis=0, keepdims=True)
    grad_shift = jnp.sum(upstream, axis=0, keepdims=True)
    gain = small[GAIN + which : GAIN + which + 1]
    scaled = upstream * gain
    mean = jnp.mean(scaled, axis=-1, keepdims=True)
    mean_normal = jnp.mean(product * gain, axis=-1, keepdims=True)
    return inv_std * (scaled - mean - normal * mean_normal), grad_gain, grad_shift


def column_sum(values):
    return jnp.sum(values.astype(f32), axis=0, keepdims=True)


def set_mask(mask, key_ids, query_ids):
    mask[...] = jnp.where(key_ids[...] == query_ids[...], 0.0, -1000000000.0)


def regroup(values, flat, out, groups):
    count = out.shape[0] // groups
    for c in range(flat.shape[0]):
        cols = slice(c * 128, (c + 1) * 128)
        flat[c] = values[:, cols]
        for g in range(groups):
            out[g * count : (g + 1) * count, cols] = flat[c, pl.ds(g, count, stride=groups), :]


def ungroup(grouped, flat, groups):
    count = grouped.shape[0] // groups
    for c in range(flat.shape[0]):
        cols = slice(c * 128, (c + 1) * 128)
        for g in range(groups):
            flat[c, pl.ds(g, count, stride=groups), :] = grouped[g * count : (g + 1) * count, cols]
    return jnp.concatenate([flat[c] for c in range(flat.shape[0])], axis=1)


def swap_groups(source, out, outer, inner):
    size = source.shape[0] // (outer * inner)
    for i in range(outer):
        for j in range(inner):
            to, at = (j * outer + i) * size, (i * inner + j) * size
            out[to : to + size, :] = source[at : at + size, :]


def both_heads(values, scale):
    lane = lax.broadcasted_iota(jnp.int32, (1, 2 * HEAD), 1)
    wide = values.astype(f32)
    parts = [jnp.where(lane // HEAD == h, wide * scale, 0.0) for h in range(2)]
    return jnp.concatenate(parts, axis=0).astype(bf16)


def own_heads(across):
    size = across.shape[1] // 2
    return jnp.concatenate([across[:HEAD, :size], across[HEAD:, size:]], axis=0).T


def key_rows(pairs, cols, start, size, rows):
    parts = [pairs[at + start : at + start + size, cols] for at in range(0, pairs.shape[0], rows)]
    return parts[0] if len(parts) == 1 else jnp.concatenate(parts, axis=0)


def attend(query, q_at, pairs, k_at, v_at, mask, mixed, lse):
    rows, size = query.shape[0], mask.shape[1] // 2
    blocks = range(rows // size)

    def pair(i, carry):
        cols = lambda at: pl.ds(pl.multiple_of(at + i * 2 * HEAD, 2 * HEAD), 2 * HEAD)
        here = [slice(b * size, (b + 1) * size) for b in blocks]
        queries = [both_heads(query[h, cols(q_at)], 0.125) for h in here]
        keys = [key_rows(pairs, cols(k_at), b * size, size, rows) for b in blocks]
        values = [key_rows(pairs, cols(v_at), b * size, size, rows).T for b in blocks]
        score = [dot_t(keys[b], queries[b]) + mask[...] for b in blocks]
        top = [jnp.max(score[b], axis=0, keepdims=True) for b in blocks]
        weight = [jnp.exp(score[b] - top[b]) for b in blocks]
        norm = [jnp.sum(weight[b], axis=0, keepdims=True) for b in blocks]
        probs = [(weight[b] * (1.0 / norm[b])).astype(bf16) for b in blocks]
        out = [own_heads(dot(values[b], probs[b])).astype(bf16) for b in blocks]
        for b in blocks:
            lse[pl.ds(i * len(blocks) + b, 1), :] = top[b] + jnp.log(norm[b])
            mixed[here[b], cols(0)] = out[b]
        return carry

    lax.fori_loop(0, HEADS // 2, pair, 0, unroll=HEADS // 2)


def attend_back(query, q_at, pairs, k_at, v_at, mask, lse, grad, out_q, out_pairs, gk_at, gv_at):
    rows, size = query.shape[0], mask.shape[1] // 2
    blocks = range(rows // size)

    def pair(i, carry):
        cols = lambda at: pl.ds(pl.multiple_of(at + i * 2 * HEAD, 2 * HEAD), 2 * HEAD)
        here = [slice(b * size, (b + 1) * size) for b in blocks]
        keys = [key_rows(pairs, cols(k_at), b * size, size, rows) for b in blocks]
        values = [key_rows(pairs, cols(v_at), b * size, size, rows) for b in blocks]
        queries = [both_heads(query[h, cols(q_at)], 0.125) for h in here]
        upstream = [both_heads(grad[h, cols(0)], 1.0) for h in here]
        logs = [lse[pl.ds(i * len(blocks) + b, 1), :] for b in blocks]
        across_keys = [keys[b].T for b in blocks]
        score = [dot_t(keys[b], queries[b]) + mask[...] for b in blocks]
        dprob = [dot_t(values[b], upstream[b]) for b in blocks]
        probs = [jnp.exp(score[b] - logs[b]) for b in blocks]
        delta = [jnp.sum(probs[b] * dprob[b], axis=0, keepdims=True) for b in blocks]
        dscore = [(probs[b] * (dprob[b] - delta[b])).astype(bf16) for b in blocks]
        grad_keys = [dot(dscore[b], queries[b]).astype(bf16) for b in blocks]
        grad_values = [dot(probs[b].astype(bf16), upstream[b]).astype(bf16) for b in blocks]
        grad_queries = [
            (own_heads(dot(across_keys[b], dscore[b])) * 0.125).astype(bf16) for b in blocks
        ]
        for b in blocks:
            out_q[here[b], cols(0)] = grad_queries[b]
            for part in range(0, pairs.shape[0], rows):
                there = slice(part + b * size, part + (b + 1) * size)
                seen = slice(part // rows * size, (part // rows + 1) * size)
                out_pairs[there, cols(gk_at)] = grad_keys[b][seen]
                out_pairs[there, cols(gv_at)] = grad_values[b][seen]
        return carry

    lax.fori_loop(0, HEADS // 2, pair, 0, unroll=HEADS // 2)


def qkv_tiles(x, w, bias, small, which, packed):
    bias[:, :D] = small[BIAS + which : BIAS + which + 1]
    bias[:, D : 2 * D] = jnp.zeros((1, D), f32)
    bias[:, 2 * D :] = small[BIAS + which + 1 : BIAS + which + 2]

    def tile(cols):
        packed[:, cols] = (dot(x[...], w[:, cols]) + bias[:, cols]).astype(bf16)

    tiles(3 * D, tile)


def across(mat, out):
    for at in range(0, mat.shape[1], 128):
        out[at : at + 128, :] = mat[:, at : at + 128].astype(f32).T.astype(bf16)


def temporal_qkv_kernel(
    chunk, slots, weights, rows, packed, small, w, raw, x, bias, flat, grouped, sem
):
    chunk.fetch(3, weights, raw, sem.at[0])
    chunk.fetch(0, weights, w, sem.at[1])
    arrived(raw, sem.at[0])
    small[...] = raw[:, :128].astype(f32).T[: small.shape[0]]
    regroup(norm_rows(rows[...].astype(f32), small, 0), flat, grouped, slots)
    x[...] = grouped[...].astype(bf16)
    arrived(w, sem.at[1])
    qkv_tiles(x, w, bias, small, 0, packed)


def temporal_mix_kernel(
    chunk, slots, weights, packed, rows, key_ids, query_ids, small,
    mixed, projected, lse, temporal, w_proj, w_fc, mask, grouped, flat, sem,
):
    chunk.fetch(1, weights, w_proj, sem.at[0])
    chunk.fetch(2, weights, w_fc, sem.at[1])
    set_mask(mask, key_ids, query_ids)
    attend(packed, 0, packed, D, 2 * D, mask, mixed, lse)
    arrived(w_proj, sem.at[0])

    def project(cols):
        bias = small[BIAS + 2 : BIAS + 3, cols]
        projected[:, cols] = (dot(mixed[...], w_proj[:, cols]) + bias).astype(bf16)

    tiles(D, project)
    arrived(w_fc, sem.at[1])

    def residual(cols):
        grouped[:, cols] = dot(projected[...], w_fc[:, cols]) + small[BIAS + 3 : BIAS + 4, cols]

    tiles(D, residual)
    temporal[...] = (rows[...].astype(f32) + ungroup(grouped, flat, slots)).astype(bf16)


def spatial_qkv_kernel(
    chunk, sources, frames, weights, rows, choose, class_rows, is_class, small,
    temporal, packed, w, x, bias, flat, grouped, sem,
):
    chunk.fetch(0, weights, w, sem.at[0])
    flat[...] = rows[...].astype(f32)
    swap_groups(flat, grouped, sources, frames)
    values = jnp.where(is_class[...] > 0, dot(choose[...], class_rows[...]), grouped[...])
    temporal[...] = values.astype(bf16)
    x[...] = norm_rows(values, small, 1).astype(bf16)
    arrived(w, sem.at[0])
    qkv_tiles(x, w, bias, small, 4, packed)


def spatial_mix_kernel(
    chunk, k_at, weights, packed, pairs, key_ids, query_ids, temporal, small,
    mixed, lse, spatial, w, mask, sem,
):
    chunk.fetch(1, weights, w, sem.at[0])
    set_mask(mask, key_ids, query_ids)
    attend(packed, 0, pairs, k_at, k_at + D, mask, mixed, lse)
    arrived(w, sem.at[0])

    def residual(cols):
        added = dot(mixed[...], w[:, cols]) + small[BIAS + 6 : BIAS + 7, cols]
        spatial[:, cols] = temporal[:, cols].astype(f32) + added

    tiles(D, residual)


def hidden_kernel(
    chunk, weights, spatial, in_bias, small, normed, activated, slope, w, sem
):
    chunk.fetch(0, weights, w, sem.at[0])
    normed[...] = norm_rows(spatial[...], small, 2).astype(bf16)
    arrived(w, sem.at[0])

    def tile(cols):
        hidden = dot(normed[...], w[:, cols]) + in_bias[:, cols]
        below = 0.5 + 0.5 * lax.erf(hidden * 0.7071067811865476)
        density = jnp.exp(hidden * hidden * -0.5) * 0.3989422804014327
        activated[:, cols] = (hidden * below).astype(bf16)
        slope[:, cols] = (below + hidden * density).astype(bf16)

    tiles(FF, tile)


def out_grad_kernel(chunk, table, activated, grad_out, grads, grad, sem):
    def tile(cols):
        turned = activated[:, cols].astype(f32).T.astype(bf16)
        grad[cols, :] = dot(turned, grad_out[...]).astype(bf16)

    tiles(FF, tile)
    chunk.store(0, table, grad, grads, sem.at[0])
    arrived(grad, sem.at[0])


def mlp_back_kernel(
    chunk_in, chunk_out, weights_in, weights_out,
    grad_out, slope, spatial, small, grad_hidden, in_bias, grad_spatial, sums,
    w_in, w_out, total, sem,
):
    chunk_out.fetch(0, weights_out, w_out, sem.at[0])
    chunk_in.fetch(0, weights_in, w_in, sem.at[1])
    arrived(w_out, sem.at[0])

    def tile(cols):
        grad = (dot_t(grad_out[...], w_out[cols, :]) * slope[:, cols].astype(f32)).astype(bf16)
        grad_hidden[:, cols] = grad
        in_bias[:, cols] = column_sum(grad)

    tiles(FF, tile)
    arrived(w_in, sem.at[1])

    def back(cols):
        total[:, cols] = dot_t(grad_hidden[...], w_in[cols, :])

    tiles(D, back, D // 2)
    back, gain, shift = norm_back(spatial[...], total[...], small, 2)
    upstream = grad_out[...].astype(f32)
    result = upstream + back
    grad_spatial[...] = result
    sums[0:1] = gain
    sums[1:2] = shift
    sums[2:3] = column_sum(upstream)
    sums[3:4] = column_sum(result.astype(bf16))
    sums[4:8] = jnp.zeros((4, D), f32)


def in_grad_kernel(chunk, table, normed, grad_hidden, grads, normed_t, grad, sem):
    across(normed, normed_t)

    def tile(cols):
        grad[:, cols] = dot(normed_t[...], grad_hidden[:, cols]).astype(bf16)

    tiles(FF, tile)
    chunk.store(0, table, grad, grads, sem.at[0])
    arrived(grad, sem.at[0])


def block_out_kernel(
    chunk, sources, frames, weights, activated, spatial, small, result, w, total, flat, sem
):
    chunk.fetch(0, weights, w, sem.at[0])
    arrived(w, sem.at[0])

    def tile(cols):
        added = dot(activated[...], w[:, cols]) + small[BIAS + 7 : BIAS + 8, cols]
        total[:, cols] = spatial[:, cols] + added

    tiles(D, tile, D // 2)
    swap_groups(total, flat, frames, sources)
    result[...] = flat[...].astype(bf16)


def spatial_attention_back_kernel(
    chunk, k_at, weights, grad_spatial, mixed, packed, pairs, key_ids, query_ids, lse,
    grad, grad_query, grad_pairs,
    w, upstream, mixed_t, grad_mixed, mask, sem,
):
    chunk.fetch(1, weights, w, sem.at[0])
    upstream[...] = grad_spatial[...].astype(bf16)
    set_mask(mask, key_ids, query_ids)
    arrived(w, sem.at[0])

    def back(cols):
        grad_mixed[:, cols] = dot_t(upstream[...], w[cols, :]).astype(bf16)

    tiles(D, back)
    across(mixed, mixed_t)

    def tile(cols):
        grad[:, cols] = dot(mixed_t[...], upstream[:, cols]).astype(bf16)

    tiles(D, tile)
    attend_back(
        packed, 0, pairs, k_at, k_at + D, mask, lse, grad_mixed, grad_query, grad_pairs, 0, D
    )


def qkv_back(normed_t, grad_packed, w, grad, total):
    def back(cols):
        total[:, cols] = dot_t(grad_packed[...], w[cols, :])

    tiles(D, back, D // 2)

    def tile(cols):
        grad[:, cols] = dot(normed_t[...], grad_packed[:, cols]).astype(bf16)

    tiles(3 * D, tile)


def spatial_qkv_back_kernel(
    chunk, sources, frames, weights, acc_spatial, grad_query, grad_pairs, temporal, grad_spatial, choose, is_class,
    small, grads, grad_temporal, class_part, sums,
    w, packed, normed, normed_t, grad, total, flat, sem,
):
    chunk.fetch(0, weights, w, sem.at[0])
    packed[:, :D] = grad_query[...]
    packed[:, D:] = grad_pairs[...]
    values = temporal[...].astype(f32)
    normed[...] = norm_rows(values, small, 1).astype(bf16)
    across(normed, normed_t)
    arrived(w, sem.at[0])
    chunk.store(1, weights[0], acc_spatial, grads, sem.at[2])
    qkv_back(normed_t, packed, w, grad, total)
    chunk.store(0, weights[0], grad, grads, sem.at[1])
    back, gain, shift = norm_back(values, total[...], small, 1)
    total[...] = jnp.where(is_class[...] > 0, 0.0, grad_spatial[...] + back)
    swap_groups(total, flat, frames, sources)
    grad_temporal[...] = flat[...].astype(bf16)
    class_part[...] = jnp.zeros_like(class_part)
    for c in range(CLIPS):
        class_part[c : c + 1] = column_sum(back * choose[:, c : c + 1].astype(f32))
    sums[0:1] = gain
    sums[1:2] = shift
    sums[2:3] = column_sum(packed[:, :D])
    sums[3:4] = column_sum(packed[:, 2 * D :])
    sums[4:8] = jnp.zeros((4, D), f32)
    arrived(grad, sem.at[1])
    arrived(acc_spatial, sem.at[2])


def temporal_proj_back_kernel(
    chunk, chunk_back, slots, weights, grad_rows, projected, mixed,
    grads, grad_mixed, sums,
    w_proj, w_fc, grad_proj, proj_t, mixed_t, acc_proj, acc_fc, grad_temporal, flat, grouped, sem,
):
    chunk.fetch(2, weights, w_fc, sem.at[0])
    chunk.fetch(1, weights, w_proj, sem.at[1])
    regroup(grad_rows[...].astype(f32), flat, grouped, slots)
    grad_temporal[...] = grouped[...].astype(bf16)
    across(projected, proj_t)

    def fc_tile(cols):
        acc_fc[:, cols] = dot(proj_t[...], grad_temporal[:, cols]).astype(bf16)

    tiles(D, fc_tile)
    chunk_back.store(1, weights[0], acc_fc, grads, sem.at[2])
    arrived(w_fc, sem.at[0])

    def fc_back(cols):
        grad_proj[:, cols] = dot_t(grad_temporal[...], w_fc[cols, :]).astype(bf16)

    tiles(D, fc_back)
    across(mixed, mixed_t)

    def proj_tile(cols):
        acc_proj[:, cols] = dot(mixed_t[...], grad_proj[:, cols]).astype(bf16)

    tiles(D, proj_tile)
    chunk_back.store(0, weights[0], acc_proj, grads, sem.at[3])
    arrived(w_proj, sem.at[1])

    def proj_back(cols):
        grad_mixed[:, cols] = dot_t(grad_proj[...], w_proj[cols, :]).astype(bf16)

    tiles(D, proj_back)
    sums[0:1] = column_sum(grad_temporal[...])
    sums[1:2] = column_sum(grad_proj[...])
    sums[2:8] = jnp.zeros((6, D), f32)
    arrived(acc_fc, sem.at[2])
    arrived(acc_proj, sem.at[3])


def temporal_attention_back_kernel(
    chunk, chunk_back, slots, weights, packed, key_ids, query_ids, lse, grad_mixed, rows, grad_temporal,
    small, in_bias, sums_m, sums_s, sums_t,
    grads, tokens_grad,
    w, mask, grad_packed, normed, normed_t, grad, total, flat, rows_small, raw, sem,
):
    chunk.fetch(0, weights, w, sem.at[0])
    set_mask(mask, key_ids, query_ids)
    attend_back(
        packed, 0, packed, D, 2 * D, mask, lse, grad_mixed, grad_packed, grad_packed, D, 2 * D
    )
    values = rows[...].astype(f32)
    regroup(norm_rows(values, small, 0), flat, total, slots)
    normed[...] = total[...].astype(bf16)
    across(normed, normed_t)
    arrived(w, sem.at[0])
    qkv_back(normed_t, grad_packed, w, grad, total)
    chunk_back.store(0, weights[0], grad, grads, sem.at[1])
    back, gain, shift = norm_back(values, ungroup(total, flat, slots), small, 0)
    tokens_grad[...] = (grad_temporal[...].astype(f32) + back).astype(bf16)
    rows_small[...] = jnp.zeros_like(rows_small)
    rows_small[0:4] = in_bias[...]
    for i, (gain_row, shift_row) in enumerate(
        ((gain, shift), (sums_s[0:1], sums_s[1:2]), (sums_m[0:1], sums_m[1:2]))
    ):
        rows_small[GAIN + i : GAIN + i + 1] = gain_row
        rows_small[SHIFT + i : SHIFT + i + 1] = shift_row
    for i, row in enumerate(
        (
            column_sum(grad_packed[:, :D]),
            column_sum(grad_packed[:, 2 * D :]),
            sums_t[1:2],
            sums_t[0:1],
            sums_s[2:3],
            sums_s[3:4],
            sums_m[3:4],
            sums_m[2:3],
        )
    ):
        rows_small[BIAS + i : BIAS + i + 1] = row
    raw[:, :128] = rows_small[...].T.astype(bf16)
    raw[:, 128:] = jnp.zeros((D, 128), bf16)
    chunk_back.store(1, weights[0], raw, grads, sem.at[2])
    arrived(grad, sem.at[1])
    arrived(raw, sem.at[2])


def on_device(
    tokens,
    class_tokens,
    clip_frames,
    cotangent,
    temporal_qkv,
    temporal_proj,
    temporal_fc,
    spatial_qkv,
    spatial_proj,
    mlp_in,
    mlp_out,
    mlp_in_bias,
    norm_gains,
    norm_shifts,
    biases,
):
    frame_size, pos_size = lax.axis_size("frame"), lax.axis_size("pos")
    frame_index, pos_index = lax.axis_index("frame"), lax.axis_index("pos")
    frame_count, pos_count = tokens.shape[1], tokens.shape[2]
    shard = norm_gains.shape[0]
    slots = pos_count + 1
    share = frame_size // MB
    my_slots = slots // share
    all_frames = frame_count * frame_size
    my_frames = all_frames // pos_size
    rows_count = all_frames * my_slots
    micro = frame_index // share

    layout = Layout()
    small = (mlp_in_bias.reshape(4, shard), norm_gains.T, norm_shifts.T, biases.T)
    keep_t, give_t = pack(layout, (temporal_qkv, temporal_proj, temporal_fc), small)
    keep, give = pack(layout, (spatial_qkv, spatial_proj, mlp_in))
    keep_out, give_out = pack(layout, (mlp_out,))
    got_t = send(give_t, layout.swap)
    got = send(tie(give, give_t), layout.swap)
    got_out = send(tie(give_out, give_t), layout.swap)
    way_t = Gather(layout, layout.chip_rows(keep_t, got_t), {})
    rest = layout.chip_rows(keep, got)
    way_s = Gather(layout, rest[:, : 2 * D], {})
    way_in = Gather(layout, rest[:, 2 * D :], {})
    way_out = Gather(layout, layout.chip_rows(keep_out, got_out), {})
    chunk_t = Chunk(layout, (3 * D, D, D, SMALL), 2 * shard)
    chunk_s = Chunk(layout, (3 * D, D), 2 * shard)
    chunk_in = Chunk(layout, (FF,), 2 * shard)
    chunk_out = Chunk(layout, (D,), 8 * shard)
    chunk_proj = Chunk(layout, (D, D), 2 * shard)
    chunk_qkv = Chunk(layout, (3 * D, SMALL), 2 * shard)
    later = range(1, layout.bits)

    def frame_hop(values):
        return lax.all_to_all(values, "frame", 0, 0, tiled=True)

    def pos_hop(values):
        parts = values.reshape(pos_size, rows_count // pos_size, D)
        return lax.all_to_all(parts, "pos", 0, 0, tiled=True).reshape(rows_count, D)

    def to_temporal(*arrays):
        parts = []
        for values in arrays:
            padded = jnp.pad(values, ((0, 0), (0, 0), (0, 1), (0, 0)))
            padded = padded.reshape(MB, frame_count, share, my_slots, D).transpose(0, 2, 1, 3, 4)
            parts.append(padded.reshape(frame_size, frame_count * my_slots, D))
        hopped = frame_hop(jnp.concatenate(parts, axis=1)).reshape(frame_size, len(arrays), -1, D)
        return [hopped[:, i].reshape(rows_count, D) for i in range(len(arrays))]

    def from_temporal(arrays, extra):
        rows = frame_count * my_slots
        parts = [values.reshape(frame_size, rows, D) for values in arrays]
        parts.append(jnp.broadcast_to(extra, (frame_size,) + extra.shape))
        hopped = frame_hop(jnp.concatenate(parts, axis=1))
        out = []
        for at in range(0, rows * len(arrays), rows):
            part = hopped[:, at : at + rows].reshape(MB, share, frame_count, my_slots, D)
            part = part.transpose(0, 2, 1, 3, 4).reshape(MB, frame_count, slots, D)
            out.append(part[:, :, :pos_count])
        return out + [hopped[:, rows * len(arrays) :]]

    def partners(values, step):
        perm = [(f, f // share * share + (f % share + step) % share) for f in range(frame_size)]
        return lax.ppermute(values, "frame", perm)

    n = rows_count
    clip_ends = jnp.cumsum(lax.dynamic_index_in_dim(clip_frames, micro, 0, keepdims=False))
    clip_of = lambda frame: jnp.sum(
        (frame[:, None] >= clip_ends[None, :]).astype(jnp.int32), axis=1
    )
    size_t = all_frames * max(1, 128 // all_frames)
    ids = jnp.arange(size_t, dtype=jnp.int32)
    ids = ids // all_frames * CLIPS + clip_of(ids % all_frames)
    ids_t = [(ids[:, None], "v"), (jnp.tile(ids, 2)[None, :], "v")]
    frame_rows = n // my_frames
    size_s = frame_rows * max(1, 128 // frame_rows)
    row_ids = jnp.arange(n, dtype=jnp.int32)
    frame_s, row_slot = row_ids // frame_rows, row_ids % my_slots
    first_source = row_ids % frame_rows < my_slots

    def key_masks(share_index):
        padding = row_slot + share_index * my_slots == slots - 1
        is_class = padding & first_source
        return is_class, is_class | ~padding

    keys_s = []
    for step in range(share):
        _, valid = key_masks((frame_index + share - step) % share)
        keys_s.append(jnp.where(valid, frame_s, -1)[:size_s])
    ids_s = [
        (jnp.concatenate(keys_s)[:, None], "v"),
        (jnp.tile(frame_s[:size_s], 2)[None, :], "v"),
    ]
    is_class, _ = key_masks(frame_index % share)
    clip_s = clip_of(pos_index * my_frames + frame_s)
    choose = (clip_s[:, None] == jnp.arange(8)[None, :]) & is_class[:, None]
    choose = (choose.astype(bf16), "v")
    class_rows = lax.dynamic_index_in_dim(class_tokens, micro, 0, keepdims=False)
    class_rows = (jnp.pad(class_rows, ((0, 8 - CLIPS), (0, 0))), "v")
    is_class = (is_class.astype(jnp.int32)[:, None], "v")

    narrow, wide, full = (n, D), (n, 3 * D), (n, FF)
    heads = lambda size: (-(-HEADS // 2 * (n // size) // 8) * 8, 2 * size)
    columns = (D // 128, n, 128)
    lse_shape_t, lse_shape_s = heads(size_t), heads(size_s)
    mask_t, mask_s = (size_t, 2 * size_t), (share * size_s, 2 * size_s)
    flops = lambda columns: 2 * n * D * columns

    some, others, every = layout.some, layout.others, layout.steps
    way_t.along(every)
    rows, grad_out = to_temporal(tokens, cotangent)
    rows, grad_out = meet(way_t, way_s, way_in, way_out, rows, grad_out)
    way_t.across(0)
    way_s.along(every)
    meet(way_t, way_s, way_in)
    for step in later:
        way_t.across(step)
    way_t.swap(1)
    grad_out = pos_hop(grad_out)
    way_in.state, grad_out = meet(way_t, way_in.state, grad_out)
    way_t.swap()
    way_s.across(0)
    way_in.along(every)
    packed_t, small_t = call(
        "temporal_qkv",
        partial(temporal_qkv_kernel, chunk_t, my_slots),
        chunk_t.load(way_t).operands() + [(rows, "v")],
        [(wide, bf16, "v"), ((32, D), f32, "v")],
        [((D, 3 * D), bf16), ((D, SMALL), bf16), (narrow, bf16), ((1, 3 * D), f32)]
        + [(columns, f32), (narrow, f32)],
        2,
        flops(3 * D),
    )
    packed_t, small_t = meet(way_s, way_in, packed_t, small_t)
    small = (small_t, "v")
    for step in later:
        way_s.across(step)
    way_s.swap(1)
    way_out.along(every)
    mixed_t, projected, lse_t, temporal = call(
        "temporal_mix",
        partial(temporal_mix_kernel, chunk_t, my_slots),
        chunk_t.operands() + [(packed_t, "v"), (rows, "v")] + ids_t + [small],
        [(narrow, bf16, "v"), (narrow, bf16, "v"), (lse_shape_t, f32, "v"), (narrow, bf16, "v")],
        [((D, D), bf16), ((D, D), bf16), (mask_t, f32), (narrow, f32), (columns, f32)],
        2,
        flops(2 * D + 4 * n),
    )
    temporal, grad_out, small_t = meet(way_s, way_in, way_out, temporal, grad_out, small_t)
    temporal = pos_hop(temporal)
    way_s.swap()
    way_in.across(0)
    way_out.across(0)
    in_bias = small_t[:4].reshape(4, -1, shard).transpose(1, 0, 2).reshape(1, FF)
    grad_out = grad_out.reshape(pos_size, my_frames, my_slots, D)
    grad_out = grad_out.transpose(1, 0, 2, 3).reshape(n, D)
    temporal, in_bias, grad_out = meet(way_s, way_in, way_out, temporal, in_bias, grad_out)
    small = (small_t, "v")
    for step in later:
        way_in.across(step)
    way_in.swap(1)
    temporal, packed_s = call(
        "spatial_qkv",
        partial(spatial_qkv_kernel, chunk_s, pos_size, my_frames),
        chunk_s.load(way_s).operands() + [(temporal, "v"), choose, class_rows, is_class, small],
        [(narrow, bf16, "v"), (wide, bf16, "v")],
        [((D, 3 * D), bf16), (narrow, bf16), ((1, 3 * D), f32)] + [(narrow, f32)] * 2,
        1,
        flops(3 * D),
    )
    temporal = (temporal, "v")
    pairs, k_at = packed_s, D
    if share > 1:
        pairs = [packed_s[:, D:]]
        for step in range(1, share):
            pairs.append(partners(packed_s[:, D:], step))
        pairs, k_at = jnp.concatenate(pairs, axis=0), 0
    all_keys = share * n
    mixed_s, lse_s, spatial = call(
        "spatial_mix",
        partial(spatial_mix_kernel, chunk_s, k_at),
        chunk_s.operands() + [(packed_s, "v"), (pairs, "v")] + ids_s + [temporal, small],
        [(narrow, bf16, "v"), (lse_shape_s, f32, "v"), (narrow, f32, "v")],
        [((D, D), bf16), (mask_s, f32)],
        1,
        flops(D + 4 * all_keys),
    )
    spatial = meet(way_in, way_out, spatial)
    way_in.swap()
    spatial = meet(way_in, way_out, spatial)
    spatial, grad_out = (spatial, "v"), (grad_out, "v")
    for step in later:
        way_out.across(step)
    way_out.swap(1)
    in_bias = (in_bias, "v")
    normed_m, activated, slope = call(
        "hidden",
        partial(hidden_kernel, chunk_in),
        chunk_in.load(way_in).operands() + [spatial, in_bias, small],
        [(narrow, bf16, "v"), (full, bf16, "v"), (full, bf16, "v")],
        [((D, FF), bf16)],
        1,
        flops(FF),
    )
    activated = (activated, "v")
    (acc_out,) = call(
        "mlp_out_grad",
        partial(out_grad_kernel, chunk_out),
        [(chunk_out.index, "s"), activated, grad_out],
        chunk_out.grads(),
        [((FF, D), bf16)],
        1,
        flops(FF),
    )
    acc_out, slope = meet(way_out, acc_out, slope)
    way_out.swap()
    back_out = chunk_out.scatter(*acc_out)
    slope = meet(way_out, back_out, slope)
    for step in reversed(later):
        back_out.across(step)
    grad_hidden, grad_in_bias, grad_spatial, sums_m = call(
        "mlp_back",
        partial(mlp_back_kernel, chunk_in, chunk_out),
        chunk_in.operands()
        + chunk_out.load(way_out).operands()
        + [grad_out, (slope, "v"), spatial, small],
        [(full, bf16, "v"), ((1, FF), f32, "v"), (narrow, f32, "v"), ((8, D), f32, "v")],
        [((D, FF), bf16), ((FF, D), bf16), (narrow, f32)],
        2,
        flops(2 * FF),
    )
    (result,) = call(
        "block_out",
        partial(block_out_kernel, chunk_out, pos_size, my_frames),
        chunk_out.operands() + [activated, spatial, small],
        [(narrow, bf16, "v")],
        [((FF, D), bf16), (narrow, f32), (narrow, f32)],
        1,
        flops(FF),
    )
    grad_hidden, grad_in_bias, result = meet(back_out, grad_hidden, grad_in_bias, result)
    back_out.across(0)
    (acc_in,) = call(
        "mlp_in_grad",
        partial(in_grad_kernel, chunk_in),
        [(chunk_in.index, "s"), (normed_m, "v"), (grad_hidden, "v")],
        chunk_in.grads(),
        [((D, n), bf16), ((D, FF), bf16)],
        1,
        flops(FF),
    )
    acc_in, grad_spatial = meet(back_out, acc_in, grad_spatial)
    back_in = chunk_in.scatter(*acc_in)
    grad_spatial, result = meet(back_in, grad_spatial, result)
    for step in reversed(later):
        back_in.across(step)
    back_out.sums()
    back_out.along(every)
    result = pos_hop(result)
    grad_spatial = (grad_spatial, "v")
    acc_sproj, grad_query, grad_pairs = call(
        "spatial_attention_back",
        partial(spatial_attention_back_kernel, chunk_s, k_at),
        chunk_s.operands()
        + [grad_spatial, (mixed_s, "v"), (packed_s, "v"), (pairs, "v")]
        + ids_s
        + [(lse_s, "v")],
        [((D, D), bf16, "v"), (narrow, bf16, "v"), ((all_keys, 2 * D), bf16, "v")],
        [((D, D), bf16), (narrow, bf16), ((D, n), bf16), (narrow, bf16)]
        + [(mask_s, f32)],
        2,
        flops(2 * D + 10 * all_keys),
    )
    own_pairs = grad_pairs[:n]
    for step in range(1, share):
        theirs = partners(grad_pairs[step * n : (step + 1) * n], share - step)
        own_pairs = (own_pairs.astype(f32) + theirs.astype(f32)).astype(bf16)
    acc_s, grad_temporal, class_part, sums_s = call(
        "spatial_qkv_back",
        partial(spatial_qkv_back_kernel, chunk_s, pos_size, my_frames),
        chunk_s.operands()
        + [(acc_sproj, "v"), (grad_query, "v"), (own_pairs, "v"), temporal, grad_spatial]
        + [choose, is_class, small],
        chunk_s.grads() + [(narrow, bf16, "v"), ((8, D), f32, "v"), ((8, D), f32, "v")],
        [((D, 3 * D), bf16), (wide, bf16), (narrow, bf16), ((D, n), bf16)]
        + [((D, 3 * D), bf16), (narrow, f32), (narrow, f32)],
        3,
        flops(6 * D),
    )
    acc_s, grad_temporal, class_part, grad_in_bias, result = meet(
        back_in, back_out, acc_s, grad_temporal, class_part, grad_in_bias, result
    )
    grad_temporal = pos_hop(grad_temporal)
    back_s = chunk_s.scatter(*acc_s)
    back_out.swap()
    meet(back_s, back_out)
    (acc_out,) = back_out.finish(chunk_out.widths)
    for step in reversed(later):
        back_s.across(step)
    back_in.across(0)
    block_in_bias = grad_in_bias.reshape(-1, 4, shard).transpose(1, 0, 2).reshape(4, D)
    class_sum = class_part + send(class_part, layout.within[0])
    grad_temporal, block_in_bias, class_sum, acc_out = meet(
        back_s, back_in, grad_temporal, block_in_bias, class_sum, acc_out
    )
    back_s.across(0)
    class_sum = class_sum + send(class_sum, layout.within[1])
    back_in.sums()
    back_in.along(some)
    grad_temporal = (grad_temporal, "v")
    acc_proj, grad_mixed_t, sums_t = call(
        "temporal_proj_back",
        partial(temporal_proj_back_kernel, chunk_t, chunk_proj, my_slots),
        chunk_t.operands()
        + [grad_temporal, (projected, "v"), (mixed_t, "v")],
        chunk_proj.grads() + [(narrow, bf16, "v"), ((8, D), f32, "v")],
        [((D, D), bf16), ((D, D), bf16), (narrow, bf16), ((D, n), bf16), ((D, n), bf16)]
        + [((D, D), bf16), ((D, D), bf16), (narrow, bf16), (columns, f32), (narrow, f32)],
        4,
        flops(4 * D),
    )
    acc_proj, grad_mixed_t, class_sum = meet(back_s, back_in, acc_proj, grad_mixed_t, class_sum)
    back_proj = chunk_proj.scatter(*acc_proj)
    grad_mixed_t = meet(back_proj, grad_mixed_t)
    for step in reversed(later):
        back_proj.across(step)
    back_in.along(others)
    back_s.sums()
    back_s.along(some)
    for perm in layout.within[2:]:
        class_sum = class_sum + send(class_sum, perm)
    acc_qkv, tokens_grad = call(
        "temporal_attention_back",
        partial(temporal_attention_back_kernel, chunk_t, chunk_qkv, my_slots),
        chunk_t.operands()
        + [(packed_t, "v")]
        + ids_t
        + [(lse_t, "v"), (grad_mixed_t, "v"), (rows, "v"), grad_temporal, small]
        + [(block_in_bias, "v"), (sums_m, "v"), (sums_s, "v"), (sums_t, "v")],
        chunk_qkv.grads() + [(narrow, bf16, "v")],
        [((D, 3 * D), bf16), (mask_t, f32), (wide, bf16), (narrow, bf16), ((D, n), bf16)]
        + [((D, 3 * D), bf16), (narrow, f32), (columns, f32), ((128, D), f32), ((D, SMALL), bf16)],
        3,
        flops(6 * D + 10 * n),
    )
    acc_qkv, tokens_grad, class_sum, result = meet(
        back_s, back_in, back_proj, acc_qkv, tokens_grad, class_sum, result
    )
    back_qkv = chunk_qkv.scatter(*acc_qkv)
    back_proj.across(0)
    meet(back_qkv, back_proj)
    for step in reversed(later):
        back_qkv.across(step)
    back_s.along(others)
    back_proj.sums()
    back_proj.along(every)
    back_in.swap()
    meet(back_qkv, back_s, back_in, back_proj)
    back_qkv.across(0)
    class_sum = jnp.concatenate([class_sum, jnp.zeros_like(class_sum)]).astype(bf16)
    tokens_grad, block_out, class_all = from_temporal([tokens_grad, result], class_sum)
    back_s.swap()
    back_proj.swap()
    (acc_in,) = back_in.finish(chunk_in.widths)
    acc_in = meet(back_qkv, back_s, back_proj, acc_in)
    back_qkv.sums()
    back_qkv.along(every)
    tokens_grad = tokens_grad.astype(f32)
    class_grad = class_all[::share, :CLIPS].astype(f32)
    acc_sqkv, acc_sproj = back_s.finish(chunk_s.widths)
    acc_tproj, acc_tfc = back_proj.finish(chunk_proj.widths)
    tokens_grad, block_out, class_grad, acc_sqkv, acc_sproj, acc_tproj, acc_tfc = meet(
        back_qkv, tokens_grad, block_out, class_grad, acc_sqkv, acc_sproj, acc_tproj, acc_tfc
    )
    back_qkv.swap()
    acc_tqkv, in_bias_grad, gains_grad, shifts_grad, biases_grad = back_qkv.finish(
        chunk_qkv.widths
    )
    return (
        block_out,
        tokens_grad,
        class_grad,
        acc_tqkv,
        acc_tproj,
        acc_tfc,
        acc_sqkv,
        acc_sproj,
        acc_in,
        acc_out,
        in_bias_grad.reshape(-1),
        gains_grad.T,
        shifts_grad.T,
        biases_grad.T,
    )


def solution(mesh):
    rows = P(AXES, None)
    wide = P(None, "frame", "pos", None)
    placed = (wide, P(), P(), wide) + (rows,) * 7 + (P(AXES),) + (rows,) * 3
    return jax.shard_map(
        on_device,
        mesh=mesh,
        in_specs=placed,
        out_specs=(wide, wide, P()) + (rows,) * 7 + (P(AXES),) + (rows,) * 3,
        check_vma=False,
    )
```

```python
from functools import partial

import jax
import jax.numpy as jnp
from jax import lax
from jax.experimental import pallas as pl
from jax.experimental.pallas import tpu as pltpu
from jax.sharding import PartitionSpec as P

D = 768
HEADS = 12
HEAD = 64
FF = 4 * D
MB = 4
CLIPS = 3
AXES = ("frame", "pos")
TILE = 768
SMALL = 256
f32, bf16 = jnp.float32, jnp.bfloat16
GAIN, SHIFT, BIAS = 4, 7, 10


def send(values, perm):
    return lax.ppermute(values, AXES, perm)


def tie(value, *before):
    return lax.optimization_barrier((value,) + before)[0] if before else value


class Layout:
    def __init__(self):
        self.frames, self.chips = lax.axis_size("frame"), lax.axis_size("pos") // 2
        self.bits = self.frames.bit_length() - 1
        self.frame, self.chip = lax.axis_index("frame"), lax.axis_index("pos") // 2
        self.core = lax.axis_index("pos") % 2
        self.core_index = self.core.astype(jnp.int32).reshape(1)
        self.swap = self.perm(lambda f, z, c: (f, z, 1 - c))
        self.steps = range(1, self.chips)
        self.some = range(self.chips * 3 // 4, self.chips)
        self.others = range(1, self.chips * 3 // 4)
        self.along = [self.perm(lambda f, z, c, i=i: (f, z ^ i, c)) for i in range(1, self.chips)]
        self.across = [
            self.perm(lambda f, z, c, k=k: (f ^ (1 << self.bit(k, c)), z, c))
            for k in range(self.bits)
        ]

        share = self.frames // MB
        steps = lambda n: [1 << k for k in range(n.bit_length() - 1)]
        self.within = [self.swap]
        self.within += [self.perm(lambda f, z, c, k=k: (f, z ^ k, c)) for k in steps(self.chips)]
        self.within += [self.perm(lambda f, z, c, k=k: (f ^ k, z, c)) for k in steps(share)]

    def bit(self, step, core):
        return (step + core) % self.bits

    def perm(self, to):
        pairs = []
        for f in range(self.frames):
            for z in range(self.chips):
                for c in range(2):
                    g, y, d = to(f, z, c)
                    pairs.append(
                        ((f * self.chips + z) * 2 + c, (g * self.chips + y) * 2 + d)
                    )
        return pairs

    def table(self):
        rows = []
        for core in (self.core, 1 - self.core):
            blocks = []
            for b in range(self.frames * self.chips):
                flags, i = b // self.chips, b % self.chips
                f = self.frame
                for k in range(self.bits):
                    if flags >> k & 1:
                        f = f ^ (1 << ((k + core) % self.bits))
                blocks.append(f * self.chips + (self.chip ^ i))
            rows.append(jnp.stack(blocks))
        return jnp.concatenate([jnp.stack(rows).reshape(-1), self.core[None]]).astype(jnp.int32)

    def pick(self, low, high):
        return jnp.where(self.core == 0, low, high), jnp.where(self.core == 0, high, low)

    def chip_rows(self, keep, got):
        return jnp.concatenate(self.pick(keep, got), axis=0)


class Way:
    def __init__(self, layout, *state):
        self.layout, self.state = layout, state


def meet(*things):
    values = tuple(t.state if isinstance(t, Way) else t for t in things)
    values = lax.optimization_barrier(values)
    out = []
    for thing, value in zip(things, values):
        if isinstance(thing, Way):
            thing.state = value
        else:
            out.append(value)
    return out[0] if len(out) == 1 else out


class Gather(Way):
    def along(self, steps):
        block, got = self.state
        new = {i: send(block, self.layout.along[i - 1]) for i in steps}
        self.state = (block, {**got, **new})

    def across(self, step):
        mine, other = self.state
        if step == 0:
            mine = tuple(a[None] for a in [mine] + [other[i] for i in self.layout.steps])
        block = merge(mine)
        self.state = ((block, send(block, self.layout.across[step])), ())

    def swap(self, count=None):
        mine, other = self.state
        other += tuple(send(a, self.layout.swap) for a in mine[len(other) : count])
        self.state = (mine, other)


class Scatter(Way):
    def __init__(self, layout, mine, other):
        near, far = [(a, send(b, layout.swap)) for a, b in zip(mine, other)]
        super().__init__(layout, near, far)
        self.count = near[0].shape[0]

    def across(self, step):
        near, far = self.state
        if far:
            far, _ = fold(far, self.count, False)
        else:
            self.count //= 2
            far, near = fold(near, self.count, True)
            near = (near,)
        self.state = (near + (send(far, self.layout.across[step]),), ())
        return far

    def sums(self):
        near, _ = self.state
        _, rows, width = near[0].shape
        own, *away = call(
            "fold_blocks",
            partial(fold_blocks_kernel, len(near)),
            [(a, "x") for a in near],
            [((rows, width), f32, "x")] + [((rows, width), bf16, "x")] * (self.count - 1),
            [],
            1,
            0,
        )
        self.state = (own, dict(zip(self.layout.steps, away)))

    def along(self, steps):
        own, away = self.state
        new = {i: send(away[i], self.layout.along[i - 1]) for i in steps}
        self.state = (own, {**away, **new})


class Return:
    def __init__(self, layout, ways):
        self.layout = layout
        shapes = [way.state[0].shape for way in ways]
        self.rows = min(r for r, _ in shapes) // 2
        width = sum(r // 2 // self.rows * w for r, w in shapes)
        kept = ((self.rows, width), f32, "x")
        parts = [[(a, "x") for a in [way.state[0], *way.state[1].values()]] for way in ways]
        self.keep, give = call(
            "sum_parts",
            sum_parts_kernel,
            [(layout.core_index, "s"), parts],
            [kept, kept],
            [],
            1,
            0,
        )
        self.got = send(give, layout.swap)


def finish(layout, returns, chunks):
    outs = []
    for rows, width in [m for group in chunks for m in group]:
        if width != SMALL:
            outs.append(((rows, width), f32, "v"))
        else:
            outs += [((count, rows), f32, "v") for count in (4, 3, 3, 8)]
    return call(
        "finish",
        partial(finish_kernel, chunks),
        [(layout.core_index, "s")] + [[(r.keep, "x"), (r.got, "x")] for r in returns],
        outs,
        [((128, 128), f32)],
        1,
        0,
    )


def total(values):
    out = values[0].astype(f32)
    for value in values[1:]:
        out = out + value.astype(f32)
    return out


class Chunk:
    def __init__(self, layout, widths, rows):
        self.layout, self.widths, self.rows = layout, widths, rows
        self.count = layout.frames * layout.chips
        self.table = layout.table()
        self.half = sum(widths) // 2
        self.whole = bool(rows % 16)
        if self.whole:
            core = layout.core.astype(jnp.int32)
            self.index = jnp.stack([jnp.zeros_like(core)] * 2 + [core])
            self.blocks, self.block_rows = 1, self.count * rows
        else:
            self.index = self.table
            self.blocks, self.block_rows = self.count, rows

    def load(self, way):
        mine, other = way.state
        if self.whole:
            order = jnp.argsort(self.table[: 2 * self.count].reshape(2, -1), axis=1)
            mine, other = [
                (jnp.concatenate(a)[o].reshape(1, self.block_rows, -1),)
                for a, o in zip((mine, other), order)
            ]
        self.mine, self.other = mine, other
        return self

    def operands(self):
        pieces = [[(a, "h") for a in side] for side in (self.mine, self.other)]
        return [[(self.index, "s")] + pieces]

    def grads(self):
        if self.whole:
            piece = [((1, self.block_rows, self.half), bf16, "x")]
            return [[piece, piece]]
        shape = (self.count // 2, self.block_rows, self.half)
        return [[[(shape, bf16, "h"), (shape, bf16, "x")], [(shape, bf16, "x")] * 2]]

    def at(self, which):
        return sum(self.widths[:which]) // 2

    def fetch(self, which, weights, dst, sem):
        self._copies(which, *weights, dst, sem, True)

    def store(self, which, table, src, grads, sem):
        self._copies(which, table, *grads, src, sem, False)

    def _copies(self, which, table, mine, other, mat, sem, into):
        at, w = self.at(which), self.widths[which] // 2
        core = table[2 * self.blocks]
        for side, pieces in ((0, mine), (1, other)):
            half = core if side == 0 else 1 - core
            first = side * self.blocks
            for piece in pieces:

                def body(b, carry, piece=piece, first=first, half=half):
                    row = pl.multiple_of(table[first + b] * self.block_rows, 16)
                    block = piece.at[b, :, at : at + w]
                    place = mat.at[
                        pl.ds(row, self.block_rows), pl.ds(pl.multiple_of(half * w, 128), w)
                    ]
                    pair = (block, place) if into else (place, block)
                    pltpu.make_async_copy(*pair, sem).start()
                    return carry

                lax.fori_loop(0, piece.shape[0], body, 0)
                first += piece.shape[0]

    def scatter(self, mine, other):
        if self.whole:
            order = self.table[: 2 * self.count].reshape(2, -1)
            mine, other = [
                a[0].reshape(self.count, self.rows, -1)[o] for a, o in zip((mine, other), order)
            ]
            half = self.count // 2
            mine, other = [(a[:half], a[half:]) for a in (mine, other)]
        return Scatter(self.layout, mine, other)


def merge_kernel(count, *refs):
    out, at = refs[count], 0
    for ref in refs[:count]:
        out[at : at + ref.shape[0]] = ref[...]
        at += ref.shape[0]


def merge(blocks):
    if blocks[0].shape[1] % 16:
        return jnp.concatenate(blocks)
    shape = (sum(a.shape[0] for a in blocks),) + blocks[0].shape[1:]
    return call(
        "merge",
        partial(merge_kernel, len(blocks)),
        [(a, "x") for a in blocks],
        [(shape, blocks[0].dtype, "x")],
        [],
        1,
        0,
    )[0]


def fold_kernel(given, halve, *refs):
    far = refs[given]
    start = far.shape[0] if halve else 0

    def block(b, carry):
        far[b] = total([ref[start + b] for ref in refs[:given]]).astype(bf16)
        if halve:
            refs[given + 1][b] = total([ref[b] for ref in refs[:given]])
        return carry

    lax.fori_loop(0, far.shape[0], block, 0)


def fold(values, count, halve):
    shape = (count,) + values[0].shape[1:]
    outs = [(shape, bf16, "x")] + [(shape, f32, "x")] * halve
    out = call(
        "fold",
        partial(fold_kernel, len(values), halve),
        [(a, "w" if halve and i < 2 else "x") for i, a in enumerate(values)],
        outs,
        [],
        1,
        0,
    )
    return out[0], out[-1]


def fold_blocks_kernel(count, *refs):
    refs, outs = refs[:count], refs[count:-1]
    for b, out in enumerate(outs):
        out[...] = total([ref[b] for ref in refs]).astype(out.dtype)


def pack_kernel(widths, small, core, *refs):
    mats, (keep, give) = refs[: len(widths)], refs[-4:-2]
    turned = refs[-2]
    at = 0
    first = core[0] == 0
    for mat, width in zip(mats, widths):
        w = width // 2
        low, high = mat[:, :w], mat[:, w:]
        keep[:, at : at + w] = jnp.where(first, low, high)
        give[:, at : at + w] = jnp.where(first, high, low)
        at += w
    if small:
        rows = keep.shape[0]
        turned[...] = jnp.zeros_like(turned)
        place = 0
        for ref in refs[len(widths) : -4]:
            count = ref.shape[0]
            turned[place : place + count, :rows] = ref[...].astype(f32)
            place += count
        values = turned[...].T[:rows].astype(bf16)
        zeros = jnp.zeros_like(values)
        keep[:, at:] = jnp.where(first, values, zeros)
        give[:, at:] = jnp.where(first, zeros, values)


def pack(layout, mats, small=()):
    rows = mats[0].shape[0]
    width = sum(m.shape[1] for m in mats) // 2 + (SMALL // 2 if small else 0)
    half = ((rows, width), bf16, "x")
    return call(
        "pack",
        partial(pack_kernel, [m.shape[1] for m in mats], len(small)),
        [(layout.core_index, "s")] + [(m, "w") for m in mats] + [(m, "w") for m in small],
        [half, half],
        [((128, 128), f32)],
        1,
        0,
    )


def sum_parts_kernel(core, groups, keep, give, sem):
    first, short, at = core[0] == 0, keep.shape[0], 0
    for parts in groups:
        values = total([p[...] for p in parts])
        rows, width = values.shape[0] // 2, values.shape[1]
        for row in range(0, rows, short):
            low, high = values[row : row + short], values[rows + row : rows + row + short]
            keep[:, at : at + width] = jnp.where(first, low, high)
            give[:, at : at + width] = jnp.where(first, high, low)
            at += width


def finish_kernel(chunks, core, *refs):
    pairs, outs, turned = refs[: len(chunks)], iter(refs[len(chunks) : -2]), refs[-2]
    first = core[0] == 0
    for (keep, got), group in zip(pairs, chunks):
        short, at = keep.shape[0], 0
        for rows, width in group:
            w = width // 2
            if width == SMALL:
                turned[...] = jnp.zeros_like(turned)
                low = jnp.where(first, keep[:, at : at + w], got[:, at : at + w])
                turned[:short, :] = low
                values, place = turned[...].T, 0
                for _ in range(4):
                    out = next(outs)
                    out[...] = values[place : place + out.shape[0], :short]
                    place += out.shape[0]
                at += w
                continue
            out = next(outs)
            for row in range(0, rows, short):
                mine, other = keep[:, at : at + w], got[:, at : at + w]
                out[row : row + short, :w] = jnp.where(first, mine, other)
                out[row : row + short, w:] = jnp.where(first, other, mine)
                at += w


def arrived(mat, sem):
    pltpu.make_async_copy(mat, mat, sem).wait()


SPACE = {"s": pltpu.SMEM, "h": pltpu.HBM, "v": pltpu.VMEM, "w": pltpu.VMEM, "x": pltpu.VMEM}
HELD = {"h": pltpu.HBM, "w": pltpu.HBM, "x": pltpu.VMEM}


def held(value, space):
    return pltpu.with_memory_space_constraint(value, HELD[space]) if space in HELD else value


def result(shape, kind, space):
    return HELD[space](shape, kind) if space in HELD else jax.ShapeDtypeStruct(shape, kind)


def flat(items):
    return [leaf for item in items for leaf in (flat(item) if isinstance(item, list) else [item])]


def nest(items, leaves):
    return [nest(item, leaves) if isinstance(item, list) else next(leaves) for item in items]


def call(name, body, ins, outs, scratch, sems, flops, alias=None):
    operands, results = flat(ins), flat(outs)
    bytes_of = lambda shape, kind: jnp.dtype(kind).itemsize * _size(shape)
    size = sum(bytes_of(a.shape, a.dtype) for a, space in operands if space in "vwx")
    size += sum(bytes_of(shape, kind) for shape, kind, space in results if space in "vwx")
    size += sum(bytes_of(shape, kind) for shape, kind in scratch)
    moved = sum(bytes_of(a.shape, a.dtype) for a, _ in operands)
    moved += sum(bytes_of(shape, kind) for shape, kind, _ in results)
    aliases = {}
    for i, o in (alias or {}).items():
        start, end = len(flat(ins[:i])), len(flat(outs[:o]))
        for k in range(len(flat([ins[i]]))):
            aliases[start + k] = end + k

    def kernel(*refs):
        leaves = iter(refs)
        body(*nest(ins, leaves), *nest(outs, leaves), *leaves)

    values = pl.pallas_call(
        kernel,
        out_shape=[result(*r) for r in results],
        in_specs=[pl.BlockSpec(memory_space=SPACE[space]) for _, space in operands],
        out_specs=[pl.BlockSpec(memory_space=SPACE[space]) for _, _, space in results],
        scratch_shapes=[pltpu.VMEM(shape, kind) for shape, kind in scratch]
        + [pltpu.SemaphoreType.DMA((sems,))],
        input_output_aliases=aliases,
        compiler_params=pltpu.CompilerParams(
            vmem_limit_bytes=min(int(size * 1.1) + (6 << 20), 60 << 20)
        ),
        cost_estimate=pl.CostEstimate(flops=flops, bytes_accessed=moved, transcendentals=0),
        name=name,
    )(*[held(a, space) for a, space in operands])
    return nest(outs, iter(values))


def _size(shape):
    total = 1
    for n in shape:
        total *= n
    return total


def tiles(width, body, size=TILE):
    def step(j, carry):
        body(pl.ds(pl.multiple_of(j * size, size), size))
        return carry

    lax.fori_loop(0, width // size, step, 0)


def dot(a, b):
    return jnp.dot(a, b, preferred_element_type=f32)


def dot_t(a, b):
    return lax.dot_general(a, b, (((1,), (1,)), ((), ())), preferred_element_type=f32)


def normalise(values):
    centred = values - jnp.mean(values, axis=-1, keepdims=True)
    inv_std = lax.rsqrt(jnp.mean(centred * centred, axis=-1, keepdims=True) + 1e-06)
    return centred * inv_std, inv_std


def norm_rows(values, small, which):
    normal, _ = normalise(values)
    return normal * small[GAIN + which : GAIN + which + 1] + small[SHIFT + which : SHIFT + which + 1]


def norm_back(values, upstream, small, which):
    normal, inv_std = normalise(values)
    product = upstream * normal
    grad_gain = jnp.sum(product, axis=0, keepdims=True)
    grad_shift = jnp.sum(upstream, axis=0, keepdims=True)
    gain = small[GAIN + which : GAIN + which + 1]
    scaled = upstream * gain
    mean = jnp.mean(scaled, axis=-1, keepdims=True)
    mean_normal = jnp.mean(product * gain, axis=-1, keepdims=True)
    return inv_std * (scaled - mean - normal * mean_normal), grad_gain, grad_shift


def column_sum(values):
    return jnp.sum(values.astype(f32), axis=0, keepdims=True)


def set_mask(mask, key_ids, query_ids):
    mask[...] = jnp.where(key_ids[...] == query_ids[...], 0.0, -1000000000.0)


def regroup(values, flat, out, groups):
    count = out.shape[0] // groups
    for c in range(flat.shape[0]):
        cols = slice(c * 128, (c + 1) * 128)
        flat[c] = values[:, cols]
        for g in range(groups):
            out[g * count : (g + 1) * count, cols] = flat[c, pl.ds(g, count, stride=groups), :]


def ungroup(grouped, flat, groups):
    count = grouped.shape[0] // groups
    for c in range(flat.shape[0]):
        cols = slice(c * 128, (c + 1) * 128)
        for g in range(groups):
            flat[c, pl.ds(g, count, stride=groups), :] = grouped[g * count : (g + 1) * count, cols]
    return jnp.concatenate([flat[c] for c in range(flat.shape[0])], axis=1)


def swap_groups(source, out, outer, inner):
    size = source.shape[0] // (outer * inner)
    for i in range(outer):
        for j in range(inner):
            to, at = (j * outer + i) * size, (i * inner + j) * size
            out[to : to + size, :] = source[at : at + size, :]


def both_heads(values, scale):
    lane = lax.broadcasted_iota(jnp.int32, (1, 2 * HEAD), 1)
    wide = values.astype(f32)
    parts = [jnp.where(lane // HEAD == h, wide * scale, 0.0) for h in range(2)]
    return jnp.concatenate(parts, axis=0).astype(bf16)


def own_heads(across):
    size = across.shape[1] // 2
    return jnp.concatenate([across[:HEAD, :size], across[HEAD:, size:]], axis=0).T


def key_rows(pairs, cols, start, size, rows):
    parts = [pairs[at + start : at + start + size, cols] for at in range(0, pairs.shape[0], rows)]
    return parts[0] if len(parts) == 1 else jnp.concatenate(parts, axis=0)


def attend(query, q_at, pairs, k_at, v_at, mask, mixed, lse):
    rows, size = query.shape[0], mask.shape[1] // 2
    blocks = range(rows // size)

    def pair(i, carry):
        cols = lambda at: pl.ds(pl.multiple_of(at + i * 2 * HEAD, 2 * HEAD), 2 * HEAD)
        here = [slice(b * size, (b + 1) * size) for b in blocks]
        queries = [both_heads(query[h, cols(q_at)], 0.125) for h in here]
        keys = [key_rows(pairs, cols(k_at), b * size, size, rows) for b in blocks]
        values = [key_rows(pairs, cols(v_at), b * size, size, rows).T for b in blocks]
        score = [dot_t(keys[b], queries[b]) + mask[...] for b in blocks]
        top = [jnp.max(score[b], axis=0, keepdims=True) for b in blocks]
        weight = [jnp.exp(score[b] - top[b]) for b in blocks]
        norm = [jnp.sum(weight[b], axis=0, keepdims=True) for b in blocks]
        probs = [(weight[b] * (1.0 / norm[b])).astype(bf16) for b in blocks]
        out = [own_heads(dot(values[b], probs[b])).astype(bf16) for b in blocks]
        for b in blocks:
            lse[pl.ds(i * len(blocks) + b, 1), :] = top[b] + jnp.log(norm[b])
            mixed[here[b], cols(0)] = out[b]
        return carry

    lax.fori_loop(0, HEADS // 2, pair, 0, unroll=HEADS // 2)


def attend_back(query, q_at, pairs, k_at, v_at, mask, lse, grad, out_q, out_pairs, gk_at, gv_at):
    rows, size = query.shape[0], mask.shape[1] // 2
    blocks = range(rows // size)

    def pair(i, carry):
        cols = lambda at: pl.ds(pl.multiple_of(at + i * 2 * HEAD, 2 * HEAD), 2 * HEAD)
        here = [slice(b * size, (b + 1) * size) for b in blocks]
        keys = [key_rows(pairs, cols(k_at), b * size, size, rows) for b in blocks]
        values = [key_rows(pairs, cols(v_at), b * size, size, rows) for b in blocks]
        queries = [both_heads(query[h, cols(q_at)], 0.125) for h in here]
        upstream = [both_heads(grad[h, cols(0)], 1.0) for h in here]
        logs = [lse[pl.ds(i * len(blocks) + b, 1), :] for b in blocks]
        across_keys = [keys[b].T for b in blocks]
        score = [dot_t(keys[b], queries[b]) + mask[...] for b in blocks]
        dprob = [dot_t(values[b], upstream[b]) for b in blocks]
        probs = [jnp.exp(score[b] - logs[b]) for b in blocks]
        delta = [jnp.sum(probs[b] * dprob[b], axis=0, keepdims=True) for b in blocks]
        dscore = [(probs[b] * (dprob[b] - delta[b])).astype(bf16) for b in blocks]
        grad_keys = [dot(dscore[b], queries[b]).astype(bf16) for b in blocks]
        grad_values = [dot(probs[b].astype(bf16), upstream[b]).astype(bf16) for b in blocks]
        grad_queries = [
            (own_heads(dot(across_keys[b], dscore[b])) * 0.125).astype(bf16) for b in blocks
        ]
        for b in blocks:
            out_q[here[b], cols(0)] = grad_queries[b]
            for part in range(0, pairs.shape[0], rows):
                there = slice(part + b * size, part + (b + 1) * size)
                seen = slice(part // rows * size, (part // rows + 1) * size)
                out_pairs[there, cols(gk_at)] = grad_keys[b][seen]
                out_pairs[there, cols(gv_at)] = grad_values[b][seen]
        return carry

    lax.fori_loop(0, HEADS // 2, pair, 0, unroll=HEADS // 2)


def qkv_tiles(x, w, bias, small, which, packed):
    bias[:, :D] = small[BIAS + which : BIAS + which + 1]
    bias[:, D : 2 * D] = jnp.zeros((1, D), f32)
    bias[:, 2 * D :] = small[BIAS + which + 1 : BIAS + which + 2]

    def tile(cols):
        packed[:, cols] = (dot(x[...], w[:, cols]) + bias[:, cols]).astype(bf16)

    tiles(3 * D, tile)


def across(mat, out):
    for at in range(0, mat.shape[1], 128):
        out[at : at + 128, :] = mat[:, at : at + 128].astype(f32).T.astype(bf16)


def temporal_qkv_kernel(
    chunk, slots, weights, rows, packed, small, w, raw, x, bias, flat, grouped, sem
):
    chunk.fetch(3, weights, raw, sem.at[0])
    chunk.fetch(0, weights, w, sem.at[1])
    arrived(raw, sem.at[0])
    small[...] = raw[:, :128].astype(f32).T[: small.shape[0]]
    regroup(norm_rows(rows[...].astype(f32), small, 0), flat, grouped, slots)
    x[...] = grouped[...].astype(bf16)
    arrived(w, sem.at[1])
    qkv_tiles(x, w, bias, small, 0, packed)


def temporal_mix_kernel(
    chunk, slots, weights, packed, rows, key_ids, query_ids, small,
    mixed, projected, lse, temporal, w_proj, w_fc, mask, grouped, flat, sem,
):
    chunk.fetch(1, weights, w_proj, sem.at[0])
    chunk.fetch(2, weights, w_fc, sem.at[1])
    set_mask(mask, key_ids, query_ids)
    attend(packed, 0, packed, D, 2 * D, mask, mixed, lse)
    arrived(w_proj, sem.at[0])

    def project(cols):
        bias = small[BIAS + 2 : BIAS + 3, cols]
        projected[:, cols] = (dot(mixed[...], w_proj[:, cols]) + bias).astype(bf16)

    tiles(D, project)
    arrived(w_fc, sem.at[1])

    def residual(cols):
        grouped[:, cols] = dot(projected[...], w_fc[:, cols]) + small[BIAS + 3 : BIAS + 4, cols]

    tiles(D, residual)
    temporal[...] = (rows[...].astype(f32) + ungroup(grouped, flat, slots)).astype(bf16)


def spatial_qkv_kernel(
    chunk, sources, frames, weights, rows, choose, class_rows, is_class, small,
    temporal, packed, w, x, bias, flat, grouped, sem,
):
    chunk.fetch(0, weights, w, sem.at[0])
    flat[...] = rows[...].astype(f32)
    swap_groups(flat, grouped, sources, frames)
    values = jnp.where(is_class[...] > 0, dot(choose[...], class_rows[...]), grouped[...])
    temporal[...] = values.astype(bf16)
    x[...] = norm_rows(values, small, 1).astype(bf16)
    arrived(w, sem.at[0])
    qkv_tiles(x, w, bias, small, 4, packed)


def spatial_mix_kernel(
    chunk, k_at, weights, packed, pairs, key_ids, query_ids, temporal, small,
    mixed, lse, spatial, w, mask, sem,
):
    chunk.fetch(1, weights, w, sem.at[0])
    set_mask(mask, key_ids, query_ids)
    attend(packed, 0, pairs, k_at, k_at + D, mask, mixed, lse)
    arrived(w, sem.at[0])

    def residual(cols):
        added = dot(mixed[...], w[:, cols]) + small[BIAS + 6 : BIAS + 7, cols]
        spatial[:, cols] = temporal[:, cols].astype(f32) + added

    tiles(D, residual)


def hidden_kernel(
    chunk, weights, spatial, in_bias, small, normed, activated, slope, w, sem
):
    chunk.fetch(0, weights, w, sem.at[0])
    normed[...] = norm_rows(spatial[...], small, 2).astype(bf16)
    arrived(w, sem.at[0])

    def tile(cols):
        hidden = dot(normed[...], w[:, cols]) + in_bias[:, cols]
        below = 0.5 + 0.5 * lax.erf(hidden * 0.7071067811865476)
        density = jnp.exp(hidden * hidden * -0.5) * 0.3989422804014327
        activated[:, cols] = (hidden * below).astype(bf16)
        slope[:, cols] = (below + hidden * density).astype(bf16)

    tiles(FF, tile)


def out_grad_kernel(chunk, table, activated, grad_out, grads, grad, sem):
    def tile(cols):
        turned = activated[:, cols].astype(f32).T.astype(bf16)
        grad[cols, :] = dot(turned, grad_out[...]).astype(bf16)

    tiles(FF, tile)
    chunk.store(0, table, grad, grads, sem.at[0])
    arrived(grad, sem.at[0])


def mlp_back_kernel(
    chunk_in, chunk_out, weights_in, weights_out,
    grad_out, slope, spatial, small, grad_hidden, in_bias, grad_spatial, sums,
    w_in, w_out, total, sem,
):
    chunk_out.fetch(0, weights_out, w_out, sem.at[0])
    chunk_in.fetch(0, weights_in, w_in, sem.at[1])
    arrived(w_out, sem.at[0])

    def tile(cols):
        grad = (dot_t(grad_out[...], w_out[cols, :]) * slope[:, cols].astype(f32)).astype(bf16)
        grad_hidden[:, cols] = grad
        in_bias[:, cols] = column_sum(grad)

    tiles(FF, tile)
    arrived(w_in, sem.at[1])

    def back(cols):
        total[:, cols] = dot_t(grad_hidden[...], w_in[cols, :])

    tiles(D, back, D // 2)
    back, gain, shift = norm_back(spatial[...], total[...], small, 2)
    upstream = grad_out[...].astype(f32)
    result = upstream + back
    grad_spatial[...] = result
    sums[0:1] = gain
    sums[1:2] = shift
    sums[2:3] = column_sum(upstream)
    sums[3:4] = column_sum(result.astype(bf16))
    sums[4:8] = jnp.zeros((4, D), f32)


def in_grad_kernel(chunk, table, normed, grad_hidden, grads, normed_t, grad, sem):
    across(normed, normed_t)

    def tile(cols):
        grad[:, cols] = dot(normed_t[...], grad_hidden[:, cols]).astype(bf16)

    tiles(FF, tile)
    chunk.store(0, table, grad, grads, sem.at[0])
    arrived(grad, sem.at[0])


def block_out_kernel(
    chunk, sources, frames, weights, activated, spatial, small, result, w, total, flat, sem
):
    chunk.fetch(0, weights, w, sem.at[0])
    arrived(w, sem.at[0])

    def tile(cols):
        added = dot(activated[...], w[:, cols]) + small[BIAS + 7 : BIAS + 8, cols]
        total[:, cols] = spatial[:, cols] + added

    tiles(D, tile, D // 2)
    swap_groups(total, flat, frames, sources)
    result[...] = flat[...].astype(bf16)


def spatial_attention_back_kernel(
    chunk, k_at, weights, grad_spatial, mixed, packed, pairs, key_ids, query_ids, lse,
    grad, grad_query, grad_pairs,
    w, upstream, mixed_t, grad_mixed, mask, sem,
):
    chunk.fetch(1, weights, w, sem.at[0])
    upstream[...] = grad_spatial[...].astype(bf16)
    set_mask(mask, key_ids, query_ids)
    arrived(w, sem.at[0])

    def back(cols):
        grad_mixed[:, cols] = dot_t(upstream[...], w[cols, :]).astype(bf16)

    tiles(D, back)
    across(mixed, mixed_t)

    def tile(cols):
        grad[:, cols] = dot(mixed_t[...], upstream[:, cols]).astype(bf16)

    tiles(D, tile)
    attend_back(
        packed, 0, pairs, k_at, k_at + D, mask, lse, grad_mixed, grad_query, grad_pairs, 0, D
    )


def qkv_back(normed_t, grad_packed, w, grad, total):
    def back(cols):
        total[:, cols] = dot_t(grad_packed[...], w[cols, :])

    tiles(D, back, D // 2)

    def tile(cols):
        grad[:, cols] = dot(normed_t[...], grad_packed[:, cols]).astype(bf16)

    tiles(3 * D, tile)


def spatial_qkv_back_kernel(
    chunk, sources, frames, weights, acc_spatial, grad_query, grad_pairs, temporal, grad_spatial, choose, is_class,
    small, grads, grad_temporal, class_part, sums,
    w, packed, normed, normed_t, grad, total, flat, sem,
):
    chunk.fetch(0, weights, w, sem.at[0])
    packed[:, :D] = grad_query[...]
    packed[:, D:] = grad_pairs[...]
    values = temporal[...].astype(f32)
    normed[...] = norm_rows(values, small, 1).astype(bf16)
    across(normed, normed_t)
    arrived(w, sem.at[0])
    chunk.store(1, weights[0], acc_spatial, grads, sem.at[2])
    qkv_back(normed_t, packed, w, grad, total)
    chunk.store(0, weights[0], grad, grads, sem.at[1])
    back, gain, shift = norm_back(values, total[...], small, 1)
    total[...] = jnp.where(is_class[...] > 0, 0.0, grad_spatial[...] + back)
    swap_groups(total, flat, frames, sources)
    grad_temporal[...] = flat[...].astype(bf16)
    class_part[...] = jnp.zeros_like(class_part)
    for c in range(CLIPS):
        class_part[c : c + 1] = column_sum(back * choose[:, c : c + 1].astype(f32))
    sums[0:1] = gain
    sums[1:2] = shift
    sums[2:3] = column_sum(packed[:, :D])
    sums[3:4] = column_sum(packed[:, 2 * D :])
    sums[4:8] = jnp.zeros((4, D), f32)
    arrived(grad, sem.at[1])
    arrived(acc_spatial, sem.at[2])


def temporal_proj_back_kernel(
    chunk, chunk_back, slots, weights, grad_rows, projected, mixed,
    grads, grad_mixed, sums,
    w_proj, w_fc, grad_proj, proj_t, mixed_t, acc_proj, acc_fc, grad_temporal, flat, grouped, sem,
):
    chunk.fetch(2, weights, w_fc, sem.at[0])
    chunk.fetch(1, weights, w_proj, sem.at[1])
    regroup(grad_rows[...].astype(f32), flat, grouped, slots)
    grad_temporal[...] = grouped[...].astype(bf16)
    across(projected, proj_t)

    def fc_tile(cols):
        acc_fc[:, cols] = dot(proj_t[...], grad_temporal[:, cols]).astype(bf16)

    tiles(D, fc_tile)
    chunk_back.store(1, weights[0], acc_fc, grads, sem.at[2])
    arrived(w_fc, sem.at[0])

    def fc_back(cols):
        grad_proj[:, cols] = dot_t(grad_temporal[...], w_fc[cols, :]).astype(bf16)

    tiles(D, fc_back)
    across(mixed, mixed_t)

    def proj_tile(cols):
        acc_proj[:, cols] = dot(mixed_t[...], grad_proj[:, cols]).astype(bf16)

    tiles(D, proj_tile)
    chunk_back.store(0, weights[0], acc_proj, grads, sem.at[3])
    arrived(w_proj, sem.at[1])

    def proj_back(cols):
        grad_mixed[:, cols] = dot_t(grad_proj[...], w_proj[cols, :]).astype(bf16)

    tiles(D, proj_back)
    sums[0:1] = column_sum(grad_temporal[...])
    sums[1:2] = column_sum(grad_proj[...])
    sums[2:8] = jnp.zeros((6, D), f32)
    arrived(acc_fc, sem.at[2])
    arrived(acc_proj, sem.at[3])


def temporal_attention_back_kernel(
    chunk, chunk_back, slots, weights, packed, key_ids, query_ids, lse, grad_mixed, rows, grad_temporal,
    small, in_bias, sums_m, sums_s, sums_t, result, class_sum,
    grads, outgoing,
    w, mask, grad_packed, normed, normed_t, grad, total, flat, rows_small, raw, sem,
):
    chunk.fetch(0, weights, w, sem.at[0])
    set_mask(mask, key_ids, query_ids)
    attend_back(
        packed, 0, packed, D, 2 * D, mask, lse, grad_mixed, grad_packed, grad_packed, D, 2 * D
    )
    values = rows[...].astype(f32)
    regroup(norm_rows(values, small, 0), flat, total, slots)
    normed[...] = total[...].astype(bf16)
    across(normed, normed_t)
    arrived(w, sem.at[0])
    qkv_back(normed_t, grad_packed, w, grad, total)
    chunk_back.store(0, weights[0], grad, grads, sem.at[1])
    back, gain, shift = norm_back(values, ungroup(total, flat, slots), small, 0)
    tokens_grad = (grad_temporal[...].astype(f32) + back).astype(bf16)
    frames = outgoing.shape[0]
    rows_each = tokens_grad.shape[0] // frames
    spread = jnp.concatenate([class_sum[...], jnp.zeros_like(class_sum)], axis=0).astype(bf16)
    for f in range(frames):
        here = slice(f * rows_each, (f + 1) * rows_each)
        outgoing[f, :rows_each] = tokens_grad[here]
        outgoing[f, rows_each : 2 * rows_each] = result[here, :]
        outgoing[f, 2 * rows_each :] = spread
    rows_small[...] = jnp.zeros_like(rows_small)
    rows_small[0:4] = in_bias[...]
    for i, (gain_row, shift_row) in enumerate(
        ((gain, shift), (sums_s[0:1], sums_s[1:2]), (sums_m[0:1], sums_m[1:2]))
    ):
        rows_small[GAIN + i : GAIN + i + 1] = gain_row
        rows_small[SHIFT + i : SHIFT + i + 1] = shift_row
    for i, row in enumerate(
        (
            column_sum(grad_packed[:, :D]),
            column_sum(grad_packed[:, 2 * D :]),
            sums_t[1:2],
            sums_t[0:1],
            sums_s[2:3],
            sums_s[3:4],
            sums_m[3:4],
            sums_m[2:3],
        )
    ):
        rows_small[BIAS + i : BIAS + i + 1] = row
    raw[:, :128] = rows_small[...].T.astype(bf16)
    raw[:, 128:] = jnp.zeros((D, 128), bf16)
    chunk_back.store(1, weights[0], raw, grads, sem.at[2])
    arrived(grad, sem.at[1])
    arrived(raw, sem.at[2])


def on_device(
    tokens,
    class_tokens,
    clip_frames,
    cotangent,
    temporal_qkv,
    temporal_proj,
    temporal_fc,
    spatial_qkv,
    spatial_proj,
    mlp_in,
    mlp_out,
    mlp_in_bias,
    norm_gains,
    norm_shifts,
    biases,
):
    frame_size, pos_size = lax.axis_size("frame"), lax.axis_size("pos")
    frame_index, pos_index = lax.axis_index("frame"), lax.axis_index("pos")
    frame_count, pos_count = tokens.shape[1], tokens.shape[2]
    shard = norm_gains.shape[0]
    slots = pos_count + 1
    share = frame_size // MB
    my_slots = slots // share
    all_frames = frame_count * frame_size
    my_frames = all_frames // pos_size
    rows_count = all_frames * my_slots
    micro = frame_index // share

    layout = Layout()
    small = (mlp_in_bias.reshape(4, shard), norm_gains.T, norm_shifts.T, biases.T)
    keep_t, give_t = pack(layout, (temporal_qkv, temporal_proj, temporal_fc), small)
    got_t = send(give_t, layout.swap)
    keep, give = pack(layout, tie((spatial_qkv, spatial_proj, mlp_in), got_t))
    keep_out, give_out = pack(layout, tie((mlp_out,), got_t))
    got = send(tie(give, give_t), layout.swap)
    got_out = send(tie(give_out, give_t), layout.swap)
    way_t = Gather(layout, layout.chip_rows(keep_t, got_t), {})
    rest = layout.chip_rows(keep, got)
    way_s = Gather(layout, rest[:, : 2 * D], {})
    way_in = Gather(layout, rest[:, 2 * D :], {})
    way_out = Gather(layout, layout.chip_rows(keep_out, got_out), {})
    chunk_t = Chunk(layout, (3 * D, D, D, SMALL), 2 * shard)
    chunk_s = Chunk(layout, (3 * D, D), 2 * shard)
    chunk_in = Chunk(layout, (FF,), 2 * shard)
    chunk_out = Chunk(layout, (D,), 8 * shard)
    chunk_proj = Chunk(layout, (D, D), 2 * shard)
    chunk_qkv = Chunk(layout, (3 * D, SMALL), 2 * shard)
    later = range(1, layout.bits)

    def frame_hop(values):
        return lax.all_to_all(values, "frame", 0, 0, tiled=True)

    def pos_hop(values):
        parts = values.reshape(pos_size, rows_count // pos_size, D)
        return lax.all_to_all(parts, "pos", 0, 0, tiled=True).reshape(rows_count, D)

    def to_temporal(*arrays):
        parts = []
        for values in arrays:
            padded = jnp.pad(values, ((0, 0), (0, 0), (0, 1), (0, 0)))
            padded = padded.reshape(MB, frame_count, share, my_slots, D).transpose(0, 2, 1, 3, 4)
            parts.append(padded.reshape(frame_size, frame_count * my_slots, D))
        hopped = frame_hop(jnp.concatenate(parts, axis=1)).reshape(frame_size, len(arrays), -1, D)
        return [hopped[:, i].reshape(rows_count, D) for i in range(len(arrays))]

    def from_temporal(hopped, count):
        rows, out = frame_count * my_slots, []
        for at in range(0, rows * count, rows):
            part = hopped[:, at : at + rows].reshape(MB, share, frame_count, my_slots, D)
            part = part.transpose(0, 2, 1, 3, 4).reshape(MB, frame_count, slots, D)
            out.append(part[:, :, :pos_count])
        return out + [hopped[:, rows * count :]]

    def partners(values, step):
        perm = [(f, f // share * share + (f % share + step) % share) for f in range(frame_size)]
        return lax.ppermute(values, "frame", perm)

    n = rows_count
    clip_ends = jnp.cumsum(lax.dynamic_index_in_dim(clip_frames, micro, 0, keepdims=False))
    clip_of = lambda frame: jnp.sum(
        (frame[:, None] >= clip_ends[None, :]).astype(jnp.int32), axis=1
    )
    size_t = all_frames * max(1, 128 // all_frames)
    ids = jnp.arange(size_t, dtype=jnp.int32)
    ids = ids // all_frames * CLIPS + clip_of(ids % all_frames)
    ids_t = [(ids[:, None], "v"), (jnp.tile(ids, 2)[None, :], "v")]
    frame_rows = n // my_frames
    size_s = frame_rows * max(1, 128 // frame_rows)
    row_ids = jnp.arange(n, dtype=jnp.int32)
    frame_s, row_slot = row_ids // frame_rows, row_ids % my_slots
    first_source = row_ids % frame_rows < my_slots

    def key_masks(share_index):
        padding = row_slot + share_index * my_slots == slots - 1
        is_class = padding & first_source
        return is_class, is_class | ~padding

    keys_s = []
    for step in range(share):
        _, valid = key_masks((frame_index + share - step) % share)
        keys_s.append(jnp.where(valid, frame_s, -1)[:size_s])
    ids_s = [
        (jnp.concatenate(keys_s)[:, None], "v"),
        (jnp.tile(frame_s[:size_s], 2)[None, :], "v"),
    ]
    is_class, _ = key_masks(frame_index % share)
    clip_s = clip_of(pos_index * my_frames + frame_s)
    choose = (clip_s[:, None] == jnp.arange(8)[None, :]) & is_class[:, None]
    choose = (choose.astype(bf16), "v")
    class_rows = lax.dynamic_index_in_dim(class_tokens, micro, 0, keepdims=False)
    class_rows = (jnp.pad(class_rows, ((0, 8 - CLIPS), (0, 0))), "v")
    is_class = (is_class.astype(jnp.int32)[:, None], "v")

    narrow, wide, full = (n, D), (n, 3 * D), (n, FF)
    heads = lambda size: (-(-HEADS // 2 * (n // size) // 8) * 8, 2 * size)
    columns = (D // 128, n, 128)
    lse_shape_t, lse_shape_s = heads(size_t), heads(size_s)
    mask_t, mask_s = (size_t, 2 * size_t), (share * size_s, 2 * size_s)
    flops = lambda columns: 2 * n * D * columns

    some, others, every = layout.some, layout.others, layout.steps
    way_t.along(every)
    rows, grad_out = to_temporal(*tie((tokens, cotangent), give))
    rows, grad_out = meet(way_t, way_s, way_in, way_out, rows, grad_out)
    way_t.across(0)
    way_s.along(every)
    meet(way_t, way_s)
    for step in later:
        way_t.across(step)
    way_t.swap(1)
    grad_out = pos_hop(grad_out)
    way_in.state, grad_out = meet(way_t, way_in.state, grad_out)
    way_t.swap()
    way_s.across(0)
    way_in.along(every)
    packed_t, small_t = call(
        "temporal_qkv",
        partial(temporal_qkv_kernel, chunk_t, my_slots),
        chunk_t.load(way_t).operands() + [(rows, "v")],
        [(wide, bf16, "v"), ((32, D), f32, "v")],
        [((D, 3 * D), bf16), ((D, SMALL), bf16), (narrow, bf16), ((1, 3 * D), f32)]
        + [(columns, f32), (narrow, f32)],
        2,
        flops(3 * D),
    )
    packed_t, small_t = meet(way_s, way_in, packed_t, small_t)
    small = (small_t, "v")
    for step in later:
        way_s.across(step)
    way_s.swap(1)
    way_out.along(every)
    mixed_t, projected, lse_t, temporal = call(
        "temporal_mix",
        partial(temporal_mix_kernel, chunk_t, my_slots),
        chunk_t.operands() + [(packed_t, "v"), (rows, "v")] + ids_t + [small],
        [(narrow, bf16, "v"), (narrow, bf16, "v"), (lse_shape_t, f32, "v"), (narrow, bf16, "v")],
        [((D, D), bf16), ((D, D), bf16), (mask_t, f32), (narrow, f32), (columns, f32)],
        2,
        flops(2 * D + 4 * n),
    )
    temporal, grad_out, small_t = meet(way_s, way_in, way_out, temporal, grad_out, small_t)
    temporal = pos_hop(temporal)
    way_s.swap()
    way_in.across(0)
    way_out.across(0)
    in_bias = small_t[:4].reshape(4, -1, shard).transpose(1, 0, 2).reshape(1, FF)
    grad_out = grad_out.reshape(pos_size, my_frames, my_slots, D)
    grad_out = grad_out.transpose(1, 0, 2, 3).reshape(n, D)
    temporal, in_bias, grad_out = meet(way_s, way_in, way_out, temporal, in_bias, grad_out)
    small = (small_t, "v")
    for step in later:
        way_in.across(step)
    way_in.swap(1)
    temporal, packed_s = call(
        "spatial_qkv",
        partial(spatial_qkv_kernel, chunk_s, pos_size, my_frames),
        chunk_s.load(way_s).operands() + [(temporal, "v"), choose, class_rows, is_class, small],
        [(narrow, bf16, "v"), (wide, bf16, "v")],
        [((D, 3 * D), bf16), (narrow, bf16), ((1, 3 * D), f32)] + [(narrow, f32)] * 2,
        1,
        flops(3 * D),
    )
    temporal = (temporal, "v")
    pairs, k_at = packed_s, D
    if share > 1:
        pairs = [packed_s[:, D:]]
        for step in range(1, share):
            pairs.append(partners(packed_s[:, D:], step))
        pairs, k_at = jnp.concatenate(pairs, axis=0), 0
    all_keys = share * n
    mixed_s, lse_s, spatial = call(
        "spatial_mix",
        partial(spatial_mix_kernel, chunk_s, k_at),
        chunk_s.operands() + [(packed_s, "v"), (pairs, "v")] + ids_s + [temporal, small],
        [(narrow, bf16, "v"), (lse_shape_s, f32, "v"), (narrow, f32, "v")],
        [((D, D), bf16), (mask_s, f32)],
        1,
        flops(D + 4 * all_keys),
    )
    spatial = meet(way_in, way_out, spatial)
    way_in.swap()
    spatial = meet(way_in, way_out, spatial)
    spatial, grad_out = (spatial, "v"), (grad_out, "v")
    for step in later:
        way_out.across(step)
    way_out.swap(1)
    in_bias = (in_bias, "v")
    normed_m, activated, slope = call(
        "hidden",
        partial(hidden_kernel, chunk_in),
        chunk_in.load(way_in).operands() + [spatial, in_bias, small],
        [(narrow, bf16, "v"), (full, bf16, "v"), (full, bf16, "v")],
        [((D, FF), bf16)],
        1,
        flops(FF),
    )
    activated = (activated, "v")
    (acc_out,) = call(
        "mlp_out_grad",
        partial(out_grad_kernel, chunk_out),
        [(chunk_out.index, "s"), activated, grad_out],
        chunk_out.grads(),
        [((FF, D), bf16)],
        1,
        flops(FF),
    )
    acc_out, slope = meet(way_out, acc_out, slope)
    way_out.swap()
    back_out = chunk_out.scatter(*acc_out)
    slope = meet(way_out, back_out, slope)
    for step in reversed(later):
        back_out.across(step)
    grad_hidden, grad_in_bias, grad_spatial, sums_m = call(
        "mlp_back",
        partial(mlp_back_kernel, chunk_in, chunk_out),
        chunk_in.operands()
        + chunk_out.load(way_out).operands()
        + [grad_out, (slope, "v"), spatial, small],
        [(full, bf16, "v"), ((1, FF), f32, "v"), (narrow, f32, "v"), ((8, D), f32, "v")],
        [((D, FF), bf16), ((FF, D), bf16), (narrow, f32)],
        2,
        flops(2 * FF),
    )
    (result,) = call(
        "block_out",
        partial(block_out_kernel, chunk_out, pos_size, my_frames),
        chunk_out.operands() + [activated, spatial, small],
        [(narrow, bf16, "v")],
        [((FF, D), bf16), (narrow, f32), (narrow, f32)],
        1,
        flops(FF),
    )
    grad_hidden, grad_in_bias, result = meet(back_out, grad_hidden, grad_in_bias, result)
    back_out.across(0)
    (acc_in,) = call(
        "mlp_in_grad",
        partial(in_grad_kernel, chunk_in),
        [(chunk_in.index, "s"), (normed_m, "v"), (grad_hidden, "v")],
        chunk_in.grads(),
        [((D, n), bf16), ((D, FF), bf16)],
        1,
        flops(FF),
    )
    acc_in, grad_spatial = meet(back_out, acc_in, grad_spatial)
    back_in = chunk_in.scatter(*acc_in)
    grad_spatial, result = meet(back_in, grad_spatial, result)
    for step in reversed(later):
        back_in.across(step)
    back_out.sums()
    back_out.along(every)
    result = pos_hop(result)
    grad_spatial = (grad_spatial, "v")
    acc_sproj, grad_query, grad_pairs = call(
        "spatial_attention_back",
        partial(spatial_attention_back_kernel, chunk_s, k_at),
        chunk_s.operands()
        + [grad_spatial, (mixed_s, "v"), (packed_s, "v"), (pairs, "v")]
        + ids_s
        + [(lse_s, "v")],
        [((D, D), bf16, "v"), (narrow, bf16, "v"), ((all_keys, 2 * D), bf16, "v")],
        [((D, D), bf16), (narrow, bf16), ((D, n), bf16), (narrow, bf16)]
        + [(mask_s, f32)],
        2,
        flops(2 * D + 10 * all_keys),
    )
    own_pairs = grad_pairs[:n]
    for step in range(1, share):
        theirs = partners(grad_pairs[step * n : (step + 1) * n], share - step)
        own_pairs = (own_pairs.astype(f32) + theirs.astype(f32)).astype(bf16)
    acc_s, grad_temporal, class_part, sums_s = call(
        "spatial_qkv_back",
        partial(spatial_qkv_back_kernel, chunk_s, pos_size, my_frames),
        chunk_s.operands()
        + [(acc_sproj, "v"), (grad_query, "v"), (own_pairs, "v"), temporal, grad_spatial]
        + [choose, is_class, small],
        chunk_s.grads() + [(narrow, bf16, "v"), ((8, D), f32, "v"), ((8, D), f32, "v")],
        [((D, 3 * D), bf16), (wide, bf16), (narrow, bf16), ((D, n), bf16)]
        + [((D, 3 * D), bf16), (narrow, f32), (narrow, f32)],
        3,
        flops(6 * D),
    )
    acc_s, grad_temporal, class_part, grad_in_bias, result = meet(
        back_in, back_out, acc_s, grad_temporal, class_part, grad_in_bias, result
    )
    grad_temporal = pos_hop(grad_temporal)
    back_s = chunk_s.scatter(*acc_s)
    meet(back_s)
    for step in reversed(later):
        back_s.across(step)
    back_in.across(0)
    block_in_bias = grad_in_bias.reshape(-1, 4, shard).transpose(1, 0, 2).reshape(4, D)
    class_sum = class_part + send(class_part, layout.within[0])
    grad_temporal, block_in_bias, class_sum = meet(
        back_s, back_in, grad_temporal, block_in_bias, class_sum
    )
    back_s.across(0)
    for perm in layout.within[1:-1]:
        class_sum = class_sum + send(class_sum, perm)
    back_in.sums()
    back_in.along(some)
    grad_temporal = (grad_temporal, "v")
    acc_proj, grad_mixed_t, sums_t = call(
        "temporal_proj_back",
        partial(temporal_proj_back_kernel, chunk_t, chunk_proj, my_slots),
        chunk_t.operands()
        + [grad_temporal, (projected, "v"), (mixed_t, "v")],
        chunk_proj.grads() + [(narrow, bf16, "v"), ((8, D), f32, "v")],
        [((D, D), bf16), ((D, D), bf16), (narrow, bf16), ((D, n), bf16), ((D, n), bf16)]
        + [((D, D), bf16), ((D, D), bf16), (narrow, bf16), (columns, f32), (narrow, f32)],
        4,
        flops(4 * D),
    )
    acc_proj, grad_mixed_t, class_sum = meet(back_s, back_in, acc_proj, grad_mixed_t, class_sum)
    back_proj = chunk_proj.scatter(*acc_proj)
    class_sum = class_sum + send(class_sum, layout.within[-1])
    grad_mixed_t, class_sum = meet(back_proj, grad_mixed_t, class_sum)
    for step in reversed(later):
        back_proj.across(step)
    back_in.along(others)
    back_s.sums()
    back_s.along(some)
    acc_qkv, outgoing = call(
        "temporal_attention_back",
        partial(temporal_attention_back_kernel, chunk_t, chunk_qkv, my_slots),
        chunk_t.operands()
        + [(packed_t, "v")]
        + ids_t
        + [(lse_t, "v"), (grad_mixed_t, "v"), (rows, "v"), grad_temporal, small]
        + [(block_in_bias, "v"), (sums_m, "v"), (sums_s, "v"), (sums_t, "v")]
        + [(result, "v"), (class_sum, "v")],
        chunk_qkv.grads() + [((frame_size, 2 * n // frame_size + 16, D), bf16, "v")],
        [((D, 3 * D), bf16), (mask_t, f32), (wide, bf16), (narrow, bf16), ((D, n), bf16)]
        + [((D, 3 * D), bf16), (narrow, f32), (columns, f32), ((128, D), f32), ((D, SMALL), bf16)],
        3,
        flops(6 * D + 10 * n),
    )
    acc_qkv, outgoing = meet(back_s, back_in, back_proj, acc_qkv, outgoing)
    back_qkv = chunk_qkv.scatter(*acc_qkv)
    back_proj.across(0)
    meet(back_qkv, back_proj)
    for step in reversed(later):
        back_qkv.across(step)
    back_s.along(others)
    back_proj.sums()
    back_proj.along(every)
    hopped = frame_hop(outgoing)
    meet(back_qkv, back_s, back_proj)
    back_qkv.across(0)
    hopped = meet(back_qkv, hopped)
    back_qkv.sums()
    back_qkv.along(every)
    own = back_qkv.state[0]
    for way in (back_in, back_s, back_proj, back_out):
        way.state = tie(way.state, own)
    most = Return(layout, [back_in, back_s, back_proj, back_out])
    tokens_grad, block_out, class_all = from_temporal(tie(hopped, own), 2)
    tokens_grad = tokens_grad.astype(f32)
    class_grad = class_all[::share, :CLIPS].astype(f32)
    tokens_grad, block_out, class_grad = meet(back_qkv, tokens_grad, block_out, class_grad)
    last = Return(layout, [back_qkv])
    (
        acc_in, acc_sqkv, acc_sproj, acc_tproj, acc_tfc, acc_out,
        acc_tqkv, in_bias_grad, gains_grad, shifts_grad, biases_grad,
    ) = finish(
        layout,
        [most, last],
        [
            [(shard, FF), (shard, 3 * D), (shard, D), (shard, D), (shard, D), (4 * shard, D)],
            [(shard, 3 * D), (shard, SMALL)],
        ],
    )
    return (
        block_out,
        tokens_grad,
        class_grad,
        acc_tqkv,
        acc_tproj,
        acc_tfc,
        acc_sqkv,
        acc_sproj,
        acc_in,
        acc_out,
        in_bias_grad.reshape(-1),
        gains_grad.T,
        shifts_grad.T,
        biases_grad.T,
    )


def solution(mesh):
    rows = P(AXES, None)
    wide = P(None, "frame", "pos", None)
    placed = (wide, P(), P(), wide) + (rows,) * 7 + (P(AXES),) + (rows,) * 3
    return jax.shard_map(
        on_device,
        mesh=mesh,
        in_specs=placed,
        out_specs=(wide, wide, P()) + (rows,) * 7 + (P(AXES),) + (rows,) * 3,
        check_vma=False,
    )
```

```python
from functools import partial

import jax
import jax.numpy as jnp
from jax import lax
from jax.experimental import pallas as pl
from jax.experimental.pallas import tpu as pltpu
from jax.sharding import PartitionSpec as P

D = 768
HEADS = 12
HEAD = 64
FF = 4 * D
MB = 4
CLIPS = 3
AXES = ("frame", "pos")
TILE = 768
SMALL = 256
f32, bf16 = jnp.float32, jnp.bfloat16
GAIN, SHIFT, BIAS = 4, 7, 10


def send(values, perm):
    return lax.ppermute(values, AXES, perm)


def tie(value, *before):
    return lax.optimization_barrier((value,) + before)[0] if before else value


class Layout:
    def __init__(self):
        self.frames, self.chips = lax.axis_size("frame"), lax.axis_size("pos") // 2
        self.bits = self.frames.bit_length() - 1
        self.frame, self.chip = lax.axis_index("frame"), lax.axis_index("pos") // 2
        self.core = lax.axis_index("pos") % 2
        self.core_index = self.core.astype(jnp.int32).reshape(1)
        self.swap = self.perm(lambda f, z, c: (f, z, 1 - c))
        self.steps = range(1, self.chips)
        self.some = range(self.chips * 3 // 4, self.chips)
        self.others = range(1, self.chips * 3 // 4)
        self.along = [self.perm(lambda f, z, c, i=i: (f, z ^ i, c)) for i in range(1, self.chips)]
        self.across = [
            self.perm(lambda f, z, c, k=k: (f ^ (1 << self.bit(k, c)), z, c))
            for k in range(self.bits)
        ]

        share = self.frames // MB
        steps = lambda n: [1 << k for k in range(n.bit_length() - 1)]
        self.within = [self.swap]
        self.within += [self.perm(lambda f, z, c, k=k: (f, z ^ k, c)) for k in steps(self.chips)]
        self.within += [self.perm(lambda f, z, c, k=k: (f ^ k, z, c)) for k in steps(share)]

    def bit(self, step, core):
        return (step + core) % self.bits

    def perm(self, to):
        pairs = []
        for f in range(self.frames):
            for z in range(self.chips):
                for c in range(2):
                    g, y, d = to(f, z, c)
                    pairs.append(
                        ((f * self.chips + z) * 2 + c, (g * self.chips + y) * 2 + d)
                    )
        return pairs

    def table(self):
        rows = []
        for core in (self.core, 1 - self.core):
            blocks = []
            for b in range(self.frames * self.chips):
                flags, i = b // self.chips, b % self.chips
                f = self.frame
                for k in range(self.bits):
                    if flags >> k & 1:
                        f = f ^ (1 << ((k + core) % self.bits))
                blocks.append(f * self.chips + (self.chip ^ i))
            rows.append(jnp.stack(blocks))
        return jnp.concatenate([jnp.stack(rows).reshape(-1), self.core[None]]).astype(jnp.int32)

    def pick(self, low, high):
        return jnp.where(self.core == 0, low, high), jnp.where(self.core == 0, high, low)

    def chip_rows(self, keep, got):
        return jnp.concatenate(self.pick(keep, got), axis=0)


class Way:
    def __init__(self, layout, *state):
        self.layout, self.state = layout, state


def meet(*things):
    values = tuple(t.state if isinstance(t, Way) else t for t in things)
    values = lax.optimization_barrier(values)
    out = []
    for thing, value in zip(things, values):
        if isinstance(thing, Way):
            thing.state = value
        else:
            out.append(value)
    return out[0] if len(out) == 1 else out


class Gather(Way):
    def along(self, steps):
        block, got = self.state
        new = {i: send(block, self.layout.along[i - 1]) for i in steps}
        self.state = (block, {**got, **new})

    def across(self, step):
        mine, other = self.state
        if step == 0:
            mine = tuple(a[None] for a in [mine] + [other[i] for i in self.layout.steps])
        block = merge(mine)
        self.state = ((block, send(block, self.layout.across[step])), ())

    def swap(self, count=None):
        mine, other = self.state
        other += tuple(send(a, self.layout.swap) for a in mine[len(other) : count])
        self.state = (mine, other)


class Scatter(Way):
    def __init__(self, layout, mine, other):
        near, far = [(a, send(b, layout.swap)) for a, b in zip(mine, other)]
        super().__init__(layout, near, far)
        self.count = near[0].shape[0]

    def across(self, step):
        near, far = self.state
        if far:
            far, _ = fold(far, self.count, False)
        else:
            self.count //= 2
            far, near = fold(near, self.count, True)
            near = (near,)
        self.state = (near + (send(far, self.layout.across[step]),), ())
        return far

    def sums(self, space="w"):
        near, _ = self.state
        _, rows, width = near[0].shape
        own, *away = call(
            "fold_blocks",
            partial(fold_blocks_kernel, len(near)),
            [(a, "x") for a in near],
            [((rows, width), f32, space)] + [((rows, width), bf16, "x")] * (self.count - 1),
            [],
            1,
            0,
        )
        self.state = (own, dict(zip(self.layout.steps, away)))

    def along(self, steps):
        own, away = self.state
        new = {i: send(away[i], self.layout.along[i - 1]) for i in steps}
        self.state = (own, {**away, **new})


class Return:
    def __init__(self, layout, ways, space):
        shapes = [way.state[0].shape for way in ways]
        self.rows = min(r for r, _ in shapes) // 2
        width = sum(r // 2 // self.rows * w for r, w in shapes)
        kept = ((self.rows, width), f32, "x")
        parts = [[(a, space) for a in [way.state[0], *way.state[1].values()]] for way in ways]
        self.keep, give = call(
            "sum_parts",
            sum_parts_kernel,
            [(layout.core_index, "s"), parts],
            [kept, kept],
            [],
            1,
            0,
        )
        self.got = send(give, layout.swap)


def finish(layout, returns, chunks):
    outs = []
    for rows, width in [m for group in chunks for m in group]:
        if width != SMALL:
            outs.append(((rows, width), f32, "v"))
        else:
            outs += [((count, rows), f32, "v") for count in (4, 3, 3, 8)]
    return call(
        "finish",
        partial(finish_kernel, chunks),
        [(layout.core_index, "s")] + [[(r.keep, "x"), (r.got, "x")] for r in returns],
        outs,
        [((128, 128), f32)],
        1,
        0,
    )


def total(values):
    out = values[0].astype(f32)
    for value in values[1:]:
        out = out + value.astype(f32)
    return out


class Chunk:
    def __init__(self, layout, widths, rows):
        self.layout, self.widths, self.rows = layout, widths, rows
        self.count = layout.frames * layout.chips
        self.table = layout.table()
        self.half = sum(widths) // 2
        self.whole = bool(rows % 16)
        if self.whole:
            core = layout.core.astype(jnp.int32)
            self.index = jnp.stack([jnp.zeros_like(core)] * 2 + [core])
            self.blocks, self.block_rows = 1, self.count * rows
        else:
            self.index = self.table
            self.blocks, self.block_rows = self.count, rows

    def load(self, way):
        mine, other = way.state
        if self.whole:
            order = jnp.argsort(self.table[: 2 * self.count].reshape(2, -1), axis=1)
            mine, other = [
                (jnp.concatenate(a)[o].reshape(1, self.block_rows, -1),)
                for a, o in zip((mine, other), order)
            ]
        self.mine, self.other = mine, other
        return self

    def operands(self):
        pieces = [[(a, "h") for a in side] for side in (self.mine, self.other)]
        return [[(self.index, "s")] + pieces]

    def grads(self):
        if self.whole:
            piece = [((1, self.block_rows, self.half), bf16, "x")]
            return [[piece, piece]]
        shape = (self.count // 2, self.block_rows, self.half)
        return [[[(shape, bf16, "h"), (shape, bf16, "x")], [(shape, bf16, "x")] * 2]]

    def at(self, which):
        return sum(self.widths[:which]) // 2

    def fetch(self, which, weights, dst, sem):
        self._copies(which, *weights, dst, sem, True)

    def store(self, which, table, src, grads, sem):
        self._copies(which, table, *grads, src, sem, False)

    def _copies(self, which, table, mine, other, mat, sem, into):
        at, w = self.at(which), self.widths[which] // 2
        core = table[2 * self.blocks]
        for side, pieces in ((0, mine), (1, other)):
            half = core if side == 0 else 1 - core
            first = side * self.blocks
            for piece in pieces:

                def body(b, carry, piece=piece, first=first, half=half):
                    row = pl.multiple_of(table[first + b] * self.block_rows, 16)
                    block = piece.at[b, :, at : at + w]
                    place = mat.at[
                        pl.ds(row, self.block_rows), pl.ds(pl.multiple_of(half * w, 128), w)
                    ]
                    pair = (block, place) if into else (place, block)
                    pltpu.make_async_copy(*pair, sem).start()
                    return carry

                lax.fori_loop(0, piece.shape[0], body, 0)
                first += piece.shape[0]

    def scatter(self, mine, other):
        if self.whole:
            order = self.table[: 2 * self.count].reshape(2, -1)
            mine, other = [
                a[0].reshape(self.count, self.rows, -1)[o] for a, o in zip((mine, other), order)
            ]
            half = self.count // 2
            mine, other = [(a[:half], a[half:]) for a in (mine, other)]
        return Scatter(self.layout, mine, other)


def merge_kernel(count, *refs):
    out, at = refs[count], 0
    for ref in refs[:count]:
        out[at : at + ref.shape[0]] = ref[...]
        at += ref.shape[0]


def merge(blocks):
    if blocks[0].shape[1] % 16:
        return jnp.concatenate(blocks)
    shape = (sum(a.shape[0] for a in blocks),) + blocks[0].shape[1:]
    return call(
        "merge",
        partial(merge_kernel, len(blocks)),
        [(a, "x") for a in blocks],
        [(shape, blocks[0].dtype, "x")],
        [],
        1,
        0,
    )[0]


def fold_kernel(given, halve, *refs):
    far = refs[given]
    start = far.shape[0] if halve else 0

    def block(b, carry):
        far[b] = total([ref[start + b] for ref in refs[:given]]).astype(bf16)
        if halve:
            refs[given + 1][b] = total([ref[b] for ref in refs[:given]])
        return carry

    lax.fori_loop(0, far.shape[0], block, 0)


def fold(values, count, halve):
    shape = (count,) + values[0].shape[1:]
    outs = [(shape, bf16, "x")] + [(shape, f32, "x")] * halve
    out = call(
        "fold",
        partial(fold_kernel, len(values), halve),
        [(a, "w" if halve and i < 2 else "x") for i, a in enumerate(values)],
        outs,
        [],
        1,
        0,
    )
    return out[0], out[-1]


def fold_blocks_kernel(count, *refs):
    refs, outs = refs[:count], refs[count:-1]
    for b, out in enumerate(outs):
        out[...] = total([ref[b] for ref in refs]).astype(out.dtype)


def pack_kernel(widths, small, core, *refs):
    mats, (keep, give) = refs[: len(widths)], refs[-4:-2]
    turned = refs[-2]
    at = 0
    first = core[0] == 0
    for mat, width in zip(mats, widths):
        w = width // 2
        low, high = mat[:, :w], mat[:, w:]
        keep[:, at : at + w] = jnp.where(first, low, high)
        give[:, at : at + w] = jnp.where(first, high, low)
        at += w
    if small:
        rows = keep.shape[0]
        turned[...] = jnp.zeros_like(turned)
        place = 0
        for ref in refs[len(widths) : -4]:
            count = ref.shape[0]
            turned[place : place + count, :rows] = ref[...].astype(f32)
            place += count
        values = turned[...].T[:rows].astype(bf16)
        zeros = jnp.zeros_like(values)
        keep[:, at:] = jnp.where(first, values, zeros)
        give[:, at:] = jnp.where(first, zeros, values)


def pack(layout, mats, small=()):
    rows = mats[0].shape[0]
    width = sum(m.shape[1] for m in mats) // 2 + (SMALL // 2 if small else 0)
    half = ((rows, width), bf16, "x")
    return call(
        "pack",
        partial(pack_kernel, [m.shape[1] for m in mats], len(small)),
        [(layout.core_index, "s")] + [(m, "w") for m in mats] + [(m, "w") for m in small],
        [half, half],
        [((128, 128), f32)],
        1,
        0,
    )


def sum_parts_kernel(core, groups, keep, give, sem):
    first, short, at = core[0] == 0, keep.shape[0], 0
    for parts in groups:
        values = total([p[...] for p in parts])
        rows, width = values.shape[0] // 2, values.shape[1]
        for row in range(0, rows, short):
            low, high = values[row : row + short], values[rows + row : rows + row + short]
            keep[:, at : at + width] = jnp.where(first, low, high)
            give[:, at : at + width] = jnp.where(first, high, low)
            at += width


def finish_kernel(chunks, core, *refs):
    pairs, outs, turned = refs[: len(chunks)], iter(refs[len(chunks) : -2]), refs[-2]
    first = core[0] == 0
    for (keep, got), group in zip(pairs, chunks):
        short, at = keep.shape[0], 0
        for rows, width in group:
            w = width // 2
            if width == SMALL:
                turned[...] = jnp.zeros_like(turned)
                low = jnp.where(first, keep[:, at : at + w], got[:, at : at + w])
                turned[:short, :] = low
                values, place = turned[...].T, 0
                for _ in range(4):
                    out = next(outs)
                    out[...] = values[place : place + out.shape[0], :short]
                    place += out.shape[0]
                at += w
                continue
            out = next(outs)
            for row in range(0, rows, short):
                mine, other = keep[:, at : at + w], got[:, at : at + w]
                out[row : row + short, :w] = jnp.where(first, mine, other)
                out[row : row + short, w:] = jnp.where(first, other, mine)
                at += w


def arrived(mat, sem):
    pltpu.make_async_copy(mat, mat, sem).wait()


SPACE = {"s": pltpu.SMEM, "h": pltpu.HBM, "v": pltpu.VMEM, "w": pltpu.VMEM, "x": pltpu.VMEM}
HELD = {"h": pltpu.HBM, "w": pltpu.HBM, "x": pltpu.VMEM}


def held(value, space):
    return pltpu.with_memory_space_constraint(value, HELD[space]) if space in HELD else value


def result(shape, kind, space):
    return HELD[space](shape, kind) if space in HELD else jax.ShapeDtypeStruct(shape, kind)


def flat(items):
    return [leaf for item in items for leaf in (flat(item) if isinstance(item, list) else [item])]


def nest(items, leaves):
    return [nest(item, leaves) if isinstance(item, list) else next(leaves) for item in items]


def call(name, body, ins, outs, scratch, sems, flops, alias=None):
    operands, results = flat(ins), flat(outs)
    bytes_of = lambda shape, kind: jnp.dtype(kind).itemsize * _size(shape)
    size = sum(bytes_of(a.shape, a.dtype) for a, space in operands if space in "vwx")
    size += sum(bytes_of(shape, kind) for shape, kind, space in results if space in "vwx")
    size += sum(bytes_of(shape, kind) for shape, kind in scratch)
    moved = sum(bytes_of(a.shape, a.dtype) for a, _ in operands)
    moved += sum(bytes_of(shape, kind) for shape, kind, _ in results)
    aliases = {}
    for i, o in (alias or {}).items():
        start, end = len(flat(ins[:i])), len(flat(outs[:o]))
        for k in range(len(flat([ins[i]]))):
            aliases[start + k] = end + k

    def kernel(*refs):
        leaves = iter(refs)
        body(*nest(ins, leaves), *nest(outs, leaves), *leaves)

    values = pl.pallas_call(
        kernel,
        out_shape=[result(*r) for r in results],
        in_specs=[pl.BlockSpec(memory_space=SPACE[space]) for _, space in operands],
        out_specs=[pl.BlockSpec(memory_space=SPACE[space]) for _, _, space in results],
        scratch_shapes=[pltpu.VMEM(shape, kind) for shape, kind in scratch]
        + [pltpu.SemaphoreType.DMA((sems,))],
        input_output_aliases=aliases,
        compiler_params=pltpu.CompilerParams(
            vmem_limit_bytes=min(int(size * 1.1) + (6 << 20), 60 << 20)
        ),
        cost_estimate=pl.CostEstimate(flops=flops, bytes_accessed=moved, transcendentals=0),
        name=name,
    )(*[held(a, space) for a, space in operands])
    return nest(outs, iter(values))


def _size(shape):
    total = 1
    for n in shape:
        total *= n
    return total


def tiles(width, body, size=TILE):
    def step(j, carry):
        body(pl.ds(pl.multiple_of(j * size, size), size))
        return carry

    lax.fori_loop(0, width // size, step, 0)


def dot(a, b):
    return jnp.dot(a, b, preferred_element_type=f32)


def dot_t(a, b):
    return lax.dot_general(a, b, (((1,), (1,)), ((), ())), preferred_element_type=f32)


def normalise(values):
    centred = values - jnp.mean(values, axis=-1, keepdims=True)
    inv_std = lax.rsqrt(jnp.mean(centred * centred, axis=-1, keepdims=True) + 1e-06)
    return centred * inv_std, inv_std


def norm_rows(values, small, which):
    normal, _ = normalise(values)
    return normal * small[GAIN + which : GAIN + which + 1] + small[SHIFT + which : SHIFT + which + 1]


def norm_back(values, upstream, small, which):
    normal, inv_std = normalise(values)
    product = upstream * normal
    grad_gain = jnp.sum(product, axis=0, keepdims=True)
    grad_shift = jnp.sum(upstream, axis=0, keepdims=True)
    gain = small[GAIN + which : GAIN + which + 1]
    scaled = upstream * gain
    mean = jnp.mean(scaled, axis=-1, keepdims=True)
    mean_normal = jnp.mean(product * gain, axis=-1, keepdims=True)
    return inv_std * (scaled - mean - normal * mean_normal), grad_gain, grad_shift


def column_sum(values):
    return jnp.sum(values.astype(f32), axis=0, keepdims=True)


def set_mask(mask, key_ids, query_ids):
    mask[...] = jnp.where(key_ids[...] == query_ids[...], 0.0, -1000000000.0)


def regroup(values, flat, out, groups):
    count = out.shape[0] // groups
    for c in range(flat.shape[0]):
        cols = slice(c * 128, (c + 1) * 128)
        flat[c] = values[:, cols]
        for g in range(groups):
            out[g * count : (g + 1) * count, cols] = flat[c, pl.ds(g, count, stride=groups), :]


def ungroup(grouped, flat, groups):
    count = grouped.shape[0] // groups
    for c in range(flat.shape[0]):
        cols = slice(c * 128, (c + 1) * 128)
        for g in range(groups):
            flat[c, pl.ds(g, count, stride=groups), :] = grouped[g * count : (g + 1) * count, cols]
    return jnp.concatenate([flat[c] for c in range(flat.shape[0])], axis=1)


def swap_groups(source, out, outer, inner):
    size = source.shape[0] // (outer * inner)
    for i in range(outer):
        for j in range(inner):
            to, at = (j * outer + i) * size, (i * inner + j) * size
            out[to : to + size, :] = source[at : at + size, :]


def both_heads(values, scale):
    lane = lax.broadcasted_iota(jnp.int32, (1, 2 * HEAD), 1)
    wide = values.astype(f32)
    parts = [jnp.where(lane // HEAD == h, wide * scale, 0.0) for h in range(2)]
    return jnp.concatenate(parts, axis=0).astype(bf16)


def own_heads(across):
    size = across.shape[1] // 2
    return jnp.concatenate([across[:HEAD, :size], across[HEAD:, size:]], axis=0).T


def key_rows(pairs, cols, start, size, rows):
    parts = [pairs[at + start : at + start + size, cols] for at in range(0, pairs.shape[0], rows)]
    return parts[0] if len(parts) == 1 else jnp.concatenate(parts, axis=0)


def attend(query, q_at, pairs, k_at, v_at, mask, mixed, lse):
    rows, size = query.shape[0], mask.shape[1] // 2
    blocks = range(rows // size)

    def pair(i, carry):
        cols = lambda at: pl.ds(pl.multiple_of(at + i * 2 * HEAD, 2 * HEAD), 2 * HEAD)
        here = [slice(b * size, (b + 1) * size) for b in blocks]
        queries = [both_heads(query[h, cols(q_at)], 0.125) for h in here]
        keys = [key_rows(pairs, cols(k_at), b * size, size, rows) for b in blocks]
        values = [key_rows(pairs, cols(v_at), b * size, size, rows).T for b in blocks]
        score = [dot_t(keys[b], queries[b]) + mask[...] for b in blocks]
        top = [jnp.max(score[b], axis=0, keepdims=True) for b in blocks]
        weight = [jnp.exp(score[b] - top[b]) for b in blocks]
        norm = [jnp.sum(weight[b], axis=0, keepdims=True) for b in blocks]
        probs = [(weight[b] * (1.0 / norm[b])).astype(bf16) for b in blocks]
        out = [own_heads(dot(values[b], probs[b])).astype(bf16) for b in blocks]
        for b in blocks:
            lse[pl.ds(i * len(blocks) + b, 1), :] = top[b] + jnp.log(norm[b])
            mixed[here[b], cols(0)] = out[b]
        return carry

    lax.fori_loop(0, HEADS // 2, pair, 0, unroll=HEADS // 2)


def attend_back(query, q_at, pairs, k_at, v_at, mask, lse, grad, out_q, out_pairs, gk_at, gv_at):
    rows, size = query.shape[0], mask.shape[1] // 2
    blocks = range(rows // size)

    def pair(i, carry):
        cols = lambda at: pl.ds(pl.multiple_of(at + i * 2 * HEAD, 2 * HEAD), 2 * HEAD)
        here = [slice(b * size, (b + 1) * size) for b in blocks]
        keys = [key_rows(pairs, cols(k_at), b * size, size, rows) for b in blocks]
        values = [key_rows(pairs, cols(v_at), b * size, size, rows) for b in blocks]
        queries = [both_heads(query[h, cols(q_at)], 0.125) for h in here]
        upstream = [both_heads(grad[h, cols(0)], 1.0) for h in here]
        logs = [lse[pl.ds(i * len(blocks) + b, 1), :] for b in blocks]
        across_keys = [keys[b].T for b in blocks]
        score = [dot_t(keys[b], queries[b]) + mask[...] for b in blocks]
        dprob = [dot_t(values[b], upstream[b]) for b in blocks]
        probs = [jnp.exp(score[b] - logs[b]) for b in blocks]
        delta = [jnp.sum(probs[b] * dprob[b], axis=0, keepdims=True) for b in blocks]
        dscore = [(probs[b] * (dprob[b] - delta[b])).astype(bf16) for b in blocks]
        grad_keys = [dot(dscore[b], queries[b]).astype(bf16) for b in blocks]
        grad_values = [dot(probs[b].astype(bf16), upstream[b]).astype(bf16) for b in blocks]
        grad_queries = [
            (own_heads(dot(across_keys[b], dscore[b])) * 0.125).astype(bf16) for b in blocks
        ]
        for b in blocks:
            out_q[here[b], cols(0)] = grad_queries[b]
            for part in range(0, pairs.shape[0], rows):
                there = slice(part + b * size, part + (b + 1) * size)
                seen = slice(part // rows * size, (part // rows + 1) * size)
                out_pairs[there, cols(gk_at)] = grad_keys[b][seen]
                out_pairs[there, cols(gv_at)] = grad_values[b][seen]
        return carry

    lax.fori_loop(0, HEADS // 2, pair, 0, unroll=HEADS // 2)


def qkv_tiles(x, w, bias, small, which, packed):
    bias[:, :D] = small[BIAS + which : BIAS + which + 1]
    bias[:, D : 2 * D] = jnp.zeros((1, D), f32)
    bias[:, 2 * D :] = small[BIAS + which + 1 : BIAS + which + 2]

    def tile(cols):
        packed[:, cols] = (dot(x[...], w[:, cols]) + bias[:, cols]).astype(bf16)

    tiles(3 * D, tile)


def across(mat, out):
    for at in range(0, mat.shape[1], 128):
        out[at : at + 128, :] = mat[:, at : at + 128].astype(f32).T.astype(bf16)


def temporal_qkv_kernel(
    chunk, slots, weights, rows, packed, small, w, raw, x, bias, flat, grouped, sem
):
    chunk.fetch(3, weights, raw, sem.at[0])
    chunk.fetch(0, weights, w, sem.at[1])
    arrived(raw, sem.at[0])
    small[...] = raw[:, :128].astype(f32).T[: small.shape[0]]
    regroup(norm_rows(rows[...].astype(f32), small, 0), flat, grouped, slots)
    x[...] = grouped[...].astype(bf16)
    arrived(w, sem.at[1])
    qkv_tiles(x, w, bias, small, 0, packed)


def temporal_mix_kernel(
    chunk, slots, weights, packed, rows, key_ids, query_ids, small,
    mixed, projected, lse, temporal, w_proj, w_fc, mask, grouped, flat, sem,
):
    chunk.fetch(1, weights, w_proj, sem.at[0])
    chunk.fetch(2, weights, w_fc, sem.at[1])
    set_mask(mask, key_ids, query_ids)
    attend(packed, 0, packed, D, 2 * D, mask, mixed, lse)
    arrived(w_proj, sem.at[0])

    def project(cols):
        bias = small[BIAS + 2 : BIAS + 3, cols]
        projected[:, cols] = (dot(mixed[...], w_proj[:, cols]) + bias).astype(bf16)

    tiles(D, project)
    arrived(w_fc, sem.at[1])

    def residual(cols):
        grouped[:, cols] = dot(projected[...], w_fc[:, cols]) + small[BIAS + 3 : BIAS + 4, cols]

    tiles(D, residual)
    temporal[...] = (rows[...].astype(f32) + ungroup(grouped, flat, slots)).astype(bf16)


def spatial_qkv_kernel(
    chunk, sources, frames, weights, rows, choose, class_rows, is_class, small,
    temporal, packed, w, x, bias, flat, grouped, sem,
):
    chunk.fetch(0, weights, w, sem.at[0])
    flat[...] = rows[...].astype(f32)
    swap_groups(flat, grouped, sources, frames)
    values = jnp.where(is_class[...] > 0, dot(choose[...], class_rows[...]), grouped[...])
    temporal[...] = values.astype(bf16)
    x[...] = norm_rows(values, small, 1).astype(bf16)
    arrived(w, sem.at[0])
    qkv_tiles(x, w, bias, small, 4, packed)


def spatial_mix_kernel(
    chunk, k_at, weights, packed, pairs, key_ids, query_ids, temporal, small,
    mixed, lse, spatial, w, mask, sem,
):
    chunk.fetch(1, weights, w, sem.at[0])
    set_mask(mask, key_ids, query_ids)
    attend(packed, 0, pairs, k_at, k_at + D, mask, mixed, lse)
    arrived(w, sem.at[0])

    def residual(cols):
        added = dot(mixed[...], w[:, cols]) + small[BIAS + 6 : BIAS + 7, cols]
        spatial[:, cols] = temporal[:, cols].astype(f32) + added

    tiles(D, residual)


def hidden_kernel(
    chunk, chunk_back, weights, index, spatial, in_bias, small, grad_out,
    normed, activated, slope, grads, w, grad, sem,
):
    chunk.fetch(0, weights, w, sem.at[0])
    normed[...] = norm_rows(spatial[...], small, 2).astype(bf16)
    arrived(w, sem.at[0])

    def tile(cols):
        hidden = dot(normed[...], w[:, cols]) + in_bias[:, cols]
        below = 0.5 + 0.5 * lax.erf(hidden * 0.7071067811865476)
        density = jnp.exp(hidden * hidden * -0.5) * 0.3989422804014327
        activated[:, cols] = (hidden * below).astype(bf16)
        slope[:, cols] = (below + hidden * density).astype(bf16)

    tiles(FF, tile)

    def back(cols):
        turned = activated[:, cols].astype(f32).T.astype(bf16)
        grad[cols, :] = dot(turned, grad_out[...]).astype(bf16)

    tiles(FF, back)
    chunk_back.store(0, index, grad, grads, sem.at[1])
    arrived(grad, sem.at[1])


def mlp_back_kernel(
    chunk_in, chunk_out, sources, frames, weights_in, weights_out,
    grad_out, slope, spatial, activated, small, block_out, grad_hidden, in_bias, grad_spatial, sums,
    w_in, w_out, total, flat, sem,
):
    chunk_out.fetch(0, weights_out, w_out, sem.at[0])
    chunk_in.fetch(0, weights_in, w_in, sem.at[1])
    arrived(w_out, sem.at[0])

    def forward(cols):
        added = dot(activated[...], w_out[:, cols]) + small[BIAS + 7 : BIAS + 8, cols]
        total[:, cols] = spatial[:, cols] + added

    tiles(D, forward, D // 2)
    swap_groups(total, flat, frames, sources)
    block_out[...] = flat[...].astype(bf16)

    def tile(cols):
        grad = (dot_t(grad_out[...], w_out[cols, :]) * slope[:, cols].astype(f32)).astype(bf16)
        grad_hidden[:, cols] = grad
        in_bias[:, cols] = column_sum(grad)

    tiles(FF, tile)
    arrived(w_in, sem.at[1])

    def back(cols):
        total[:, cols] = dot_t(grad_hidden[...], w_in[cols, :])

    tiles(D, back, D // 2)
    back, gain, shift = norm_back(spatial[...], total[...], small, 2)
    upstream = grad_out[...].astype(f32)
    result = upstream + back
    grad_spatial[...] = result
    sums[0:1] = gain
    sums[1:2] = shift
    sums[2:3] = column_sum(upstream)
    sums[3:4] = column_sum(result.astype(bf16))
    sums[4:8] = jnp.zeros((4, D), f32)


def in_grad_kernel(chunk, table, normed, grad_hidden, grads, normed_t, grad, sem):
    across(normed, normed_t)

    def tile(cols):
        grad[:, cols] = dot(normed_t[...], grad_hidden[:, cols]).astype(bf16)

    tiles(FF, tile)
    chunk.store(0, table, grad, grads, sem.at[0])
    arrived(grad, sem.at[0])


def spatial_attention_back_kernel(
    chunk, k_at, weights, grad_spatial, mixed, packed, pairs, key_ids, query_ids, lse,
    grad, grad_query, grad_pairs,
    w, upstream, mixed_t, grad_mixed, mask, sem,
):
    chunk.fetch(1, weights, w, sem.at[0])
    upstream[...] = grad_spatial[...].astype(bf16)
    set_mask(mask, key_ids, query_ids)
    arrived(w, sem.at[0])

    def back(cols):
        grad_mixed[:, cols] = dot_t(upstream[...], w[cols, :]).astype(bf16)

    tiles(D, back)
    across(mixed, mixed_t)

    def tile(cols):
        grad[:, cols] = dot(mixed_t[...], upstream[:, cols]).astype(bf16)

    tiles(D, tile)
    attend_back(
        packed, 0, pairs, k_at, k_at + D, mask, lse, grad_mixed, grad_query, grad_pairs, 0, D
    )


def qkv_back(normed_t, grad_packed, w, grad, total):
    def back(cols):
        total[:, cols] = dot_t(grad_packed[...], w[cols, :])

    tiles(D, back, D // 2)

    def tile(cols):
        grad[:, cols] = dot(normed_t[...], grad_packed[:, cols]).astype(bf16)

    tiles(3 * D, tile)


def spatial_qkv_back_kernel(
    chunk, sources, frames, weights, acc_spatial, grad_query, grad_pairs, temporal, grad_spatial, choose, is_class,
    small, grads, grad_temporal, class_part, sums,
    w, packed, normed, normed_t, grad, total, flat, sem,
):
    chunk.fetch(0, weights, w, sem.at[0])
    packed[:, :D] = grad_query[...]
    packed[:, D:] = grad_pairs[...]
    values = temporal[...].astype(f32)
    normed[...] = norm_rows(values, small, 1).astype(bf16)
    across(normed, normed_t)
    arrived(w, sem.at[0])
    chunk.store(1, weights[0], acc_spatial, grads, sem.at[2])
    qkv_back(normed_t, packed, w, grad, total)
    chunk.store(0, weights[0], grad, grads, sem.at[1])
    back, gain, shift = norm_back(values, total[...], small, 1)
    total[...] = jnp.where(is_class[...] > 0, 0.0, grad_spatial[...] + back)
    swap_groups(total, flat, frames, sources)
    grad_temporal[...] = flat[...].astype(bf16)
    class_part[...] = jnp.zeros_like(class_part)
    for c in range(CLIPS):
        class_part[c : c + 1] = column_sum(back * choose[:, c : c + 1].astype(f32))
    sums[0:1] = gain
    sums[1:2] = shift
    sums[2:3] = column_sum(packed[:, :D])
    sums[3:4] = column_sum(packed[:, 2 * D :])
    sums[4:8] = jnp.zeros((4, D), f32)
    arrived(grad, sem.at[1])
    arrived(acc_spatial, sem.at[2])


def temporal_proj_back_kernel(
    chunk, chunk_back, slots, weights, grad_rows, projected, mixed,
    grads, grad_mixed, sums,
    w_proj, w_fc, grad_proj, proj_t, mixed_t, acc_proj, acc_fc, grad_temporal, flat, grouped, sem,
):
    chunk.fetch(2, weights, w_fc, sem.at[0])
    chunk.fetch(1, weights, w_proj, sem.at[1])
    regroup(grad_rows[...].astype(f32), flat, grouped, slots)
    grad_temporal[...] = grouped[...].astype(bf16)
    across(projected, proj_t)

    def fc_tile(cols):
        acc_fc[:, cols] = dot(proj_t[...], grad_temporal[:, cols]).astype(bf16)

    tiles(D, fc_tile)
    chunk_back.store(1, weights[0], acc_fc, grads, sem.at[2])
    arrived(w_fc, sem.at[0])

    def fc_back(cols):
        grad_proj[:, cols] = dot_t(grad_temporal[...], w_fc[cols, :]).astype(bf16)

    tiles(D, fc_back)
    across(mixed, mixed_t)

    def proj_tile(cols):
        acc_proj[:, cols] = dot(mixed_t[...], grad_proj[:, cols]).astype(bf16)

    tiles(D, proj_tile)
    chunk_back.store(0, weights[0], acc_proj, grads, sem.at[3])
    arrived(w_proj, sem.at[1])

    def proj_back(cols):
        grad_mixed[:, cols] = dot_t(grad_proj[...], w_proj[cols, :]).astype(bf16)

    tiles(D, proj_back)
    sums[0:1] = column_sum(grad_temporal[...])
    sums[1:2] = column_sum(grad_proj[...])
    sums[2:8] = jnp.zeros((6, D), f32)
    arrived(acc_fc, sem.at[2])
    arrived(acc_proj, sem.at[3])


def temporal_attention_back_kernel(
    chunk, chunk_back, slots, weights, packed, key_ids, query_ids, lse, grad_mixed, rows, grad_temporal,
    small, in_bias, sums_m, sums_s, sums_t, result, class_sum,
    grads, outgoing,
    w, mask, grad_packed, normed, normed_t, grad, total, flat, rows_small, raw, sem,
):
    chunk.fetch(0, weights, w, sem.at[0])
    set_mask(mask, key_ids, query_ids)
    attend_back(
        packed, 0, packed, D, 2 * D, mask, lse, grad_mixed, grad_packed, grad_packed, D, 2 * D
    )
    values = rows[...].astype(f32)
    regroup(norm_rows(values, small, 0), flat, total, slots)
    normed[...] = total[...].astype(bf16)
    across(normed, normed_t)
    arrived(w, sem.at[0])
    qkv_back(normed_t, grad_packed, w, grad, total)
    chunk_back.store(0, weights[0], grad, grads, sem.at[1])
    back, gain, shift = norm_back(values, ungroup(total, flat, slots), small, 0)
    tokens_grad = (grad_temporal[...].astype(f32) + back).astype(bf16)
    frames = outgoing.shape[0]
    rows_each = tokens_grad.shape[0] // frames
    spread = jnp.concatenate([class_sum[...], jnp.zeros_like(class_sum)], axis=0).astype(bf16)
    for f in range(frames):
        here = slice(f * rows_each, (f + 1) * rows_each)
        outgoing[f, :rows_each] = tokens_grad[here]
        outgoing[f, rows_each : 2 * rows_each] = result[here, :]
        outgoing[f, 2 * rows_each :] = spread
    rows_small[...] = jnp.zeros_like(rows_small)
    rows_small[0:4] = in_bias[...]
    for i, (gain_row, shift_row) in enumerate(
        ((gain, shift), (sums_s[0:1], sums_s[1:2]), (sums_m[0:1], sums_m[1:2]))
    ):
        rows_small[GAIN + i : GAIN + i + 1] = gain_row
        rows_small[SHIFT + i : SHIFT + i + 1] = shift_row
    for i, row in enumerate(
        (
            column_sum(grad_packed[:, :D]),
            column_sum(grad_packed[:, 2 * D :]),
            sums_t[1:2],
            sums_t[0:1],
            sums_s[2:3],
            sums_s[3:4],
            sums_m[3:4],
            sums_m[2:3],
        )
    ):
        rows_small[BIAS + i : BIAS + i + 1] = row
    raw[:, :128] = rows_small[...].T.astype(bf16)
    raw[:, 128:] = jnp.zeros((D, 128), bf16)
    chunk_back.store(1, weights[0], raw, grads, sem.at[2])
    arrived(grad, sem.at[1])
    arrived(raw, sem.at[2])


def on_device(
    tokens,
    class_tokens,
    clip_frames,
    cotangent,
    temporal_qkv,
    temporal_proj,
    temporal_fc,
    spatial_qkv,
    spatial_proj,
    mlp_in,
    mlp_out,
    mlp_in_bias,
    norm_gains,
    norm_shifts,
    biases,
):
    frame_size, pos_size = lax.axis_size("frame"), lax.axis_size("pos")
    frame_index, pos_index = lax.axis_index("frame"), lax.axis_index("pos")
    frame_count, pos_count = tokens.shape[1], tokens.shape[2]
    shard = norm_gains.shape[0]
    slots = pos_count + 1
    share = frame_size // MB
    my_slots = slots // share
    all_frames = frame_count * frame_size
    my_frames = all_frames // pos_size
    rows_count = all_frames * my_slots
    micro = frame_index // share

    layout = Layout()
    small = (mlp_in_bias.reshape(4, shard), norm_gains.T, norm_shifts.T, biases.T)
    keep_t, give_t = pack(layout, (temporal_qkv, temporal_proj, temporal_fc), small)
    got_t = send(give_t, layout.swap)
    keep, give = pack(layout, tie((spatial_qkv, spatial_proj, mlp_in), got_t))
    keep_out, give_out = pack(layout, tie((mlp_out,), got_t))
    got = send(tie(give, give_t), layout.swap)
    got_out = send(tie(give_out, give_t), layout.swap)
    way_t = Gather(layout, layout.chip_rows(keep_t, got_t), {})
    rest = layout.chip_rows(keep, got)
    way_s = Gather(layout, rest[:, : 2 * D], {})
    way_in = Gather(layout, rest[:, 2 * D :], {})
    way_out = Gather(layout, layout.chip_rows(keep_out, got_out), {})
    chunk_t = Chunk(layout, (3 * D, D, D, SMALL), 2 * shard)
    chunk_s = Chunk(layout, (3 * D, D), 2 * shard)
    chunk_in = Chunk(layout, (FF,), 2 * shard)
    chunk_out = Chunk(layout, (D,), 8 * shard)
    chunk_proj = Chunk(layout, (D, D), 2 * shard)
    chunk_qkv = Chunk(layout, (3 * D, SMALL), 2 * shard)
    later = range(1, layout.bits)

    def frame_hop(values):
        return lax.all_to_all(values, "frame", 0, 0, tiled=True)

    def pos_hop(values):
        parts = values.reshape(pos_size, rows_count // pos_size, D)
        return lax.all_to_all(parts, "pos", 0, 0, tiled=True).reshape(rows_count, D)

    def to_temporal(*arrays):
        parts = []
        for values in arrays:
            padded = jnp.pad(values, ((0, 0), (0, 0), (0, 1), (0, 0)))
            padded = padded.reshape(MB, frame_count, share, my_slots, D).transpose(0, 2, 1, 3, 4)
            parts.append(padded.reshape(frame_size, frame_count * my_slots, D))
        hopped = frame_hop(jnp.concatenate(parts, axis=1)).reshape(frame_size, len(arrays), -1, D)
        return [hopped[:, i].reshape(rows_count, D) for i in range(len(arrays))]

    def from_temporal(hopped, count):
        rows, out = frame_count * my_slots, []
        for at in range(0, rows * count, rows):
            part = hopped[:, at : at + rows].reshape(MB, share, frame_count, my_slots, D)
            part = part.transpose(0, 2, 1, 3, 4).reshape(MB, frame_count, slots, D)
            out.append(part[:, :, :pos_count])
        return out + [hopped[:, rows * count :]]

    def partners(values, step):
        perm = [(f, f // share * share + (f % share + step) % share) for f in range(frame_size)]
        return lax.ppermute(values, "frame", perm)

    n = rows_count
    clip_ends = jnp.cumsum(lax.dynamic_index_in_dim(clip_frames, micro, 0, keepdims=False))
    clip_of = lambda frame: jnp.sum(
        (frame[:, None] >= clip_ends[None, :]).astype(jnp.int32), axis=1
    )
    size_t = all_frames * max(1, 128 // all_frames)
    ids = jnp.arange(size_t, dtype=jnp.int32)
    ids = ids // all_frames * CLIPS + clip_of(ids % all_frames)
    ids_t = [(ids[:, None], "v"), (jnp.tile(ids, 2)[None, :], "v")]
    frame_rows = n // my_frames
    size_s = frame_rows * max(1, 128 // frame_rows)
    row_ids = jnp.arange(n, dtype=jnp.int32)
    frame_s, row_slot = row_ids // frame_rows, row_ids % my_slots
    first_source = row_ids % frame_rows < my_slots

    def key_masks(share_index):
        padding = row_slot + share_index * my_slots == slots - 1
        is_class = padding & first_source
        return is_class, is_class | ~padding

    keys_s = []
    for step in range(share):
        _, valid = key_masks((frame_index + share - step) % share)
        keys_s.append(jnp.where(valid, frame_s, -1)[:size_s])
    ids_s = [
        (jnp.concatenate(keys_s)[:, None], "v"),
        (jnp.tile(frame_s[:size_s], 2)[None, :], "v"),
    ]
    is_class, _ = key_masks(frame_index % share)
    clip_s = clip_of(pos_index * my_frames + frame_s)
    choose = (clip_s[:, None] == jnp.arange(8)[None, :]) & is_class[:, None]
    choose = (choose.astype(bf16), "v")
    class_rows = lax.dynamic_index_in_dim(class_tokens, micro, 0, keepdims=False)
    class_rows = (jnp.pad(class_rows, ((0, 8 - CLIPS), (0, 0))), "v")
    is_class = (is_class.astype(jnp.int32)[:, None], "v")

    narrow, wide, full = (n, D), (n, 3 * D), (n, FF)
    heads = lambda size: (-(-HEADS // 2 * (n // size) // 8) * 8, 2 * size)
    columns = (D // 128, n, 128)
    lse_shape_t, lse_shape_s = heads(size_t), heads(size_s)
    mask_t, mask_s = (size_t, 2 * size_t), (share * size_s, 2 * size_s)
    flops = lambda columns: 2 * n * D * columns

    some, others, every = layout.some, layout.others, layout.steps
    way_t.along(every)
    rows, grad_out = to_temporal(*tie((tokens, cotangent), give))
    rows, grad_out = meet(way_t, way_s, way_in, way_out, rows, grad_out)
    way_t.across(0)
    way_s.along(every)
    meet(way_t, way_s)
    for step in later:
        way_t.across(step)
    way_t.swap(1)
    grad_out = pos_hop(grad_out)
    way_in.state, grad_out = meet(way_t, way_in.state, grad_out)
    way_t.swap()
    way_s.across(0)
    way_in.along(every)
    packed_t, small_t = call(
        "temporal_qkv",
        partial(temporal_qkv_kernel, chunk_t, my_slots),
        chunk_t.load(way_t).operands() + [(rows, "v")],
        [(wide, bf16, "v"), ((32, D), f32, "v")],
        [((D, 3 * D), bf16), ((D, SMALL), bf16), (narrow, bf16), ((1, 3 * D), f32)]
        + [(columns, f32), (narrow, f32)],
        2,
        flops(3 * D),
    )
    packed_t, small_t = meet(way_s, way_in, packed_t, small_t)
    small = (small_t, "v")
    for step in later:
        way_s.across(step)
    way_s.swap(1)
    way_out.along(every)
    mixed_t, projected, lse_t, temporal = call(
        "temporal_mix",
        partial(temporal_mix_kernel, chunk_t, my_slots),
        chunk_t.operands() + [(packed_t, "v"), (rows, "v")] + ids_t + [small],
        [(narrow, bf16, "v"), (narrow, bf16, "v"), (lse_shape_t, f32, "v"), (narrow, bf16, "v")],
        [((D, D), bf16), ((D, D), bf16), (mask_t, f32), (narrow, f32), (columns, f32)],
        2,
        flops(2 * D + 4 * n),
    )
    temporal, grad_out, small_t = meet(way_s, way_in, way_out, temporal, grad_out, small_t)
    temporal = pos_hop(temporal)
    way_s.swap()
    way_in.across(0)
    way_out.across(0)
    in_bias = small_t[:4].reshape(4, -1, shard).transpose(1, 0, 2).reshape(1, FF)
    grad_out = grad_out.reshape(pos_size, my_frames, my_slots, D)
    grad_out = grad_out.transpose(1, 0, 2, 3).reshape(n, D)
    temporal, in_bias, grad_out = meet(way_s, way_in, way_out, temporal, in_bias, grad_out)
    small = (small_t, "v")
    for step in later:
        way_in.across(step)
    way_in.swap(1)
    temporal, packed_s = call(
        "spatial_qkv",
        partial(spatial_qkv_kernel, chunk_s, pos_size, my_frames),
        chunk_s.load(way_s).operands() + [(temporal, "v"), choose, class_rows, is_class, small],
        [(narrow, bf16, "v"), (wide, bf16, "v")],
        [((D, 3 * D), bf16), (narrow, bf16), ((1, 3 * D), f32)] + [(narrow, f32)] * 2,
        1,
        flops(3 * D),
    )
    temporal = (temporal, "v")
    pairs, k_at = packed_s, D
    if share > 1:
        pairs = [packed_s[:, D:]]
        for step in range(1, share):
            pairs.append(partners(packed_s[:, D:], step))
        pairs, k_at = jnp.concatenate(pairs, axis=0), 0
    all_keys = share * n
    mixed_s, lse_s, spatial = call(
        "spatial_mix",
        partial(spatial_mix_kernel, chunk_s, k_at),
        chunk_s.operands() + [(packed_s, "v"), (pairs, "v")] + ids_s + [temporal, small],
        [(narrow, bf16, "v"), (lse_shape_s, f32, "v"), (narrow, f32, "v")],
        [((D, D), bf16), (mask_s, f32)],
        1,
        flops(D + 4 * all_keys),
    )
    spatial = meet(way_in, way_out, spatial)
    way_in.swap()
    spatial = meet(way_in, way_out, spatial)
    spatial, grad_out = (spatial, "v"), (grad_out, "v")
    for step in later:
        way_out.across(step)
    way_out.swap(1)
    in_bias = (in_bias, "v")
    normed_m, activated, slope, acc_out = call(
        "hidden",
        partial(hidden_kernel, chunk_in, chunk_out),
        chunk_in.load(way_in).operands()
        + [(chunk_out.index, "s"), spatial, in_bias, small, grad_out],
        [(narrow, bf16, "v"), (full, bf16, "v"), (full, bf16, "v")] + chunk_out.grads(),
        [((D, FF), bf16), ((FF, D), bf16)],
        2,
        flops(2 * FF),
    )
    activated = (activated, "v")
    acc_out, slope = meet(way_out, acc_out, slope)
    way_out.swap()
    back_out = chunk_out.scatter(*acc_out)
    slope = meet(way_out, back_out, slope)
    for step in reversed(later):
        back_out.across(step)
    result, grad_hidden, grad_in_bias, grad_spatial, sums_m = call(
        "mlp_back",
        partial(mlp_back_kernel, chunk_in, chunk_out, pos_size, my_frames),
        chunk_in.operands()
        + chunk_out.load(way_out).operands()
        + [grad_out, (slope, "v"), spatial, activated, small],
        [(narrow, bf16, "v"), (full, bf16, "v"), ((1, FF), f32, "v"), (narrow, f32, "v"), ((8, D), f32, "v")],
        [((D, FF), bf16), ((FF, D), bf16), (narrow, f32), (narrow, f32)],
        2,
        flops(3 * FF),
    )
    grad_hidden, grad_in_bias, result = meet(back_out, grad_hidden, grad_in_bias, result)
    back_out.across(0)
    (acc_in,) = call(
        "mlp_in_grad",
        partial(in_grad_kernel, chunk_in),
        [(chunk_in.index, "s"), (normed_m, "v"), (grad_hidden, "v")],
        chunk_in.grads(),
        [((D, n), bf16), ((D, FF), bf16)],
        1,
        flops(FF),
    )
    acc_in, grad_spatial = meet(back_out, acc_in, grad_spatial)
    back_in = chunk_in.scatter(*acc_in)
    grad_spatial, result = meet(back_in, grad_spatial, result)
    for step in reversed(later):
        back_in.across(step)
    back_out.sums()
    back_out.along(every)
    result = pos_hop(result)
    grad_spatial = (grad_spatial, "v")
    acc_sproj, grad_query, grad_pairs = call(
        "spatial_attention_back",
        partial(spatial_attention_back_kernel, chunk_s, k_at),
        chunk_s.operands()
        + [grad_spatial, (mixed_s, "v"), (packed_s, "v"), (pairs, "v")]
        + ids_s
        + [(lse_s, "v")],
        [((D, D), bf16, "v"), (narrow, bf16, "v"), ((all_keys, 2 * D), bf16, "v")],
        [((D, D), bf16), (narrow, bf16), ((D, n), bf16), (narrow, bf16)]
        + [(mask_s, f32)],
        2,
        flops(2 * D + 10 * all_keys),
    )
    own_pairs = grad_pairs[:n]
    for step in range(1, share):
        theirs = partners(grad_pairs[step * n : (step + 1) * n], share - step)
        own_pairs = (own_pairs.astype(f32) + theirs.astype(f32)).astype(bf16)
    acc_s, grad_temporal, class_part, sums_s = call(
        "spatial_qkv_back",
        partial(spatial_qkv_back_kernel, chunk_s, pos_size, my_frames),
        chunk_s.operands()
        + [(acc_sproj, "v"), (grad_query, "v"), (own_pairs, "v"), temporal, grad_spatial]
        + [choose, is_class, small],
        chunk_s.grads() + [(narrow, bf16, "v"), ((8, D), f32, "v"), ((8, D), f32, "v")],
        [((D, 3 * D), bf16), (wide, bf16), (narrow, bf16), ((D, n), bf16)]
        + [((D, 3 * D), bf16), (narrow, f32), (narrow, f32)],
        3,
        flops(6 * D),
    )
    acc_s, grad_temporal, class_part, grad_in_bias, result = meet(
        back_in, back_out, acc_s, grad_temporal, class_part, grad_in_bias, result
    )
    back_s = chunk_s.scatter(*acc_s)
    grad_temporal = pos_hop(grad_temporal)
    back_in.across(0)
    class_sum = class_part + send(class_part, layout.within[0])
    block_in_bias = grad_in_bias.reshape(-1, 4, shard).transpose(1, 0, 2).reshape(4, D)
    grad_temporal, block_in_bias, class_sum = meet(
        back_s, back_in, grad_temporal, block_in_bias, class_sum
    )
    for step in reversed(later):
        back_s.across(step)
    back_in.sums()
    back_in.along(some)
    class_sum = class_sum + send(class_sum, layout.within[1])
    grad_temporal = (grad_temporal, "v")
    acc_proj, grad_mixed_t, sums_t = call(
        "temporal_proj_back",
        partial(temporal_proj_back_kernel, chunk_t, chunk_proj, my_slots),
        chunk_t.operands()
        + [grad_temporal, (projected, "v"), (mixed_t, "v")],
        chunk_proj.grads() + [(narrow, bf16, "v"), ((8, D), f32, "v")],
        [((D, D), bf16), ((D, D), bf16), (narrow, bf16), ((D, n), bf16), ((D, n), bf16)]
        + [((D, D), bf16), ((D, D), bf16), (narrow, bf16), (columns, f32), (narrow, f32)],
        4,
        flops(4 * D),
    )
    acc_proj, grad_mixed_t, class_sum = meet(back_s, back_in, acc_proj, grad_mixed_t, class_sum)
    back_proj = chunk_proj.scatter(*acc_proj)
    for perm in layout.within[2:]:
        class_sum = class_sum + send(class_sum, perm)
    grad_mixed_t, class_sum = meet(back_proj, grad_mixed_t, class_sum)
    for step in reversed(later):
        back_proj.across(step)
    back_s.across(0)
    back_in.along(others)
    acc_qkv, outgoing = call(
        "temporal_attention_back",
        partial(temporal_attention_back_kernel, chunk_t, chunk_qkv, my_slots),
        chunk_t.operands()
        + [(packed_t, "v")]
        + ids_t
        + [(lse_t, "v"), (grad_mixed_t, "v"), (rows, "v"), grad_temporal, small]
        + [(block_in_bias, "v"), (sums_m, "v"), (sums_s, "v"), (sums_t, "v")]
        + [(result, "v"), (class_sum, "v")],
        chunk_qkv.grads() + [((frame_size, 2 * n // frame_size + 16, D), bf16, "v")],
        [((D, 3 * D), bf16), (mask_t, f32), (wide, bf16), (narrow, bf16), ((D, n), bf16)]
        + [((D, 3 * D), bf16), (narrow, f32), (columns, f32), ((128, D), f32), ((D, SMALL), bf16)],
        3,
        flops(6 * D + 10 * n),
    )
    acc_qkv, outgoing = meet(back_s, back_in, back_proj, acc_qkv, outgoing)
    back_qkv = chunk_qkv.scatter(*acc_qkv)
    meet(back_qkv)
    for step in reversed(later):
        back_qkv.across(step)
    back_proj.across(0)
    back_s.sums()
    back_s.along(every)
    hopped = frame_hop(outgoing)
    meet(back_qkv, back_s, back_proj)
    back_qkv.across(0)
    back_proj.sums()
    back_proj.along(every)
    hopped = meet(back_qkv, back_proj, hopped)
    back_qkv.sums("x")
    back_qkv.along(every)
    own = back_qkv.state[0]
    for way in (back_in, back_s, back_proj, back_out):
        way.state = tie(way.state, own)
    most = Return(layout, [back_in, back_s, back_proj, back_out], "w")
    tokens_grad, block_out, class_all = from_temporal(tie(hopped, back_qkv.state[1][1]), 2)
    tokens_grad = tokens_grad.astype(f32)
    class_grad = class_all[::share, :CLIPS].astype(f32)
    tokens_grad, block_out, class_grad = meet(back_qkv, tokens_grad, block_out, class_grad)
    last = Return(layout, [back_qkv], "x")
    (
        acc_in, acc_sqkv, acc_sproj, acc_tproj, acc_tfc, acc_out,
        acc_tqkv, in_bias_grad, gains_grad, shifts_grad, biases_grad,
    ) = finish(
        layout,
        [most, last],
        [
            [(shard, FF), (shard, 3 * D), (shard, D), (shard, D), (shard, D), (4 * shard, D)],
            [(shard, 3 * D), (shard, SMALL)],
        ],
    )
    return (
        block_out,
        tokens_grad,
        class_grad,
        acc_tqkv,
        acc_tproj,
        acc_tfc,
        acc_sqkv,
        acc_sproj,
        acc_in,
        acc_out,
        in_bias_grad.reshape(-1),
        gains_grad.T,
        shifts_grad.T,
        biases_grad.T,
    )


def solution(mesh):
    rows = P(AXES, None)
    wide = P(None, "frame", "pos", None)
    placed = (wide, P(), P(), wide) + (rows,) * 7 + (P(AXES),) + (rows,) * 3
    return jax.shard_map(
        on_device,
        mesh=mesh,
        in_specs=placed,
        out_specs=(wide, wide, P()) + (rows,) * 7 + (P(AXES),) + (rows,) * 3,
        check_vma=False,
    )
```

```python
from functools import partial

import jax
import jax.numpy as jnp
from jax import lax
from jax.experimental import pallas as pl
from jax.experimental.pallas import tpu as pltpu
from jax.sharding import PartitionSpec as P

D = 768
HEADS = 12
HEAD = 64
FF = 4 * D
MB = 4
CLIPS = 3
AXES = ("frame", "pos")
TILE = 768
SMALL = 256
f32, bf16 = jnp.float32, jnp.bfloat16
GAIN, SHIFT, BIAS = 4, 7, 10


def send(values, perm):
    return lax.ppermute(values, AXES, perm)


def tie(value, *before):
    return lax.optimization_barrier((value,) + before)[0] if before else value


class Layout:
    def __init__(self):
        self.frames, self.chips = lax.axis_size("frame"), lax.axis_size("pos") // 2
        self.bits = self.frames.bit_length() - 1
        self.frame, self.chip = lax.axis_index("frame"), lax.axis_index("pos") // 2
        self.core = lax.axis_index("pos") % 2
        self.core_index = self.core.astype(jnp.int32).reshape(1)
        self.swap = self.perm(lambda f, z, c: (f, z, 1 - c))
        self.steps = range(1, self.chips)
        self.some = range(self.chips * 3 // 4, self.chips)
        self.others = range(1, self.chips * 3 // 4)
        self.along = [self.perm(lambda f, z, c, i=i: (f, z ^ i, c)) for i in range(1, self.chips)]
        self.across = [
            self.perm(lambda f, z, c, k=k: (f ^ (1 << self.bit(k, c)), z, c))
            for k in range(self.bits)
        ]

        share = self.frames // MB
        steps = lambda n: [1 << k for k in range(n.bit_length() - 1)]
        self.within = [self.swap]
        self.within += [self.perm(lambda f, z, c, k=k: (f, z ^ k, c)) for k in steps(self.chips)]
        self.within += [self.perm(lambda f, z, c, k=k: (f ^ k, z, c)) for k in steps(share)]

    def bit(self, step, core):
        return (step + core) % self.bits

    def perm(self, to):
        pairs = []
        for f in range(self.frames):
            for z in range(self.chips):
                for c in range(2):
                    g, y, d = to(f, z, c)
                    pairs.append(
                        ((f * self.chips + z) * 2 + c, (g * self.chips + y) * 2 + d)
                    )
        return pairs

    def table(self):
        rows = []
        for core in (self.core, 1 - self.core):
            blocks = []
            for b in range(self.frames * self.chips):
                flags, i = b // self.chips, b % self.chips
                f = self.frame
                for k in range(self.bits):
                    if flags >> k & 1:
                        f = f ^ (1 << ((k + core) % self.bits))
                blocks.append(f * self.chips + (self.chip ^ i))
            rows.append(jnp.stack(blocks))
        return jnp.concatenate([jnp.stack(rows).reshape(-1), self.core[None]]).astype(jnp.int32)

    def pick(self, low, high):
        return jnp.where(self.core == 0, low, high), jnp.where(self.core == 0, high, low)

    def chip_rows(self, keep, got):
        return jnp.concatenate(self.pick(keep, got), axis=0)


class Way:
    def __init__(self, layout, *state):
        self.layout, self.state = layout, state


def meet(*things):
    values = tuple(t.state if isinstance(t, Way) else t for t in things)
    values = lax.optimization_barrier(values)
    out = []
    for thing, value in zip(things, values):
        if isinstance(thing, Way):
            thing.state = value
        else:
            out.append(value)
    return out[0] if len(out) == 1 else out


class Gather(Way):
    def along(self, steps):
        block, got = self.state
        new = {i: send(block, self.layout.along[i - 1]) for i in steps}
        self.state = (block, {**got, **new})

    def across(self, step):
        mine, other = self.state
        if step == 0:
            mine = tuple(a[None] for a in [mine] + [other[i] for i in self.layout.steps])
        block = merge(mine)
        self.state = ((block, send(block, self.layout.across[step])), ())

    def swap(self, count=None):
        mine, other = self.state
        other += tuple(send(a, self.layout.swap) for a in mine[len(other) : count])
        self.state = (mine, other)


class Scatter(Way):
    def __init__(self, layout, mine, other):
        near, far = [(a, send(b, layout.swap)) for a, b in zip(mine, other)]
        super().__init__(layout, near, far)
        self.count = near[0].shape[0]

    def across(self, step):
        near, far = self.state
        if far:
            far, _ = fold(far, self.count, False)
        else:
            self.count //= 2
            far, near = fold(near, self.count, True)
            near = (near,)
        self.state = (near + (send(far, self.layout.across[step]),), ())
        return far

    def sums(self, space="w"):
        near, _ = self.state
        _, rows, width = near[0].shape
        own, *away = call(
            "fold_blocks",
            partial(fold_blocks_kernel, len(near)),
            [(a, "x") for a in near],
            [((rows, width), f32, space)] + [((rows, width), bf16, "x")] * (self.count - 1),
            [],
            1,
            0,
        )
        self.state = (own, dict(zip(self.layout.steps, away)))

    def along(self, steps):
        own, away = self.state
        new = {i: send(away[i], self.layout.along[i - 1]) for i in steps}
        self.state = (own, {**away, **new})


class Return:
    def __init__(self, layout, ways, space):
        shapes = [way.state[0].shape for way in ways]
        self.rows = min(r for r, _ in shapes) // 2
        width = sum(r // 2 // self.rows * w for r, w in shapes)
        kept = ((self.rows, width), f32, "x")
        parts = [[(a, space) for a in [way.state[0], *way.state[1].values()]] for way in ways]
        self.keep, give = call(
            "sum_parts",
            sum_parts_kernel,
            [(layout.core_index, "s"), parts],
            [kept, kept],
            [],
            1,
            0,
        )
        self.got = send(give, layout.swap)


def finish(layout, returns, chunks):
    outs = []
    for rows, width in [m for group in chunks for m in group]:
        if width != SMALL:
            outs.append(((rows, width), f32, "v"))
        else:
            outs += [((count, rows), f32, "v") for count in (4, 3, 3, 8)]
    return call(
        "finish",
        partial(finish_kernel, chunks),
        [(layout.core_index, "s")] + [[(r.keep, "x"), (r.got, "x")] for r in returns],
        outs,
        [((128, 128), f32)],
        1,
        0,
    )


def total(values):
    out = values[0].astype(f32)
    for value in values[1:]:
        out = out + value.astype(f32)
    return out


class Chunk:
    def __init__(self, layout, widths, rows):
        self.layout, self.widths, self.rows = layout, widths, rows
        self.count = layout.frames * layout.chips
        self.table = layout.table()
        self.half = sum(widths) // 2
        self.whole = bool(rows % 16)
        if self.whole:
            core = layout.core.astype(jnp.int32)
            self.index = jnp.stack([jnp.zeros_like(core)] * 2 + [core])
            self.blocks, self.block_rows = 1, self.count * rows
        else:
            self.index = self.table
            self.blocks, self.block_rows = self.count, rows

    def load(self, way):
        mine, other = way.state
        if self.whole:
            order = jnp.argsort(self.table[: 2 * self.count].reshape(2, -1), axis=1)
            mine, other = [
                (jnp.concatenate(a)[o].reshape(1, self.block_rows, -1),)
                for a, o in zip((mine, other), order)
            ]
        self.mine, self.other = mine, other
        return self

    def operands(self):
        pieces = [[(a, "h") for a in side] for side in (self.mine, self.other)]
        return [[(self.index, "s")] + pieces]

    def grads(self):
        if self.whole:
            piece = [((1, self.block_rows, self.half), bf16, "x")]
            return [[piece, piece]]
        shape = (self.count // 2, self.block_rows, self.half)
        return [[[(shape, bf16, "h"), (shape, bf16, "x")], [(shape, bf16, "x")] * 2]]

    def at(self, which):
        return sum(self.widths[:which]) // 2

    def fetch(self, which, weights, dst, sem):
        self._copies(which, *weights, dst, sem, True)

    def store(self, which, table, src, grads, sem):
        self._copies(which, table, *grads, src, sem, False)

    def _copies(self, which, table, mine, other, mat, sem, into):
        at, w = self.at(which), self.widths[which] // 2
        core = table[2 * self.blocks]
        for side, pieces in ((0, mine), (1, other)):
            half = core if side == 0 else 1 - core
            first = side * self.blocks
            for piece in pieces:

                def body(b, carry, piece=piece, first=first, half=half):
                    row = pl.multiple_of(table[first + b] * self.block_rows, 16)
                    block = piece.at[b, :, at : at + w]
                    place = mat.at[
                        pl.ds(row, self.block_rows), pl.ds(pl.multiple_of(half * w, 128), w)
                    ]
                    pair = (block, place) if into else (place, block)
                    pltpu.make_async_copy(*pair, sem).start()
                    return carry

                lax.fori_loop(0, piece.shape[0], body, 0)
                first += piece.shape[0]

    def scatter(self, mine, other):
        if self.whole:
            order = self.table[: 2 * self.count].reshape(2, -1)
            mine, other = [
                a[0].reshape(self.count, self.rows, -1)[o] for a, o in zip((mine, other), order)
            ]
            half = self.count // 2
            mine, other = [(a[:half], a[half:]) for a in (mine, other)]
        return Scatter(self.layout, mine, other)


def merge_kernel(count, *refs):
    out, at = refs[count], 0
    for ref in refs[:count]:
        out[at : at + ref.shape[0]] = ref[...]
        at += ref.shape[0]


def merge(blocks):
    if blocks[0].shape[1] % 16:
        return jnp.concatenate(blocks)
    shape = (sum(a.shape[0] for a in blocks),) + blocks[0].shape[1:]
    return call(
        "merge",
        partial(merge_kernel, len(blocks)),
        [(a, "x") for a in blocks],
        [(shape, blocks[0].dtype, "x")],
        [],
        1,
        0,
    )[0]


def fold_kernel(given, halve, *refs):
    far = refs[given]
    start = far.shape[0] if halve else 0

    def block(b, carry):
        far[b] = total([ref[start + b] for ref in refs[:given]]).astype(bf16)
        if halve:
            refs[given + 1][b] = total([ref[b] for ref in refs[:given]])
        return carry

    lax.fori_loop(0, far.shape[0], block, 0)


def fold(values, count, halve):
    shape = (count,) + values[0].shape[1:]
    outs = [(shape, bf16, "x")] + [(shape, f32, "x")] * halve
    out = call(
        "fold",
        partial(fold_kernel, len(values), halve),
        [(a, "w" if halve and i < 2 else "x") for i, a in enumerate(values)],
        outs,
        [],
        1,
        0,
    )
    return out[0], out[-1]


def fold_blocks_kernel(count, *refs):
    refs, outs = refs[:count], refs[count:-1]
    for b, out in enumerate(outs):
        out[...] = total([ref[b] for ref in refs]).astype(out.dtype)


def pack_kernel(widths, small, core, *refs):
    mats, (keep, give) = refs[: len(widths)], refs[-4:-2]
    turned = refs[-2]
    at = 0
    first = core[0] == 0
    for mat, width in zip(mats, widths):
        w = width // 2
        low, high = mat[:, :w], mat[:, w:]
        keep[:, at : at + w] = jnp.where(first, low, high)
        give[:, at : at + w] = jnp.where(first, high, low)
        at += w
    if small:
        rows = keep.shape[0]
        turned[...] = jnp.zeros_like(turned)
        place = 0
        for ref in refs[len(widths) : -4]:
            for at_row in range(0, ref.shape[1], rows):
                count = ref.shape[0]
                turned[place : place + count, :rows] = ref[:, at_row : at_row + rows].astype(f32)
                place += count
        values = turned[...].T[:rows].astype(bf16)
        zeros = jnp.zeros_like(values)
        keep[:, at:] = jnp.where(first, values, zeros)
        give[:, at:] = jnp.where(first, zeros, values)


def pack(layout, mats, small=()):
    rows = mats[0].shape[0]
    width = sum(m.shape[1] for m in mats) // 2 + (SMALL // 2 if small else 0)
    half = ((rows, width), bf16, "x")
    return call(
        "pack",
        partial(pack_kernel, [m.shape[1] for m in mats], len(small)),
        [(layout.core_index, "s")] + [(m, "w") for m in mats] + [(m, "w") for m in small],
        [half, half],
        [((128, 128), f32)],
        1,
        0,
    )


def sum_parts_kernel(core, groups, keep, give, sem):
    first, short, at = core[0] == 0, keep.shape[0], 0
    for parts in groups:
        values = total([p[...] for p in parts])
        rows, width = values.shape[0] // 2, values.shape[1]
        for row in range(0, rows, short):
            low, high = values[row : row + short], values[rows + row : rows + row + short]
            keep[:, at : at + width] = jnp.where(first, low, high)
            give[:, at : at + width] = jnp.where(first, high, low)
            at += width


def finish_kernel(chunks, core, *refs):
    pairs, outs, turned = refs[: len(chunks)], iter(refs[len(chunks) : -2]), refs[-2]
    first = core[0] == 0
    for (keep, got), group in zip(pairs, chunks):
        short, at = keep.shape[0], 0
        for rows, width in group:
            w = width // 2
            if width == SMALL:
                turned[...] = jnp.zeros_like(turned)
                low = jnp.where(first, keep[:, at : at + w], got[:, at : at + w])
                turned[:short, :] = low
                values, place = turned[...].T, 0
                for _ in range(4):
                    out = next(outs)
                    out[...] = values[place : place + out.shape[0], :short]
                    place += out.shape[0]
                at += w
                continue
            out = next(outs)
            for row in range(0, rows, short):
                mine, other = keep[:, at : at + w], got[:, at : at + w]
                out[row : row + short, :w] = jnp.where(first, mine, other)
                out[row : row + short, w:] = jnp.where(first, other, mine)
                at += w


def arrived(mat, sem):
    pltpu.make_async_copy(mat, mat, sem).wait()


SPACE = {"s": pltpu.SMEM, "h": pltpu.HBM, "v": pltpu.VMEM, "w": pltpu.VMEM, "x": pltpu.VMEM}
HELD = {"h": pltpu.HBM, "w": pltpu.HBM, "x": pltpu.VMEM}


def held(value, space):
    return pltpu.with_memory_space_constraint(value, HELD[space]) if space in HELD else value


def result(shape, kind, space):
    return HELD[space](shape, kind) if space in HELD else jax.ShapeDtypeStruct(shape, kind)


def flat(items):
    return [leaf for item in items for leaf in (flat(item) if isinstance(item, list) else [item])]


def nest(items, leaves):
    return [nest(item, leaves) if isinstance(item, list) else next(leaves) for item in items]


def call(name, body, ins, outs, scratch, sems, flops, alias=None):
    operands, results = flat(ins), flat(outs)
    bytes_of = lambda shape, kind: jnp.dtype(kind).itemsize * _size(shape)
    size = sum(bytes_of(a.shape, a.dtype) for a, space in operands if space in "vwx")
    size += sum(bytes_of(shape, kind) for shape, kind, space in results if space in "vwx")
    size += sum(bytes_of(shape, kind) for shape, kind in scratch)
    moved = sum(bytes_of(a.shape, a.dtype) for a, _ in operands)
    moved += sum(bytes_of(shape, kind) for shape, kind, _ in results)
    aliases = {}
    for i, o in (alias or {}).items():
        start, end = len(flat(ins[:i])), len(flat(outs[:o]))
        for k in range(len(flat([ins[i]]))):
            aliases[start + k] = end + k

    def kernel(*refs):
        leaves = iter(refs)
        body(*nest(ins, leaves), *nest(outs, leaves), *leaves)

    values = pl.pallas_call(
        kernel,
        out_shape=[result(*r) for r in results],
        in_specs=[pl.BlockSpec(memory_space=SPACE[space]) for _, space in operands],
        out_specs=[pl.BlockSpec(memory_space=SPACE[space]) for _, _, space in results],
        scratch_shapes=[pltpu.VMEM(shape, kind) for shape, kind in scratch]
        + [pltpu.SemaphoreType.DMA((sems,))],
        input_output_aliases=aliases,
        compiler_params=pltpu.CompilerParams(
            vmem_limit_bytes=min(int(size * 1.1) + (6 << 20), 60 << 20)
        ),
        cost_estimate=pl.CostEstimate(flops=flops, bytes_accessed=moved, transcendentals=0),
        name=name,
    )(*[held(a, space) for a, space in operands])
    return nest(outs, iter(values))


def _size(shape):
    total = 1
    for n in shape:
        total *= n
    return total


def tiles(width, body, size=TILE):
    def step(j, carry):
        body(pl.ds(pl.multiple_of(j * size, size), size))
        return carry

    lax.fori_loop(0, width // size, step, 0)


def dot(a, b):
    return jnp.dot(a, b, preferred_element_type=f32)


def dot_t(a, b):
    return lax.dot_general(a, b, (((1,), (1,)), ((), ())), preferred_element_type=f32)


def normalise(values):
    centred = values - jnp.mean(values, axis=-1, keepdims=True)
    inv_std = lax.rsqrt(jnp.mean(centred * centred, axis=-1, keepdims=True) + 1e-06)
    return centred * inv_std, inv_std


def norm_rows(values, small, which):
    normal, _ = normalise(values)
    return normal * small[GAIN + which : GAIN + which + 1] + small[SHIFT + which : SHIFT + which + 1]


def norm_back(values, upstream, small, which):
    normal, inv_std = normalise(values)
    product = upstream * normal
    grad_gain = jnp.sum(product, axis=0, keepdims=True)
    grad_shift = jnp.sum(upstream, axis=0, keepdims=True)
    gain = small[GAIN + which : GAIN + which + 1]
    scaled = upstream * gain
    mean = jnp.mean(scaled, axis=-1, keepdims=True)
    mean_normal = jnp.mean(product * gain, axis=-1, keepdims=True)
    return inv_std * (scaled - mean - normal * mean_normal), grad_gain, grad_shift


def column_sum(values):
    return jnp.sum(values.astype(f32), axis=0, keepdims=True)


def set_mask(mask, key_ids, query_ids):
    mask[...] = jnp.where(key_ids[...] == query_ids[...], 0.0, -1000000000.0)


def regroup(values, flat, out, groups):
    count = out.shape[0] // groups
    for c in range(flat.shape[0]):
        cols = slice(c * 128, (c + 1) * 128)
        flat[c] = values[:, cols]
        for g in range(groups):
            out[g * count : (g + 1) * count, cols] = flat[c, pl.ds(g, count, stride=groups), :]


def ungroup(grouped, flat, groups):
    count = grouped.shape[0] // groups
    for c in range(flat.shape[0]):
        cols = slice(c * 128, (c + 1) * 128)
        for g in range(groups):
            flat[c, pl.ds(g, count, stride=groups), :] = grouped[g * count : (g + 1) * count, cols]
    return jnp.concatenate([flat[c] for c in range(flat.shape[0])], axis=1)


def swap_groups(source, out, outer, inner):
    size = source.shape[0] // (outer * inner)
    for i in range(outer):
        for j in range(inner):
            to, at = (j * outer + i) * size, (i * inner + j) * size
            out[to : to + size, :] = source[at : at + size, :]


def both_heads(values, scale):
    lane = lax.broadcasted_iota(jnp.int32, (1, 2 * HEAD), 1)
    wide = values.astype(f32)
    parts = [jnp.where(lane // HEAD == h, wide * scale, 0.0) for h in range(2)]
    return jnp.concatenate(parts, axis=0).astype(bf16)


def own_heads(across):
    size = across.shape[1] // 2
    return jnp.concatenate([across[:HEAD, :size], across[HEAD:, size:]], axis=0).T


def key_rows(pairs, cols, start, size, rows):
    parts = [pairs[at + start : at + start + size, cols] for at in range(0, pairs.shape[0], rows)]
    return parts[0] if len(parts) == 1 else jnp.concatenate(parts, axis=0)


def attend(query, q_at, pairs, k_at, v_at, mask, mixed, lse):
    rows, size = query.shape[0], mask.shape[1] // 2
    blocks = range(rows // size)

    def pair(i, carry):
        cols = lambda at: pl.ds(pl.multiple_of(at + i * 2 * HEAD, 2 * HEAD), 2 * HEAD)
        here = [slice(b * size, (b + 1) * size) for b in blocks]
        queries = [both_heads(query[h, cols(q_at)], 0.125) for h in here]
        keys = [key_rows(pairs, cols(k_at), b * size, size, rows) for b in blocks]
        values = [key_rows(pairs, cols(v_at), b * size, size, rows).T for b in blocks]
        score = [dot_t(keys[b], queries[b]) + mask[...] for b in blocks]
        top = [jnp.max(score[b], axis=0, keepdims=True) for b in blocks]
        weight = [jnp.exp(score[b] - top[b]) for b in blocks]
        norm = [jnp.sum(weight[b], axis=0, keepdims=True) for b in blocks]
        probs = [(weight[b] * (1.0 / norm[b])).astype(bf16) for b in blocks]
        out = [own_heads(dot(values[b], probs[b])).astype(bf16) for b in blocks]
        for b in blocks:
            lse[pl.ds(i * len(blocks) + b, 1), :] = top[b] + jnp.log(norm[b])
            mixed[here[b], cols(0)] = out[b]
        return carry

    lax.fori_loop(0, HEADS // 2, pair, 0, unroll=HEADS // 2)


def attend_back(query, q_at, pairs, k_at, v_at, mask, lse, grad, out_q, out_pairs, gk_at, gv_at):
    rows, size = query.shape[0], mask.shape[1] // 2
    blocks = range(rows // size)

    def pair(i, carry):
        cols = lambda at: pl.ds(pl.multiple_of(at + i * 2 * HEAD, 2 * HEAD), 2 * HEAD)
        here = [slice(b * size, (b + 1) * size) for b in blocks]
        keys = [key_rows(pairs, cols(k_at), b * size, size, rows) for b in blocks]
        values = [key_rows(pairs, cols(v_at), b * size, size, rows) for b in blocks]
        queries = [both_heads(query[h, cols(q_at)], 0.125) for h in here]
        upstream = [both_heads(grad[h, cols(0)], 1.0) for h in here]
        logs = [lse[pl.ds(i * len(blocks) + b, 1), :] for b in blocks]
        across_keys = [keys[b].T for b in blocks]
        score = [dot_t(keys[b], queries[b]) + mask[...] for b in blocks]
        dprob = [dot_t(values[b], upstream[b]) for b in blocks]
        probs = [jnp.exp(score[b] - logs[b]) for b in blocks]
        delta = [jnp.sum(probs[b] * dprob[b], axis=0, keepdims=True) for b in blocks]
        dscore = [(probs[b] * (dprob[b] - delta[b])).astype(bf16) for b in blocks]
        grad_keys = [dot(dscore[b], queries[b]).astype(bf16) for b in blocks]
        grad_values = [dot(probs[b].astype(bf16), upstream[b]).astype(bf16) for b in blocks]
        grad_queries = [
            (own_heads(dot(across_keys[b], dscore[b])) * 0.125).astype(bf16) for b in blocks
        ]
        for b in blocks:
            out_q[here[b], cols(0)] = grad_queries[b]
            for part in range(0, pairs.shape[0], rows):
                there = slice(part + b * size, part + (b + 1) * size)
                seen = slice(part // rows * size, (part // rows + 1) * size)
                out_pairs[there, cols(gk_at)] = grad_keys[b][seen]
                out_pairs[there, cols(gv_at)] = grad_values[b][seen]
        return carry

    lax.fori_loop(0, HEADS // 2, pair, 0, unroll=HEADS // 2)


def qkv_tiles(x, w, bias, small, which, packed):
    bias[:, :D] = small[BIAS + which : BIAS + which + 1]
    bias[:, D : 2 * D] = jnp.zeros((1, D), f32)
    bias[:, 2 * D :] = small[BIAS + which + 1 : BIAS + which + 2]

    def tile(cols):
        packed[:, cols] = (dot(x[...], w[:, cols]) + bias[:, cols]).astype(bf16)

    tiles(3 * D, tile)


def across(mat, out):
    for at in range(0, mat.shape[1], 128):
        out[at : at + 128, :] = mat[:, at : at + 128].astype(f32).T.astype(bf16)


def temporal_qkv_kernel(
    chunk, slots, weights, rows, packed, small, w, raw, x, bias, flat, grouped, sem
):
    chunk.fetch(3, weights, raw, sem.at[0])
    chunk.fetch(0, weights, w, sem.at[1])
    arrived(raw, sem.at[0])
    small[...] = raw[:, :128].astype(f32).T[: small.shape[0]]
    regroup(norm_rows(rows[...].astype(f32), small, 0), flat, grouped, slots)
    x[...] = grouped[...].astype(bf16)
    arrived(w, sem.at[1])
    qkv_tiles(x, w, bias, small, 0, packed)


def temporal_mix_kernel(
    chunk, slots, weights, packed, rows, key_ids, query_ids, small,
    mixed, projected, lse, temporal, w_proj, w_fc, mask, grouped, flat, sem,
):
    chunk.fetch(1, weights, w_proj, sem.at[0])
    chunk.fetch(2, weights, w_fc, sem.at[1])
    set_mask(mask, key_ids, query_ids)
    attend(packed, 0, packed, D, 2 * D, mask, mixed, lse)
    arrived(w_proj, sem.at[0])

    def project(cols):
        bias = small[BIAS + 2 : BIAS + 3, cols]
        projected[:, cols] = (dot(mixed[...], w_proj[:, cols]) + bias).astype(bf16)

    tiles(D, project)
    arrived(w_fc, sem.at[1])

    def residual(cols):
        grouped[:, cols] = dot(projected[...], w_fc[:, cols]) + small[BIAS + 3 : BIAS + 4, cols]

    tiles(D, residual)
    temporal[...] = (rows[...].astype(f32) + ungroup(grouped, flat, slots)).astype(bf16)


def spatial_qkv_kernel(
    chunk, sources, frames, weights, rows, choose, class_rows, is_class, small,
    temporal, packed, w, x, bias, flat, grouped, sem,
):
    chunk.fetch(0, weights, w, sem.at[0])
    flat[...] = rows[...].astype(f32)
    swap_groups(flat, grouped, sources, frames)
    values = jnp.where(is_class[...] > 0, dot(choose[...], class_rows[...]), grouped[...])
    temporal[...] = values.astype(bf16)
    x[...] = norm_rows(values, small, 1).astype(bf16)
    arrived(w, sem.at[0])
    qkv_tiles(x, w, bias, small, 4, packed)


def spatial_mix_kernel(
    chunk, k_at, weights, packed, pairs, key_ids, query_ids, temporal, small,
    mixed, lse, spatial, w, mask, sem,
):
    chunk.fetch(1, weights, w, sem.at[0])
    set_mask(mask, key_ids, query_ids)
    attend(packed, 0, pairs, k_at, k_at + D, mask, mixed, lse)
    arrived(w, sem.at[0])

    def residual(cols):
        added = dot(mixed[...], w[:, cols]) + small[BIAS + 6 : BIAS + 7, cols]
        spatial[:, cols] = temporal[:, cols].astype(f32) + added

    tiles(D, residual)


def hidden_kernel(
    chunk, chunk_back, weights, index, spatial, in_bias, small, grad_out,
    normed, activated, slope, grads, w, grad, sem,
):
    chunk.fetch(0, weights, w, sem.at[0])
    normed[...] = norm_rows(spatial[...], small, 2).astype(bf16)
    arrived(w, sem.at[0])

    def tile(cols):
        hidden = dot(normed[...], w[:, cols]) + in_bias[:, cols]
        below = 0.5 + 0.5 * lax.erf(hidden * 0.7071067811865476)
        density = jnp.exp(hidden * hidden * -0.5) * 0.3989422804014327
        activated[:, cols] = (hidden * below).astype(bf16)
        slope[:, cols] = (below + hidden * density).astype(bf16)

    tiles(FF, tile)

    def back(cols):
        turned = activated[:, cols].astype(f32).T.astype(bf16)
        grad[cols, :] = dot(turned, grad_out[...]).astype(bf16)

    tiles(FF, back)
    chunk_back.store(0, index, grad, grads, sem.at[1])
    arrived(grad, sem.at[1])


def mlp_back_kernel(
    chunk_in, chunk_out, sources, frames, weights_in, weights_out,
    grad_out, slope, spatial, activated, small, block_out, grad_hidden, in_bias, grad_spatial, sums,
    w_in, w_out, total, flat, sem,
):
    chunk_out.fetch(0, weights_out, w_out, sem.at[0])
    chunk_in.fetch(0, weights_in, w_in, sem.at[1])
    arrived(w_out, sem.at[0])

    def forward(cols):
        added = dot(activated[...], w_out[:, cols]) + small[BIAS + 7 : BIAS + 8, cols]
        total[:, cols] = spatial[:, cols] + added

    tiles(D, forward, D // 2)
    swap_groups(total, flat, frames, sources)
    block_out[...] = flat[...].astype(bf16)

    def tile(cols):
        grad = (dot_t(grad_out[...], w_out[cols, :]) * slope[:, cols].astype(f32)).astype(bf16)
        grad_hidden[:, cols] = grad
        in_bias[:, cols] = column_sum(grad)

    tiles(FF, tile)
    arrived(w_in, sem.at[1])

    def back(cols):
        total[:, cols] = dot_t(grad_hidden[...], w_in[cols, :])

    tiles(D, back, D // 2)
    back, gain, shift = norm_back(spatial[...], total[...], small, 2)
    upstream = grad_out[...].astype(f32)
    result = upstream + back
    grad_spatial[...] = result
    sums[0:1] = gain
    sums[1:2] = shift
    sums[2:3] = column_sum(upstream)
    sums[3:4] = column_sum(result.astype(bf16))
    sums[4:8] = jnp.zeros((4, D), f32)


def in_grad_kernel(chunk, table, normed, grad_hidden, grads, normed_t, grad, sem):
    across(normed, normed_t)

    def tile(cols):
        grad[:, cols] = dot(normed_t[...], grad_hidden[:, cols]).astype(bf16)

    tiles(FF, tile)
    chunk.store(0, table, grad, grads, sem.at[0])
    arrived(grad, sem.at[0])


def spatial_attention_back_kernel(
    chunk, k_at, weights, grad_spatial, mixed, packed, pairs, key_ids, query_ids, lse,
    grad, grad_query, grad_pairs,
    w, upstream, mixed_t, grad_mixed, mask, sem,
):
    chunk.fetch(1, weights, w, sem.at[0])
    upstream[...] = grad_spatial[...].astype(bf16)
    set_mask(mask, key_ids, query_ids)
    arrived(w, sem.at[0])

    def back(cols):
        grad_mixed[:, cols] = dot_t(upstream[...], w[cols, :]).astype(bf16)

    tiles(D, back)
    across(mixed, mixed_t)

    def tile(cols):
        grad[:, cols] = dot(mixed_t[...], upstream[:, cols]).astype(bf16)

    tiles(D, tile)
    attend_back(
        packed, 0, pairs, k_at, k_at + D, mask, lse, grad_mixed, grad_query, grad_pairs, 0, D
    )


def qkv_back(normed_t, grad_packed, w, grad, total):
    def back(cols):
        total[:, cols] = dot_t(grad_packed[...], w[cols, :])

    tiles(D, back, D // 2)

    def tile(cols):
        grad[:, cols] = dot(normed_t[...], grad_packed[:, cols]).astype(bf16)

    tiles(3 * D, tile)


def spatial_qkv_back_kernel(
    chunk, sources, frames, weights, acc_spatial, grad_query, grad_pairs, temporal, grad_spatial, choose, is_class,
    small, grads, grad_temporal, class_part, sums,
    w, packed, normed, normed_t, grad, total, flat, sem,
):
    chunk.fetch(0, weights, w, sem.at[0])
    packed[:, :D] = grad_query[...]
    packed[:, D:] = grad_pairs[...]
    values = temporal[...].astype(f32)
    normed[...] = norm_rows(values, small, 1).astype(bf16)
    across(normed, normed_t)
    arrived(w, sem.at[0])
    chunk.store(1, weights[0], acc_spatial, grads, sem.at[2])
    qkv_back(normed_t, packed, w, grad, total)
    chunk.store(0, weights[0], grad, grads, sem.at[1])
    back, gain, shift = norm_back(values, total[...], small, 1)
    total[...] = jnp.where(is_class[...] > 0, 0.0, grad_spatial[...] + back)
    swap_groups(total, flat, frames, sources)
    grad_temporal[...] = flat[...].astype(bf16)
    class_part[...] = jnp.zeros_like(class_part)
    for c in range(CLIPS):
        class_part[c : c + 1] = column_sum(back * choose[:, c : c + 1].astype(f32))
    sums[0:1] = gain
    sums[1:2] = shift
    sums[2:3] = column_sum(packed[:, :D])
    sums[3:4] = column_sum(packed[:, 2 * D :])
    sums[4:8] = jnp.zeros((4, D), f32)
    arrived(grad, sem.at[1])
    arrived(acc_spatial, sem.at[2])


def temporal_proj_back_kernel(
    chunk, chunk_back, slots, weights, grad_rows, projected, mixed,
    grads, grad_mixed, sums,
    w_proj, w_fc, grad_proj, proj_t, mixed_t, acc_proj, acc_fc, grad_temporal, flat, grouped, sem,
):
    chunk.fetch(2, weights, w_fc, sem.at[0])
    chunk.fetch(1, weights, w_proj, sem.at[1])
    regroup(grad_rows[...].astype(f32), flat, grouped, slots)
    grad_temporal[...] = grouped[...].astype(bf16)
    across(projected, proj_t)

    def fc_tile(cols):
        acc_fc[:, cols] = dot(proj_t[...], grad_temporal[:, cols]).astype(bf16)

    tiles(D, fc_tile)
    chunk_back.store(1, weights[0], acc_fc, grads, sem.at[2])
    arrived(w_fc, sem.at[0])

    def fc_back(cols):
        grad_proj[:, cols] = dot_t(grad_temporal[...], w_fc[cols, :]).astype(bf16)

    tiles(D, fc_back)
    across(mixed, mixed_t)

    def proj_tile(cols):
        acc_proj[:, cols] = dot(mixed_t[...], grad_proj[:, cols]).astype(bf16)

    tiles(D, proj_tile)
    chunk_back.store(0, weights[0], acc_proj, grads, sem.at[3])
    arrived(w_proj, sem.at[1])

    def proj_back(cols):
        grad_mixed[:, cols] = dot_t(grad_proj[...], w_proj[cols, :]).astype(bf16)

    tiles(D, proj_back)
    sums[0:1] = column_sum(grad_temporal[...])
    sums[1:2] = column_sum(grad_proj[...])
    sums[2:8] = jnp.zeros((6, D), f32)
    arrived(acc_fc, sem.at[2])
    arrived(acc_proj, sem.at[3])


def temporal_attention_back_kernel(
    chunk, chunk_back, slots, weights, packed, key_ids, query_ids, lse, grad_mixed, rows, grad_temporal,
    small, in_bias, sums_m, sums_s, sums_t, result, class_sum,
    grads, outgoing,
    w, mask, grad_packed, normed, normed_t, grad, total, flat, rows_small, raw, sem,
):
    chunk.fetch(0, weights, w, sem.at[0])
    set_mask(mask, key_ids, query_ids)
    attend_back(
        packed, 0, packed, D, 2 * D, mask, lse, grad_mixed, grad_packed, grad_packed, D, 2 * D
    )
    values = rows[...].astype(f32)
    regroup(norm_rows(values, small, 0), flat, total, slots)
    normed[...] = total[...].astype(bf16)
    across(normed, normed_t)
    arrived(w, sem.at[0])
    qkv_back(normed_t, grad_packed, w, grad, total)
    chunk_back.store(0, weights[0], grad, grads, sem.at[1])
    back, gain, shift = norm_back(values, ungroup(total, flat, slots), small, 0)
    tokens_grad = (grad_temporal[...].astype(f32) + back).astype(bf16)
    frames = outgoing.shape[0]
    rows_each = tokens_grad.shape[0] // frames
    spread = jnp.concatenate([class_sum[...], jnp.zeros_like(class_sum)], axis=0).astype(bf16)
    for f in range(frames):
        here = slice(f * rows_each, (f + 1) * rows_each)
        outgoing[f, :rows_each] = tokens_grad[here]
        outgoing[f, rows_each : 2 * rows_each] = result[here, :]
        outgoing[f, 2 * rows_each :] = spread
    rows_small[...] = jnp.zeros_like(rows_small)
    rows_small[0:4] = in_bias[...]
    for i, (gain_row, shift_row) in enumerate(
        ((gain, shift), (sums_s[0:1], sums_s[1:2]), (sums_m[0:1], sums_m[1:2]))
    ):
        rows_small[GAIN + i : GAIN + i + 1] = gain_row
        rows_small[SHIFT + i : SHIFT + i + 1] = shift_row
    for i, row in enumerate(
        (
            column_sum(grad_packed[:, :D]),
            column_sum(grad_packed[:, 2 * D :]),
            sums_t[1:2],
            sums_t[0:1],
            sums_s[2:3],
            sums_s[3:4],
            sums_m[3:4],
            sums_m[2:3],
        )
    ):
        rows_small[BIAS + i : BIAS + i + 1] = row
    raw[:, :128] = rows_small[...].T.astype(bf16)
    raw[:, 128:] = jnp.zeros((D, 128), bf16)
    chunk_back.store(1, weights[0], raw, grads, sem.at[2])
    arrived(grad, sem.at[1])
    arrived(raw, sem.at[2])


def on_device(
    tokens,
    class_tokens,
    clip_frames,
    cotangent,
    temporal_qkv,
    temporal_proj,
    temporal_fc,
    spatial_qkv,
    spatial_proj,
    mlp_in,
    mlp_out,
    mlp_in_bias,
    norm_gains,
    norm_shifts,
    biases,
):
    frame_size, pos_size = lax.axis_size("frame"), lax.axis_size("pos")
    frame_index, pos_index = lax.axis_index("frame"), lax.axis_index("pos")
    frame_count, pos_count = tokens.shape[1], tokens.shape[2]
    shard = norm_gains.shape[0]
    slots = pos_count + 1
    share = frame_size // MB
    my_slots = slots // share
    all_frames = frame_count * frame_size
    my_frames = all_frames // pos_size
    rows_count = all_frames * my_slots
    micro = frame_index // share

    layout = Layout()
    small = (mlp_in_bias.reshape(1, 4 * shard), norm_gains.T, norm_shifts.T, biases.T)
    keep_t, give_t = pack(layout, (temporal_qkv, temporal_proj, temporal_fc), small)
    got_t = send(give_t, layout.swap)
    keep, give = pack(layout, tie((spatial_qkv, spatial_proj, mlp_in), got_t))
    keep_out, give_out = pack(layout, tie((mlp_out,), got_t))
    got = send(tie(give, give_t), layout.swap)
    got_out = send(tie(give_out, give_t), layout.swap)
    way_t = Gather(layout, layout.chip_rows(keep_t, got_t), {})
    rest = layout.chip_rows(keep, got)
    way_s = Gather(layout, rest[:, : 2 * D], {})
    way_in = Gather(layout, rest[:, 2 * D :], {})
    way_out = Gather(layout, layout.chip_rows(keep_out, got_out), {})
    chunk_t = Chunk(layout, (3 * D, D, D, SMALL), 2 * shard)
    chunk_s = Chunk(layout, (3 * D, D), 2 * shard)
    chunk_in = Chunk(layout, (FF,), 2 * shard)
    chunk_out = Chunk(layout, (D,), 8 * shard)
    chunk_proj = Chunk(layout, (D, D), 2 * shard)
    chunk_qkv = Chunk(layout, (3 * D, SMALL), 2 * shard)
    later = range(1, layout.bits)

    def frame_hop(values):
        return lax.all_to_all(values, "frame", 0, 0, tiled=True)

    def pos_hop(values):
        parts = values.reshape(pos_size, rows_count // pos_size, D)
        return lax.all_to_all(parts, "pos", 0, 0, tiled=True).reshape(rows_count, D)

    def to_temporal(*arrays):
        parts = []
        for values in arrays:
            padded = jnp.pad(values, ((0, 0), (0, 0), (0, 1), (0, 0)))
            padded = padded.reshape(MB, frame_count, share, my_slots, D).transpose(0, 2, 1, 3, 4)
            parts.append(padded.reshape(frame_size, frame_count * my_slots, D))
        hopped = frame_hop(jnp.concatenate(parts, axis=1)).reshape(frame_size, len(arrays), -1, D)
        return [hopped[:, i].reshape(rows_count, D) for i in range(len(arrays))]

    def from_temporal(hopped, count):
        rows, out = frame_count * my_slots, []
        for at in range(0, rows * count, rows):
            part = hopped[:, at : at + rows].reshape(MB, share, frame_count, my_slots, D)
            part = part.transpose(0, 2, 1, 3, 4).reshape(MB, frame_count, slots, D)
            out.append(part[:, :, :pos_count])
        return out + [hopped[:, rows * count :]]

    def partners(values, step):
        perm = [(f, f // share * share + (f % share + step) % share) for f in range(frame_size)]
        return lax.ppermute(values, "frame", perm)

    n = rows_count
    clip_ends = jnp.cumsum(lax.dynamic_index_in_dim(clip_frames, micro, 0, keepdims=False))
    clip_of = lambda frame: jnp.sum(
        (frame[:, None] >= clip_ends[None, :]).astype(jnp.int32), axis=1
    )
    size_t = all_frames * max(1, 128 // all_frames)
    ids = jnp.arange(size_t, dtype=jnp.int32)
    ids = ids // all_frames * CLIPS + clip_of(ids % all_frames)
    ids_t = [(ids[:, None], "v"), (jnp.tile(ids, 2)[None, :], "v")]
    frame_rows = n // my_frames
    size_s = frame_rows * max(1, 128 // frame_rows)
    row_ids = jnp.arange(n, dtype=jnp.int32)
    frame_s, row_slot = row_ids // frame_rows, row_ids % my_slots
    first_source = row_ids % frame_rows < my_slots

    def key_masks(share_index):
        padding = row_slot + share_index * my_slots == slots - 1
        is_class = padding & first_source
        return is_class, is_class | ~padding

    keys_s = []
    for step in range(share):
        _, valid = key_masks((frame_index + share - step) % share)
        keys_s.append(jnp.where(valid, frame_s, -1)[:size_s])
    ids_s = [
        (jnp.concatenate(keys_s)[:, None], "v"),
        (jnp.tile(frame_s[:size_s], 2)[None, :], "v"),
    ]
    is_class, _ = key_masks(frame_index % share)
    clip_s = clip_of(pos_index * my_frames + frame_s)
    choose = (clip_s[:, None] == jnp.arange(8)[None, :]) & is_class[:, None]
    choose = (choose.astype(bf16), "v")
    class_rows = lax.dynamic_index_in_dim(class_tokens, micro, 0, keepdims=False)
    class_rows = (jnp.pad(class_rows, ((0, 8 - CLIPS), (0, 0))), "v")
    is_class = (is_class.astype(jnp.int32)[:, None], "v")

    narrow, wide, full = (n, D), (n, 3 * D), (n, FF)
    heads = lambda size: (-(-HEADS // 2 * (n // size) // 8) * 8, 2 * size)
    columns = (D // 128, n, 128)
    lse_shape_t, lse_shape_s = heads(size_t), heads(size_s)
    mask_t, mask_s = (size_t, 2 * size_t), (share * size_s, 2 * size_s)
    flops = lambda columns: 2 * n * D * columns

    some, others, every = layout.some, layout.others, layout.steps
    way_t.along(every)
    rows, grad_out = to_temporal(*tie((tokens, cotangent), give))
    rows, grad_out = meet(way_t, way_s, way_in, way_out, rows, grad_out)
    way_t.across(0)
    way_s.along(every)
    meet(way_t, way_s)
    for step in later:
        way_t.across(step)
    way_t.swap(1)
    grad_out = pos_hop(grad_out)
    way_in.state, grad_out = meet(way_t, way_in.state, grad_out)
    way_t.swap()
    way_s.across(0)
    way_in.along(every)
    packed_t, small_t = call(
        "temporal_qkv",
        partial(temporal_qkv_kernel, chunk_t, my_slots),
        chunk_t.load(way_t).operands() + [(rows, "v")],
        [(wide, bf16, "v"), ((32, D), f32, "v")],
        [((D, 3 * D), bf16), ((D, SMALL), bf16), (narrow, bf16), ((1, 3 * D), f32)]
        + [(columns, f32), (narrow, f32)],
        2,
        flops(3 * D),
    )
    packed_t, small_t = meet(way_s, way_in, packed_t, small_t)
    small = (small_t, "v")
    for step in later:
        way_s.across(step)
    way_s.swap(1)
    way_out.along(every)
    mixed_t, projected, lse_t, temporal = call(
        "temporal_mix",
        partial(temporal_mix_kernel, chunk_t, my_slots),
        chunk_t.operands() + [(packed_t, "w"), (rows, "w")] + ids_t + [small],
        [(narrow, bf16, "v"), (narrow, bf16, "v"), (lse_shape_t, f32, "v"), (narrow, bf16, "v")],
        [((D, D), bf16), ((D, D), bf16), (mask_t, f32), (narrow, f32), (columns, f32)],
        2,
        flops(2 * D + 4 * n),
    )
    temporal, grad_out, small_t = meet(way_s, way_in, way_out, temporal, grad_out, small_t)
    temporal = pos_hop(temporal)
    way_s.swap()
    way_in.across(0)
    in_bias = small_t[:4].reshape(4, -1, shard).transpose(1, 0, 2).reshape(1, FF)
    grad_out = grad_out.reshape(pos_size, my_frames, my_slots, D)
    grad_out = grad_out.transpose(1, 0, 2, 3).reshape(n, D)
    for step in later:
        way_in.across(step)
    temporal, in_bias, grad_out = meet(way_s, way_out, temporal, in_bias, grad_out)
    way_out.across(0)
    small = (small_t, "v")
    way_in.swap(1)
    temporal, packed_s = call(
        "spatial_qkv",
        partial(spatial_qkv_kernel, chunk_s, pos_size, my_frames),
        chunk_s.load(way_s).operands() + [(temporal, "w"), choose, class_rows, is_class, small],
        [(narrow, bf16, "v"), (wide, bf16, "v")],
        [((D, 3 * D), bf16), (narrow, bf16), ((1, 3 * D), f32)] + [(narrow, f32)] * 2,
        1,
        flops(3 * D),
    )
    temporal = (temporal, "v")
    pairs, k_at = packed_s, D
    if share > 1:
        pairs = [packed_s[:, D:]]
        for step in range(1, share):
            pairs.append(partners(packed_s[:, D:], step))
        pairs, k_at = jnp.concatenate(pairs, axis=0), 0
    all_keys = share * n
    mixed_s, lse_s, spatial = call(
        "spatial_mix",
        partial(spatial_mix_kernel, chunk_s, k_at),
        chunk_s.operands() + [(packed_s, "v"), (pairs, "v")] + ids_s + [temporal, small],
        [(narrow, bf16, "v"), (lse_shape_s, f32, "v"), (narrow, f32, "v")],
        [((D, D), bf16), (mask_s, f32)],
        1,
        flops(D + 4 * all_keys),
    )
    for step in later:
        way_out.across(step)
    spatial = meet(way_in, spatial)
    way_in.swap()
    spatial = meet(way_in, spatial)
    spatial, grad_out = (spatial, "v"), (grad_out, "v")
    way_out.swap(1)
    in_bias = (in_bias, "v")
    normed_m, activated, slope, acc_out = call(
        "hidden",
        partial(hidden_kernel, chunk_in, chunk_out),
        chunk_in.load(way_in).operands()
        + [(chunk_out.index, "s"), spatial, in_bias, small, grad_out],
        [(narrow, bf16, "v"), (full, bf16, "v"), (full, bf16, "v")] + chunk_out.grads(),
        [((D, FF), bf16), ((FF, D), bf16)],
        2,
        flops(2 * FF),
    )
    activated = (activated, "v")
    acc_out, slope = meet(way_out, acc_out, slope)
    way_out.swap()
    back_out = chunk_out.scatter(*acc_out)
    slope = meet(way_out, back_out, slope)
    for step in reversed(later):
        back_out.across(step)
    result, grad_hidden, grad_in_bias, grad_spatial, sums_m = call(
        "mlp_back",
        partial(mlp_back_kernel, chunk_in, chunk_out, pos_size, my_frames),
        chunk_in.operands()
        + chunk_out.load(way_out).operands()
        + [grad_out, (slope, "v"), spatial, activated, small],
        [(narrow, bf16, "v"), (full, bf16, "v"), ((1, FF), f32, "v"), (narrow, f32, "v"), ((8, D), f32, "v")],
        [((D, FF), bf16), ((FF, D), bf16), (narrow, f32), (narrow, f32)],
        2,
        flops(3 * FF),
    )
    grad_hidden, grad_in_bias, result = meet(back_out, grad_hidden, grad_in_bias, result)
    back_out.across(0)
    (acc_in,) = call(
        "mlp_in_grad",
        partial(in_grad_kernel, chunk_in),
        [(chunk_in.index, "s"), (normed_m, "v"), (grad_hidden, "v")],
        chunk_in.grads(),
        [((D, n), bf16), ((D, FF), bf16)],
        1,
        flops(FF),
    )
    acc_in, grad_spatial = meet(back_out, acc_in, grad_spatial)
    back_in = chunk_in.scatter(*acc_in)
    back_out.sums()
    back_out.along(some)
    grad_spatial = (grad_spatial, "v")
    acc_sproj, grad_query, grad_pairs = call(
        "spatial_attention_back",
        partial(spatial_attention_back_kernel, chunk_s, k_at),
        chunk_s.operands()
        + [grad_spatial, (mixed_s, "v"), (packed_s, "v"), (pairs, "v")]
        + ids_s
        + [(lse_s, "v")],
        [((D, D), bf16, "v"), (narrow, bf16, "v"), ((all_keys, 2 * D), bf16, "v")],
        [((D, D), bf16), (narrow, bf16), ((D, n), bf16), (narrow, bf16)]
        + [(mask_s, f32)],
        2,
        flops(2 * D + 10 * all_keys),
    )
    grad_query, result = meet(back_in, back_out, grad_query, result)
    for step in reversed(later):
        back_in.across(step)
    result = pos_hop(result)
    own_pairs = grad_pairs[:n]
    for step in range(1, share):
        theirs = partners(grad_pairs[step * n : (step + 1) * n], share - step)
        own_pairs = (own_pairs.astype(f32) + theirs.astype(f32)).astype(bf16)
    acc_s, grad_temporal, class_part, sums_s = call(
        "spatial_qkv_back",
        partial(spatial_qkv_back_kernel, chunk_s, pos_size, my_frames),
        chunk_s.operands()
        + [(acc_sproj, "w"), (grad_query, "w"), (own_pairs, "w")]
        + [(temporal[0], "w"), (grad_spatial[0], "w"), choose, is_class, small],
        chunk_s.grads() + [(narrow, bf16, "v"), ((8, D), f32, "v"), ((8, D), f32, "v")],
        [((D, 3 * D), bf16), (wide, bf16), (narrow, bf16), ((D, n), bf16)]
        + [((D, 3 * D), bf16), (narrow, f32), (narrow, f32)],
        3,
        flops(6 * D),
    )
    acc_s, grad_temporal, class_part, grad_in_bias, result = meet(
        back_in, acc_s, grad_temporal, class_part, grad_in_bias, result
    )
    back_s = chunk_s.scatter(*acc_s)
    grad_temporal = pos_hop(grad_temporal)
    back_in.across(0)
    class_sum = class_part + send(class_part, layout.within[0])
    block_in_bias = grad_in_bias.reshape(-1, 4, shard).transpose(1, 0, 2).reshape(4, D)
    grad_temporal, block_in_bias, class_sum = meet(
        back_s, back_in, back_out, grad_temporal, block_in_bias, class_sum
    )
    for step in reversed(later):
        back_s.across(step)
    back_in.sums()
    back_in.along(some)
    back_out.along(others)
    class_sum = class_sum + send(class_sum, layout.within[1])
    grad_temporal = (grad_temporal, "v")
    acc_proj, grad_mixed_t, sums_t = call(
        "temporal_proj_back",
        partial(temporal_proj_back_kernel, chunk_t, chunk_proj, my_slots),
        chunk_t.operands()
        + [grad_temporal, (projected, "v"), (mixed_t, "v")],
        chunk_proj.grads() + [(narrow, bf16, "v"), ((8, D), f32, "v")],
        [((D, D), bf16), ((D, D), bf16), (narrow, bf16), ((D, n), bf16), ((D, n), bf16)]
        + [((D, D), bf16), ((D, D), bf16), (narrow, bf16), (columns, f32), (narrow, f32)],
        4,
        flops(4 * D),
    )
    acc_proj, grad_mixed_t, class_sum = meet(
        back_s, back_in, back_out, acc_proj, grad_mixed_t, class_sum
    )
    back_proj = chunk_proj.scatter(*acc_proj)
    for perm in layout.within[2:]:
        class_sum = class_sum + send(class_sum, perm)
    grad_mixed_t, class_sum = meet(back_proj, grad_mixed_t, class_sum)
    for step in reversed(later):
        back_proj.across(step)
    back_s.across(0)
    back_in.along(others)
    acc_qkv, outgoing = call(
        "temporal_attention_back",
        partial(temporal_attention_back_kernel, chunk_t, chunk_qkv, my_slots),
        chunk_t.operands()
        + [(packed_t, "v")]
        + ids_t
        + [(lse_t, "v"), (grad_mixed_t, "v"), (rows, "v"), grad_temporal, small]
        + [(block_in_bias, "v"), (sums_m, "v"), (sums_s, "v"), (sums_t, "v")]
        + [(result, "v"), (class_sum, "v")],
        chunk_qkv.grads() + [((frame_size, 2 * n // frame_size + 16, D), bf16, "v")],
        [((D, 3 * D), bf16), (mask_t, f32), (wide, bf16), (narrow, bf16), ((D, n), bf16)]
        + [((D, 3 * D), bf16), (narrow, f32), (columns, f32), ((128, D), f32), ((D, SMALL), bf16)],
        3,
        flops(6 * D + 10 * n),
    )
    acc_qkv, outgoing = meet(back_s, back_in, back_proj, acc_qkv, outgoing)
    back_qkv = chunk_qkv.scatter(*acc_qkv)
    meet(back_qkv)
    for step in reversed(later):
        back_qkv.across(step)
    back_proj.across(0)
    back_s.sums()
    back_s.along(every)
    hopped = frame_hop(outgoing)
    meet(back_qkv, back_s, back_proj)
    back_qkv.across(0)
    back_proj.sums()
    back_proj.along(every)
    hopped = meet(back_qkv, back_proj, hopped)
    back_qkv.sums("x")
    back_qkv.along(every)
    own = back_qkv.state[0]
    for way in (back_in, back_s, back_proj, back_out):
        way.state = tie(way.state, own)
    most = Return(layout, [back_in, back_s, back_proj, back_out], "w")
    tokens_grad, block_out, class_all = from_temporal(tie(hopped, back_qkv.state[1][1]), 2)
    tokens_grad = tokens_grad.astype(f32)
    class_grad = class_all[::share, :CLIPS].astype(f32)
    tokens_grad, block_out, class_grad = meet(back_qkv, tokens_grad, block_out, class_grad)
    last = Return(layout, [back_qkv], "x")
    (
        acc_in, acc_sqkv, acc_sproj, acc_tproj, acc_tfc, acc_out,
        acc_tqkv, in_bias_grad, gains_grad, shifts_grad, biases_grad,
    ) = finish(
        layout,
        [most, last],
        [
            [(shard, FF), (shard, 3 * D), (shard, D), (shard, D), (shard, D), (4 * shard, D)],
            [(shard, 3 * D), (shard, SMALL)],
        ],
    )
    return (
        block_out,
        tokens_grad,
        class_grad,
        acc_tqkv,
        acc_tproj,
        acc_tfc,
        acc_sqkv,
        acc_sproj,
        acc_in,
        acc_out,
        in_bias_grad.reshape(-1),
        gains_grad.T,
        shifts_grad.T,
        biases_grad.T,
    )


def solution(mesh):
    rows = P(AXES, None)
    wide = P(None, "frame", "pos", None)
    placed = (wide, P(), P(), wide) + (rows,) * 7 + (P(AXES),) + (rows,) * 3
    return jax.shard_map(
        on_device,
        mesh=mesh,
        in_specs=placed,
        out_specs=(wide, wide, P()) + (rows,) * 7 + (P(AXES),) + (rows,) * 3,
        check_vma=False,
    )
```

```python
from functools import partial

import jax
import jax.numpy as jnp
from jax import lax
from jax.experimental import pallas as pl
from jax.experimental.pallas import tpu as pltpu
from jax.sharding import PartitionSpec as P

D = 768
HEADS = 12
HEAD = 64
FF = 4 * D
MB = 4
CLIPS = 3
AXES = ("frame", "pos")
TILE = 768
SMALL = 256
f32, bf16 = jnp.float32, jnp.bfloat16
GAIN, SHIFT, BIAS = 4, 7, 10


def send(values, perm):
    return lax.ppermute(values, AXES, perm)


def tie(value, *before):
    return lax.optimization_barrier((value,) + before)[0] if before else value


class Layout:
    def __init__(self):
        self.frames, self.chips = lax.axis_size("frame"), lax.axis_size("pos") // 2
        self.bits = self.frames.bit_length() - 1
        self.frame, self.chip = lax.axis_index("frame"), lax.axis_index("pos") // 2
        self.core = lax.axis_index("pos") % 2
        self.core_index = self.core.astype(jnp.int32).reshape(1)
        self.swap = self.perm(lambda f, z, c: (f, z, 1 - c))
        self.steps = range(1, self.chips)
        self.some = range(self.chips * 3 // 4, self.chips)
        self.others = range(1, self.chips * 3 // 4)
        self.along = [self.perm(lambda f, z, c, i=i: (f, z ^ i, c)) for i in range(1, self.chips)]
        self.across = [
            self.perm(lambda f, z, c, k=k: (f ^ (1 << self.bit(k, c)), z, c))
            for k in range(self.bits)
        ]

        share = self.frames // MB
        steps = lambda n: [1 << k for k in range(n.bit_length() - 1)]
        self.within = [self.swap]
        self.within += [self.perm(lambda f, z, c, k=k: (f, z ^ k, c)) for k in steps(self.chips)]
        self.within += [self.perm(lambda f, z, c, k=k: (f ^ k, z, c)) for k in steps(share)]

    def bit(self, step, core):
        return (step + core) % self.bits

    def perm(self, to):
        pairs = []
        for f in range(self.frames):
            for z in range(self.chips):
                for c in range(2):
                    g, y, d = to(f, z, c)
                    pairs.append(
                        ((f * self.chips + z) * 2 + c, (g * self.chips + y) * 2 + d)
                    )
        return pairs

    def table(self):
        rows = []
        for core in (self.core, 1 - self.core):
            blocks = []
            for b in range(self.frames * self.chips):
                flags, i = b // self.chips, b % self.chips
                f = self.frame
                for k in range(self.bits):
                    if flags >> k & 1:
                        f = f ^ (1 << ((k + core) % self.bits))
                blocks.append(f * self.chips + (self.chip ^ i))
            rows.append(jnp.stack(blocks))
        return jnp.concatenate([jnp.stack(rows).reshape(-1), self.core[None]]).astype(jnp.int32)

    def pick(self, low, high):
        return jnp.where(self.core == 0, low, high), jnp.where(self.core == 0, high, low)

    def chip_rows(self, keep, got):
        return jnp.concatenate(self.pick(keep, got), axis=0)


class Way:
    def __init__(self, layout, *state):
        self.layout, self.state = layout, state


def meet(*things):
    values = tuple(t.state if isinstance(t, Way) else t for t in things)
    values = lax.optimization_barrier(values)
    out = []
    for thing, value in zip(things, values):
        if isinstance(thing, Way):
            thing.state = value
        else:
            out.append(value)
    return out[0] if len(out) == 1 else out


class Gather(Way):
    def along(self, steps):
        block, got = self.state
        new = {i: send(block, self.layout.along[i - 1]) for i in steps}
        self.state = (block, {**got, **new})

    def across(self, step):
        mine, other = self.state
        if step == 0:
            mine = tuple(a[None] for a in [mine] + [other[i] for i in self.layout.steps])
        block = merge(mine)
        self.state = ((block, send(block, self.layout.across[step])), ())

    def swap(self, count=None):
        mine, other = self.state
        other += tuple(send(a, self.layout.swap) for a in mine[len(other) : count])
        self.state = (mine, other)


class Scatter(Way):
    def __init__(self, layout, mine, other):
        near, far = [(a, send(b, layout.swap)) for a, b in zip(mine, other)]
        super().__init__(layout, near, far)
        self.count = near[0].shape[0]

    def across(self, step):
        near, far = self.state
        if far:
            far, _ = fold(far, self.count, False)
        else:
            self.count //= 2
            far, near = fold(near, self.count, True)
            near = (near,)
        self.state = (near + (send(far, self.layout.across[step]),), ())
        return far

    def sums(self, space="w"):
        near, _ = self.state
        _, rows, width = near[0].shape
        own, *away = call(
            "fold_blocks",
            partial(fold_blocks_kernel, len(near)),
            [(a, "x") for a in near],
            [((rows, width), f32, space)] + [((rows, width), bf16, "x")] * (self.count - 1),
            [],
            1,
            0,
        )
        self.state = (own, dict(zip(self.layout.steps, away)))

    def along(self, steps):
        own, away = self.state
        new = {i: send(away[i], self.layout.along[i - 1]) for i in steps}
        self.state = (own, {**away, **new})


class Return:
    def __init__(self, layout, ways, space):
        shapes = [way.state[0].shape for way in ways]
        self.rows = min(r for r, _ in shapes) // 2
        width = sum(r // 2 // self.rows * w for r, w in shapes)
        kept = ((self.rows, width), f32, "x")
        parts = [[(a, space) for a in [way.state[0], *way.state[1].values()]] for way in ways]
        self.keep, give = call(
            "sum_parts",
            sum_parts_kernel,
            [(layout.core_index, "s"), parts],
            [kept, kept],
            [],
            1,
            0,
        )
        self.got = send(give, layout.swap)


def finish(layout, returns, chunks):
    outs = []
    for rows, width in [m for group in chunks for m in group]:
        if width != SMALL:
            outs.append(((rows, width), f32, "v"))
        else:
            outs += [((count, rows), f32, "v") for count in (4, 3, 3, 8)]
    return call(
        "finish",
        partial(finish_kernel, chunks),
        [(layout.core_index, "s")] + [[(r.keep, "x"), (r.got, "x")] for r in returns],
        outs,
        [((128, 128), f32)],
        1,
        0,
    )


def total(values):
    out = values[0].astype(f32)
    for value in values[1:]:
        out = out + value.astype(f32)
    return out


class Chunk:
    def __init__(self, layout, widths, rows):
        self.layout, self.widths, self.rows = layout, widths, rows
        self.count = layout.frames * layout.chips
        self.table = layout.table()
        self.half = sum(widths) // 2
        self.whole = bool(rows % 16)
        if self.whole:
            core = layout.core.astype(jnp.int32)
            self.index = jnp.stack([jnp.zeros_like(core)] * 2 + [core])
            self.blocks, self.block_rows = 1, self.count * rows
        else:
            self.index = self.table
            self.blocks, self.block_rows = self.count, rows

    def load(self, way):
        mine, other = way.state
        if self.whole:
            order = jnp.argsort(self.table[: 2 * self.count].reshape(2, -1), axis=1)
            mine, other = [
                (jnp.concatenate(a)[o].reshape(1, self.block_rows, -1),)
                for a, o in zip((mine, other), order)
            ]
        self.mine, self.other = mine, other
        return self

    def operands(self):
        pieces = [[(a, "h") for a in side] for side in (self.mine, self.other)]
        return [[(self.index, "s")] + pieces]

    def grads(self):
        if self.whole:
            piece = [((1, self.block_rows, self.half), bf16, "x")]
            return [[piece, piece]]
        shape = (self.count // 2, self.block_rows, self.half)
        return [[[(shape, bf16, "h"), (shape, bf16, "x")], [(shape, bf16, "x")] * 2]]

    def at(self, which):
        return sum(self.widths[:which]) // 2

    def fetch(self, which, weights, dst, sem):
        self._copies(which, *weights, dst, sem, True)

    def store(self, which, table, src, grads, sem):
        self._copies(which, table, *grads, src, sem, False)

    def _copies(self, which, table, mine, other, mat, sem, into):
        at, w = self.at(which), self.widths[which] // 2
        core = table[2 * self.blocks]
        for side, pieces in ((0, mine), (1, other)):
            half = core if side == 0 else 1 - core
            first = side * self.blocks
            for piece in pieces:

                def body(b, carry, piece=piece, first=first, half=half):
                    row = pl.multiple_of(table[first + b] * self.block_rows, 16)
                    block = piece.at[b, :, at : at + w]
                    place = mat.at[
                        pl.ds(row, self.block_rows), pl.ds(pl.multiple_of(half * w, 128), w)
                    ]
                    pair = (block, place) if into else (place, block)
                    pltpu.make_async_copy(*pair, sem).start()
                    return carry

                lax.fori_loop(0, piece.shape[0], body, 0)
                first += piece.shape[0]

    def scatter(self, mine, other):
        if self.whole:
            order = self.table[: 2 * self.count].reshape(2, -1)
            mine, other = [
                a[0].reshape(self.count, self.rows, -1)[o] for a, o in zip((mine, other), order)
            ]
            half = self.count // 2
            mine, other = [(a[:half], a[half:]) for a in (mine, other)]
        return Scatter(self.layout, mine, other)


def merge_kernel(count, *refs):
    out, at = refs[count], 0
    for ref in refs[:count]:
        out[at : at + ref.shape[0]] = ref[...]
        at += ref.shape[0]


def merge(blocks):
    if blocks[0].shape[1] % 16:
        return jnp.concatenate(blocks)
    shape = (sum(a.shape[0] for a in blocks),) + blocks[0].shape[1:]
    return call(
        "merge",
        partial(merge_kernel, len(blocks)),
        [(a, "x") for a in blocks],
        [(shape, blocks[0].dtype, "x")],
        [],
        1,
        0,
    )[0]


def fold_kernel(given, halve, *refs):
    far = refs[given]
    start = far.shape[0] if halve else 0

    def block(b, carry):
        far[b] = total([ref[start + b] for ref in refs[:given]]).astype(bf16)
        if halve:
            refs[given + 1][b] = total([ref[b] for ref in refs[:given]])
        return carry

    lax.fori_loop(0, far.shape[0], block, 0)


def fold(values, count, halve):
    shape = (count,) + values[0].shape[1:]
    outs = [(shape, bf16, "x")] + [(shape, f32, "x")] * halve
    out = call(
        "fold",
        partial(fold_kernel, len(values), halve),
        [(a, "w" if halve and i < 2 else "x") for i, a in enumerate(values)],
        outs,
        [],
        1,
        0,
    )
    return out[0], out[-1]


def fold_blocks_kernel(count, *refs):
    refs, outs = refs[:count], refs[count:-1]
    for b, out in enumerate(outs):
        out[...] = total([ref[b] for ref in refs]).astype(out.dtype)


def pack_kernel(widths, small, core, *refs):
    mats, (keep, give) = refs[: len(widths)], refs[-4:-2]
    turned = refs[-2]
    at = 0
    first = core[0] == 0
    for mat, width in zip(mats, widths):
        w = width // 2
        low, high = mat[:, :w], mat[:, w:]
        keep[:, at : at + w] = jnp.where(first, low, high)
        give[:, at : at + w] = jnp.where(first, high, low)
        at += w
    if small:
        rows = keep.shape[0]
        turned[...] = jnp.zeros_like(turned)
        place = 0
        for ref in refs[len(widths) : -4]:
            for at_row in range(0, ref.shape[1], rows):
                count = ref.shape[0]
                turned[place : place + count, :rows] = ref[:, at_row : at_row + rows].astype(f32)
                place += count
        values = turned[...].T[:rows].astype(bf16)
        zeros = jnp.zeros_like(values)
        keep[:, at:] = jnp.where(first, values, zeros)
        give[:, at:] = jnp.where(first, zeros, values)


def pack(layout, mats, small=()):
    rows = mats[0].shape[0]
    width = sum(m.shape[1] for m in mats) // 2 + (SMALL // 2 if small else 0)
    half = ((rows, width), bf16, "x")
    return call(
        "pack",
        partial(pack_kernel, [m.shape[1] for m in mats], len(small)),
        [(layout.core_index, "s")] + [(m, "w") for m in mats] + [(m, "w") for m in small],
        [half, half],
        [((128, 128), f32)],
        1,
        0,
    )


def sum_parts_kernel(core, groups, keep, give, sem):
    first, short, at = core[0] == 0, keep.shape[0], 0
    for parts in groups:
        values = total([p[...] for p in parts])
        rows, width = values.shape[0] // 2, values.shape[1]
        for row in range(0, rows, short):
            low, high = values[row : row + short], values[rows + row : rows + row + short]
            keep[:, at : at + width] = jnp.where(first, low, high)
            give[:, at : at + width] = jnp.where(first, high, low)
            at += width


def finish_kernel(chunks, core, *refs):
    pairs, outs, turned = refs[: len(chunks)], iter(refs[len(chunks) : -2]), refs[-2]
    first = core[0] == 0
    for (keep, got), group in zip(pairs, chunks):
        short, at = keep.shape[0], 0
        for rows, width in group:
            w = width // 2
            if width == SMALL:
                turned[...] = jnp.zeros_like(turned)
                low = jnp.where(first, keep[:, at : at + w], got[:, at : at + w])
                turned[:short, :] = low
                values, place = turned[...].T, 0
                for _ in range(4):
                    out = next(outs)
                    out[...] = values[place : place + out.shape[0], :short]
                    place += out.shape[0]
                at += w
                continue
            out = next(outs)
            for row in range(0, rows, short):
                mine, other = keep[:, at : at + w], got[:, at : at + w]
                out[row : row + short, :w] = jnp.where(first, mine, other)
                out[row : row + short, w:] = jnp.where(first, other, mine)
                at += w


def arrived(mat, sem):
    pltpu.make_async_copy(mat, mat, sem).wait()


SPACE = {"s": pltpu.SMEM, "h": pltpu.HBM, "v": pltpu.VMEM, "w": pltpu.VMEM, "x": pltpu.VMEM}
HELD = {"h": pltpu.HBM, "w": pltpu.HBM, "x": pltpu.VMEM}


def held(value, space):
    return pltpu.with_memory_space_constraint(value, HELD[space]) if space in HELD else value


def result(shape, kind, space):
    return HELD[space](shape, kind) if space in HELD else jax.ShapeDtypeStruct(shape, kind)


def flat(items):
    return [leaf for item in items for leaf in (flat(item) if isinstance(item, list) else [item])]


def nest(items, leaves):
    return [nest(item, leaves) if isinstance(item, list) else next(leaves) for item in items]


def call(name, body, ins, outs, scratch, sems, flops, alias=None):
    operands, results = flat(ins), flat(outs)
    bytes_of = lambda shape, kind: jnp.dtype(kind).itemsize * _size(shape)
    size = sum(bytes_of(a.shape, a.dtype) for a, space in operands if space in "vwx")
    size += sum(bytes_of(shape, kind) for shape, kind, space in results if space in "vwx")
    size += sum(bytes_of(shape, kind) for shape, kind in scratch)
    moved = sum(bytes_of(a.shape, a.dtype) for a, _ in operands)
    moved += sum(bytes_of(shape, kind) for shape, kind, _ in results)
    aliases = {}
    for i, o in (alias or {}).items():
        start, end = len(flat(ins[:i])), len(flat(outs[:o]))
        for k in range(len(flat([ins[i]]))):
            aliases[start + k] = end + k

    def kernel(*refs):
        leaves = iter(refs)
        body(*nest(ins, leaves), *nest(outs, leaves), *leaves)

    values = pl.pallas_call(
        kernel,
        out_shape=[result(*r) for r in results],
        in_specs=[pl.BlockSpec(memory_space=SPACE[space]) for _, space in operands],
        out_specs=[pl.BlockSpec(memory_space=SPACE[space]) for _, _, space in results],
        scratch_shapes=[pltpu.VMEM(shape, kind) for shape, kind in scratch]
        + [pltpu.SemaphoreType.DMA((sems,))],
        input_output_aliases=aliases,
        compiler_params=pltpu.CompilerParams(
            vmem_limit_bytes=min(int(size * 1.1) + (6 << 20), 60 << 20)
        ),
        cost_estimate=pl.CostEstimate(flops=flops, bytes_accessed=moved, transcendentals=0),
        name=name,
    )(*[held(a, space) for a, space in operands])
    return nest(outs, iter(values))


def _size(shape):
    total = 1
    for n in shape:
        total *= n
    return total


def tiles(width, body, size=TILE):
    def step(j, carry):
        body(pl.ds(pl.multiple_of(j * size, size), size))
        return carry

    lax.fori_loop(0, width // size, step, 0)


def dot(a, b):
    return jnp.dot(a, b, preferred_element_type=f32)


def dot_t(a, b):
    return lax.dot_general(a, b, (((1,), (1,)), ((), ())), preferred_element_type=f32)


def normalise(values):
    centred = values - jnp.mean(values, axis=-1, keepdims=True)
    inv_std = lax.rsqrt(jnp.mean(centred * centred, axis=-1, keepdims=True) + 1e-06)
    return centred * inv_std, inv_std


def norm_rows(values, small, which):
    normal, _ = normalise(values)
    return normal * small[GAIN + which : GAIN + which + 1] + small[SHIFT + which : SHIFT + which + 1]


def norm_back(values, upstream, small, which):
    normal, inv_std = normalise(values)
    product = upstream * normal
    grad_gain = jnp.sum(product, axis=0, keepdims=True)
    grad_shift = jnp.sum(upstream, axis=0, keepdims=True)
    gain = small[GAIN + which : GAIN + which + 1]
    scaled = upstream * gain
    mean = jnp.mean(scaled, axis=-1, keepdims=True)
    mean_normal = jnp.mean(product * gain, axis=-1, keepdims=True)
    return inv_std * (scaled - mean - normal * mean_normal), grad_gain, grad_shift


def column_sum(values):
    return jnp.sum(values.astype(f32), axis=0, keepdims=True)


def set_mask(mask, key_ids, query_ids):
    mask[...] = jnp.where(key_ids[...] == query_ids[...], 0.0, -1000000000.0)


def regroup(values, flat, out, groups):
    count = out.shape[0] // groups
    for c in range(flat.shape[0]):
        cols = slice(c * 128, (c + 1) * 128)
        flat[c] = values[:, cols]
        for g in range(groups):
            out[g * count : (g + 1) * count, cols] = flat[c, pl.ds(g, count, stride=groups), :]


def ungroup(grouped, flat, groups):
    count = grouped.shape[0] // groups
    for c in range(flat.shape[0]):
        cols = slice(c * 128, (c + 1) * 128)
        for g in range(groups):
            flat[c, pl.ds(g, count, stride=groups), :] = grouped[g * count : (g + 1) * count, cols]
    return jnp.concatenate([flat[c] for c in range(flat.shape[0])], axis=1)


def swap_groups(source, out, outer, inner):
    size = source.shape[0] // (outer * inner)
    for i in range(outer):
        for j in range(inner):
            to, at = (j * outer + i) * size, (i * inner + j) * size
            out[to : to + size, :] = source[at : at + size, :]


def both_heads(values, scale):
    lane = lax.broadcasted_iota(jnp.int32, (1, 2 * HEAD), 1)
    wide = values.astype(f32)
    parts = [jnp.where(lane // HEAD == h, wide * scale, 0.0) for h in range(2)]
    return jnp.concatenate(parts, axis=0).astype(bf16)


def own_heads(across):
    size = across.shape[1] // 2
    return jnp.concatenate([across[:HEAD, :size], across[HEAD:, size:]], axis=0).T


def key_rows(pairs, cols, start, size, rows):
    parts = [pairs[at + start : at + start + size, cols] for at in range(0, pairs.shape[0], rows)]
    return parts[0] if len(parts) == 1 else jnp.concatenate(parts, axis=0)


def attend(query, q_at, pairs, k_at, v_at, mask, mixed, lse):
    rows, size = query.shape[0], mask.shape[1] // 2
    blocks = range(rows // size)

    def pair(i, carry):
        cols = lambda at: pl.ds(pl.multiple_of(at + i * 2 * HEAD, 2 * HEAD), 2 * HEAD)
        here = [slice(b * size, (b + 1) * size) for b in blocks]
        queries = [both_heads(query[h, cols(q_at)], 0.125) for h in here]
        keys = [key_rows(pairs, cols(k_at), b * size, size, rows) for b in blocks]
        values = [key_rows(pairs, cols(v_at), b * size, size, rows).T for b in blocks]
        score = [dot_t(keys[b], queries[b]) + mask[...] for b in blocks]
        top = [jnp.max(score[b], axis=0, keepdims=True) for b in blocks]
        weight = [jnp.exp(score[b] - top[b]) for b in blocks]
        norm = [jnp.sum(weight[b], axis=0, keepdims=True) for b in blocks]
        probs = [(weight[b] * (1.0 / norm[b])).astype(bf16) for b in blocks]
        out = [own_heads(dot(values[b], probs[b])).astype(bf16) for b in blocks]
        for b in blocks:
            lse[pl.ds(i * len(blocks) + b, 1), :] = top[b] + jnp.log(norm[b])
            mixed[here[b], cols(0)] = out[b]
        return carry

    lax.fori_loop(0, HEADS // 2, pair, 0, unroll=HEADS // 2)


def attend_back(query, q_at, pairs, k_at, v_at, mask, lse, grad, out_q, out_pairs, gk_at, gv_at):
    rows, size = query.shape[0], mask.shape[1] // 2
    blocks = range(rows // size)

    def pair(i, carry):
        cols = lambda at: pl.ds(pl.multiple_of(at + i * 2 * HEAD, 2 * HEAD), 2 * HEAD)
        here = [slice(b * size, (b + 1) * size) for b in blocks]
        keys = [key_rows(pairs, cols(k_at), b * size, size, rows) for b in blocks]
        values = [key_rows(pairs, cols(v_at), b * size, size, rows) for b in blocks]
        queries = [both_heads(query[h, cols(q_at)], 0.125) for h in here]
        upstream = [both_heads(grad[h, cols(0)], 1.0) for h in here]
        logs = [lse[pl.ds(i * len(blocks) + b, 1), :] for b in blocks]
        across_keys = [keys[b].T for b in blocks]
        score = [dot_t(keys[b], queries[b]) + mask[...] for b in blocks]
        dprob = [dot_t(values[b], upstream[b]) for b in blocks]
        probs = [jnp.exp(score[b] - logs[b]) for b in blocks]
        delta = [jnp.sum(probs[b] * dprob[b], axis=0, keepdims=True) for b in blocks]
        dscore = [(probs[b] * (dprob[b] - delta[b])).astype(bf16) for b in blocks]
        grad_keys = [dot(dscore[b], queries[b]).astype(bf16) for b in blocks]
        grad_values = [dot(probs[b].astype(bf16), upstream[b]).astype(bf16) for b in blocks]
        grad_queries = [
            (own_heads(dot(across_keys[b], dscore[b])) * 0.125).astype(bf16) for b in blocks
        ]
        for b in blocks:
            out_q[here[b], cols(0)] = grad_queries[b]
            for part in range(0, pairs.shape[0], rows):
                there = slice(part + b * size, part + (b + 1) * size)
                seen = slice(part // rows * size, (part // rows + 1) * size)
                out_pairs[there, cols(gk_at)] = grad_keys[b][seen]
                out_pairs[there, cols(gv_at)] = grad_values[b][seen]
        return carry

    lax.fori_loop(0, HEADS // 2, pair, 0, unroll=HEADS // 2)


def qkv_tiles(x, w, bias, small, which, packed):
    bias[:, :D] = small[BIAS + which : BIAS + which + 1]
    bias[:, D : 2 * D] = jnp.zeros((1, D), f32)
    bias[:, 2 * D :] = small[BIAS + which + 1 : BIAS + which + 2]

    def tile(cols):
        packed[:, cols] = (dot(x[...], w[:, cols]) + bias[:, cols]).astype(bf16)

    tiles(3 * D, tile)


def across(mat, out):
    for at in range(0, mat.shape[1], 128):
        out[at : at + 128, :] = mat[:, at : at + 128].astype(f32).T.astype(bf16)


def temporal_qkv_kernel(
    chunk, slots, weights, rows, packed, small, w, raw, x, bias, flat, grouped, sem
):
    chunk.fetch(3, weights, raw, sem.at[0])
    chunk.fetch(0, weights, w, sem.at[1])
    arrived(raw, sem.at[0])
    small[...] = raw[:, :128].astype(f32).T[: small.shape[0]]
    regroup(norm_rows(rows[...].astype(f32), small, 0), flat, grouped, slots)
    x[...] = grouped[...].astype(bf16)
    arrived(w, sem.at[1])
    qkv_tiles(x, w, bias, small, 0, packed)


def temporal_mix_kernel(
    chunk, slots, weights, packed, rows, key_ids, query_ids, small,
    mixed, projected, lse, temporal, w_proj, w_fc, mask, grouped, flat, sem,
):
    chunk.fetch(1, weights, w_proj, sem.at[0])
    chunk.fetch(2, weights, w_fc, sem.at[1])
    set_mask(mask, key_ids, query_ids)
    attend(packed, 0, packed, D, 2 * D, mask, mixed, lse)
    arrived(w_proj, sem.at[0])

    def project(cols):
        bias = small[BIAS + 2 : BIAS + 3, cols]
        projected[:, cols] = (dot(mixed[...], w_proj[:, cols]) + bias).astype(bf16)

    tiles(D, project)
    arrived(w_fc, sem.at[1])

    def residual(cols):
        grouped[:, cols] = dot(projected[...], w_fc[:, cols]) + small[BIAS + 3 : BIAS + 4, cols]

    tiles(D, residual)
    temporal[...] = (rows[...].astype(f32) + ungroup(grouped, flat, slots)).astype(bf16)


def spatial_qkv_kernel(
    chunk, sources, frames, weights, rows, choose, class_rows, is_class, small,
    temporal, packed, w, x, bias, flat, grouped, sem,
):
    chunk.fetch(0, weights, w, sem.at[0])
    flat[...] = rows[...].astype(f32)
    swap_groups(flat, grouped, sources, frames)
    values = jnp.where(is_class[...] > 0, dot(choose[...], class_rows[...]), grouped[...])
    temporal[...] = values.astype(bf16)
    x[...] = norm_rows(values, small, 1).astype(bf16)
    arrived(w, sem.at[0])
    qkv_tiles(x, w, bias, small, 4, packed)


def spatial_mix_kernel(
    chunk, k_at, weights, packed, pairs, key_ids, query_ids, temporal, small,
    mixed, lse, spatial, w, mask, sem,
):
    chunk.fetch(1, weights, w, sem.at[0])
    set_mask(mask, key_ids, query_ids)
    attend(packed, 0, pairs, k_at, k_at + D, mask, mixed, lse)
    arrived(w, sem.at[0])

    def residual(cols):
        added = dot(mixed[...], w[:, cols]) + small[BIAS + 6 : BIAS + 7, cols]
        spatial[:, cols] = temporal[:, cols].astype(f32) + added

    tiles(D, residual)


def hidden_kernel(
    chunk, chunk_back, weights, index, spatial, in_bias, small, grad_out,
    normed, activated, slope, grads, w, grad, sem,
):
    chunk.fetch(0, weights, w, sem.at[0])
    normed[...] = norm_rows(spatial[...], small, 2).astype(bf16)
    arrived(w, sem.at[0])

    def tile(cols):
        hidden = dot(normed[...], w[:, cols]) + in_bias[:, cols]
        below = 0.5 + 0.5 * lax.erf(hidden * 0.7071067811865476)
        density = jnp.exp(hidden * hidden * -0.5) * 0.3989422804014327
        activated[:, cols] = (hidden * below).astype(bf16)
        slope[:, cols] = (below + hidden * density).astype(bf16)

    tiles(FF, tile)

    def back(cols):
        turned = activated[:, cols].astype(f32).T.astype(bf16)
        grad[cols, :] = dot(turned, grad_out[...]).astype(bf16)

    tiles(FF, back)
    chunk_back.store(0, index, grad, grads, sem.at[1])
    arrived(grad, sem.at[1])


def mlp_back_kernel(
    chunk_in, chunk_out, sources, frames, weights_in, weights_out,
    grad_out, slope, spatial, activated, small, block_out, grad_hidden, in_bias, grad_spatial, sums,
    w_in, w_out, total, flat, sem,
):
    chunk_out.fetch(0, weights_out, w_out, sem.at[0])
    chunk_in.fetch(0, weights_in, w_in, sem.at[1])
    arrived(w_out, sem.at[0])

    def forward(cols):
        added = dot(activated[...], w_out[:, cols]) + small[BIAS + 7 : BIAS + 8, cols]
        total[:, cols] = spatial[:, cols] + added

    tiles(D, forward, D // 2)
    swap_groups(total, flat, frames, sources)
    block_out[...] = flat[...].astype(bf16)

    def tile(cols):
        grad = (dot_t(grad_out[...], w_out[cols, :]) * slope[:, cols].astype(f32)).astype(bf16)
        grad_hidden[:, cols] = grad
        in_bias[:, cols] = column_sum(grad)

    tiles(FF, tile)
    arrived(w_in, sem.at[1])

    def back(cols):
        total[:, cols] = dot_t(grad_hidden[...], w_in[cols, :])

    tiles(D, back, D // 2)
    back, gain, shift = norm_back(spatial[...], total[...], small, 2)
    upstream = grad_out[...].astype(f32)
    result = upstream + back
    grad_spatial[...] = result
    sums[0:1] = gain
    sums[1:2] = shift
    sums[2:3] = column_sum(upstream)
    sums[3:4] = column_sum(result.astype(bf16))
    sums[4:8] = jnp.zeros((4, D), f32)


def in_grad_kernel(chunk, table, normed, grad_hidden, grads, normed_t, grad, sem):
    across(normed, normed_t)

    def tile(cols):
        grad[:, cols] = dot(normed_t[...], grad_hidden[:, cols]).astype(bf16)

    tiles(FF, tile)
    chunk.store(0, table, grad, grads, sem.at[0])
    arrived(grad, sem.at[0])


def spatial_attention_back_kernel(
    chunk, k_at, weights, grad_spatial, mixed, packed, pairs, key_ids, query_ids, lse,
    grad, grad_query, grad_pairs,
    w, upstream, mixed_t, grad_mixed, mask, sem,
):
    chunk.fetch(1, weights, w, sem.at[0])
    upstream[...] = grad_spatial[...].astype(bf16)
    set_mask(mask, key_ids, query_ids)
    arrived(w, sem.at[0])

    def back(cols):
        grad_mixed[:, cols] = dot_t(upstream[...], w[cols, :]).astype(bf16)

    tiles(D, back)
    across(mixed, mixed_t)

    def tile(cols):
        grad[:, cols] = dot(mixed_t[...], upstream[:, cols]).astype(bf16)

    tiles(D, tile)
    attend_back(
        packed, 0, pairs, k_at, k_at + D, mask, lse, grad_mixed, grad_query, grad_pairs, 0, D
    )


def qkv_back(normed_t, grad_packed, w, grad, total):
    def back(cols):
        total[:, cols] = dot_t(grad_packed[...], w[cols, :])

    tiles(D, back, D // 2)

    def tile(cols):
        grad[:, cols] = dot(normed_t[...], grad_packed[:, cols]).astype(bf16)

    tiles(3 * D, tile)


def spatial_qkv_back_kernel(
    chunk, sources, frames, weights, acc_spatial, grad_query, grad_pairs, temporal, grad_spatial, choose, is_class,
    small, grads, grad_temporal, class_part, sums,
    w, packed, normed, normed_t, grad, total, flat, sem,
):
    chunk.fetch(0, weights, w, sem.at[0])
    packed[:, :D] = grad_query[...]
    packed[:, D:] = grad_pairs[...]
    values = temporal[...].astype(f32)
    normed[...] = norm_rows(values, small, 1).astype(bf16)
    across(normed, normed_t)
    arrived(w, sem.at[0])
    chunk.store(1, weights[0], acc_spatial, grads, sem.at[2])
    qkv_back(normed_t, packed, w, grad, total)
    chunk.store(0, weights[0], grad, grads, sem.at[1])
    back, gain, shift = norm_back(values, total[...], small, 1)
    total[...] = jnp.where(is_class[...] > 0, 0.0, grad_spatial[...] + back)
    swap_groups(total, flat, frames, sources)
    grad_temporal[...] = flat[...].astype(bf16)
    class_part[...] = jnp.zeros_like(class_part)
    for c in range(CLIPS):
        class_part[c : c + 1] = column_sum(back * choose[:, c : c + 1].astype(f32))
    sums[0:1] = gain
    sums[1:2] = shift
    sums[2:3] = column_sum(packed[:, :D])
    sums[3:4] = column_sum(packed[:, 2 * D :])
    sums[4:8] = jnp.zeros((4, D), f32)
    arrived(grad, sem.at[1])
    arrived(acc_spatial, sem.at[2])


def temporal_proj_back_kernel(
    chunk, chunk_back, slots, weights, grad_rows, projected, mixed,
    grads, grad_mixed, sums,
    w_proj, w_fc, grad_proj, proj_t, mixed_t, acc_proj, acc_fc, grad_temporal, flat, grouped, sem,
):
    chunk.fetch(2, weights, w_fc, sem.at[0])
    chunk.fetch(1, weights, w_proj, sem.at[1])
    regroup(grad_rows[...].astype(f32), flat, grouped, slots)
    grad_temporal[...] = grouped[...].astype(bf16)
    across(projected, proj_t)

    def fc_tile(cols):
        acc_fc[:, cols] = dot(proj_t[...], grad_temporal[:, cols]).astype(bf16)

    tiles(D, fc_tile)
    chunk_back.store(1, weights[0], acc_fc, grads, sem.at[2])
    arrived(w_fc, sem.at[0])

    def fc_back(cols):
        grad_proj[:, cols] = dot_t(grad_temporal[...], w_fc[cols, :]).astype(bf16)

    tiles(D, fc_back)
    across(mixed, mixed_t)

    def proj_tile(cols):
        acc_proj[:, cols] = dot(mixed_t[...], grad_proj[:, cols]).astype(bf16)

    tiles(D, proj_tile)
    chunk_back.store(0, weights[0], acc_proj, grads, sem.at[3])
    arrived(w_proj, sem.at[1])

    def proj_back(cols):
        grad_mixed[:, cols] = dot_t(grad_proj[...], w_proj[cols, :]).astype(bf16)

    tiles(D, proj_back)
    sums[0:1] = column_sum(grad_temporal[...])
    sums[1:2] = column_sum(grad_proj[...])
    sums[2:8] = jnp.zeros((6, D), f32)
    arrived(acc_fc, sem.at[2])
    arrived(acc_proj, sem.at[3])


def temporal_attention_back_kernel(
    chunk, chunk_back, slots, weights, packed, key_ids, query_ids, lse, grad_mixed, rows, grad_temporal,
    small, in_bias, sums_m, sums_s, sums_t, result, class_sum,
    grads, outgoing,
    w, mask, grad_packed, normed, normed_t, grad, total, flat, rows_small, raw, sem,
):
    chunk.fetch(0, weights, w, sem.at[0])
    set_mask(mask, key_ids, query_ids)
    attend_back(
        packed, 0, packed, D, 2 * D, mask, lse, grad_mixed, grad_packed, grad_packed, D, 2 * D
    )
    values = rows[...].astype(f32)
    regroup(norm_rows(values, small, 0), flat, total, slots)
    normed[...] = total[...].astype(bf16)
    across(normed, normed_t)
    arrived(w, sem.at[0])
    qkv_back(normed_t, grad_packed, w, grad, total)
    chunk_back.store(0, weights[0], grad, grads, sem.at[1])
    back, gain, shift = norm_back(values, ungroup(total, flat, slots), small, 0)
    tokens_grad = (grad_temporal[...].astype(f32) + back).astype(bf16)
    frames = outgoing.shape[0]
    rows_each = tokens_grad.shape[0] // frames
    spread = jnp.concatenate([class_sum[...], jnp.zeros_like(class_sum)], axis=0).astype(bf16)
    for f in range(frames):
        here = slice(f * rows_each, (f + 1) * rows_each)
        outgoing[f, :rows_each] = tokens_grad[here]
        outgoing[f, rows_each : 2 * rows_each] = result[here, :]
        outgoing[f, 2 * rows_each :] = spread
    rows_small[...] = jnp.zeros_like(rows_small)
    rows_small[0:4] = in_bias[...]
    for i, (gain_row, shift_row) in enumerate(
        ((gain, shift), (sums_s[0:1], sums_s[1:2]), (sums_m[0:1], sums_m[1:2]))
    ):
        rows_small[GAIN + i : GAIN + i + 1] = gain_row
        rows_small[SHIFT + i : SHIFT + i + 1] = shift_row
    for i, row in enumerate(
        (
            column_sum(grad_packed[:, :D]),
            column_sum(grad_packed[:, 2 * D :]),
            sums_t[1:2],
            sums_t[0:1],
            sums_s[2:3],
            sums_s[3:4],
            sums_m[3:4],
            sums_m[2:3],
        )
    ):
        rows_small[BIAS + i : BIAS + i + 1] = row
    raw[:, :128] = rows_small[...].T.astype(bf16)
    raw[:, 128:] = jnp.zeros((D, 128), bf16)
    chunk_back.store(1, weights[0], raw, grads, sem.at[2])
    arrived(grad, sem.at[1])
    arrived(raw, sem.at[2])


def on_device(
    tokens,
    class_tokens,
    clip_frames,
    cotangent,
    temporal_qkv,
    temporal_proj,
    temporal_fc,
    spatial_qkv,
    spatial_proj,
    mlp_in,
    mlp_out,
    mlp_in_bias,
    norm_gains,
    norm_shifts,
    biases,
):
    frame_size, pos_size = lax.axis_size("frame"), lax.axis_size("pos")
    frame_index, pos_index = lax.axis_index("frame"), lax.axis_index("pos")
    frame_count, pos_count = tokens.shape[1], tokens.shape[2]
    shard = norm_gains.shape[0]
    slots = pos_count + 1
    share = frame_size // MB
    my_slots = slots // share
    all_frames = frame_count * frame_size
    my_frames = all_frames // pos_size
    rows_count = all_frames * my_slots
    micro = frame_index // share

    layout = Layout()
    small = (mlp_in_bias.reshape(1, 4 * shard), norm_gains.T, norm_shifts.T, biases.T)
    keep_t, give_t = pack(layout, (temporal_qkv, temporal_proj, temporal_fc), small)
    got_t = send(give_t, layout.swap)
    keep, give = pack(layout, tie((spatial_qkv, spatial_proj, mlp_in), got_t))
    keep_out, give_out = pack(layout, tie((mlp_out,), got_t))
    got = send(tie(give, give_t), layout.swap)
    got_out = send(tie(give_out, give_t), layout.swap)
    way_t = Gather(layout, layout.chip_rows(keep_t, got_t), {})
    rest = layout.chip_rows(keep, got)
    way_s = Gather(layout, rest[:, : 2 * D], {})
    way_in = Gather(layout, rest[:, 2 * D :], {})
    way_out = Gather(layout, layout.chip_rows(keep_out, got_out), {})
    chunk_t = Chunk(layout, (3 * D, D, D, SMALL), 2 * shard)
    chunk_s = Chunk(layout, (3 * D, D), 2 * shard)
    chunk_in = Chunk(layout, (FF,), 2 * shard)
    chunk_out = Chunk(layout, (D,), 8 * shard)
    chunk_proj = Chunk(layout, (D, D), 2 * shard)
    chunk_qkv = Chunk(layout, (3 * D, SMALL), 2 * shard)
    later = range(1, layout.bits)

    def frame_hop(values):
        return lax.all_to_all(values, "frame", 0, 0, tiled=True)

    def pos_hop(values):
        parts = values.reshape(pos_size, rows_count // pos_size, D)
        return lax.all_to_all(parts, "pos", 0, 0, tiled=True).reshape(rows_count, D)

    def to_temporal(*arrays):
        parts = []
        for values in arrays:
            padded = jnp.pad(values, ((0, 0), (0, 0), (0, 1), (0, 0)))
            padded = padded.reshape(MB, frame_count, share, my_slots, D).transpose(0, 2, 1, 3, 4)
            parts.append(padded.reshape(frame_size, frame_count * my_slots, D))
        hopped = frame_hop(jnp.concatenate(parts, axis=1)).reshape(frame_size, len(arrays), -1, D)
        return [hopped[:, i].reshape(rows_count, D) for i in range(len(arrays))]

    def from_temporal(hopped, count):
        rows, out = frame_count * my_slots, []
        for at in range(0, rows * count, rows):
            part = hopped[:, at : at + rows].reshape(MB, share, frame_count, my_slots, D)
            part = part.transpose(0, 2, 1, 3, 4).reshape(MB, frame_count, slots, D)
            out.append(part[:, :, :pos_count])
        return out + [hopped[:, rows * count :]]

    def partners(values, step):
        perm = [(f, f // share * share + (f % share + step) % share) for f in range(frame_size)]
        return lax.ppermute(values, "frame", perm)

    n = rows_count
    clip_ends = jnp.cumsum(lax.dynamic_index_in_dim(clip_frames, micro, 0, keepdims=False))
    clip_of = lambda frame: jnp.sum(
        (frame[:, None] >= clip_ends[None, :]).astype(jnp.int32), axis=1
    )
    size_t = all_frames * max(1, 128 // all_frames)
    ids = jnp.arange(size_t, dtype=jnp.int32)
    ids = ids // all_frames * CLIPS + clip_of(ids % all_frames)
    ids_t = [(ids[:, None], "v"), (jnp.tile(ids, 2)[None, :], "v")]
    frame_rows = n // my_frames
    size_s = frame_rows * max(1, 128 // frame_rows)
    row_ids = jnp.arange(n, dtype=jnp.int32)
    frame_s, row_slot = row_ids // frame_rows, row_ids % my_slots
    first_source = row_ids % frame_rows < my_slots

    def key_masks(share_index):
        padding = row_slot + share_index * my_slots == slots - 1
        is_class = padding & first_source
        return is_class, is_class | ~padding

    keys_s = []
    for step in range(share):
        _, valid = key_masks((frame_index + share - step) % share)
        keys_s.append(jnp.where(valid, frame_s, -1)[:size_s])
    ids_s = [
        (jnp.concatenate(keys_s)[:, None], "v"),
        (jnp.tile(frame_s[:size_s], 2)[None, :], "v"),
    ]
    is_class, _ = key_masks(frame_index % share)
    clip_s = clip_of(pos_index * my_frames + frame_s)
    choose = (clip_s[:, None] == jnp.arange(8)[None, :]) & is_class[:, None]
    choose = (choose.astype(bf16), "v")
    class_rows = lax.dynamic_index_in_dim(class_tokens, micro, 0, keepdims=False)
    class_rows = (jnp.pad(class_rows, ((0, 8 - CLIPS), (0, 0))), "v")
    is_class = (is_class.astype(jnp.int32)[:, None], "v")

    narrow, wide, full = (n, D), (n, 3 * D), (n, FF)
    heads = lambda size: (-(-HEADS // 2 * (n // size) // 8) * 8, 2 * size)
    columns = (D // 128, n, 128)
    lse_shape_t, lse_shape_s = heads(size_t), heads(size_s)
    mask_t, mask_s = (size_t, 2 * size_t), (share * size_s, 2 * size_s)
    flops = lambda columns: 2 * n * D * columns

    some, others, every = layout.some, layout.others, layout.steps
    way_t.along(every)
    rows, grad_out = to_temporal(*tie((tokens, cotangent), give))
    rows, grad_out = meet(way_t, way_s, way_in, way_out, rows, grad_out)
    way_t.across(0)
    way_s.along(every)
    meet(way_t, way_s)
    for step in later:
        way_t.across(step)
    way_t.swap(1)
    grad_out = pos_hop(grad_out)
    way_in.state, grad_out = meet(way_t, way_in.state, grad_out)
    way_t.swap()
    way_s.across(0)
    way_in.along(every)
    packed_t, small_t = call(
        "temporal_qkv",
        partial(temporal_qkv_kernel, chunk_t, my_slots),
        chunk_t.load(way_t).operands() + [(rows, "v")],
        [(wide, bf16, "v"), ((32, D), f32, "v")],
        [((D, 3 * D), bf16), ((D, SMALL), bf16), (narrow, bf16), ((1, 3 * D), f32)]
        + [(columns, f32), (narrow, f32)],
        2,
        flops(3 * D),
    )
    packed_t, small_t = meet(way_s, way_in, packed_t, small_t)
    small = (small_t, "v")
    for step in later:
        way_s.across(step)
    way_s.swap(1)
    way_out.along(every)
    mixed_t, projected, lse_t, temporal = call(
        "temporal_mix",
        partial(temporal_mix_kernel, chunk_t, my_slots),
        chunk_t.operands() + [(packed_t, "w"), (rows, "w")] + ids_t + [small],
        [(narrow, bf16, "v"), (narrow, bf16, "v"), (lse_shape_t, f32, "v"), (narrow, bf16, "v")],
        [((D, D), bf16), ((D, D), bf16), (mask_t, f32), (narrow, f32), (columns, f32)],
        2,
        flops(2 * D + 4 * n),
    )
    temporal, grad_out, small_t = meet(way_s, way_in, way_out, temporal, grad_out, small_t)
    temporal = pos_hop(temporal)
    way_s.swap()
    way_in.across(0)
    in_bias = small_t[:4].reshape(4, -1, shard).transpose(1, 0, 2).reshape(1, FF)
    grad_out = grad_out.reshape(pos_size, my_frames, my_slots, D)
    grad_out = grad_out.transpose(1, 0, 2, 3).reshape(n, D)
    for step in later:
        way_in.across(step)
    temporal, in_bias, grad_out = meet(way_s, way_out, temporal, in_bias, grad_out)
    way_out.across(0)
    small = (small_t, "v")
    way_in.swap(1)
    temporal, packed_s = call(
        "spatial_qkv",
        partial(spatial_qkv_kernel, chunk_s, pos_size, my_frames),
        chunk_s.load(way_s).operands() + [(temporal, "w"), choose, class_rows, is_class, small],
        [(narrow, bf16, "v"), (wide, bf16, "v")],
        [((D, 3 * D), bf16), (narrow, bf16), ((1, 3 * D), f32)] + [(narrow, f32)] * 2,
        1,
        flops(3 * D),
    )
    temporal = (temporal, "v")
    pairs, k_at = packed_s, D
    if share > 1:
        pairs = [packed_s[:, D:]]
        for step in range(1, share):
            pairs.append(partners(packed_s[:, D:], step))
        pairs, k_at = jnp.concatenate(pairs, axis=0), 0
    all_keys = share * n
    mixed_s, lse_s, spatial = call(
        "spatial_mix",
        partial(spatial_mix_kernel, chunk_s, k_at),
        chunk_s.operands() + [(packed_s, "v"), (pairs, "v")] + ids_s + [temporal, small],
        [(narrow, bf16, "v"), (lse_shape_s, f32, "v"), (narrow, f32, "v")],
        [((D, D), bf16), (mask_s, f32)],
        1,
        flops(D + 4 * all_keys),
    )
    for step in later:
        way_out.across(step)
    spatial = meet(way_in, spatial)
    way_in.swap()
    spatial = meet(way_in, spatial)
    spatial, grad_out = (spatial, "v"), (grad_out, "v")
    way_out.swap(1)
    in_bias = (in_bias, "v")
    normed_m, activated, slope, acc_out = call(
        "hidden",
        partial(hidden_kernel, chunk_in, chunk_out),
        chunk_in.load(way_in).operands()
        + [(chunk_out.index, "s"), spatial, in_bias, small, grad_out],
        [(narrow, bf16, "v"), (full, bf16, "v"), (full, bf16, "v")] + chunk_out.grads(),
        [((D, FF), bf16), ((FF, D), bf16)],
        2,
        flops(2 * FF),
    )
    activated = (activated, "v")
    acc_out, slope = meet(way_out, acc_out, slope)
    way_out.swap()
    back_out = chunk_out.scatter(*acc_out)
    slope = meet(way_out, back_out, slope)
    for step in reversed(later):
        back_out.across(step)
    result, grad_hidden, grad_in_bias, grad_spatial, sums_m = call(
        "mlp_back",
        partial(mlp_back_kernel, chunk_in, chunk_out, pos_size, my_frames),
        chunk_in.operands()
        + chunk_out.load(way_out).operands()
        + [grad_out, (slope, "v"), spatial, activated, small],
        [(narrow, bf16, "v"), (full, bf16, "v"), ((1, FF), f32, "v"), (narrow, f32, "v"), ((8, D), f32, "v")],
        [((D, FF), bf16), ((FF, D), bf16), (narrow, f32), (narrow, f32)],
        2,
        flops(3 * FF),
    )
    grad_hidden, grad_in_bias, result = meet(back_out, grad_hidden, grad_in_bias, result)
    back_out.across(0)
    (acc_in,) = call(
        "mlp_in_grad",
        partial(in_grad_kernel, chunk_in),
        [(chunk_in.index, "s"), (normed_m, "v"), (grad_hidden, "v")],
        chunk_in.grads(),
        [((D, n), bf16), ((D, FF), bf16)],
        1,
        flops(FF),
    )
    acc_in, grad_spatial = meet(back_out, acc_in, grad_spatial)
    back_in = chunk_in.scatter(*acc_in)
    back_out.sums()
    back_out.along(some)
    grad_spatial = (grad_spatial, "v")
    acc_sproj, grad_query, grad_pairs = call(
        "spatial_attention_back",
        partial(spatial_attention_back_kernel, chunk_s, k_at),
        chunk_s.operands()
        + [grad_spatial, (mixed_s, "v"), (packed_s, "v"), (pairs, "v")]
        + ids_s
        + [(lse_s, "v")],
        [((D, D), bf16, "v"), (narrow, bf16, "v"), ((all_keys, 2 * D), bf16, "v")],
        [((D, D), bf16), (narrow, bf16), ((D, n), bf16), (narrow, bf16)]
        + [(mask_s, f32)],
        2,
        flops(2 * D + 10 * all_keys),
    )
    grad_query, result = meet(back_in, back_out, grad_query, result)
    for step in reversed(later):
        back_in.across(step)
    result = pos_hop(result)
    own_pairs = grad_pairs[:n]
    for step in range(1, share):
        theirs = partners(grad_pairs[step * n : (step + 1) * n], share - step)
        own_pairs = (own_pairs.astype(f32) + theirs.astype(f32)).astype(bf16)
    acc_s, grad_temporal, class_part, sums_s = call(
        "spatial_qkv_back",
        partial(spatial_qkv_back_kernel, chunk_s, pos_size, my_frames),
        chunk_s.operands()
        + [(acc_sproj, "w"), (grad_query, "w"), (own_pairs, "w")]
        + [(temporal[0], "w"), (grad_spatial[0], "w"), choose, is_class, small],
        chunk_s.grads() + [(narrow, bf16, "v"), ((8, D), f32, "v"), ((8, D), f32, "v")],
        [((D, 3 * D), bf16), (wide, bf16), (narrow, bf16), ((D, n), bf16)]
        + [((D, 3 * D), bf16), (narrow, f32), (narrow, f32)],
        3,
        flops(6 * D),
    )
    acc_s, grad_temporal, class_part, grad_in_bias, result = meet(
        back_in, acc_s, grad_temporal, class_part, grad_in_bias, result
    )
    back_s = chunk_s.scatter(*acc_s)
    grad_temporal = pos_hop(grad_temporal)
    back_in.across(0)
    class_sum = class_part + send(class_part, layout.within[0])
    block_in_bias = grad_in_bias.reshape(-1, 4, shard).transpose(1, 0, 2).reshape(4, D)
    grad_temporal, block_in_bias, class_sum = meet(
        back_s, back_in, back_out, grad_temporal, block_in_bias, class_sum
    )
    for step in reversed(later):
        back_s.across(step)
    back_in.sums()
    back_in.along(some)
    back_out.along(others)
    class_sum = class_sum + send(class_sum, layout.within[1])
    grad_temporal = (grad_temporal, "v")
    acc_proj, grad_mixed_t, sums_t = call(
        "temporal_proj_back",
        partial(temporal_proj_back_kernel, chunk_t, chunk_proj, my_slots),
        chunk_t.operands()
        + [grad_temporal, (projected, "v"), (mixed_t, "v")],
        chunk_proj.grads() + [(narrow, bf16, "v"), ((8, D), f32, "v")],
        [((D, D), bf16), ((D, D), bf16), (narrow, bf16), ((D, n), bf16), ((D, n), bf16)]
        + [((D, D), bf16), ((D, D), bf16), (narrow, bf16), (columns, f32), (narrow, f32)],
        4,
        flops(4 * D),
    )
    acc_proj, grad_mixed_t, class_sum = meet(
        back_s, back_in, back_out, acc_proj, grad_mixed_t, class_sum
    )
    back_proj = chunk_proj.scatter(*acc_proj)
    for perm in layout.within[2:]:
        class_sum = class_sum + send(class_sum, perm)
    grad_mixed_t, class_sum = meet(back_proj, grad_mixed_t, class_sum)
    for step in reversed(later):
        back_proj.across(step)
    back_s.across(0)
    back_in.along(others)
    acc_qkv, outgoing = call(
        "temporal_attention_back",
        partial(temporal_attention_back_kernel, chunk_t, chunk_qkv, my_slots),
        chunk_t.operands()
        + [(packed_t, "v")]
        + ids_t
        + [(lse_t, "v"), (grad_mixed_t, "v"), (rows, "v"), grad_temporal, small]
        + [(block_in_bias, "v"), (sums_m, "v"), (sums_s, "v"), (sums_t, "v")]
        + [(result, "v"), (class_sum, "v")],
        chunk_qkv.grads() + [((frame_size, 2 * n // frame_size + 16, D), bf16, "v")],
        [((D, 3 * D), bf16), (mask_t, f32), (wide, bf16), (narrow, bf16), ((D, n), bf16)]
        + [((D, 3 * D), bf16), (narrow, f32), (columns, f32), ((128, D), f32), ((D, SMALL), bf16)],
        3,
        flops(6 * D + 10 * n),
    )
    acc_qkv, outgoing = meet(back_s, back_in, back_proj, acc_qkv, outgoing)
    back_qkv = chunk_qkv.scatter(*acc_qkv)
    back_proj.across(0)
    back_s.sums()
    meet(back_qkv, back_proj, back_s)
    for step in reversed(later):
        back_qkv.across(step)
    back_s.along(every)
    back_proj.sums()
    back_proj.along(some)
    hopped = frame_hop(outgoing)
    meet(back_qkv, back_s, back_proj)
    back_qkv.across(0)
    back_proj.along(others)
    hopped = meet(back_qkv, back_proj, hopped)
    back_qkv.sums("x")
    back_qkv.along(every)
    own = back_qkv.state[0]
    for way in (back_in, back_s, back_proj, back_out):
        way.state = tie(way.state, own)
    most = Return(layout, [back_in, back_s, back_proj, back_out], "w")
    tokens_grad, block_out, class_all = from_temporal(tie(hopped, back_qkv.state[1][1]), 2)
    tokens_grad = tokens_grad.astype(f32)
    class_grad = class_all[::share, :CLIPS].astype(f32)
    tokens_grad, block_out, class_grad = meet(back_qkv, tokens_grad, block_out, class_grad)
    last = Return(layout, [back_qkv], "x")
    (
        acc_in, acc_sqkv, acc_sproj, acc_tproj, acc_tfc, acc_out,
        acc_tqkv, in_bias_grad, gains_grad, shifts_grad, biases_grad,
    ) = finish(
        layout,
        [most, last],
        [
            [(shard, FF), (shard, 3 * D), (shard, D), (shard, D), (shard, D), (4 * shard, D)],
            [(shard, 3 * D), (shard, SMALL)],
        ],
    )
    return (
        block_out,
        tokens_grad,
        class_grad,
        acc_tqkv,
        acc_tproj,
        acc_tfc,
        acc_sqkv,
        acc_sproj,
        acc_in,
        acc_out,
        in_bias_grad.reshape(-1),
        gains_grad.T,
        shifts_grad.T,
        biases_grad.T,
    )


def solution(mesh):
    rows = P(AXES, None)
    wide = P(None, "frame", "pos", None)
    placed = (wide, P(), P(), wide) + (rows,) * 7 + (P(AXES),) + (rows,) * 3
    return jax.shard_map(
        on_device,
        mesh=mesh,
        in_specs=placed,
        out_specs=(wide, wide, P()) + (rows,) * 7 + (P(AXES),) + (rows,) * 3,
        check_vma=False,
    )
```
